32 devices in a mesh: seq: 32 (over z, y, x, core).
Axes of the slice: x: 2, y: 2, z: 4, core: 2. Of those that a mesh axis runs over, the one named last changes fastest.
Arguments:
- hidden_in: bfloat16 [8192, 1024], P('seq'), may hold values from -6 to 6
- doc_start: int32 [8192], P('seq'), may hold values from 0 to 8191, as said below
- norm_gain: float32 [1024], replicated, may hold values from 0.5 to 1.5
- w_z: bfloat16 [1024, 1536], P('seq'), may hold values from -0.1875 to 0.1875
- w_xbc: bfloat16 [1024, 1792], P('seq'), may hold values from -0.1875 to 0.1875
- w_dt: bfloat16 [1024, 24], P('seq'), may hold values from -0.1875 to 0.1875
- conv_weight: float32 [4, 1792], replicated, may hold values from -3 to 3
- conv_bias: float32 [1792], replicated, may hold values from -3 to 3
- dt_bias: float32 [24], replicated, may hold values from -4 to 0
- a_log: float32 [24], replicated, may hold values from -9 to -2
- d_skip: float32 [24], replicated, may hold values from 0.5 to 1.5
- ssm_gain: float32 [1536], replicated, may hold values from 0.5 to 1.5
- w_ssm_out: bfloat16 [1536, 1024], P('seq'), may hold values from -0.15625 to 0.15625
- w_q: bfloat16 [1024, 512], P('seq'), may hold values from -0.1875 to 0.1875
- w_kv: bfloat16 [1024, 256], P('seq'), may hold values from -0.1875 to 0.1875
- w_o: bfloat16 [512, 1024], P('seq'), may hold values from -3 to 3
- ffn_gain: float32 [1024], replicated, may hold values from 0.5 to 1.5
- w_gate: bfloat16 [1024, 2048], P('seq'), may hold values from -0.1875 to 0.1875
- w_up: bfloat16 [1024, 2048], P('seq'), may hold values from -0.1875 to 0.1875
- w_down: bfloat16 [2048, 1024], P('seq'), may hold values from -0.125 to 0.125
- cotangent: bfloat16 [8192, 1024], P('seq'), may hold values from -6 to 6
Outputs:
- layer_out: bfloat16 [8192, 1024], P('seq')
- grad_input: bfloat16 [8192, 1024], P('seq')
- grad_norm_gain: float32 [1024], replicated
- grad_w_z: float32 [1024, 1536], P('seq')
- grad_w_xbc: float32 [1024, 1792], P('seq')
- grad_w_dt: float32 [1024, 24], P('seq')
- grad_conv_weight: float32 [4, 1792], replicated
- grad_conv_bias: float32 [1792], replicated
- grad_dt_bias: float32 [24], replicated
- grad_a_log: float32 [24], replicated
- grad_d_skip: float32 [24], replicated
- grad_ssm_gain: float32 [1536], replicated
- grad_w_ssm_out: float32 [1536, 1024], P('seq')
- grad_w_q: float32 [1024, 512], P('seq')
- grad_w_kv: float32 [1024, 256], P('seq')
- grad_w_o: float32 [512, 1024], P('seq')
- grad_ffn_gain: float32 [1024], replicated
- grad_w_gate: float32 [1024, 2048], P('seq')
- grad_w_up: float32 [1024, 2048], P('seq')
- grad_w_down: float32 [2048, 1024], P('seq')
The draws below stay inside these ranges and needn't reach their ends.
Inputs may be any that keep to these rules, and one draw needn't show every extreme that they name: doc_start[t] is the position of the first token of the document that holds token t: it never falls along the tokens and is at most t. One document begins on the first device and ends on the last.
All inputs are finite; a program needn't handle non-finite values.
Results may differ from the reference program's by a relative error of at most 0.03.
The reference program's roundings to bfloat16 on the way count: a program that leaves them out, or rounds other values in their place, can miss the bound.
Values may be sent and summed in bfloat16 or wider, within the bound.
A program may use at most 320 MiB of HBM per device.

```python
import jax
import jax.numpy as jnp
from jax import lax

D = 1024
FF = 2048
MHEADS = 24
MHEAD_DIM = 64
STATE = 128
CONV = 4
QHEADS = 8
KVHEADS = 2
HEAD_DIM = 64
TOK_DEV = 256
SSM = 1536
XBC = 1792
QW = 512
KVW = 256
TOKENS = 8192


def draw_doc_start(key, part):
    key = jax.random.fold_in(key, 7)
    key_one, key_two, key_three = jax.random.split(key, 3)
    long_start = jax.random.randint(key_one, (), 2, TOK_DEV)
    inner_start = jax.random.randint(key_two, (), 1, long_start)
    tail_start = TOKENS - jax.random.randint(key_three, (), 1, TOK_DEV)
    positions = jnp.arange(TOKENS, dtype=jnp.int32)
    starts = jnp.where(positions >= tail_start, tail_start, jnp.where(positions >= long_start, long_start, jnp.where(positions >= inner_start, inner_start, 0)))
    return starts.astype(jnp.int32)


def block_scale(stream_key, extent, pieces, least, high):
    gain = 1.0
    for position, blocks in pieces:
        heights = jax.random.uniform(jax.random.fold_in(jax.random.fold_in(stream_key, 6), position), (blocks,), jnp.float32, least / len(pieces), high / len(pieces))
        gain = gain * jnp.repeat(jnp.exp(heights), extent[position] // blocks).reshape((-1,) + (1,) * (len(extent) - 1 - position))
    return gain


def centred(own_key, shape, scale, most, cuts=(), kind=jnp.bfloat16):
    entries = jax.random.normal(own_key, shape, jnp.float32) * scale
    if len(cuts) > 0:
        entries = block_scale(own_key, shape, cuts, -0.22, 0.18) * entries
    return jnp.clip(entries, min=-most, max=most).astype(kind)


def setup_inputs(seed: int = 0) -> dict:
    streams_of = jax.random.split(jax.random.key(seed), 22)
    return {
        "hidden_in": centred(streams_of[0], (TOKENS, D), 1.0, 6.0, ((0, 32),)),
        "doc_start": draw_doc_start(jax.random.fold_in(streams_of[21], 71), 0),
        "norm_gain": jnp.clip(1.0 + 0.1 * jax.random.normal(streams_of[2], (D,), jnp.float32), 0.5, 1.5),
        "w_z": centred(streams_of[3], (D, SSM), D ** -0.5, 0.1875, ((0, 32),)),
        "w_xbc": centred(streams_of[4], (D, XBC), D ** -0.5, 0.1875, ((0, 32),)),
        "w_dt": centred(streams_of[5], (D, MHEADS), D ** -0.5, 0.1875, ((0, 32),)),
        "conv_weight": centred(streams_of[6], (CONV, XBC), CONV ** -0.5, 3.0, (), jnp.float32),
        "conv_bias": centred(streams_of[7], (XBC,), 0.5, 3.0, (), jnp.float32),
        "dt_bias": jnp.clip(jax.random.uniform(streams_of[8], (MHEADS,), jnp.float32, -4.0, 0.0), -4.0, 0.0),
        "a_log": jnp.clip(jax.random.uniform(streams_of[9], (MHEADS,), jnp.float32, -9.0, -2.0), -9.0, -2.0),
        "d_skip": jnp.clip(jax.random.uniform(streams_of[10], (MHEADS,), jnp.float32, 0.5, 1.5), 0.5, 1.5),
        "ssm_gain": jnp.clip(1.0 + 0.1 * jax.random.normal(streams_of[11], (SSM,), jnp.float32), 0.5, 1.5),
        "w_ssm_out": centred(streams_of[12], (SSM, D), SSM ** -0.5, 0.15625, ((0, 32),)),
        "w_q": centred(streams_of[13], (D, QW), D ** -0.5, 0.1875, ((0, 32),)),
        "w_kv": centred(streams_of[14], (D, KVW), D ** -0.5, 0.1875, ((0, 32),)),
        "w_o": centred(streams_of[15], (QW, D), 4 ** -0.5, 3.0, ((0, 32),)),
        "ffn_gain": jnp.clip(1.0 + 0.1 * jax.random.normal(streams_of[16], (D,), jnp.float32), 0.5, 1.5),
        "w_gate": centred(streams_of[17], (D, FF), D ** -0.5, 0.1875, ((0, 32),)),
        "w_up": centred(streams_of[18], (D, FF), D ** -0.5, 0.1875, ((0, 32),)),
        "w_down": centred(streams_of[19], (FF, D), FF ** -0.5, 0.125, ((0, 32),)),
        "cotangent": centred(streams_of[20], (TOKENS, D), 1.0, 6.0, ((0, 32),)),
    }


epsilon = 1e-05
rope_base = 100000000000.0
masked = -1e+30
highest = lax.Precision.HIGHEST

@jax.custom_vjp
def low(v):
    return lax.optimization_barrier(v.astype(jnp.bfloat16)).astype(jnp.float32)

@jax.custom_vjp
def low_back(v):
    return v

def low_keep(v):
    return (low(v), None)

def low_pass(kept, grad):
    return (grad,)

def back_keep(v):
    return (v, None)

def back_low(kept, grad):
    return (low(grad),)
low.defvjp(low_keep, low_pass)
low_back.defvjp(back_keep, back_low)

def product(left_side, right_side):
    return jnp.dot(left_side, right_side, precision=highest)

def rms_scale(values, gain_vec):
    return values * lax.rsqrt(lax.optimization_barrier(jnp.mean(values * values, axis=-1, keepdims=True)) + epsilon) * gain_vec

def rotate(values, positions, direction):
    row_count = values.shape[0]
    halves = values.reshape(row_count, -1, 2, HEAD_DIM // 2)
    frequency = rope_base ** (-jnp.arange(HEAD_DIM // 2, dtype=jnp.float32) / (HEAD_DIM // 2))
    angles = positions.astype(jnp.float32)[:, None] * frequency[None, :]
    cosine_part = jnp.cos(angles)[:, None, :]
    sine_part = direction * jnp.sin(angles)[:, None, :]
    first_half = halves[:, :, 0]
    second_half = halves[:, :, 1]
    rotated = jnp.stack([first_half * cosine_part - second_half * sine_part, second_half * cosine_part + first_half * sine_part], axis=2)
    return rotated.reshape(values.shape)

def conv_apply(extended, tap_weights, tap_bias, starts, offset):
    row_count = extended.shape[0] - (CONV - 1)
    places = offset + jnp.arange(row_count, dtype=jnp.int32)
    summed = jnp.zeros((row_count, extended.shape[1]), jnp.float32) + tap_bias[None, :]
    for tap_index in range(CONV):
        lag_rows = CONV - 1 - tap_index
        keep_tap = (places - lag_rows >= starts)[:, None]
        summed = summed + jnp.where(keep_tap, extended[tap_index:tap_index + row_count] * tap_weights[tap_index][None, :], 0.0)
    return jax.nn.silu(summed)

def decay_terms(dt_raw, dt_bias, a_log):
    step_dt = jax.nn.softplus(dt_raw + dt_bias[None, :])
    log_decay = jnp.cumsum(-step_dt * jnp.exp(a_log)[None, :], axis=0)
    return (step_dt, log_decay)

def block_summary(mixed_in, dt_raw, dt_bias, a_log, starts, offset):
    row_count = mixed_in.shape[0]
    ssm_x = mixed_in[:, :SSM].reshape(row_count, MHEADS, MHEAD_DIM)
    input_b = mixed_in[:, SSM:SSM + STATE]
    step_dt, log_decay = decay_terms(dt_raw, dt_bias, a_log)
    places = offset + jnp.arange(row_count, dtype=jnp.int32)
    end_keep = (places >= starts[row_count - 1])[:, None]
    end_weight = jnp.exp(jnp.where(end_keep, log_decay[row_count - 1][None, :] - log_decay, masked)) * step_dt
    local_state = jnp.einsum('shp,sn->hpn', ssm_x * end_weight[:, :, None], input_b, precision=highest)
    passing = jnp.exp(log_decay[row_count - 1]) * (starts[row_count - 1] < offset).astype(jnp.float32)
    return (passing, local_state)

def block_output(mixed_in, dt_raw, dt_bias, a_log, d_skip, states_in, starts, offset):
    row_count = mixed_in.shape[0]
    ssm_x = mixed_in[:, :SSM].reshape(row_count, MHEADS, MHEAD_DIM)
    input_b = mixed_in[:, SSM:SSM + STATE]
    output_c = mixed_in[:, SSM + STATE:]
    step_dt, log_decay = decay_terms(dt_raw, dt_bias, a_log)
    places = offset + jnp.arange(row_count, dtype=jnp.int32)
    row_order = jnp.arange(row_count, dtype=jnp.int32)
    same_doc = (places[None, :] >= starts[:, None]) & (row_order[None, :] <= row_order[:, None])
    affinity = jnp.dot(output_c, input_b.T, precision=highest)
    log_t = log_decay.T
    decay_gap = jnp.where(same_doc[None, :, :], log_t[:, :, None] - log_t[:, None, :], masked)
    mixing = affinity[None, :, :] * jnp.exp(decay_gap) * step_dt.T[:, None, :]
    inner_terms = jnp.einsum('hts,shp->thp', mixing, ssm_x, precision=highest)
    carried = jnp.exp(log_decay) * (starts < offset).astype(jnp.float32)[:, None]
    from_prev = jnp.einsum('hpn,tn->thp', states_in, output_c, precision=highest) * carried[:, :, None]
    return inner_terms + from_prev + d_skip[None, :, None] * ssm_x

def gated_norm(ssm_values, gate_values, gain_vec):
    return rms_scale(ssm_values * jax.nn.silu(gate_values), gain_vec)

def forward(values, starts, params):
    norm_gain, w_z, w_xbc, w_dt, conv_weight, conv_bias, dt_bias, a_log, d_skip, ssm_gain, w_ssm_out, w_q, w_kv, w_o, ffn_gain, w_gate, w_up, w_down = params
    token_count = values.shape[0]
    positions = jnp.arange(token_count, dtype=jnp.int32)
    normed_one = low(rms_scale(values, norm_gain))
    gate_z = low_back(product(normed_one, w_z))
    xbc_raw = low(low_back(product(normed_one, w_xbc)))
    dt_raw = low_back(product(normed_one, w_dt))
    query_raw = low_back(product(normed_one, w_q))
    kv_raw = low_back(product(normed_one, w_kv))
    half_kv = KVW // 2
    queries = low(rotate(query_raw, positions, 1.0))
    key_rows = low(rotate(kv_raw[:, :half_kv], positions, 1.0))
    value_rows = low(kv_raw[:, half_kv:])
    extended = jnp.concatenate([jnp.zeros((CONV - 1, XBC), jnp.float32), xbc_raw], axis=0)
    conv_out = conv_apply(extended, conv_weight, conv_bias, starts, 0)
    block_count = token_count // TOK_DEV
    scan_items = (conv_out.reshape(block_count, TOK_DEV, XBC), dt_raw.reshape(block_count, TOK_DEV, MHEADS), starts.reshape(block_count, TOK_DEV), jnp.arange(block_count, dtype=jnp.int32) * TOK_DEV)

    def block_step(state_now, scan_item):
        conv_part, dt_part, start_part, first_part = scan_item
        passing, local_state = block_summary(conv_part, dt_part, dt_bias, a_log, start_part, first_part)
        output = block_output(conv_part, dt_part, dt_bias, a_log, d_skip, state_now, start_part, first_part)
        return (passing[:, None, None] * state_now + local_state, output)
    state_zero = jnp.zeros((MHEADS, MHEAD_DIM, STATE), jnp.float32)
    state_last, ssm_blocks = lax.scan(jax.checkpoint(block_step), state_zero, scan_items)
    ssm_flat = ssm_blocks.reshape(token_count, SSM)
    normed_ssm = low(gated_norm(ssm_flat, gate_z, ssm_gain))
    ssm_branch = product(normed_ssm, w_ssm_out)
    group_size = QHEADS // KVHEADS
    key_heads = key_rows.reshape(token_count, KVHEADS, HEAD_DIM)
    value_heads = value_rows.reshape(token_count, KVHEADS, HEAD_DIM)
    scale = HEAD_DIM ** (-0.5)
    attend_items = (queries.reshape(block_count, TOK_DEV, KVHEADS, group_size, HEAD_DIM), positions.reshape(block_count, TOK_DEV), starts.reshape(block_count, TOK_DEV))

    def attend_block(scan_item):
        query_block, query_pos, query_starts = scan_item
        scores = jnp.einsum('tgrd,ngd->grtn', query_block, key_heads, precision=highest) * scale
        scores = low_back(scores)
        allowed = (positions[None, :] <= query_pos[:, None]) & (positions[None, :] >= query_starts[:, None])
        scores = jnp.where(allowed[None, None], scores, masked)
        top_score = lax.optimization_barrier(jnp.max(scores, axis=-1, keepdims=True))
        expo = jnp.where(allowed[None, None], jnp.exp(scores - top_score), 0.0)
        row_sum = lax.optimization_barrier(jnp.sum(expo, axis=-1, keepdims=True))
        mixed = jnp.einsum('grtn,ngd->tgrd', low(expo), value_heads, precision=highest)
        return mixed / jnp.transpose(row_sum, (2, 0, 1, 3))
    attention = lax.map(jax.checkpoint(attend_block), attend_items).reshape(token_count, QW)
    attention = low(low_back(attention))
    attn_branch = product(attention, w_o)
    after_mix = values + low_back(ssm_branch + attn_branch)
    normed_two = low(rms_scale(after_mix, ffn_gain))
    gate_pre = low_back(product(normed_two, w_gate))
    up_pre = low_back(product(normed_two, w_up))
    activated = low(jax.nn.silu(gate_pre) * up_pre)
    return after_mix + product(activated, w_down)

def reference(hidden_in, doc_start, norm_gain, w_z, w_xbc, w_dt, conv_weight, conv_bias, dt_bias, a_log, d_skip, ssm_gain, w_ssm_out, w_q, w_kv, w_o, ffn_gain, w_gate, w_up, w_down, cotangent):
    params = tuple((weight_item.astype(jnp.float32) for weight_item in (norm_gain, w_z, w_xbc, w_dt, conv_weight, conv_bias, dt_bias, a_log, d_skip, ssm_gain, w_ssm_out, w_q, w_kv, w_o, ffn_gain, w_gate, w_up, w_down)))
    inputs32 = hidden_in.astype(jnp.float32)

    def run_layer(values, weight_set):
        return forward(values, doc_start, weight_set)
    result, pullback = jax.vjp(run_layer, inputs32, params)
    grad_values, grads = pullback(cotangent.astype(jnp.float32))
    return (result.astype(jnp.bfloat16), grad_values.astype(jnp.bfloat16), grads[0], grads[1], grads[2], grads[3], grads[4], grads[5], grads[6], grads[7], grads[8], grads[9], grads[10], grads[11], grads[12], grads[13], grads[14], grads[15], grads[16], grads[17])
```

```python
from functools import partial
import math

import jax
import jax.numpy as jnp
from jax import lax
from jax.experimental import pallas as pl
from jax.experimental.pallas import tpu as pltpu
from jax.sharding import PartitionSpec as P
import numpy as np

MHEADS = 24
MHEAD_DIM = 64
STATE = 128
CONV = 4
QHEADS = 8
KVHEADS = 2
HEAD_DIM = 64
SSM = 1536
XBC = 1792
QW = 512
KVW = 256
DT_PAD = 128


epsilon = 1e-05
rope_base = 100000000000.0
masked = -1e30


def from_behind(value, axis, steps):
    count = lax.axis_size(axis)
    first, last = (max(0, -steps), min(count, count - steps))
    return lax.ppermute(value, axis, [(source, source + steps) for source in range(first, last)])


MESH = pl.DeviceIdType.MESH


def lattice(count):
    sizes, left, turn = [1, 1, 1], count // 2, 0
    while left > 1:
        factor = 2 if left % 2 == 0 else left
        sizes[turn % 3] *= factor
        left //= factor
        turn += 1
    return sizes[0], sizes[1], sizes[2], 2


def coordinates(sizes):
    me = lax.axis_index("seq")
    _, size_1, size_2, cores = sizes
    return (
        me // (size_1 * size_2 * cores),
        me // (size_2 * cores) % size_1,
        me // cores % size_2,
        me % cores,
    )


def device_at(sizes, place):
    index = place[0]
    for size, at in zip(sizes[1:], place[1:]):
        index = index * size + at
    return index


def partners(sizes, place, axis):
    found = []
    for step in range(1, sizes[axis]):
        other = list(place)
        other[axis] = (place[axis] + step) % sizes[axis]
        found.append(other)
    return found


def greet(sizes, place, more=()):
    barrier = pltpu.get_barrier_semaphore()
    met = [
        device_at(sizes, other) for axis in range(4) for other in partners(sizes, place, axis)
    ] + list(more)
    for other in met:
        pl.semaphore_signal(barrier, inc=1, device_id=(other,), device_id_type=MESH)
    pl.semaphore_wait(barrier, len(met))


def block_cuts(shapes, target):
    cuts = []
    for number, (rows, columns) in enumerate(shapes):
        pieces = max(1, round(rows * columns / target))
        width = max(128, (columns // pieces + 127) // 128 * 128)
        across = -(-columns // width)
        height = rows
        if across < pieces and rows % 32 == 0:
            height = max(32, rows // -(-pieces // across) // 32 * 32)
        for top in range(0, rows, height):
            for start in range(0, columns, width):
                size = (min(height, rows - top), min(width, columns - start))
                cuts.append((number, (pl.ds(top, size[0]), pl.ds(start, size[1]))))
    return cuts


def gather_everywhere(arrays, collective_id, target, edge=None):
    sizes = lattice(lax.axis_size("seq"))
    cuts = block_cuts([array.shape for array in arrays], target)
    kinds = len(arrays)
    most = max(sizes[:3])
    extra = 0 if edge is None else 1

    def kernel(*refs):
        ins, refs = refs[:kinds], refs[kinds:]
        edge_in, refs = refs[:extra], refs[extra:]
        outs, refs = refs[:kinds], refs[kinds:]
        edge_out, refs = refs[:extra], refs[extra:]
        local_sem, send_sem, recv_sem, edge_sems = refs
        place = coordinates(sizes)
        sent = []

        def region(cut, at):
            number, window = cut
            return outs[number].at[*at, *window]

        def push(cut, at, other, slot, source=None):
            copy = pltpu.make_async_remote_copy(
                src_ref=region(cut, at) if source is None else source,
                dst_ref=region(cut, at),
                send_sem=send_sem.at[slot],
                recv_sem=recv_sem.at[slot],
                device_id=(device_at(sizes, other),),
                device_id_type=MESH,
            )
            copy.start()
            sent.append(copy)

        def arrival(cut, at, slot):
            here = region(cut, at)
            pltpu.make_async_remote_copy(
                src_ref=here,
                dst_ref=here,
                send_sem=send_sem.at[slot],
                recv_sem=recv_sem.at[slot],
                device_id=(device_at(sizes, partners(sizes, place, 3)[0]),),
                device_id_type=MESH,
            ).wait_recv()

        me, count = lax.axis_index("seq"), lax.axis_size("seq")
        following, previous = lax.rem(me + 1, count), lax.rem(me + count - 1, count)
        greet(sizes, place, [following, previous] if extra else [])
        if extra:
            edge_copy = pltpu.make_async_remote_copy(
                src_ref=edge_in[0].at[pl.ds(edge.shape[0] - HALO, HALO), :],
                dst_ref=edge_out[0],
                send_sem=edge_sems.at[0],
                recv_sem=edge_sems.at[1],
                device_id=(following,),
                device_id_type=MESH,
            )
            edge_copy.start()
        sibling = partners(sizes, place, 3)[0]
        line, mine = slice(None), list(place)
        locals_ = []
        for turn, cut in enumerate(cuts):
            number, window = cut
            source = ins[number].at[*window]
            copy = pltpu.make_async_copy(source, region(cut, mine), local_sem.at[turn])
            copy.start()
            locals_.append(copy)
            for step, other in enumerate(partners(sizes, place, 0)):
                push(cut, mine, other, (turn, 0, step), source)

        def before(axis, step):
            at = list(place)
            at[axis] = (place[axis] - step - 1 + sizes[axis]) % sizes[axis]
            return at

        def shape_of(stage, order, at):
            if stage == 0:
                return at
            if stage == 1:
                return [line] + list(at[1:])
            full = [line] + list(at[1:])
            full[order[0]] = line
            return full

        waits = []

        def advance(turn, stage):
            cut = cuts[turn]
            order = (1, 2) if turn % 2 == 0 else (2, 1)
            if stage == 0:
                locals_[turn].wait()
                for step in range(sizes[0] - 1):
                    arrival(cut, before(0, step), (turn, 0, step))
                fresh = [[line, place[1], place[2], place[3]]]
            else:
                axis = order[stage - 1]
                fresh = []
                for step in range(sizes[axis] - 1):
                    at = shape_of(stage, order, before(axis, step))
                    arrival(cut, at, (turn, stage, step))
                    fresh.append(at)
            if stage < 2:
                axis = order[stage]
                at = shape_of(stage + 1, order, place)
                for step, other in enumerate(partners(sizes, place, axis)):
                    push(cut, at, other, (turn, stage + 1, step))
            for step, at in enumerate(fresh):
                push(cut, at, sibling, (turn, 3 + stage, step))
                there = list(at)
                there[3] = sibling[3]
                waits.append((cut, there, (turn, 3 + stage, step)))

        for tick in range(len(cuts) + 2):
            for stage in range(3):
                turn = tick - stage
                if 0 <= turn < len(cuts):
                    advance(turn, stage)
        for cut, at, slot in waits:
            arrival(cut, at, slot)
        for copy in sent:
            copy.wait_send()
        if extra:
            edge_copy.wait()

    hbm = pl.BlockSpec(memory_space=pl.ANY)
    edges = [] if edge is None else [edge]
    gathered = pl.pallas_call(
        kernel,
        out_shape=[jax.ShapeDtypeStruct(sizes + a.shape, a.dtype) for a in arrays]
        + [jax.ShapeDtypeStruct((HALO, e.shape[1]), e.dtype) for e in edges],
        in_specs=[hbm] * (kinds + extra),
        out_specs=[hbm] * (kinds + extra),
        scratch_shapes=[
            pltpu.SemaphoreType.DMA((len(cuts),)),
            pltpu.SemaphoreType.DMA((len(cuts), 6, most)),
            pltpu.SemaphoreType.DMA((len(cuts), 6, most)),
            pltpu.SemaphoreType.DMA((2,)),
        ],
        compiler_params=pltpu.CompilerParams(
            collective_id=collective_id, has_side_effects=True
        ),
        name="gather_everywhere",
    )(*arrays, *edges)
    return [g.reshape(-1, a.shape[1]) for g, a in zip(gathered, arrays)] + list(gathered[kinds:])


def scatter_sums(parts, small, collective_id, target):
    sizes = lattice(lax.axis_size("seq"))
    count = lax.axis_size("seq")
    shapes = [(p.shape[0] // count, p.shape[1]) for p in parts]
    views = [p.reshape(sizes + s) for p, s in zip(parts, shapes)]
    cuts = block_cuts(shapes, target)
    kinds = len(parts)
    most = max(sizes[:3])
    wide = max(sizes[1:3])
    extra = 0 if small is None else 1

    def kernel(*refs):
        ins, refs = refs[:kinds], refs[kinds:]
        small_in, refs = refs[:extra], refs[extra:]
        outs, refs = refs[:kinds], refs[kinds:]
        small_out, refs = refs[:extra], refs[extra:]
        own, core_in, first_in, second_in, last_in = [
            refs[i * kinds : (i + 1) * kinds] for i in range(5)
        ]
        refs = refs[5 * kinds :]
        local_sem, send_sem, recv_sem = refs[:3]
        place = coordinates(sizes)
        sibling = partners(sizes, place, 3)[0]
        sent, locals_ = [], []

        def push(source, target_ref, other, sems, slot):
            copy = pltpu.make_async_remote_copy(
                src_ref=source,
                dst_ref=target_ref,
                send_sem=sems[0].at[slot],
                recv_sem=sems[1].at[slot],
                device_id=(device_at(sizes, other),),
                device_id_type=MESH,
            )
            copy.start()
            sent.append(copy)

        def arrival(here, sems, slot):
            pltpu.make_async_remote_copy(
                src_ref=here,
                dst_ref=here,
                send_sem=sems[0].at[slot],
                recv_sem=sems[1].at[slot],
                device_id=(device_at(sizes, sibling),),
                device_id_type=MESH,
            ).wait_recv()

        main_sems = (send_sem, recv_sem)
        greet(sizes, place)
        for turn, (number, window) in enumerate(cuts):
            push(
                ins[number].at[:, :, :, sibling[3], *window],
                core_in[number].at[:, :, :, *window],
                sibling,
                main_sems,
                (turn, 0, 0),
            )
            copy = pltpu.make_async_copy(
                ins[number].at[:, :, :, place[3], *window],
                own[number].at[:, :, :, *window],
                local_sem.at[turn],
            )
            copy.start()
            locals_.append(copy)

        def kept(number, window, order, stage, at):
            index = [slice(None), slice(None), slice(None)]
            if stage >= 1:
                index[order[1]] = at[order[1]]
            if stage >= 2:
                index[order[0]] = at[order[0]]
            if stage >= 3:
                index[0] = at[0]
            return own[number].at[*index, *window]

        def landed(number, window, order, stage, step):
            if stage == 1:
                return first_in[number].at[step, :, pl.ds(0, sizes[order[0]]), *window]
            if stage == 2:
                return second_in[number].at[step, :, *window]
            return last_in[number].at[step, *window]

        def advance(turn, stage):
            number, window = cuts[turn]
            order = (1, 2) if turn % 2 == 0 else (2, 1)
            axes = (order[1], order[0], 0)
            if stage == 0:
                locals_[turn].wait()
                arrival(core_in[number].at[:, :, :, *window], main_sems, (turn, 0, 0))
                pieces = [core_in[number].at[:, :, :, *window]]
                lead = sizes[:3]
            else:
                steps = range(sizes[axes[stage - 1]] - 1)
                pieces = [landed(number, window, order, stage, step) for step in steps]
                for step in steps:
                    arrival(pieces[step], main_sems, (turn, stage, step))
                lead = ((sizes[0], sizes[order[0]]), (sizes[0],), ())[stage - 1]
            target_ref = kept(number, window, order, stage, place)

            def total(index):
                value = target_ref[index].astype(jnp.float32)
                for piece in pieces:
                    value = value + piece[index].astype(jnp.float32)
                return value

            if stage == 3:
                outs[number][window] = total((...,))
                return
            amount = math.prod(lead)

            def add(flat, carry):
                index, rest = [], flat
                for size in lead[::-1]:
                    index.insert(0, rest % size)
                    rest = rest // size
                target_ref[tuple(index)] = total(tuple(index)).astype(jnp.bfloat16)
                return carry

            lax.fori_loop(0, amount, add, 0)
            for step, other in enumerate(partners(sizes, place, axes[stage])):
                push(
                    kept(number, window, order, stage + 1, other),
                    landed(number, window, order, stage + 1, step),
                    other,
                    main_sems,
                    (turn, stage + 1, step),
                )

        if extra:
            boxes, small_sems = refs[3:7], refs[7:9]

        def small_step(tick):
            axes = (3, 2, 1, 0)
            if tick > 0:
                axis = axes[tick - 1]
                box = boxes[axis]
                for step in range(sizes[axis] - 1):
                    behind = (place[axis] - step - 1 + sizes[axis]) % sizes[axis]
                    arrival(box.at[behind], small_sems, (axis, step))
                value = box[0]
                for at in range(1, sizes[axis]):
                    value = value + box[at]
            else:
                value = small_in[0][...]
            if tick == 4:
                small_out[0][...] = value
                return
            axis = axes[tick]
            boxes[axis][place[axis]] = value
            here = boxes[axis].at[place[axis]]
            for step, other in enumerate(partners(sizes, place, axis)):
                push(here, here, other, small_sems, (axis, step))

        for tick in range(max(len(cuts) + 3, 5)):
            for stage in range(4):
                turn = tick - stage
                if 0 <= turn < len(cuts):
                    advance(turn, stage)
            if extra and tick < 5:
                small_step(tick)
        for copy in sent:
            copy.wait_send()

    hbm = pl.BlockSpec(memory_space=pl.ANY)
    vmem = pl.BlockSpec(memory_space=pltpu.VMEM)
    scratch = []
    for lead in (
        sizes[:3],
        sizes[:3],
        (wide - 1, sizes[0], wide),
        (wide - 1, sizes[0]),
        (sizes[0] - 1,),
    ):
        scratch += [pltpu.VMEM(lead + s, jnp.bfloat16) for s in shapes]
    scratch += [
        pltpu.SemaphoreType.DMA((len(cuts),)),
        pltpu.SemaphoreType.DMA((len(cuts), 4, most)),
        pltpu.SemaphoreType.DMA((len(cuts), 4, most)),
    ]
    if extra:
        scratch += [pltpu.VMEM((size,) + small.shape, jnp.float32) for size in sizes]
        scratch += [pltpu.SemaphoreType.DMA((4, most)) for _ in range(2)]
    out_shape = [jax.ShapeDtypeStruct(s, jnp.float32) for s in shapes]
    small_args = [] if small is None else [small]
    out_shape += [jax.ShapeDtypeStruct(small.shape, jnp.float32)] if extra else []
    return pl.pallas_call(
        kernel,
        out_shape=out_shape,
        in_specs=[hbm] * kinds + [vmem] * extra,
        out_specs=[vmem] * (kinds + extra),
        scratch_shapes=scratch,
        compiler_params=pltpu.CompilerParams(
            collective_id=collective_id,
            has_side_effects=True,
            vmem_limit_bytes=56 * 1024 * 1024,
        ),
        name="scatter_sums",
    )(*views, *small_args)


KEYS_STEP = 512


def attention_forward(queries, kv_all, row_starts, bounds):
    groups, rows, _ = queries.shape
    total = kv_all.shape[0]
    half_kv = KVW // 2
    group_size = QHEADS // KVHEADS

    def kernel(
        bounds_ref, q_ref, kv_ref, starts_ref, out_ref, log_ref, flat_ref, max_ref, acc_ref
    ):
        first_row = bounds_ref[0]
        local_rows = rows // group_size
        starts = starts_ref[...]
        places = first_row + lax.broadcasted_iota(jnp.int32, (1, rows), 1) % local_rows
        max_ref[...] = jnp.full(max_ref.shape, masked, jnp.float32)
        acc_ref[...] = jnp.zeros(acc_ref.shape, jnp.float32)

        def block(step, kind):
            first_key = pl.multiple_of(step * KEYS_STEP, KEYS_STEP)
            piece = kv_ref[pl.ds(first_key, KEYS_STEP), :]
            flipped = jnp.transpose(piece[:, half_kv:])
            ones = jnp.ones((16, KEYS_STEP), jnp.bfloat16)
            if kind:
                key_pos = first_key + lax.broadcasted_iota(jnp.int32, (KEYS_STEP, 1), 0)
                allowed = key_pos >= starts
                if kind == 2:
                    allowed = allowed & (key_pos <= places)
            for group in range(groups):
                scores = lax.dot_general(
                    piece[:, group * HEAD_DIM : (group + 1) * HEAD_DIM],
                    q_ref[group],
                    (((1,), (1,)), ((), ())),
                    preferred_element_type=jnp.float32,
                )
                if kind:
                    scores = jnp.where(allowed, scores, masked)
                old = max_ref[group]
                new = jnp.maximum(old, jnp.max(scores, axis=0, keepdims=True))
                max_ref[group] = new
                weights = jnp.exp(scores - new).astype(jnp.bfloat16)
                values = jnp.concatenate(
                    [flipped[group * HEAD_DIM : (group + 1) * HEAD_DIM], ones], axis=0
                )
                acc_ref[group] = acc_ref[group] * jnp.exp(old - new) + jnp.dot(
                    values, weights, preferred_element_type=jnp.float32
                )

        def body(step, carry):
            kind_of = jnp.where(
                (step + 1) * KEYS_STEP > first_row,
                2,
                jnp.where(step * KEYS_STEP < bounds_ref[1], 1, 0),
            )
            for kind in range(3):
                pl.when(kind_of == kind)(partial(block, step, kind))
            return carry

        lax.fori_loop(bounds_ref[2], bounds_ref[3], body, 0)
        for group in range(groups):
            row_sum = acc_ref[group, HEAD_DIM : HEAD_DIM + 1, :]
            out = acc_ref[group, :HEAD_DIM, :] / row_sum
            out_ref[group] = out
            log_ref[group] = max_ref[group] + jnp.log(row_sum)
            for part in range(group_size):
                head = group * group_size + part
                flat_ref[:, head * HEAD_DIM : (head + 1) * HEAD_DIM] = jnp.transpose(
                    out[:, part * local_rows : (part + 1) * local_rows]
                ).astype(jnp.bfloat16)

    vmem = pl.BlockSpec(memory_space=pltpu.VMEM)
    return pl.pallas_call(
        kernel,
        out_shape=(
            jax.ShapeDtypeStruct((groups, HEAD_DIM, rows), jnp.float32),
            jax.ShapeDtypeStruct((groups, 1, rows), jnp.float32),
            jax.ShapeDtypeStruct((rows // group_size, QW), jnp.bfloat16),
        ),
        in_specs=[pl.BlockSpec(memory_space=pltpu.SMEM), vmem, vmem, vmem],
        out_specs=(vmem, vmem, vmem),
        scratch_shapes=[
            pltpu.VMEM((groups, 1, rows), jnp.float32),
            pltpu.VMEM((groups, HEAD_DIM + 16, rows), jnp.float32),
        ],
        compiler_params=pltpu.CompilerParams(vmem_limit_bytes=56 * 1024 * 1024),
        cost_estimate=pl.CostEstimate(
            flops=4 * groups * rows * total * HEAD_DIM,
            bytes_accessed=2 * total * KVW,
            transcendentals=groups * rows * total,
        ),
        name="attention_forward",
    )(bounds, queries, kv_all, row_starts)


def attention_backward(queries, grads, kv_all, row_starts, log_total, outputs, bounds):
    groups, rows, _ = queries.shape
    total = kv_all.shape[0]
    half_kv = KVW // 2

    def kernel(
        bounds_ref,
        q_ref,
        g_ref,
        kv_ref,
        starts_ref,
        log_ref,
        outputs_ref,
        dkv_ref,
        dq_ref,
        delta_ref,
    ):
        first_row = bounds_ref[0]
        local_rows = rows // (QHEADS // KVHEADS)
        starts = starts_ref[...]
        places = first_row + lax.broadcasted_iota(jnp.int32, (1, rows), 1) % local_rows
        dq_ref[...] = jnp.zeros(dq_ref.shape, jnp.float32)
        for group in range(groups):
            flipped_grads = jnp.transpose(g_ref[group].astype(jnp.float32))
            delta_ref[group] = jnp.sum(
                flipped_grads * outputs_ref[group], axis=0, keepdims=True
            )

        def block(step, kind):
            first_key = pl.multiple_of(step * KEYS_STEP, KEYS_STEP)
            piece = kv_ref[pl.ds(first_key, KEYS_STEP), :]
            flipped = jnp.transpose(piece[:, :half_kv])
            if kind:
                key_pos = first_key + lax.broadcasted_iota(jnp.int32, (KEYS_STEP, 1), 0)
                allowed = key_pos >= starts
                if kind == 2:
                    allowed = allowed & (key_pos <= places)
            found = []
            for group in range(groups):
                low, high = group * HEAD_DIM, (group + 1) * HEAD_DIM
                scores = lax.dot_general(
                    piece[:, low:high],
                    q_ref[group],
                    (((1,), (1,)), ((), ())),
                    preferred_element_type=jnp.float32,
                )
                if kind:
                    scores = jnp.where(allowed, scores, masked)
                weights = jnp.exp(scores - log_ref[group])
                grad_weights = lax.dot_general(
                    piece[:, half_kv + low : half_kv + high],
                    g_ref[group],
                    (((1,), (1,)), ((), ())),
                    preferred_element_type=jnp.float32,
                )
                grad_scores = (weights * (grad_weights - delta_ref[group])).astype(jnp.bfloat16)
                dq_ref[group] += jnp.dot(
                    flipped[low:high], grad_scores, preferred_element_type=jnp.float32
                )
                found.append(
                    jnp.dot(grad_scores, q_ref[group], preferred_element_type=jnp.float32)
                )
                found.append(
                    jnp.dot(
                        weights.astype(jnp.bfloat16),
                        g_ref[group],
                        preferred_element_type=jnp.float32,
                    )
                )
            dkv_ref[pl.ds(first_key, KEYS_STEP), :] = jnp.concatenate(
                found[0::2] + found[1::2], axis=1
            ).astype(dkv_ref.dtype)

        def body(step, carry):
            kind_of = jnp.where(
                (step + 1) * KEYS_STEP > first_row,
                2,
                jnp.where(step * KEYS_STEP < bounds_ref[1], 1, 0),
            )
            for kind in range(3):
                pl.when(kind_of == kind)(partial(block, step, kind))
            return carry

        def clear(step, carry):
            first_key = pl.multiple_of(step * KEYS_STEP, KEYS_STEP)
            dkv_ref[pl.ds(first_key, KEYS_STEP), :] = jnp.zeros(
                (KEYS_STEP, KVW), dkv_ref.dtype
            )
            return carry

        lax.fori_loop(0, bounds_ref[2], clear, 0)
        lax.fori_loop(bounds_ref[2], bounds_ref[3], body, 0)
        lax.fori_loop(bounds_ref[3], total // KEYS_STEP, clear, 0)

    vmem = pl.BlockSpec(memory_space=pltpu.VMEM)
    return pl.pallas_call(
        kernel,
        out_shape=(
            jax.ShapeDtypeStruct((total, KVW), jnp.bfloat16),
            jax.ShapeDtypeStruct((groups, HEAD_DIM, rows), jnp.float32),
        ),
        in_specs=[pl.BlockSpec(memory_space=pltpu.SMEM)] + [vmem] * 6,
        out_specs=(vmem, vmem),
        scratch_shapes=[pltpu.VMEM((groups, 1, rows), jnp.float32)],
        compiler_params=pltpu.CompilerParams(vmem_limit_bytes=60 * 1024 * 1024),
        cost_estimate=pl.CostEstimate(
            flops=10 * groups * rows * total * HEAD_DIM,
            bytes_accessed=4 * total * KVW,
            transcendentals=groups * rows * total,
        ),
        name="attention_backward",
    )(bounds, queries, grads, kv_all, row_starts, log_total, outputs)


HALO = 16
VMEM_SPEC = pl.BlockSpec(memory_space=pltpu.VMEM)
BIG_VMEM = pltpu.CompilerParams(vmem_limit_bytes=58 * 1024 * 1024)


def dot_parts(value, exact, parts, axes=((1,), (0,))):
    total, left = None, value
    for _ in range(parts):
        piece = left.astype(jnp.bfloat16)
        left = left - piece.astype(jnp.float32)
        term = lax.dot_general(piece, exact, (axes, ((), ())), preferred_element_type=jnp.float32)
        total = term if total is None else total + term
    return total


def dot_left(exact, value, parts):
    total, left = None, value
    for _ in range(parts):
        piece = left.astype(jnp.bfloat16)
        left = left - piece.astype(jnp.float32)
        term = jnp.dot(exact, piece, preferred_element_type=jnp.float32)
        total = term if total is None else total + term
    return total


def matmul_pair(left_side, right_side, axes):
    left_high = left_side.astype(jnp.bfloat16)
    left_low = (left_side - left_high.astype(jnp.float32)).astype(jnp.bfloat16)
    right_high = right_side.astype(jnp.bfloat16)
    right_low = (right_side - right_high.astype(jnp.float32)).astype(jnp.bfloat16)
    dims = (axes, ((), ()))
    product = partial(
        lax.dot_general, dimension_numbers=dims, preferred_element_type=jnp.float32
    )
    return (
        product(left_high, right_high)
        + product(left_low, right_high)
        + product(left_high, right_low)
    )


def stacked(value, first):
    high = value.astype(jnp.bfloat16)
    low = (value - high.astype(jnp.float32)).astype(jnp.bfloat16)
    return [high, low, high] if first else [high, high, low]


def dot_fast(left_side, right_side, axes):
    return lax.dot_general(
        left_side.astype(jnp.bfloat16),
        right_side.astype(jnp.bfloat16),
        (axes, ((), ())),
        preferred_element_type=jnp.float32,
    )


NN = ((1,), (0,))
NT = ((1,), (1,))
TN = ((0,), (0,))


def head_spread():
    head = lax.broadcasted_iota(jnp.int32, (128, SSM), 0)
    column = lax.broadcasted_iota(jnp.int32, (128, SSM), 1)
    return jnp.where(column // MHEAD_DIM == head, 1.0, 0.0).astype(jnp.bfloat16)


def rope_table(rows, count):
    half = HEAD_DIM // 2
    frequency = rope_base ** (-np.arange(half) / half)
    tables = []
    for places in (np.arange(rows), rows * np.arange(count)):
        angles = np.tile(places[:, None] * frequency[None, :], (1, 4))
        tables += [np.cos(angles).astype(np.float32), np.sin(angles).astype(np.float32)]
    return tables


def rope_now(device, base_cos_ref, base_sin_ref, far_cos_ref, far_sin_ref):
    base_cos, base_sin = base_cos_ref[...], base_sin_ref[...]
    far_cos, far_sin = far_cos_ref[pl.ds(device, 1), :], far_sin_ref[pl.ds(device, 1), :]
    cosine_part = far_cos * base_cos - far_sin * base_sin
    sine_part = far_sin * base_cos + far_cos * base_sin
    lane = lax.broadcasted_iota(jnp.int32, base_cos.shape, 1)
    return cosine_part, jnp.where(lane % HEAD_DIM < HEAD_DIM // 2, -sine_part, sine_part)


def rope_lanes(values, cosine_all, sine_all):
    width = values.shape[1]
    repeat = width // cosine_all.shape[1]
    half = HEAD_DIM // 2
    column = lax.broadcasted_iota(jnp.int32, values.shape, 1)
    partner = jnp.where(
        column % HEAD_DIM < half,
        pltpu.roll(values, width - half, 1),
        pltpu.roll(values, half, 1),
    )
    if repeat > 1:
        cosine_all = jnp.concatenate([cosine_all] * repeat, axis=1)
        sine_all = jnp.concatenate([sine_all] * repeat, axis=1)
    return values * cosine_all + partner * sine_all


def mixer_forward(
    hidden, halo, norm_gain, weights, conv_weight, conv_bias, dt_bias, a_log, starts, tables
):
    rows, model = hidden.shape
    groups = QHEADS // KVHEADS
    half_kv = KVW // 2
    first_row = (lax.axis_index("seq") * rows).astype(jnp.int32).reshape(1)
    pieces = [
        (0, 0, SSM // 2),
        (0, SSM // 2, SSM // 2),
        (1, 0, XBC // 2),
        (1, XBC // 2, XBC // 2),
        (2, 0, QW),
        (2, QW, KVW),
        (2, QW + KVW, DT_PAD),
    ]
    load_order = (2, 3, 4, 5, 6, 0, 1)

    def kernel(
        first_ref,
        hidden_ref,
        halo_ref,
        gain_ref,
        z_hbm,
        xbc_hbm,
        small_hbm,
        tap_ref,
        bias_ref,
        dt_bias_ref,
        a_log_ref,
        starts_ref,
        base_cos_ref,
        base_sin_ref,
        far_cos_ref,
        far_sin_ref,
        normed_ref,
        gate_ref,
        ext_ref,
        pre_ref,
        q_ref,
        kv_ref,
        dt_pre_ref,
        log_ref,
        state_ref,
        passing_ref,
        z_ref,
        xbc_ref,
        small_ref,
        normed_ext,
        ext_f32,
        sems,
    ):
        weight_hbm, weight_refs = (z_hbm, xbc_hbm, small_hbm), (z_ref, xbc_ref, small_ref)
        copies = [
            pltpu.make_async_copy(
                weight_hbm[which].at[:, pl.ds(start, width)],
                weight_refs[which].at[:, pl.ds(start, width)],
                sems.at[number],
            )
            for number, (which, start, width) in enumerate(pieces)
        ]
        for number in load_order:
            copies[number].start()
        cosine_all, sine_all = rope_now(
            first_ref[0] // rows, base_cos_ref, base_sin_ref, far_cos_ref, far_sin_ref
        )

        def norm(block):
            values = block.astype(jnp.float32)
            scale = lax.rsqrt(jnp.mean(values * values, axis=1, keepdims=True) + epsilon)
            return (values * scale * gain_ref[...]).astype(jnp.bfloat16)

        normed_ext[:HALO, :] = norm(halo_ref[...])
        normed = norm(hidden_ref[...])
        normed_ext[HALO:, :] = normed
        normed_ref[...] = normed

        def project(number, values):
            copies[number].wait()
            which, start, width = pieces[number]
            return jnp.dot(
                values,
                weight_refs[which][:, start : start + width],
                preferred_element_type=jnp.float32,
            )

        for number in (2, 3):
            _, start, width = pieces[number]
            part = project(number, normed_ext[...]).astype(jnp.bfloat16)
            ext_ref[:, start : start + width] = part
            ext_f32[:, start : start + width] = part.astype(jnp.float32)
        turned = rope_lanes(project(4, normed), cosine_all, sine_all).astype(jnp.bfloat16)
        turned = turned * jnp.bfloat16(HEAD_DIM ** (-0.5))
        for head in range(QHEADS):
            place = head % groups * rows
            q_ref[head // groups, place : place + rows, :] = turned[
                :, head * HEAD_DIM : (head + 1) * HEAD_DIM
            ]
        kv_raw = project(5, normed)
        kv_ref[:, :half_kv] = rope_lanes(
            kv_raw[:, :half_kv], cosine_all, sine_all
        ).astype(jnp.bfloat16)
        kv_ref[:, half_kv:] = kv_raw[:, half_kv:].astype(jnp.bfloat16)
        dt_pre = project(6, normed) + dt_bias_ref[...]
        dt_pre_ref[...] = dt_pre
        step_dt = jax.nn.softplus(dt_pre)
        order = lax.broadcasted_iota(jnp.int32, (rows, rows), 0)
        other = lax.broadcasted_iota(jnp.int32, (rows, rows), 1)
        lower = jnp.where(other <= order, 1.0, 0.0).astype(jnp.bfloat16)
        log_decay = dot_left(lower, -step_dt * jnp.exp(a_log_ref[...]), 3)
        log_ref[...] = log_decay
        for number in (0, 1):
            _, start, width = pieces[number]
            gate_ref[:, start : start + width] = project(number, normed)

        starts_now = starts_ref[...]
        places = first_ref[0] + lax.broadcasted_iota(jnp.int32, (rows, 1), 0)
        pre = jnp.zeros((rows, XBC), jnp.float32) + bias_ref[...]
        for tap in range(CONV):
            lag = CONV - 1 - tap
            kept = jnp.where(places - lag >= starts_now, 1.0, 0.0)
            pre = pre + ext_f32[HALO - lag : HALO - lag + rows, :] * kept * tap_ref[tap : tap + 1, :]
        pre_ref[...] = pre
        conv_out = pre * jax.nn.sigmoid(pre)
        last = log_decay[rows - 1 : rows, :]
        last_start = starts_ref[rows - 1 : rows, :]
        weight = jnp.exp(jnp.where(places >= last_start, last - log_decay, masked)) * step_dt
        spread = dot_parts(weight, head_spread(), 2)
        state_ref[...] = matmul_pair(
            conv_out[:, :SSM] * spread, conv_out[:, SSM : SSM + STATE], TN
        )
        passing_ref[...] = jnp.exp(last) * jnp.where(last_start < first_ref[0], 1.0, 0.0)

    f32 = jnp.float32
    shape = jax.ShapeDtypeStruct
    return pl.pallas_call(
        kernel,
        out_shape=(
            shape((rows, model), jnp.bfloat16),
            shape((rows, SSM), f32),
            shape((HALO + rows, XBC), jnp.bfloat16),
            shape((rows, XBC), f32),
            shape((KVHEADS, groups * rows, HEAD_DIM), jnp.bfloat16),
            shape((rows, KVW), jnp.bfloat16),
            shape((rows, DT_PAD), f32),
            shape((rows, DT_PAD), f32),
            shape((SSM, STATE), f32),
            shape((1, DT_PAD), f32),
        ),
        in_specs=[pl.BlockSpec(memory_space=pltpu.SMEM)]
        + [VMEM_SPEC] * 3
        + [pl.BlockSpec(memory_space=pl.ANY)] * 3
        + [VMEM_SPEC] * 9,
        out_specs=[VMEM_SPEC] * 10,
        scratch_shapes=[
            *[pltpu.VMEM(w.shape, jnp.bfloat16) for w in weights],
            pltpu.VMEM((HALO + rows, model), jnp.bfloat16),
            pltpu.VMEM((HALO + rows, XBC), f32),
            pltpu.SemaphoreType.DMA((len(pieces),)),
        ],
        compiler_params=BIG_VMEM,
        name="mixer_forward",
    )(
        first_row,
        hidden,
        halo,
        norm_gain[None],
        *weights,
        conv_weight,
        conv_bias[None],
        dt_bias,
        a_log,
        starts[:, None],
        *tables,
    )


def document_mask(first_row, starts, rows, flip):
    if flip:
        token = lax.broadcasted_iota(jnp.int32, (rows, rows), 1)
        source = lax.broadcasted_iota(jnp.int32, (rows, rows), 0)
    else:
        token = lax.broadcasted_iota(jnp.int32, (rows, rows), 0)
        source = lax.broadcasted_iota(jnp.int32, (rows, rows), 1)
    allowed = (first_row + source >= starts) & (source <= token)
    return jnp.where(allowed, 0.0, masked)


def mixer_output(pre, dt_pre, log_decay, states_in, gate_z, ssm_gain, skip_lanes, starts):
    rows = pre.shape[0]
    first_row = (lax.axis_index("seq") * rows).astype(jnp.int32).reshape(1)

    def kernel(
        first_ref,
        pre_ref,
        dt_pre_ref,
        log_ref,
        state_ref,
        gate_ref,
        gain_ref,
        skip_ref,
        starts_ref,
        normed_ref,
        y_ref,
        input_ref,
    ):
        pre_now = pre_ref[...]
        conv_out = pre_now * jax.nn.sigmoid(pre_now)
        ssm_x = conv_out[:, :SSM]
        input_b = conv_out[:, SSM : SSM + STATE]
        output_c = conv_out[:, SSM + STATE :]
        spread = head_spread()
        log_decay_now = log_ref[...]
        log_rows = jnp.transpose(log_decay_now)
        step_dt = jax.nn.softplus(dt_pre_ref[...])
        scaled_x = ssm_x * dot_parts(step_dt, spread, 2)
        for part, piece in enumerate(stacked(scaled_x, False)):
            input_ref[part * rows : (part + 1) * rows, :] = piece
        carried = jnp.exp(log_decay_now) * jnp.where(starts_ref[...] < first_ref[0], 1.0, 0.0)
        y_ref[...] = (
            matmul_pair(output_c, state_ref[...], NT) * dot_parts(carried, spread, 2)
            + skip_ref[...] * ssm_x
        )
        affinity = matmul_pair(output_c, input_b, NT)
        closed = document_mask(first_ref[0], starts_ref[...], rows, False)
        for pair in range(MHEADS // 2):
            found = []
            for head in (2 * pair, 2 * pair + 1):
                gap = log_decay_now[:, head : head + 1] - log_rows[head : head + 1, :] + closed
                mixing = affinity * jnp.exp(gap)
                found.append(
                    jnp.dot(
                        jnp.concatenate(stacked(mixing, True), axis=1),
                        input_ref[:, head * MHEAD_DIM : (head + 1) * MHEAD_DIM],
                        preferred_element_type=jnp.float32,
                    )
                )
            columns = slice(2 * pair * MHEAD_DIM, (2 * pair + 2) * MHEAD_DIM)
            y_ref[:, columns] += jnp.concatenate(found, axis=1)
        gate_now = gate_ref[...]
        gated = y_ref[...] * gate_now * jax.nn.sigmoid(gate_now)
        scale = lax.rsqrt(jnp.mean(gated * gated, axis=1, keepdims=True) + epsilon)
        normed_ref[...] = (gated * scale * gain_ref[...]).astype(jnp.bfloat16)

    return pl.pallas_call(
        kernel,
        out_shape=(
            jax.ShapeDtypeStruct((rows, SSM), jnp.bfloat16),
            jax.ShapeDtypeStruct((rows, SSM), jnp.float32),
        ),
        in_specs=[pl.BlockSpec(memory_space=pltpu.SMEM)] + [VMEM_SPEC] * 8,
        out_specs=[VMEM_SPEC] * 2,
        scratch_shapes=[pltpu.VMEM((3 * rows, SSM), jnp.bfloat16)],
        compiler_params=BIG_VMEM,
        name="mixer_output",
    )(
        first_row,
        pre,
        dt_pre,
        log_decay,
        states_in,
        gate_z,
        ssm_gain[None],
        skip_lanes,
        starts[:, None],
    )


def mixer_backward(
    grad_normed, y, gate_z, ssm_gain, pre, dt_pre, log_decay, states_in, skip_lanes, starts
):
    rows = pre.shape[0]
    first_row = (lax.axis_index("seq") * rows).astype(jnp.int32).reshape(1)

    def kernel(
        first_ref,
        grad_ref,
        y_ref,
        gate_ref,
        gain_ref,
        pre_ref,
        dt_pre_ref,
        log_ref,
        state_ref,
        skip_ref,
        starts_ref,
        starts_row_ref,
        grad_gate_ref,
        gain_grad_ref,
        grad_y_ref,
        state_grad_ref,
        input_grad_ref,
        b_grad_ref,
        c_grad_ref,
        log_grad_ref,
        skip_grad_ref,
        input_ref,
        low_ref,
        sums_ref,
    ):
        gate_now = gate_ref[...]
        sigmoid_gate = jax.nn.sigmoid(gate_now)
        silu_gate = gate_now * sigmoid_gate
        y_now = y_ref[...]
        gated = y_now * silu_gate
        scale = lax.rsqrt(jnp.mean(gated * gated, axis=1, keepdims=True) + epsilon)
        grad_now = grad_ref[...]
        gain_grad_ref[...] = jnp.sum(gated * scale * grad_now, axis=0, keepdims=True)
        scaled = grad_now * gain_ref[...]
        grad_gated = scale * scaled - gated * (
            scale * scale * scale * jnp.mean(gated * scaled, axis=1, keepdims=True)
        )
        grad_gate_ref[...] = (
            grad_gated * y_now * sigmoid_gate * (1.0 + gate_now * (1.0 - sigmoid_gate))
        ).astype(jnp.bfloat16)
        grad_y = grad_gated * silu_gate
        grad_y_ref[...] = grad_y
        for part, piece in enumerate(stacked(grad_y, False)):
            low_ref[part * rows : (part + 1) * rows, :] = piece

        pre_now = pre_ref[...]
        conv_out = pre_now * jax.nn.sigmoid(pre_now)
        ssm_x = conv_out[:, :SSM]
        input_b = conv_out[:, SSM : SSM + STATE]
        output_c = conv_out[:, SSM + STATE :]
        spread = head_spread()
        log_decay_now = log_ref[...]
        log_rows = jnp.transpose(log_decay_now)
        step_dt = jax.nn.softplus(dt_pre_ref[...])
        scaled_x = ssm_x * dot_parts(step_dt, spread, 2)
        high, low, _ = stacked(scaled_x, True)
        input_ref[:rows, :] = high
        input_ref[rows:, :] = low
        carried = jnp.exp(log_decay_now) * jnp.where(starts_ref[...] < first_ref[0], 1.0, 0.0)
        carried_lanes = dot_parts(carried, spread, 2)
        from_state = matmul_pair(output_c, state_ref[...], NT)
        log_grad = carried * dot_parts(grad_y * from_state, spread, 2, NT)
        grad_from_state = grad_y * carried_lanes
        state_grad_ref[...] = matmul_pair(grad_from_state, output_c, TN)
        c_grad = matmul_pair(grad_from_state, state_ref[...], NN)
        skip_grad_ref[...] = dot_parts(
            jnp.sum(grad_y * ssm_x, axis=0, keepdims=True), spread, 3, NT
        )

        affinity = matmul_pair(input_b, output_c, NT)
        closed = document_mask(first_ref[0], starts_row_ref[...], rows, True)
        affinity_grad = jnp.zeros((rows, rows), jnp.float32)
        sums_ref[...] = jnp.zeros(sums_ref.shape, jnp.float32)
        lane = lax.broadcasted_iota(jnp.int32, (rows, DT_PAD), 1)
        for pair in range(MHEADS // 2):
            found = []
            for head in (2 * pair, 2 * pair + 1):
                columns = slice(head * MHEAD_DIM, (head + 1) * MHEAD_DIM)
                gap = log_rows[head : head + 1, :] - log_decay_now[:, head : head + 1] + closed
                decay = jnp.exp(gap)
                mixing = affinity * decay
                found.append(
                    jnp.dot(
                        jnp.concatenate(stacked(mixing, True), axis=1),
                        low_ref[:, columns],
                        preferred_element_type=jnp.float32,
                    )
                )
                grad_mixing = jnp.zeros((rows, rows), jnp.float32)
                for one, two in ((0, 0), (1, 0), (0, 2)):
                    grad_mixing = grad_mixing + lax.dot_general(
                        input_ref[one * rows : (one + 1) * rows, columns],
                        low_ref[two * rows : (two + 1) * rows, columns],
                        (NT, ((), ())),
                        preferred_element_type=jnp.float32,
                    )
                affinity_grad = affinity_grad + grad_mixing * decay
                both = grad_mixing * mixing
                sums_ref[head : head + 1, :] = jnp.sum(both, axis=0, keepdims=True)
                log_grad = log_grad - jnp.where(
                    lane == head, jnp.sum(both, axis=1, keepdims=True), 0.0
                )
            columns = slice(2 * pair * MHEAD_DIM, (2 * pair + 2) * MHEAD_DIM)
            input_grad_ref[:, columns] = jnp.concatenate(found, axis=1)
        log_grad_ref[...] = log_grad + jnp.transpose(sums_ref[...])
        b_grad_ref[...] = matmul_pair(affinity_grad, output_c, NN)
        c_grad_ref[...] = c_grad + matmul_pair(jnp.transpose(affinity_grad), input_b, NN)

    f32 = jnp.float32
    shape = jax.ShapeDtypeStruct
    return pl.pallas_call(
        kernel,
        out_shape=(
            shape((rows, SSM), jnp.bfloat16),
            shape((1, SSM), f32),
            shape((rows, SSM), f32),
            shape((SSM, STATE), f32),
            shape((rows, SSM), f32),
            shape((rows, STATE), f32),
            shape((rows, STATE), f32),
            shape((rows, DT_PAD), f32),
            shape((1, DT_PAD), f32),
        ),
        in_specs=[pl.BlockSpec(memory_space=pltpu.SMEM)] + [VMEM_SPEC] * 11,
        out_specs=[VMEM_SPEC] * 9,
        scratch_shapes=[
            pltpu.VMEM((2 * rows, SSM), jnp.bfloat16),
            pltpu.VMEM((3 * rows, SSM), jnp.bfloat16),
            pltpu.VMEM((DT_PAD, rows), f32),
        ],
        compiler_params=BIG_VMEM,
        name="mixer_backward",
    )(
        first_row,
        grad_normed,
        y,
        gate_z,
        ssm_gain[None],
        pre,
        dt_pre,
        log_decay,
        states_in,
        skip_lanes,
        starts[:, None],
        starts[None],
    )


def mixer_input_backward(
    grad_end,
    states_in,
    passing,
    grad_y,
    input_grad,
    b_grad,
    c_grad,
    log_grad,
    pre,
    dt_pre,
    log_decay,
    ext,
    conv_weight,
    a_log,
    skip_lanes,
    starts,
):
    rows = pre.shape[0]
    first_row = (lax.axis_index("seq") * rows).astype(jnp.int32).reshape(1)

    def kernel(
        first_ref,
        end_ref,
        state_ref,
        passing_ref,
        grad_y_ref,
        input_grad_ref,
        b_grad_ref,
        c_grad_ref,
        log_grad_ref,
        pre_ref,
        dt_pre_ref,
        log_ref,
        ext_ref,
        tap_ref,
        a_log_ref,
        skip_ref,
        starts_ref,
        raw_grad_ref,
        tap_grad_ref,
        bias_grad_ref,
        dt_grad_ref,
        dt_sum_ref,
        a_log_grad_ref,
        ext_f32,
        sum_ref,
    ):
        pre_now = pre_ref[...]
        sigmoid_pre = jax.nn.sigmoid(pre_now)
        conv_out = pre_now * sigmoid_pre
        ssm_x = conv_out[:, :SSM]
        input_b = conv_out[:, SSM : SSM + STATE]
        spread = head_spread()
        log_decay_now = log_ref[...]
        dt_pre_now = dt_pre_ref[...]
        step_dt = jax.nn.softplus(dt_pre_now)
        step_lanes = dot_parts(step_dt, spread, 2)
        starts_now = starts_ref[...]
        row = lax.broadcasted_iota(jnp.int32, (rows, 1), 0)
        places = first_ref[0] + row
        last = log_decay_now[rows - 1 : rows, :]
        last_start = starts_ref[rows - 1 : rows, :]
        weight = jnp.exp(jnp.where(places >= last_start, last - log_decay_now, masked))
        weight_lanes = dot_parts(weight, spread, 2)
        weighted = ssm_x * step_lanes * weight_lanes
        grad_weighted = matmul_pair(input_b, end_ref[...], NT)
        b_total = b_grad_ref[...] + matmul_pair(weighted, end_ref[...], NN)
        input_total = input_grad_ref[...] + grad_weighted * weight_lanes
        weight_term = dot_parts(grad_weighted * weighted, spread, 3, NT)
        state_dot = end_ref[...] * state_ref[...]
        passing_grad = jnp.sum(
            jnp.transpose(dot_left(spread, state_dot, 3)), axis=0, keepdims=True
        )
        log_grad_now = log_grad_ref[...] - weight_term
        end_term = jnp.sum(weight_term, axis=0, keepdims=True) + passing_grad * passing_ref[...]
        log_grad_now = log_grad_now + jnp.where(row == rows - 1, end_term, 0.0)
        order = lax.broadcasted_iota(jnp.int32, (rows, rows), 0)
        other = lax.broadcasted_iota(jnp.int32, (rows, rows), 1)
        upper = jnp.where(other >= order, 1.0, 0.0).astype(jnp.bfloat16)
        step_grad = dot_left(upper, log_grad_now, 3)
        rate = jnp.exp(a_log_ref[...])
        a_log_grad_ref[...] = jnp.sum(-step_dt * rate * step_grad, axis=0, keepdims=True)
        dt_grad = dot_parts(input_total * ssm_x, spread, 3, NT) - rate * step_grad
        dt_raw_grad = dt_grad * jax.nn.sigmoid(dt_pre_now)
        valid = lax.broadcasted_iota(jnp.int32, (rows, DT_PAD), 1) < MHEADS
        dt_raw_grad = jnp.where(valid, dt_raw_grad, 0.0)
        dt_grad_ref[...] = dt_raw_grad.astype(jnp.bfloat16)
        dt_sum_ref[...] = jnp.sum(dt_raw_grad, axis=0, keepdims=True)
        x_grad = input_total * step_lanes + skip_ref[...] * grad_y_ref[...]
        slope = sigmoid_pre * (1.0 + pre_now * (1.0 - sigmoid_pre))
        pre_grad = jnp.concatenate([x_grad, b_total, c_grad_ref[...]], axis=1) * slope
        bias_grad_ref[...] = jnp.sum(pre_grad, axis=0, keepdims=True)
        ext_f32[...] = ext_ref[...].astype(jnp.float32)
        sum_ref[...] = jnp.zeros(sum_ref.shape, jnp.float32)
        for tap in range(CONV):
            lag = CONV - 1 - tap
            kept = pre_grad * jnp.where(places - lag >= starts_now, 1.0, 0.0)
            window = slice(HALO - lag, HALO - lag + rows)
            tap_grad_ref[tap : tap + 1, :] = jnp.sum(
                kept * ext_f32[window, :], axis=0, keepdims=True
            )
            sum_ref[window, :] += kept * tap_ref[tap : tap + 1, :]
        raw_grad_ref[...] = sum_ref[...]

    f32 = jnp.float32
    shape = jax.ShapeDtypeStruct
    return pl.pallas_call(
        kernel,
        out_shape=(
            shape((HALO + rows, XBC), f32),
            shape((CONV, XBC), f32),
            shape((1, XBC), f32),
            shape((rows, DT_PAD), jnp.bfloat16),
            shape((1, DT_PAD), f32),
            shape((1, DT_PAD), f32),
        ),
        in_specs=[pl.BlockSpec(memory_space=pltpu.SMEM)] + [VMEM_SPEC] * 16,
        out_specs=[VMEM_SPEC] * 6,
        scratch_shapes=[
            pltpu.VMEM((HALO + rows, XBC), f32),
            pltpu.VMEM((HALO + rows, XBC), f32),
        ],
        compiler_params=BIG_VMEM,
        name="mixer_input_backward",
    )(
        first_row,
        grad_end,
        states_in,
        passing,
        grad_y,
        input_grad,
        b_grad,
        c_grad,
        log_grad,
        pre,
        dt_pre,
        log_decay,
        ext,
        conv_weight,
        a_log,
        skip_lanes,
        starts[:, None],
    )


def exchange_scan(slices, decays, reverse, collective_id):
    count, part, lanes = slices.shape
    fresh = decays.ndim == 3
    kinds = 2 if fresh else 1

    def kernel(*refs):
        state_ref, decay_ref, refs = refs[0], refs[1], refs[2:]
        out_ref, refs = refs[0], refs[1:]
        if fresh:
            column_ref, refs = refs[0], refs[1:]
            got_ref, result_ref, got_decay_ref, *sems = refs
        else:
            column_ref = decay_ref
            got_ref, result_ref, *sems = refs
        send_sem, recv_sem = sems
        me = lax.axis_index("seq")
        barrier = pltpu.get_barrier_semaphore()

        def greet_one(step, carry):
            other = lax.rem(me + step, count)
            pl.semaphore_signal(barrier, inc=1, device_id=(other,), device_id_type=MESH)
            return carry

        lax.fori_loop(1, count, greet_one, 0)
        pl.semaphore_wait(barrier, count - 1)

        def copies(step, turn):
            other = lax.rem(me + step, count)
            pairs = [(state_ref, got_ref)]
            if fresh:
                pairs.append((decay_ref, got_decay_ref))
            if turn == 1:
                pairs = [(result_ref, out_ref)]
            return [
                pltpu.make_async_remote_copy(
                    src_ref=source.at[other],
                    dst_ref=target.at[me],
                    send_sem=send_sem.at[turn, kind, step],
                    recv_sem=recv_sem.at[turn, kind, step],
                    device_id=(other,),
                    device_id_type=MESH,
                )
                for kind, (source, target) in enumerate(pairs)
            ]

        def swap(turn):
            def start(step, carry):
                for copy in copies(step, turn):
                    copy.start()
                return carry

            lax.fori_loop(1, count, start, 0)

        def settle(turn):
            def finish(step, carry):
                for copy in copies(step, turn):
                    copy.wait()
                return carry

            lax.fori_loop(1, count, finish, 0)

        swap(0)
        got_ref[me] = state_ref[me]
        if fresh:
            got_decay_ref[me] = decay_ref[me]
        settle(0)
        if fresh:
            columns = jnp.concatenate(
                [
                    got_decay_ref[place, 0:1, :].astype(jnp.float32)
                    + got_decay_ref[place, 1:2, :].astype(jnp.float32)
                    for place in range(count)
                ]
                + [jnp.zeros((128 - count, lanes), jnp.float32)] * (1 if count < 128 else 0),
                axis=0,
            )
            column_ref[...] = jnp.transpose(columns)
        state = jnp.zeros((part, lanes), jnp.float32)
        order = range(count - 1, -1, -1) if reverse else range(count)
        for place in order:
            result_ref[place] = state
            state = column_ref[:part, place : place + 1] * state + got_ref[place].astype(
                jnp.float32
            )
        swap(1)
        out_ref[me] = result_ref[me]
        settle(1)

    out_shape = [jax.ShapeDtypeStruct(slices.shape, jnp.float32)]
    scratch = [pltpu.VMEM(slices.shape, kind) for kind in (jnp.bfloat16, jnp.float32)]
    if fresh:
        out_shape.append(jax.ShapeDtypeStruct((lanes, 128), jnp.float32))
        scratch.append(pltpu.VMEM(decays.shape, jnp.bfloat16))
    scratch += [pltpu.SemaphoreType.DMA((2, kinds, count)) for _ in range(2)]
    return pl.pallas_call(
        kernel,
        out_shape=out_shape,
        in_specs=[VMEM_SPEC] * 2,
        out_specs=[VMEM_SPEC] * len(out_shape),
        scratch_shapes=scratch,
        compiler_params=pltpu.CompilerParams(
            collective_id=collective_id,
            has_side_effects=True,
            vmem_limit_bytes=48 * 1024 * 1024,
        ),
        name="exchange_scan",
    )(slices, decays)


def slice_rows(values, count):
    part = values.shape[0] // count
    padded = -(-part // 16) * 16
    sliced = values.astype(jnp.bfloat16).reshape(count, part, values.shape[1])
    return jnp.pad(sliced, ((0, 0), (0, padded - part), (0, 0)))


def join_rows(slices, rows):
    count = slices.shape[0]
    return slices[:, : rows // count].reshape(rows, slices.shape[2])


def states_before(passing, local_state, collective_id):
    count = lax.axis_size("seq")
    part = SSM // count
    decay_rows = jnp.repeat(passing, MHEAD_DIM).reshape(count, 1, part)
    decay_rows = jnp.pad(decay_rows, ((0, 0), (0, 0), (0, 128 - part)))
    decay_high = decay_rows.astype(jnp.bfloat16)
    decay_low = (decay_rows - decay_high.astype(jnp.float32)).astype(jnp.bfloat16)
    decay_slices = jnp.concatenate(
        [decay_high, decay_low, jnp.zeros((count, 14, 128), jnp.bfloat16)], axis=1
    )
    states, columns = exchange_scan(
        slice_rows(local_state, count), decay_slices, False, collective_id
    )
    return join_rows(states, SSM), columns


def grads_after(columns, grad_states_in, collective_id):
    count = lax.axis_size("seq")
    (grads,) = exchange_scan(slice_rows(grad_states_in, count), columns, True, collective_id)
    return join_rows(grads, SSM)


def feed_forward(hidden, normed_ssm, attention, ffn_gain, cotangent, late, packed):
    rows, model = hidden.shape
    count = lax.axis_size("seq")
    f32, low = jnp.float32, jnp.bfloat16
    if packed:
        unit = late[0].shape[0] // count
        ffn = (late[0].shape[1] - 4 * model) // 2
        views = [late[0].reshape(count, unit, late[0].shape[1])]
        rows_of = {"down": 2 * unit, "ssm": unit + unit // 2, "o": unit // 2}
    else:
        unit = late[0].shape[0] // count
        ffn = late[0].shape[1] // 2
        views = list(late)
        rows_of = {"down": late[1].shape[0] // count}
        rows_of["ssm"] = late[2].shape[0] // count
        rows_of["o"] = late[3].shape[0] // count
    span = 1024
    steps = ffn // span
    half = unit // 2

    def layout(flat, gate_up, down, ssm, out):
        if not packed:
            return [
                (flat[2], ssm),
                (flat[3], out),
                *[
                    (flat[0].at[:, pl.ds(i * span, span)], gate_up.at[:, pl.ds(i * span, span)])
                    for i in range(2 * steps)
                ],
                (flat[1], down),
            ]
        base = 2 * ffn

        def group(number, first, size):
            return flat[0].at[:, pl.ds(first, size), pl.ds(base + number * model, model)]

        return [
            (group(2, 0, unit), ssm.at[:, pl.ds(0, unit), :]),
            (group(3, 0, half), ssm.at[:, pl.ds(unit, half), :]),
            (group(3, half, half), out),
            *[
                (flat[0].at[:, :, pl.ds(i * span, span)], gate_up.at[:, :, pl.ds(i * span, span)])
                for i in range(2 * steps)
            ],
            (group(0, 0, unit), down.at[:, pl.ds(0, unit), :]),
            (group(1, 0, unit), down.at[:, pl.ds(unit, unit), :]),
        ]

    kinds = len(views)
    early = 3 if packed else 2
    total = early + 2 * steps + (2 if packed else 1)

    def kernel(*refs):
        hidden_ref, ssm_ref, attn_ref, gain_ref, cot_ref = refs[:5]
        flats = refs[5 : 5 + kinds]
        refs = refs[5 + kinds :]
        layer_ref, mix_ref, attn_grad_ref, ssm_grad_ref, gain_grad_ref = refs[:5]
        grad_flats = refs[5 : 5 + kinds]
        refs = refs[5 + kinds :]
        weights, grads = refs[:4], refs[4:8]
        gate_ref, up_ref, act_ref, two_ref, after_ref, grad_two_ref, in_sem, out_sem = refs[8:]
        w_gate_up, w_down, w_ssm, w_o = weights
        g_gate_up, g_down, g_ssm, g_o = grads
        loads = [
            pltpu.make_async_copy(source, target, in_sem.at[i])
            for i, (source, target) in enumerate(layout(flats, w_gate_up, w_down, w_ssm, w_o))
        ]
        for copy in loads:
            copy.start()
        stores = [
            pltpu.make_async_copy(source, target, out_sem.at[i])
            for i, (target, source) in enumerate(
                layout(grad_flats, g_gate_up, g_down, g_ssm, g_o)
            )
        ]

        def whole(ref, start=0, width=None):
            value = ref[..., start : start + (ref.shape[-1] if width is None else width)]
            return value.reshape(-1, value.shape[-1])

        def product(left_side, right_side, axes):
            return lax.dot_general(
                left_side, right_side, (axes, ((), ())), preferred_element_type=f32
            )

        def keep(ref, value, start=0):
            ref[..., start : start + value.shape[1]] = value.astype(low).reshape(
                *ref.shape[:-1], value.shape[1]
            )

        for copy in loads[:early]:
            copy.wait()
        after = (
            hidden_ref[...].astype(f32)
            + product(ssm_ref[...], whole(w_ssm), NN)
            + product(attn_ref[...], whole(w_o), NN)
        )
        after_ref[...] = after
        scale = lax.rsqrt(jnp.mean(after * after, axis=1, keepdims=True) + epsilon)
        two_ref[...] = (after * scale * gain_ref[...]).astype(low)
        for step in range(steps):
            columns = slice(step * span, (step + 1) * span)
            loads[early + step].wait()
            loads[early + steps + step].wait()
            gate = product(two_ref[...], whole(w_gate_up, step * span, span), NN)
            up = product(two_ref[...], whole(w_gate_up, ffn + step * span, span), NN)
            gate_ref[:, columns] = gate
            up_ref[:, columns] = up
            act_ref[:, columns] = (gate * jax.nn.sigmoid(gate) * up).astype(low)
        for copy in loads[early + 2 * steps :]:
            copy.wait()
        layer_ref[...] = (after_ref[...] + product(act_ref[...], whole(w_down), NN)).astype(low)
        cot = cot_ref[...]
        rows_down = rows_of["down"]
        devices = span // rows_down if packed else span
        grad_two = jnp.zeros((rows, model), f32)
        for step in range(steps):
            columns = slice(step * span, (step + 1) * span)
            w_part = w_down[step * devices : (step + 1) * devices].reshape(span, model)
            grad_act = product(cot, w_part, NT)
            gate, up = gate_ref[:, columns], up_ref[:, columns]
            sigmoid_gate = jax.nn.sigmoid(gate)
            grad_gate = (
                grad_act * up * sigmoid_gate * (1.0 + gate * (1.0 - sigmoid_gate))
            ).astype(low)
            grad_up = (grad_act * gate * sigmoid_gate).astype(low)
            grad_two = grad_two + product(
                grad_gate, whole(w_gate_up, step * span, span), NT
            )
            grad_two = grad_two + product(
                grad_up, whole(w_gate_up, ffn + step * span, span), NT
            )
            keep(g_gate_up, product(two_ref[...], grad_gate, TN), step * span)
            stores[early + step].start()
            keep(g_gate_up, product(two_ref[...], grad_up, TN), ffn + step * span)
            stores[early + steps + step].start()
        grad_two_ref[...] = grad_two
        keep(g_down, product(act_ref[...], cot, TN))
        for copy in stores[early + 2 * steps :]:
            copy.start()
        after = after_ref[...]
        grad_two = grad_two_ref[...]
        scale = lax.rsqrt(jnp.mean(after * after, axis=1, keepdims=True) + epsilon)
        gain_grad_ref[...] = jnp.sum(after * scale * grad_two, axis=0, keepdims=True)
        scaled = grad_two * gain_ref[...]
        mix = (
            cot.astype(f32)
            + scale * scaled
            - after * (scale * scale * scale * jnp.mean(after * scaled, axis=1, keepdims=True))
        )
        mix_ref[...] = mix
        mix_low = mix.astype(low)
        attn_grad = product(mix_low, whole(w_o), NT).astype(low)
        group_size = QHEADS // KVHEADS
        for head in range(QHEADS):
            place = head % group_size * rows
            attn_grad_ref[head // group_size, place : place + rows, :] = attn_grad[
                :, head * HEAD_DIM : (head + 1) * HEAD_DIM
            ]
        ssm_grad_ref[...] = product(mix_low, whole(w_ssm), NT)
        keep(g_ssm, product(ssm_ref[...], mix_low, TN))
        keep(g_o, product(attn_ref[...], mix_low, TN))
        for copy in stores[:early]:
            copy.start()
        for copy in stores:
            copy.wait()

    shape = jax.ShapeDtypeStruct
    hbm = pl.BlockSpec(memory_space=pl.ANY)
    buffers = [
        (count, unit, 2 * ffn),
        (count, rows_of["down"], model),
        (count, rows_of["ssm"], model),
        (count, rows_of["o"], model),
    ]
    if not packed:
        buffers = [w.shape for w in late]
    outs = pl.pallas_call(
        kernel,
        out_shape=[
            shape((rows, model), low),
            shape((rows, model), f32),
            shape((KVHEADS, QHEADS // KVHEADS * rows, HEAD_DIM), low),
            shape((rows, SSM), f32),
            shape((1, model), f32),
        ]
        + [shape(view.shape, low) for view in views],
        in_specs=[VMEM_SPEC] * 5 + [hbm] * kinds,
        out_specs=[VMEM_SPEC] * 5 + [hbm] * kinds,
        scratch_shapes=[pltpu.VMEM(size, low) for size in buffers + buffers]
        + [
            pltpu.VMEM((rows, ffn), f32),
            pltpu.VMEM((rows, ffn), f32),
            pltpu.VMEM((rows, ffn), low),
            pltpu.VMEM((rows, model), low),
            pltpu.VMEM((rows, model), f32),
            pltpu.VMEM((rows, model), f32),
            pltpu.SemaphoreType.DMA((total,)),
            pltpu.SemaphoreType.DMA((total,)),
        ],
        compiler_params=BIG_VMEM,
        name="feed_forward",
    )(hidden, normed_ssm, attention, ffn_gain[None], cotangent, *views)
    return outs[:5], [g.reshape(w.shape) for g, w in zip(outs[5:], late)]


def projection_backward(
    normed_one,
    hidden,
    norm_gain,
    grad_mix,
    grad_gate_z,
    grad_ext,
    returned,
    grad_dt,
    grad_query,
    grad_kv,
    tables,
    weights,
):
    rows, model = hidden.shape
    f32, low = jnp.float32, jnp.bfloat16
    groups = QHEADS // KVHEADS
    half_kv = KVW // 2
    first_row = (lax.axis_index("seq") * rows).astype(jnp.int32).reshape(1)
    widths = [w.shape[1] for w in weights]

    def kernel(
        first_ref,
        normed_ref,
        hidden_ref,
        gain_ref,
        mix_ref,
        gate_ref,
        ext_ref,
        returned_ref,
        dt_ref,
        query_ref,
        kv_ref,
        base_cos_ref,
        base_sin_ref,
        far_cos_ref,
        far_sin_ref,
        *refs,
    ):
        weight_hbm, refs = refs[:3], refs[3:]
        input_ref, gain_grad_ref, refs = refs[0], refs[1], refs[2:]
        weight_grad_hbm, refs = refs[:3], refs[3:]
        weight_refs, weight_grad_refs, refs = refs[:3], refs[3:6], refs[6:]
        xbc_ref, small_ref, turned_ref, in_sem, out_sem = refs
        loads = [
            pltpu.make_async_copy(source, target, in_sem.at[i])
            for i, (source, target) in enumerate(zip(weight_hbm, weight_refs))
        ]
        for copy in loads:
            copy.start()
        stores = [
            pltpu.make_async_copy(source, target, out_sem.at[i])
            for i, (source, target) in enumerate(zip(weight_grad_refs, weight_grad_hbm))
        ]
        edge = rows - HALO
        xbc_ref[:edge, :] = ext_ref[HALO : HALO + edge, :].astype(low)
        xbc_ref[edge:, :] = (ext_ref[HALO + edge :, :] + returned_ref[...]).astype(low)
        for head in range(QHEADS):
            place = head % groups * rows
            turned_ref[:, head * HEAD_DIM : (head + 1) * HEAD_DIM] = jnp.transpose(
                query_ref[head // groups, :, place : place + rows]
            )
        cosine_all, sine_all = rope_now(
            first_ref[0] // rows, base_cos_ref, base_sin_ref, far_cos_ref, far_sin_ref
        )
        sine_all = -sine_all
        small_ref[:, :QW] = rope_lanes(
            turned_ref[...] * HEAD_DIM ** (-0.5), cosine_all, sine_all
        ).astype(low)
        kv = kv_ref[...]
        small_ref[:, QW : QW + half_kv] = rope_lanes(kv[:, :half_kv], cosine_all, sine_all).astype(
            low
        )
        small_ref[:, QW + half_kv : QW + KVW] = kv[:, half_kv:].astype(low)
        small_ref[:, QW + KVW :] = dt_ref[...]
        normed = normed_ref[...]
        grad_normed = jnp.zeros((rows, model), f32)
        for number, value_ref in enumerate((gate_ref, xbc_ref, small_ref)):
            loads[number].wait()
            for start in range(0, widths[number], 512):
                columns = slice(start, min(start + 512, widths[number]))
                part = value_ref[:, columns]
                grad_normed = grad_normed + lax.dot_general(
                    part,
                    weight_refs[number][:, columns],
                    (NT, ((), ())),
                    preferred_element_type=f32,
                )
                weight_grad_refs[number][:, columns] = lax.dot_general(
                    normed, part, (TN, ((), ())), preferred_element_type=f32
                ).astype(low)
            stores[number].start()
        values = hidden_ref[...].astype(f32)
        scale = lax.rsqrt(jnp.mean(values * values, axis=1, keepdims=True) + epsilon)
        gain_grad_ref[...] = jnp.sum(values * scale * grad_normed, axis=0, keepdims=True)
        scaled = grad_normed * gain_ref[...]
        input_ref[...] = (
            mix_ref[...]
            + scale * scaled
            - values * (scale * scale * scale * jnp.mean(values * scaled, axis=1, keepdims=True))
        ).astype(low)
        for copy in stores:
            copy.wait()

    shape = jax.ShapeDtypeStruct
    hbm = pl.BlockSpec(memory_space=pl.ANY)
    return pl.pallas_call(
        kernel,
        out_shape=[shape((rows, model), low), shape((1, model), f32)]
        + [shape(w.shape, low) for w in weights],
        in_specs=[pl.BlockSpec(memory_space=pltpu.SMEM)] + [VMEM_SPEC] * 14 + [hbm] * 3,
        out_specs=[VMEM_SPEC] * 2 + [hbm] * 3,
        scratch_shapes=[pltpu.VMEM(w.shape, low) for w in list(weights) * 2]
        + [
            pltpu.VMEM((rows, XBC), low),
            pltpu.VMEM((rows, QW + KVW + DT_PAD), low),
            pltpu.VMEM((rows, QW), f32),
            pltpu.SemaphoreType.DMA((3,)),
            pltpu.SemaphoreType.DMA((3,)),
        ],
        compiler_params=BIG_VMEM,
        name="projection_backward",
    )(
        first_row,
        normed_one,
        hidden,
        norm_gain[None],
        grad_mix,
        grad_gate_z,
        grad_ext,
        returned,
        grad_dt,
        grad_query,
        grad_kv,
        *tables,
        *weights,
    )


def per_device(
    hidden_in,
    doc_start,
    norm_gain,
    w_z,
    w_xbc,
    w_dt,
    conv_weight,
    conv_bias,
    dt_bias,
    a_log,
    d_skip,
    ssm_gain,
    w_ssm_out,
    w_q,
    w_kv,
    w_o,
    ffn_gain,
    w_gate,
    w_up,
    w_down,
    cotangent,
):
    local_rows, model = hidden_in.shape
    count = lax.axis_size("seq")
    first_row = lax.axis_index("seq") * local_rows
    group_size = QHEADS // KVHEADS
    unit, ffn = w_gate.shape
    rows_down, rows_out, rows_o = w_down.shape[0], w_ssm_out.shape[0], w_o.shape[0]
    stacked_rows = rows_down + rows_out + rows_o
    layers = stacked_rows // unit
    packed = unit % 32 == 0 and (rows_down, 2 * rows_out, 2 * rows_o) == (2 * unit, 3 * unit, unit)

    stacked_shard = jnp.concatenate([w_down, w_ssm_out, w_o], axis=0)
    late_shard = jnp.concatenate(
        [w_gate, w_up]
        + [stacked_shard[layer * unit : (layer + 1) * unit] for layer in range(layers)],
        axis=1,
    )
    late_full = lax.all_gather(late_shard, "seq", axis=0, tiled=True)
    small_shard = jnp.concatenate(
        [w_q, w_kv, jnp.pad(w_dt, ((0, 0), (0, DT_PAD - MHEADS)))], axis=1
    )
    *mixer_weights, halo = gather_everywhere(
        [w_xbc, small_shard, w_z], 0, 32768, hidden_in
    )
    mixer_weights = [mixer_weights[2], mixer_weights[0], mixer_weights[1]]

    tables = rope_table(local_rows, count)
    dt_bias_row = jnp.pad(dt_bias, (0, DT_PAD - MHEADS))[None]
    a_log_row = jnp.pad(a_log, (0, DT_PAD - MHEADS))[None]
    skip_lanes = jnp.repeat(d_skip, MHEAD_DIM)[None]
    (
        normed_one,
        gate_z,
        xbc_ext,
        conv_pre,
        grouped_q,
        kv_local,
        dt_pre,
        log_decay,
        local_state,
        passing,
    ) = mixer_forward(
        hidden_in,
        halo,
        norm_gain,
        mixer_weights,
        conv_weight,
        conv_bias,
        dt_bias_row,
        a_log_row,
        doc_start,
        tables,
    )
    states_in, decay_columns = states_before(passing[0, :MHEADS], local_state, 4)
    (kv_all,) = gather_everywhere([kv_local], 1, 16384)
    normed_ssm, ssm_y = mixer_output(
        conv_pre, dt_pre, log_decay, states_in, gate_z, ssm_gain, skip_lanes, doc_start
    )
    row_starts = jnp.tile(doc_start, group_size)[None]
    bounds = jnp.stack(
        [
            first_row,
            doc_start[local_rows - 1],
            doc_start[0] // KEYS_STEP,
            (first_row + local_rows - 1) // KEYS_STEP + 1,
        ]
    ).astype(jnp.int32)
    attn_grouped, log_total, attn_low = attention_forward(grouped_q, kv_all, row_starts, bounds)

    if packed:
        late = [late_full]
    else:
        stacked_full = (
            late_full[:, 2 * ffn :]
            .reshape(count, unit, layers, model)
            .transpose(0, 2, 1, 3)
            .reshape(count, stacked_rows, model)
        )
        late = [
            late_full[:, : 2 * ffn],
            stacked_full[:, :rows_down].reshape(-1, model),
            stacked_full[:, rows_down : rows_down + rows_out].reshape(-1, model),
            stacked_full[:, rows_down + rows_out :].reshape(-1, model),
        ]
    (layer_out, grad_mix, grad_attn_grouped, grad_normed_ssm, grad_ffn_gain), late_grads = (
        feed_forward(hidden_in, normed_ssm, attn_low, ffn_gain, cotangent, late, packed)
    )
    if packed:
        late_grad = late_grads[0]
    else:
        grad_stacked = jnp.concatenate(
            [g.reshape(count, -1, model) for g in late_grads[1:]], axis=1
        )
        grad_stacked = (
            grad_stacked.reshape(count, layers, unit, model)
            .transpose(0, 2, 1, 3)
            .reshape(count * unit, layers * model)
        )
        late_grad = jnp.concatenate([late_grads[0], grad_stacked], axis=1)
    late_sum = lax.psum_scatter(late_grad, "seq", scatter_dimension=0, tiled=True).astype(
        jnp.float32
    )
    shard_gate, shard_up = late_sum[:, :ffn], late_sum[:, ffn : 2 * ffn]
    stacked_sum = (
        late_sum[:, 2 * ffn :]
        .reshape(unit, layers, model)
        .transpose(1, 0, 2)
        .reshape(stacked_rows, model)
    )
    shard_down = stacked_sum[:rows_down]
    shard_ssm_out = stacked_sum[rows_down : rows_down + rows_out]
    shard_o = stacked_sum[rows_down + rows_out :]

    (
        grad_gate_z,
        grad_ssm_gain,
        grad_ssm_y,
        grad_states_in,
        grad_input_part,
        grad_b_part,
        grad_c,
        grad_log_part,
        grad_d_skip,
    ) = mixer_backward(
        grad_normed_ssm,
        ssm_y,
        gate_z,
        ssm_gain,
        conv_pre,
        dt_pre,
        log_decay,
        states_in,
        skip_lanes,
        doc_start,
    )
    grad_end = grads_after(decay_columns, grad_states_in, 5)
    grad_ext, grad_conv_weight, grad_conv_bias, grad_dt_raw, grad_dt_bias, grad_a_log = (
        mixer_input_backward(
            grad_end,
            states_in,
            passing,
            grad_ssm_y,
            grad_input_part,
            grad_b_part,
            grad_c,
            grad_log_part,
            conv_pre,
            dt_pre,
            log_decay,
            xbc_ext,
            conv_weight,
            a_log_row,
            skip_lanes,
            doc_start,
        )
    )
    returned = from_behind(grad_ext[:HALO], "seq", -1)
    key_terms, grad_query_grouped = attention_backward(
        grouped_q, grad_attn_grouped, kv_all, row_starts, log_total, attn_grouped, bounds
    )
    (grad_kv_local,) = scatter_sums([key_terms], None, 2, 16384)
    grad_input, grad_norm_gain, *mixer_grads = projection_backward(
        normed_one,
        hidden_in,
        norm_gain,
        grad_mix,
        grad_gate_z,
        grad_ext,
        returned,
        grad_dt_raw,
        grad_query_grouped,
        grad_kv_local,
        tables,
        mixer_weights,
    )

    small = [
        grad_norm_gain[0],
        grad_ssm_gain[0],
        grad_ffn_gain[0],
        grad_conv_weight.reshape(-1),
        grad_conv_bias[0],
        grad_dt_bias[0, :MHEADS],
        grad_a_log[0, :MHEADS],
        grad_d_skip[0, :MHEADS],
    ]
    sizes = [item.shape[0] for item in small]
    small_flat = jnp.concatenate(small)
    small_flat = jnp.pad(small_flat, (0, -small_flat.shape[0] % 1024)).reshape(-1, 128)
    shard_z, shard_xbc, shard_small, small_sum = scatter_sums(mixer_grads, small_flat, 3, 32768)
    starts = [sum(sizes[:i]) for i in range(len(sizes) + 1)]
    small_sum = small_sum.reshape(-1)
    sums = [small_sum[a:b] for a, b in zip(starts[:-1], starts[1:])]
    return (
        layer_out,
        grad_input,
        sums[0],
        shard_z,
        shard_xbc,
        shard_small[:, QW + KVW : QW + KVW + MHEADS],
        sums[3].reshape(conv_weight.shape),
        sums[4],
        sums[5],
        sums[6],
        sums[7],
        sums[1],
        shard_ssm_out,
        shard_small[:, :QW],
        shard_small[:, QW : QW + KVW],
        shard_o,
        sums[2],
        shard_gate,
        shard_up,
        shard_down,
    )


def solution(mesh):
    placed = (
        P("seq", None),
        P("seq"),
        P(),
        P("seq", None),
        P("seq", None),
        P("seq", None),
        P(),
        P(),
        P(),
        P(),
        P(),
        P(),
        P("seq", None),
        P("seq", None),
        P("seq", None),
        P("seq", None),
        P(),
        P("seq", None),
        P("seq", None),
        P("seq", None),
        P("seq", None),
    )
    return jax.shard_map(
        per_device,
        mesh=mesh,
        in_specs=placed,
        out_specs=(
            P("seq", None),
            P("seq", None),
            P(),
            P("seq", None),
            P("seq", None),
            P("seq", None),
            P(),
            P(),
            P(),
            P(),
            P(),
            P(),
            P("seq", None),
            P("seq", None),
            P("seq", None),
            P("seq", None),
            P(),
            P("seq", None),
            P("seq", None),
            P("seq", None),
        ),
        check_vma=False,
    )
```

```python
from functools import partial
import math

import jax
import jax.numpy as jnp
from jax import lax
from jax.experimental import pallas as pl
from jax.experimental.pallas import tpu as pltpu
from jax.sharding import PartitionSpec as P
import numpy as np

MHEADS = 24
MHEAD_DIM = 64
STATE = 128
CONV = 4
QHEADS = 8
KVHEADS = 2
HEAD_DIM = 64
SSM = 1536
XBC = 1792
QW = 512
KVW = 256
DT_PAD = 128


epsilon = 1e-05
rope_base = 100000000000.0
masked = -1e30


def from_behind(value, axis, steps):
    count = lax.axis_size(axis)
    first, last = (max(0, -steps), min(count, count - steps))
    return lax.ppermute(value, axis, [(source, source + steps) for source in range(first, last)])


MESH = pl.DeviceIdType.MESH
HALO = 16
VMEM_SPEC = pl.BlockSpec(memory_space=pltpu.VMEM)


def lattice(count):
    sizes, left, turn = [1, 1, 1], count // 2, 0
    while left > 1:
        factor = 2 if left % 2 == 0 else left
        sizes[turn % 3] *= factor
        left //= factor
        turn += 1
    return sizes[0], sizes[1], sizes[2], 2


def coordinates(sizes):
    me = lax.axis_index("seq")
    _, size_1, size_2, cores = sizes
    return (
        me // (size_1 * size_2 * cores),
        me // (size_2 * cores) % size_1,
        me // cores % size_2,
        me % cores,
    )


def device_at(sizes, place):
    index = place[0]
    for size, at in zip(sizes[1:], place[1:]):
        index = index * size + at
    return index


def partners(sizes, place, axis):
    found = []
    for step in range(1, sizes[axis]):
        other = list(place)
        other[axis] = (place[axis] + step) % sizes[axis]
        found.append(other)
    return found


def greet(sizes, place, more=()):
    barrier = pltpu.get_barrier_semaphore()
    met = [
        device_at(sizes, other) for axis in range(4) for other in partners(sizes, place, axis)
    ] + list(more)
    for other in met:
        pl.semaphore_signal(barrier, inc=1, device_id=(other,), device_id_type=MESH)
    pl.semaphore_wait(barrier, len(met))


def block_cuts(shapes, target):
    cuts = []
    for number, (rows, columns) in enumerate(shapes):
        pieces = max(1, round(rows * columns / target))
        width = max(128, (columns // pieces + 127) // 128 * 128)
        across = -(-columns // width)
        height = rows
        if across < pieces and rows % 32 == 0:
            height = max(32, rows // -(-pieces // across) // 32 * 32)
        for top in range(0, rows, height):
            for start in range(0, columns, width):
                size = (min(height, rows - top), min(width, columns - start))
                cuts.append((number, (pl.ds(top, size[0]), pl.ds(start, size[1]))))
    return cuts


def run_together(programs):
    waiting = list(programs)
    while waiting:
        for program in list(waiting):
            try:
                next(program)
            except StopIteration:
                waiting.remove(program)


ORDERS = ((0, 1, 2), (0, 2, 1))


def axis_order(turn):
    return ORDERS[turn % len(ORDERS)]


def tick_count(cuts, stages):
    return -(-len(cuts) // len(ORDERS)) + stages - 1


def tick_turns(cuts, number):
    first = number * len(ORDERS)
    return range(first, min(first + len(ORDERS), len(cuts))) if number >= 0 else range(0)


def gather_program(sizes, cuts, ins, outs, local_sem, send_sem, recv_sem):
    place = coordinates(sizes)
    sibling = partners(sizes, place, 3)[0]

    def region(turn, at):
        number, window = cuts[turn]
        return outs[number].at[*at, *window]

    def before(axis, step):
        at = list(place)
        at[axis] = (place[axis] - step - 1 + sizes[axis]) % sizes[axis]
        return at

    def widened(order, stage, at):
        full = list(at)
        for axis in order[:stage]:
            full[axis] = slice(None)
        return full

    def remote(turn, slot, step, source, target, other):
        return pltpu.make_async_remote_copy(
            src_ref=source,
            dst_ref=target,
            send_sem=send_sem.at[turn, slot, step],
            recv_sem=recv_sem.at[turn, slot, step],
            device_id=(device_at(sizes, other),),
            device_id_type=MESH,
        )

    def outgoing(turn, stage, step):
        order = axis_order(turn)
        here = region(turn, widened(order, stage, place))
        number, window = cuts[turn]
        source = ins[number].at[*window] if stage == 0 else here
        other = partners(sizes, place, order[stage])[step]
        return remote(turn, stage, step, source, here, other)

    def incoming(turn, stage, step):
        order = axis_order(turn)
        here = region(turn, widened(order, stage, before(order[stage], step)))
        return remote(turn, stage, step, here, here, sibling)

    def fresh(turn, stage, step, core):
        order = axis_order(turn)
        if stage == 0:
            at = widened(order, 1, place)
        else:
            at = widened(order, stage, before(order[stage], step))
        at[3] = core
        return region(turn, at)

    def across(turn, stage, step):
        here = fresh(turn, stage, step, place[3])
        return remote(turn, 3 + stage, step, here, here, sibling)

    def from_across(turn, stage, step):
        here = fresh(turn, stage, step, sibling[3])
        return remote(turn, 3 + stage, step, here, here, sibling)

    def hops(turn, stage):
        return range(sizes[axis_order(turn)[stage]] - 1)

    def pieces(turn, stage):
        return range(1) if stage == 0 else hops(turn, stage)

    def local(turn):
        number, window = cuts[turn]
        return pltpu.make_async_copy(
            ins[number].at[*window], region(turn, list(place)), local_sem.at[turn]
        )

    for turn in range(len(cuts)):
        local(turn).start()
        for step in hops(turn, 0):
            outgoing(turn, 0, step).start()
    yield

    def advance(turn, stage):
        for step in hops(turn, stage):
            incoming(turn, stage, step).wait_recv()
        if stage == 0:
            local(turn).wait()
        if stage < 2:
            for step in hops(turn, stage + 1):
                outgoing(turn, stage + 1, step).start()
        for step in pieces(turn, stage):
            across(turn, stage, step).start()

    for tick in range(tick_count(cuts, 3)):
        for stage in range(3):
            for turn in tick_turns(cuts, tick - stage):
                advance(turn, stage)
        yield
    for turn in range(len(cuts)):
        for stage in range(3):
            for step in pieces(turn, stage):
                from_across(turn, stage, step).wait_recv()
            for step in pieces(turn, stage):
                across(turn, stage, step).wait_send()
            for step in hops(turn, stage):
                outgoing(turn, stage, step).wait_send()


def gather_scratch(sizes, cuts):
    most = max(sizes[:3])
    return [
        pltpu.SemaphoreType.DMA((len(cuts),)),
        pltpu.SemaphoreType.DMA((len(cuts), 6, most)),
        pltpu.SemaphoreType.DMA((len(cuts), 6, most)),
    ]


def gather_everywhere(arrays, collective_id, target, edge):
    sizes = lattice(lax.axis_size("seq"))
    cuts = block_cuts([array.shape for array in arrays], target)
    kinds = len(arrays)

    def kernel(*refs):
        ins, edge_in, refs = refs[:kinds], refs[kinds], refs[kinds + 1 :]
        outs, edge_out, refs = refs[:kinds], refs[kinds], refs[kinds + 1 :]
        *sems, edge_sems = refs
        me, count = lax.axis_index("seq"), lax.axis_size("seq")
        following, previous = lax.rem(me + 1, count), lax.rem(me + count - 1, count)
        greet(sizes, coordinates(sizes), [following, previous])
        edge_copy = pltpu.make_async_remote_copy(
            src_ref=edge_in.at[pl.ds(edge.shape[0] - HALO, HALO), :],
            dst_ref=edge_out,
            send_sem=edge_sems.at[0],
            recv_sem=edge_sems.at[1],
            device_id=(following,),
            device_id_type=MESH,
        )
        edge_copy.start()
        run_together([gather_program(sizes, cuts, ins, outs, *sems)])
        edge_copy.wait()

    hbm = pl.BlockSpec(memory_space=pl.ANY)
    gathered = pl.pallas_call(
        kernel,
        out_shape=[jax.ShapeDtypeStruct(sizes + a.shape, a.dtype) for a in arrays]
        + [jax.ShapeDtypeStruct((HALO, edge.shape[1]), edge.dtype)],
        in_specs=[hbm] * (kinds + 1),
        out_specs=[hbm] * (kinds + 1),
        scratch_shapes=gather_scratch(sizes, cuts) + [pltpu.SemaphoreType.DMA((2,))],
        compiler_params=pltpu.CompilerParams(
            collective_id=collective_id,
            has_side_effects=True,
            vmem_limit_bytes=62 * 1024 * 1024,
        ),
        name="gather_everywhere",
    )(*arrays, edge)
    return [g.reshape(-1, a.shape[1]) for g, a in zip(gathered, arrays)] + [gathered[kinds]]


def scatter_plan(shapes, small, target):
    sizes = lattice(lax.axis_size("seq"))
    cuts = block_cuts(shapes, target)
    kinds = len(shapes)
    most = max(sizes[:3])
    used = [axis_order(turn)[::-1] for turn in range(len(cuts))]
    pairs = [[[axis for axis in range(3) if axis != axes[0]] for axes in used]][0]
    first_lead = tuple(max(sizes[pair[i]] for pair in pairs) for i in range(2))
    first_step = max(sizes[axes[0]] for axes in used) - 1
    second_lead = max(sizes[axes[2]] for axes in used)
    second_step = max(sizes[axes[1]] for axes in used) - 1
    last_step = max(sizes[axes[2]] for axes in used) - 1
    extra = 0 if small is None else 1

    def program(ins, small_in, outs, small_out, refs):
        own, core_in, first_in, second_in, last_in = [
            refs[i * kinds : (i + 1) * kinds] for i in range(5)
        ]
        refs = refs[5 * kinds :]
        local_sem, send_sem, recv_sem = refs[:3]
        place = coordinates(sizes)
        sibling = partners(sizes, place, 3)[0]
        sent = []

        def push(source, target_ref, other, sems, slot):
            copy = pltpu.make_async_remote_copy(
                src_ref=source,
                dst_ref=target_ref,
                send_sem=sems[0].at[slot],
                recv_sem=sems[1].at[slot],
                device_id=(device_at(sizes, other),),
                device_id_type=MESH,
            )
            copy.start()
            sent.append(copy)

        def arrival(here, sems, slot):
            pltpu.make_async_remote_copy(
                src_ref=here,
                dst_ref=here,
                send_sem=sems[0].at[slot],
                recv_sem=sems[1].at[slot],
                device_id=(device_at(sizes, sibling),),
                device_id_type=MESH,
            ).wait_recv()

        main_sems = (send_sem, recv_sem)

        def core_copy(turn):
            number, window = cuts[turn]
            return pltpu.make_async_remote_copy(
                src_ref=ins[number].at[:, :, :, sibling[3], *window],
                dst_ref=core_in[number].at[:, :, :, *window],
                send_sem=send_sem.at[turn, 0, 0],
                recv_sem=recv_sem.at[turn, 0, 0],
                device_id=(device_at(sizes, sibling),),
                device_id_type=MESH,
            )

        def local_copy(turn):
            number, window = cuts[turn]
            return pltpu.make_async_copy(
                ins[number].at[:, :, :, place[3], *window],
                own[number].at[:, :, :, *window],
                local_sem.at[turn],
            )

        for turn in range(len(cuts)):
            core_copy(turn).start()
            local_copy(turn).start()
        yield

        def kept(number, window, axes, stage, at):
            index = [slice(None), slice(None), slice(None)]
            for axis in axes[:stage]:
                index[axis] = at[axis]
            return own[number].at[*index, *window]

        def landed(number, window, axes, stage, step):
            if stage == 3:
                return last_in[number].at[step, *window]
            left = [sizes[axis] for axis in range(3) if axis not in axes[:stage]]
            box = (first_in, second_in)[stage - 1][number]
            return box.at[step, *[pl.ds(0, size) for size in left], *window]

        def advance(turn, stage):
            number, window = cuts[turn]
            axes = axis_order(turn)[::-1]
            lead = tuple(sizes[axis] for axis in range(3) if axis not in axes[:stage])
            if stage == 0:
                local_copy(turn).wait()
                arrival(core_in[number].at[:, :, :, *window], main_sems, (turn, 0, 0))
                pieces = [core_in[number].at[:, :, :, *window]]
            else:
                steps = range(sizes[axes[stage - 1]] - 1)
                pieces = [landed(number, window, axes, stage, step) for step in steps]
                for step in steps:
                    arrival(pieces[step], main_sems, (turn, stage, step))
            target_ref = kept(number, window, axes, stage, place)

            def total(index):
                value = target_ref[index].astype(jnp.float32)
                for piece in pieces:
                    value = value + piece[index].astype(jnp.float32)
                return value

            if stage == 3:
                outs[number][window] = total((...,))
                return
            amount = math.prod(lead)

            def add(flat, carry):
                index, rest = [], flat
                for size in lead[::-1]:
                    index.insert(0, rest % size)
                    rest = rest // size
                target_ref[tuple(index)] = total(tuple(index)).astype(jnp.bfloat16)
                return carry

            lax.fori_loop(0, amount, add, 0)
            for step in range(sizes[axes[stage]] - 1):
                onward(turn, stage, step).start()

        def onward(turn, stage, step):
            number, window = cuts[turn]
            axes = axis_order(turn)[::-1]
            other = partners(sizes, place, axes[stage])[step]
            return pltpu.make_async_remote_copy(
                src_ref=kept(number, window, axes, stage + 1, other),
                dst_ref=landed(number, window, axes, stage + 1, step),
                send_sem=send_sem.at[turn, stage + 1, step],
                recv_sem=recv_sem.at[turn, stage + 1, step],
                device_id=(device_at(sizes, other),),
                device_id_type=MESH,
            )

        if extra:
            boxes, small_sems = refs[3:7], refs[7:9]

        def small_step(tick):
            axes = (3, 2, 1, 0)
            if tick > 0:
                axis = axes[tick - 1]
                box = boxes[axis]
                for step in range(sizes[axis] - 1):
                    behind = (place[axis] - step - 1 + sizes[axis]) % sizes[axis]
                    arrival(box.at[behind], small_sems, (axis, step))
                value = box[0]
                for at in range(1, sizes[axis]):
                    value = value + box[at]
            else:
                value = small_in[0][...]
            if tick == 4:
                small_out[0][...] = value
                return
            axis = axes[tick]
            boxes[axis][place[axis]] = value
            here = boxes[axis].at[place[axis]]
            for step, other in enumerate(partners(sizes, place, axis)):
                push(here, here, other, small_sems, (axis, step))

        for tick in range(max(tick_count(cuts, 4), 5)):
            for stage in range(4):
                for turn in tick_turns(cuts, tick - stage):
                    advance(turn, stage)
            if extra and tick < 5:
                small_step(tick)
            yield
        for copy in sent:
            copy.wait_send()
        for turn in range(len(cuts)):
            core_copy(turn).wait_send()
            axes = axis_order(turn)[::-1]
            for stage in range(3):
                for step in range(sizes[axes[stage]] - 1):
                    onward(turn, stage, step).wait_send()

    scratch = []
    for lead in (
        sizes[:3],
        sizes[:3],
        (first_step,) + first_lead,
        (second_step, second_lead),
        (last_step,),
    ):
        scratch += [pltpu.VMEM(lead + s, jnp.bfloat16) for s in shapes]
    scratch += [
        pltpu.SemaphoreType.DMA((len(cuts),)),
        pltpu.SemaphoreType.DMA((len(cuts), 4, most)),
        pltpu.SemaphoreType.DMA((len(cuts), 4, most)),
    ]
    if extra:
        scratch += [pltpu.VMEM((size,) + small.shape, jnp.float32) for size in sizes]
        scratch += [pltpu.SemaphoreType.DMA((4, most)) for _ in range(2)]
    return program, scratch


def scatter_sums(parts, small, collective_id, target):
    sizes = lattice(lax.axis_size("seq"))
    count = lax.axis_size("seq")
    shapes = [(p.shape[0] // count, p.shape[1]) for p in parts]
    views = [p.reshape(sizes + s) for p, s in zip(parts, shapes)]
    program, scratch = scatter_plan(shapes, small, target)
    kinds = len(parts)

    def kernel(*refs):
        ins, small_in, refs = refs[:kinds], refs[kinds : kinds + 1], refs[kinds + 1 :]
        outs, small_out, refs = refs[:kinds], refs[kinds : kinds + 1], refs[kinds + 1 :]
        greet(sizes, coordinates(sizes))
        run_together([program(ins, small_in, outs, small_out, refs)])

    return pl.pallas_call(
        kernel,
        out_shape=[jax.ShapeDtypeStruct(s, jnp.float32) for s in shapes]
        + [jax.ShapeDtypeStruct(small.shape, jnp.float32)],
        in_specs=[pl.BlockSpec(memory_space=pl.ANY)] * kinds + [VMEM_SPEC],
        out_specs=[VMEM_SPEC] * (kinds + 1),
        scratch_shapes=scratch,
        compiler_params=pltpu.CompilerParams(
            collective_id=collective_id,
            has_side_effects=True,
            vmem_limit_bytes=62 * 1024 * 1024,
        ),
        name="scatter_sums",
    )(*views, small)


def greet_chips(chips):
    me = lax.axis_index("seq")
    chip, core = me // 2, me % 2
    barrier = pltpu.get_barrier_semaphore()

    def greet_one(step, carry):
        other = lax.rem(chip + step, chips) * 2 + core
        pl.semaphore_signal(barrier, inc=1, device_id=(other,), device_id_type=MESH)
        return carry

    lax.fori_loop(1, chips, greet_one, 0)
    pl.semaphore_signal(barrier, inc=1, device_id=(chip * 2 + 1 - core,), device_id_type=MESH)
    pl.semaphore_wait(barrier, chips)


def exchange_program(chips, part, reverse, own_ref, decay_ref, out_ref, chip_decay_ref, refs):
    (
        mine_low,
        other_low,
        other_decay,
        payload,
        landed,
        result,
        prefix,
        pair_sems,
        far_send,
        far_recv,
    ) = refs
    padded = own_ref.shape[2]
    me = lax.axis_index("seq")
    chip, core = me // 2, me % 2
    sibling = chip * 2 + 1 - core
    f32, low = jnp.float32, jnp.bfloat16

    def pair_copy(source, target, slot):
        return pltpu.make_async_remote_copy(
            src_ref=source,
            dst_ref=target,
            send_sem=pair_sems.at[slot, 0],
            recv_sem=pair_sems.at[slot, 1],
            device_id=(sibling,),
            device_id_type=MESH,
        )

    def far_copy(step, turn, source, target):
        other = lax.rem(chip + step, chips)
        return pltpu.make_async_remote_copy(
            src_ref=source.at[other],
            dst_ref=target.at[chip],
            send_sem=far_send.at[turn, step],
            recv_sem=far_recv.at[turn, step],
            device_id=(other * 2 + core,),
            device_id_type=MESH,
        )

    def far_start(turn, source, target):
        def start(step, carry):
            far_copy(step, turn, source, target).start()
            return carry

        lax.fori_loop(1, chips, start, 0)

    def far_wait(turn, source, target):
        def finish(step, carry):
            far_copy(step, turn, source, target).wait()
            return carry

        lax.fori_loop(1, chips, finish, 0)

    def by_row(vector, half, shape, first=0):
        place = (
            lax.broadcasted_iota(jnp.int32, shape, 0) + first
        ) * part + lax.broadcasted_iota(jnp.int32, shape, 1)
        head = (half * (chips * part) + place) // MHEAD_DIM
        lane = lax.broadcasted_iota(jnp.int32, shape, 2)
        picked = jnp.where(lane == head, vector.reshape(1, 1, 128), 0.0)
        return jnp.sum(picked, axis=2, keepdims=True)

    mine_low[...] = own_ref[...].astype(low)
    first_copies = [
        pair_copy(mine_low, other_low, 0),
        pair_copy(decay_ref, other_decay, 1),
    ]
    for copy in first_copies:
        copy.start()
    yield
    for copy in first_copies:
        copy.wait()
    own_decay, far_decay = decay_ref[0:1, :], other_decay[0:1, :]
    second_core = core == 1
    decays = (
        jnp.where(second_core, far_decay, own_decay),
        jnp.where(second_core, own_decay, far_decay),
    )
    weighted = 0 if reverse else 1
    whole = (chips, padded, 128)
    half_own = own_ref[core]
    half_far = other_low[core].astype(f32)
    earlier = jnp.where(second_core, half_far, half_own)
    later = jnp.where(second_core, half_own, half_far)
    factor = by_row(decays[weighted], core, whole)
    total = earlier + factor * later if reverse else factor * earlier + later
    payload[:, :padded, :] = total.astype(low)
    if not reverse:
        both = decays[0] * decays[1]
        high = both.astype(low).astype(f32)
        row = lax.broadcasted_iota(jnp.int32, (16, 128), 0)
        tail = jnp.where(row == 0, high, jnp.where(row == 1, both - high, 0.0)).astype(low)
        for other in range(chips):
            payload[other, padded:, :] = tail
    far_start(0, payload, landed)
    landed[chip] = payload[chip]
    yield
    far_wait(0, payload, landed)
    if not reverse:
        for other in range(chips):
            rows = landed[other, padded:, :].astype(f32)
            chip_decay_ref[other : other + 1, :] = rows[0:1, :] + rows[1:2, :]
    state = jnp.zeros((1, padded, 128), f32)
    order = range(chips - 1, -1, -1) if reverse else range(chips)
    for other in order:
        result[other] = state[0]
        step_factor = by_row(chip_decay_ref[other : other + 1, :], core, (1, padded, 128), chip)
        state = step_factor * state + landed[other, :padded, :].astype(f32)[None]
    far_start(1, result, prefix)
    prefix[chip] = result[chip]
    yield
    far_wait(1, result, prefix)
    out_ref[core] = prefix[...]
    last_copy = pair_copy(prefix, out_ref.at[core], 2)
    last_copy.start()
    yield
    last_copy.wait()
    moved = (core == 0) if reverse else second_core
    step_decay = decays[1] if reverse else decays[0]
    for half in range(2):
        factor = jnp.where(moved, by_row(step_decay, half, whole), 1.0)
        extra = jnp.where(moved, other_low[half].astype(f32), 0.0)
        out_ref[half] = factor * out_ref[half] + extra


def exchange_scratch(chips, padded, reverse):
    low, f32 = jnp.bfloat16, jnp.float32
    sent_rows = padded if reverse else padded + 16
    return [
        pltpu.VMEM((2, chips, padded, 128), low),
        pltpu.VMEM((2, chips, padded, 128), low),
        pltpu.VMEM((8, 128), f32),
        pltpu.VMEM((chips, sent_rows, 128), low),
        pltpu.VMEM((chips, sent_rows, 128), low),
        pltpu.VMEM((chips, padded, 128), f32),
        pltpu.VMEM((chips, padded, 128), f32),
        pltpu.SemaphoreType.DMA((3, 2)),
        pltpu.SemaphoreType.DMA((2, chips)),
        pltpu.SemaphoreType.DMA((2, chips)),
    ]


def slice_rows(values, chips):
    part = values.shape[0] // (2 * chips)
    padded = -(-part // 16) * 16
    sliced = values.reshape(2, chips, part, values.shape[1])
    return jnp.pad(sliced, ((0, 0), (0, 0), (0, padded - part), (0, 0)))


def join_rows(slices, rows):
    chips = slices.shape[1]
    return slices[:, :, : rows // (2 * chips)].reshape(rows, slices.shape[3])


def front(kv_local, local_state, passing, late, mixer_args, attention_args, collective_id, targets):
    count = lax.axis_size("seq")
    sizes, chips = lattice(count), count // 2
    cuts = block_cuts([kv_local.shape], targets[0])
    late_cuts = block_cuts([w.shape for w in late], targets[1])
    states = slice_rows(local_state, chips)
    part, padded = SSM // count, states.shape[2]
    fused = part == padded
    kinds = len(late)
    shape = jax.ShapeDtypeStruct
    rows = mixer_args[0].shape[0]
    groups, query_rows, _ = attention_args[0].shape
    tokens = kv_local.shape[0] * count
    comm_scratch = (
        gather_scratch(sizes, cuts)
        + gather_scratch(sizes, late_cuts)
        + exchange_scratch(chips, padded, False)
    )
    compute_scratch = (
        [pltpu.VMEM((3 * rows, SSM), jnp.bfloat16)]
        + attention_scratch(groups, query_rows)
        + [
            pltpu.VMEM(sizes + kv_local.shape, kv_local.dtype),
            pltpu.SemaphoreType.DMA((1,)),
        ]
    )
    extra_in = list(mixer_args) + list(attention_args) if fused else []
    extra_out = mixer_output_shapes(rows) + attention_shapes(groups, query_rows) if fused else []

    def kernel(*refs):
        kv_ref, state_ref, decay_ref, refs = refs[0], refs[1], refs[2], refs[3:]
        late_in, refs = refs[:kinds], refs[kinds:]
        ins, refs = refs[: len(extra_in)], refs[len(extra_in) :]
        kv_out, state_out, chip_decay_ref, refs = refs[0], refs[1], refs[2], refs[3:]
        late_out, refs = refs[:kinds], refs[kinds:]
        outs, refs = refs[: len(extra_out)], refs[len(extra_out) :]
        comm, refs = refs[: len(comm_scratch)], refs[len(comm_scratch) :]
        greet_chips(chips)
        exchange = exchange_program(
            chips, part, False, state_ref, decay_ref, state_out, chip_decay_ref, comm[6:]
        )
        keys = gather_program(sizes, cuts, [kv_ref], [kv_out], *comm[:3])
        weights = gather_program(sizes, late_cuts, late_in, late_out, *comm[3:6])
        run_together([exchange, keys])
        next(weights)
        if not fused:
            for _ in weights:
                pass
            return
        input_ref, max_ref, acc_ref, kv_vmem, kv_sem = refs
        load = pltpu.make_async_copy(kv_out, kv_vmem, kv_sem.at[0])
        load.start()
        mixer_output_body(
            *ins[:3], state_out[...].reshape(SSM, STATE), *ins[3:7], *outs[:2], input_ref
        )
        load.wait()
        next(weights)
        left = tick_count(late_cuts, 3) - 1
        steps = tokens // KEYS_STEP
        attention_forward_body(
            ins[7],
            kv_vmem.reshape(tokens, kv_local.shape[1]),
            ins[8],
            *outs[2:],
            max_ref,
            acc_ref,
            spread_ticks(weights, left, steps),
        )
        for _ in weights:
            pass

    hbm = pl.BlockSpec(memory_space=pl.ANY)
    kv_all, states_in, chip_decay, *rest = pl.pallas_call(
        kernel,
        out_shape=[
            shape(sizes + kv_local.shape, kv_local.dtype),
            shape(states.shape, jnp.float32),
            shape((chips, 128), jnp.float32),
        ]
        + [shape(sizes + w.shape, w.dtype) for w in late]
        + extra_out,
        in_specs=[hbm, VMEM_SPEC, VMEM_SPEC] + [hbm] * kinds + [VMEM_SPEC] * len(extra_in),
        out_specs=[hbm, VMEM_SPEC, VMEM_SPEC] + [hbm] * kinds + [VMEM_SPEC] * len(extra_out),
        scratch_shapes=comm_scratch + (compute_scratch if fused else []),
        compiler_params=pltpu.CompilerParams(
            collective_id=collective_id,
            has_side_effects=True,
            vmem_limit_bytes=62 * 1024 * 1024,
        ),
        name="front",
    )(kv_local, states, passing, *late, *extra_in)
    kv_all = kv_all.reshape(-1, kv_local.shape[1])
    late_full = [w.reshape(-1, w.shape[-1]) for w in rest[:kinds]]
    states_in = join_rows(states_in, SSM)
    computed = rest[kinds:]
    if not fused:
        computed = mixer_output(*mixer_args[:3], states_in, *mixer_args[3:])
        computed = list(computed) + list(
            attention_forward(attention_args[0], kv_all, attention_args[1])
        )
    return kv_all, states_in, chip_decay, late_full, computed


def back(key_terms, mixer_args, passing, chip_decay, late_grads, collective_id, targets):
    count = lax.axis_size("seq")
    sizes, chips = lattice(count), count // 2
    shape = (key_terms.shape[0] // count, key_terms.shape[1])
    late_shapes = [(g.shape[0] // count, g.shape[1]) for g in late_grads]
    keys, keys_scratch = scatter_plan([shape], None, targets[0])
    weights, weights_scratch = scatter_plan(late_shapes, None, targets[1])
    part = SSM // count
    padded = -(-part // 16) * 16
    fused = part == padded
    rows = mixer_args[0].shape[0]
    state_shape = (2, chips, padded, STATE)
    kinds = len(late_grads)
    if fused:
        first_in, mixer_shapes = list(mixer_args), mixer_backward_shapes(rows, state_shape)
        compute_scratch = mixer_backward_scratch(rows)
    else:
        mixer_out = list(mixer_backward(mixer_args))
        first_in, mixer_shapes = [slice_rows(mixer_out[3], chips)], []
        compute_scratch = []
    known = len(first_in)
    made = len(mixer_shapes)

    def kernel(kv_ref, decay_ref, chip_decay_ref, *refs):
        late_in, refs = refs[:kinds], refs[kinds:]
        ins, refs = refs[:known], refs[known:]
        kv_out, state_out, refs = refs[0], refs[1], refs[2:]
        late_out, refs = refs[:kinds], refs[kinds:]
        outs, refs = refs[:made], refs[made:]
        keys_refs, refs = refs[: len(keys_scratch)], refs[len(keys_scratch) :]
        weights_refs, refs = refs[: len(weights_scratch)], refs[len(weights_scratch) :]
        mixer_refs, refs = refs[: len(compute_scratch)], refs[len(compute_scratch) :]
        greet_chips(chips)
        runs = [
            keys([kv_ref], [], [kv_out], [], keys_refs),
            weights(late_in, [], late_out, [], weights_refs),
        ]

        def tick():
            for run in runs:
                next(run)

        tick()
        if fused:
            mixer_backward_body(*ins, *outs, *mixer_refs, tick)
            own_ref = outs[3]
        else:
            own_ref = ins[0]
        exchange = exchange_program(
            chips, part, True, own_ref, decay_ref, state_out, chip_decay_ref, refs
        )
        run_together([exchange] + runs)

    hbm = pl.BlockSpec(memory_space=pl.ANY)
    kv_sum, grad_end, *rest = pl.pallas_call(
        kernel,
        out_shape=[
            jax.ShapeDtypeStruct(shape, jnp.float32),
            jax.ShapeDtypeStruct(state_shape, jnp.float32),
        ]
        + [jax.ShapeDtypeStruct(s, jnp.float32) for s in late_shapes]
        + mixer_shapes,
        in_specs=[hbm] + [VMEM_SPEC] * 2 + [hbm] * kinds + [VMEM_SPEC] * known,
        out_specs=[VMEM_SPEC] * (2 + kinds + made),
        scratch_shapes=keys_scratch
        + weights_scratch
        + compute_scratch
        + exchange_scratch(chips, padded, True),
        compiler_params=pltpu.CompilerParams(
            collective_id=collective_id,
            has_side_effects=True,
            vmem_limit_bytes=63 * 1024 * 1024,
        ),
        name="back",
    )(
        key_terms.reshape(sizes + shape),
        passing,
        chip_decay,
        *[g.reshape(sizes + s) for g, s in zip(late_grads, late_shapes)],
        *first_in,
    )
    if fused:
        mixer_out = rest[kinds:]
    return kv_sum, join_rows(grad_end, SSM), rest[:kinds], mixer_out


KEYS_STEP = 512


def attention_forward_body(
    q_ref, kv_ref, starts_ref, out_ref, log_ref, flat_ref, max_ref, acc_ref, ticks
):
    groups, rows, _ = q_ref.shape
    group_size = QHEADS // KVHEADS
    local_rows = rows // group_size
    half_kv = KVW // 2
    steps = kv_ref.shape[0] // KEYS_STEP
    first_row = lax.axis_index("seq") * local_rows
    used = (first_row + local_rows - 1) // KEYS_STEP + 1
    starts = starts_ref[...]
    places = first_row + lax.broadcasted_iota(jnp.int32, (1, rows), 1) % local_rows
    max_ref[...] = jnp.full(max_ref.shape, masked, jnp.float32)
    acc_ref[...] = jnp.zeros(acc_ref.shape, jnp.float32)

    def block(step, general):
        first_key = pl.multiple_of(step * KEYS_STEP, KEYS_STEP)
        piece = kv_ref[pl.ds(first_key, KEYS_STEP), :]
        flipped = jnp.transpose(piece[:, half_kv:])
        ones = jnp.ones((16, KEYS_STEP), jnp.bfloat16)
        if general:
            key_pos = first_key + lax.broadcasted_iota(jnp.int32, (KEYS_STEP, 1), 0)
            allowed = (key_pos >= starts) & (key_pos <= places)
        else:
            row_open = starts <= first_key
        for group in range(groups):
            scores = lax.dot_general(
                piece[:, group * HEAD_DIM : (group + 1) * HEAD_DIM],
                q_ref[group],
                (((1,), (1,)), ((), ())),
                preferred_element_type=jnp.float32,
            )
            if general:
                scores = jnp.where(allowed, scores, masked)
            old = max_ref[group]
            new = jnp.maximum(old, jnp.max(scores, axis=0, keepdims=True))
            if general:
                shift = new
            else:
                new = jnp.where(row_open, new, old)
                shift = jnp.where(row_open, new, -masked)
            max_ref[group] = new
            weights = jnp.exp(scores - shift).astype(jnp.bfloat16)
            values = jnp.concatenate(
                [flipped[group * HEAD_DIM : (group + 1) * HEAD_DIM], ones], axis=0
            )
            acc_ref[group] = acc_ref[group] * jnp.exp(old - new) + jnp.dot(
                values, weights, preferred_element_type=jnp.float32
            )

    def body(step, carry):
        general = (step == 0) | ((step + 1) * KEYS_STEP > first_row)
        pl.when((step < used) & general)(partial(block, step, True))
        pl.when((step < used) & jnp.logical_not(general))(partial(block, step, False))
        for at, tick in ticks:
            pl.when(step == at)(tick)
        return carry

    lax.fori_loop(0, steps, body, 0)
    for group in range(groups):
        row_sum = acc_ref[group, HEAD_DIM : HEAD_DIM + 1, :]
        out = acc_ref[group, :HEAD_DIM, :] / row_sum
        out_ref[group] = out
        log_ref[group] = max_ref[group] + jnp.log(row_sum)
        for part in range(group_size):
            head = group * group_size + part
            flat_ref[:, head * HEAD_DIM : (head + 1) * HEAD_DIM] = jnp.transpose(
                out[:, part * local_rows : (part + 1) * local_rows]
            ).astype(jnp.bfloat16)


def attention_shapes(groups, rows):
    return [
        jax.ShapeDtypeStruct((groups, HEAD_DIM, rows), jnp.float32),
        jax.ShapeDtypeStruct((groups, 1, rows), jnp.float32),
        jax.ShapeDtypeStruct((rows // (QHEADS // KVHEADS), QW), jnp.bfloat16),
    ]


def attention_scratch(groups, rows):
    return [
        pltpu.VMEM((groups, 1, rows), jnp.float32),
        pltpu.VMEM((groups, HEAD_DIM + 16, rows), jnp.float32),
    ]


def attention_forward(queries, kv_all, row_starts):
    groups, rows, _ = queries.shape

    def kernel(*refs):
        attention_forward_body(*refs, [])

    return pl.pallas_call(
        kernel,
        out_shape=attention_shapes(groups, rows),
        in_specs=[VMEM_SPEC] * 3,
        out_specs=[VMEM_SPEC] * 3,
        scratch_shapes=attention_scratch(groups, rows),
        compiler_params=BIG_VMEM,
        name="attention_forward",
    )(queries, kv_all, row_starts)


def spread_ticks(program, ticks, steps):
    def make_tick():
        def tick():
            next(program, None)

        return tick

    return [(number * steps // ticks, make_tick()) for number in range(ticks)]


def attention_backward(
    queries, grads, kv_all, row_starts, log_total, outputs, late_grads, collective_id, target
):
    groups, rows, _ = queries.shape
    total = kv_all.shape[0]
    half_kv = KVW // 2
    group_size = QHEADS // KVHEADS
    local_rows = rows // group_size
    count = lax.axis_size("seq")
    sizes = lattice(count)
    shapes = [(g.shape[0] // count, g.shape[1]) for g in late_grads]
    views = [g.reshape(sizes + s) for g, s in zip(late_grads, shapes)]
    program, scratch = scatter_plan(shapes, None, target)
    kinds = len(shapes)
    ticks = max(tick_count(block_cuts(shapes, target), 4), 5)
    steps = total // KEYS_STEP

    def kernel(q_ref, g_ref, kv_ref, starts_ref, log_ref, outputs_ref, *refs):
        ins, dkv_ref, dq_ref, refs = refs[:kinds], refs[kinds], refs[kinds + 1], refs[kinds + 2 :]
        outs, delta_ref, refs = refs[:kinds], refs[kinds], refs[kinds + 1 :]
        greet(sizes, coordinates(sizes))
        sums = program(ins, [], outs, [], refs)
        next(sums)
        first_row = lax.axis_index("seq") * local_rows
        used = (first_row + local_rows - 1) // KEYS_STEP + 1
        starts = starts_ref[...]
        places = first_row + lax.broadcasted_iota(jnp.int32, (1, rows), 1) % local_rows
        dq_ref[...] = jnp.zeros(dq_ref.shape, jnp.float32)
        for group in range(groups):
            flipped_grads = jnp.transpose(g_ref[group].astype(jnp.float32))
            delta_ref[group] = jnp.sum(flipped_grads * outputs_ref[group], axis=0, keepdims=True)

        def block(step, general):
            first_key = pl.multiple_of(step * KEYS_STEP, KEYS_STEP)
            piece = kv_ref[pl.ds(first_key, KEYS_STEP), :]
            flipped = jnp.transpose(piece[:, :half_kv])
            if general:
                key_pos = first_key + lax.broadcasted_iota(jnp.int32, (KEYS_STEP, 1), 0)
                allowed = (key_pos >= starts) & (key_pos <= places)
            else:
                row_open = starts <= first_key
            found = []
            for group in range(groups):
                low, high = group * HEAD_DIM, (group + 1) * HEAD_DIM
                scores = lax.dot_general(
                    piece[:, low:high],
                    q_ref[group],
                    (((1,), (1,)), ((), ())),
                    preferred_element_type=jnp.float32,
                )
                shift = log_ref[group]
                if general:
                    scores = jnp.where(allowed, scores, masked)
                else:
                    shift = jnp.where(row_open, shift, -masked)
                weights = jnp.exp(scores - shift)
                grad_weights = lax.dot_general(
                    piece[:, half_kv + low : half_kv + high],
                    g_ref[group],
                    (((1,), (1,)), ((), ())),
                    preferred_element_type=jnp.float32,
                )
                grad_scores = (weights * (grad_weights - delta_ref[group])).astype(jnp.bfloat16)
                dq_ref[group] += jnp.dot(
                    flipped[low:high], grad_scores, preferred_element_type=jnp.float32
                )
                found.append(
                    jnp.dot(grad_scores, q_ref[group], preferred_element_type=jnp.float32)
                )
                found.append(
                    jnp.dot(
                        weights.astype(jnp.bfloat16),
                        g_ref[group],
                        preferred_element_type=jnp.float32,
                    )
                )
            dkv_ref[pl.ds(first_key, KEYS_STEP), :] = jnp.concatenate(
                found[0::2] + found[1::2], axis=1
            ).astype(dkv_ref.dtype)

        def clear(step):
            first_key = pl.multiple_of(step * KEYS_STEP, KEYS_STEP)
            dkv_ref[pl.ds(first_key, KEYS_STEP), :] = jnp.zeros((KEYS_STEP, KVW), dkv_ref.dtype)

        marks = spread_ticks(sums, ticks, steps)

        def body(step, carry):
            general = (step == 0) | ((step + 1) * KEYS_STEP > first_row)
            pl.when((step < used) & general)(partial(block, step, True))
            pl.when((step < used) & jnp.logical_not(general))(partial(block, step, False))
            pl.when(step >= used)(partial(clear, step))
            for at, tick in marks:
                pl.when(step == at)(tick)
            return carry

        lax.fori_loop(0, steps, body, 0)
        for _ in sums:
            pass

    hbm = pl.BlockSpec(memory_space=pl.ANY)
    key_terms, query_grads, *late_sums = pl.pallas_call(
        kernel,
        out_shape=[
            jax.ShapeDtypeStruct((total, KVW), jnp.bfloat16),
            jax.ShapeDtypeStruct((groups, HEAD_DIM, rows), jnp.float32),
        ]
        + [jax.ShapeDtypeStruct(s, jnp.float32) for s in shapes],
        in_specs=[VMEM_SPEC] * 6 + [hbm] * kinds,
        out_specs=[VMEM_SPEC] * (2 + kinds),
        scratch_shapes=[pltpu.VMEM((groups, 1, rows), jnp.float32)] + scratch,
        compiler_params=pltpu.CompilerParams(
            collective_id=collective_id,
            has_side_effects=True,
            vmem_limit_bytes=62 * 1024 * 1024,
        ),
        name="attention_backward",
    )(queries, grads, kv_all, row_starts, log_total, outputs, *views)
    return key_terms, query_grads, late_sums


BIG_VMEM = pltpu.CompilerParams(vmem_limit_bytes=62 * 1024 * 1024)


def dot_parts(value, exact, parts, axes=((1,), (0,))):
    total, left = None, value
    for _ in range(parts):
        piece = left.astype(jnp.bfloat16)
        left = left - piece.astype(jnp.float32)
        term = lax.dot_general(piece, exact, (axes, ((), ())), preferred_element_type=jnp.float32)
        total = term if total is None else total + term
    return total


def dot_left(exact, value, parts):
    total, left = None, value
    for _ in range(parts):
        piece = left.astype(jnp.bfloat16)
        left = left - piece.astype(jnp.float32)
        term = jnp.dot(exact, piece, preferred_element_type=jnp.float32)
        total = term if total is None else total + term
    return total


def matmul_pair(left_side, right_side, axes):
    left_high = left_side.astype(jnp.bfloat16)
    left_low = (left_side - left_high.astype(jnp.float32)).astype(jnp.bfloat16)
    right_high = right_side.astype(jnp.bfloat16)
    right_low = (right_side - right_high.astype(jnp.float32)).astype(jnp.bfloat16)
    dims = (axes, ((), ()))
    product = partial(
        lax.dot_general, dimension_numbers=dims, preferred_element_type=jnp.float32
    )
    return (
        product(left_high, right_high)
        + product(left_low, right_high)
        + product(left_high, right_low)
    )


def stacked(value, first):
    high = value.astype(jnp.bfloat16)
    low = (value - high.astype(jnp.float32)).astype(jnp.bfloat16)
    return [high, low, high] if first else [high, high, low]


def dot_fast(left_side, right_side, axes):
    return lax.dot_general(
        left_side.astype(jnp.bfloat16),
        right_side.astype(jnp.bfloat16),
        (axes, ((), ())),
        preferred_element_type=jnp.float32,
    )


NN = ((1,), (0,))
NT = ((1,), (1,))
TN = ((0,), (0,))


def head_spread():
    head = lax.broadcasted_iota(jnp.int32, (128, SSM), 0)
    column = lax.broadcasted_iota(jnp.int32, (128, SSM), 1)
    return jnp.where(column // MHEAD_DIM == head, 1.0, 0.0).astype(jnp.bfloat16)


def rope_table(rows, count):
    half = HEAD_DIM // 2
    frequency = rope_base ** (-np.arange(half) / half)
    tables = []
    for places in (np.arange(rows), rows * np.arange(count)):
        angles = np.tile(places[:, None] * frequency[None, :], (1, 4))
        tables += [np.cos(angles).astype(np.float32), np.sin(angles).astype(np.float32)]
    return tables


def rope_now(device, base_cos_ref, base_sin_ref, far_cos_ref, far_sin_ref):
    base_cos, base_sin = base_cos_ref[...], base_sin_ref[...]
    far_cos, far_sin = far_cos_ref[pl.ds(device, 1), :], far_sin_ref[pl.ds(device, 1), :]
    cosine_part = far_cos * base_cos - far_sin * base_sin
    sine_part = far_sin * base_cos + far_cos * base_sin
    lane = lax.broadcasted_iota(jnp.int32, base_cos.shape, 1)
    return cosine_part, jnp.where(lane % HEAD_DIM < HEAD_DIM // 2, -sine_part, sine_part)


def rope_lanes(values, cosine_all, sine_all):
    width = values.shape[1]
    repeat = width // cosine_all.shape[1]
    half = HEAD_DIM // 2
    column = lax.broadcasted_iota(jnp.int32, values.shape, 1)
    partner = jnp.where(
        column % HEAD_DIM < half,
        pltpu.roll(values, width - half, 1),
        pltpu.roll(values, half, 1),
    )
    if repeat > 1:
        cosine_all = jnp.concatenate([cosine_all] * repeat, axis=1)
        sine_all = jnp.concatenate([sine_all] * repeat, axis=1)
    return values * cosine_all + partner * sine_all


def mixer_forward(
    hidden, halo, norm_gain, weights, conv_weight, conv_bias, dt_bias, a_log, starts, tables
):
    rows, model = hidden.shape
    groups = QHEADS // KVHEADS
    half_kv = KVW // 2
    first_row = (lax.axis_index("seq") * rows).astype(jnp.int32).reshape(1)
    pieces = [
        (0, 0, SSM // 2),
        (0, SSM // 2, SSM // 2),
        (1, 0, XBC // 2),
        (1, XBC // 2, XBC // 2),
        (2, 0, QW),
        (2, QW, KVW),
        (2, QW + KVW, DT_PAD),
    ]
    load_order = (2, 3, 4, 5, 6, 0, 1)

    def kernel(
        first_ref,
        hidden_ref,
        halo_ref,
        gain_ref,
        z_hbm,
        xbc_hbm,
        small_hbm,
        tap_ref,
        bias_ref,
        dt_bias_ref,
        a_log_ref,
        starts_ref,
        base_cos_ref,
        base_sin_ref,
        far_cos_ref,
        far_sin_ref,
        normed_ref,
        gate_ref,
        ext_ref,
        pre_ref,
        q_ref,
        kv_ref,
        dt_pre_ref,
        log_ref,
        state_ref,
        passing_ref,
        z_ref,
        xbc_ref,
        small_ref,
        normed_ext,
        ext_f32,
        sems,
    ):
        weight_hbm, weight_refs = (z_hbm, xbc_hbm, small_hbm), (z_ref, xbc_ref, small_ref)
        copies = [
            pltpu.make_async_copy(
                weight_hbm[which].at[:, pl.ds(start, width)],
                weight_refs[which].at[:, pl.ds(start, width)],
                sems.at[number],
            )
            for number, (which, start, width) in enumerate(pieces)
        ]
        for number in load_order:
            copies[number].start()
        cosine_all, sine_all = rope_now(
            first_ref[0] // rows, base_cos_ref, base_sin_ref, far_cos_ref, far_sin_ref
        )

        def norm(block):
            values = block.astype(jnp.float32)
            scale = lax.rsqrt(jnp.mean(values * values, axis=1, keepdims=True) + epsilon)
            return (values * scale * gain_ref[...]).astype(jnp.bfloat16)

        normed_ext[:HALO, :] = norm(halo_ref[...])
        normed = norm(hidden_ref[...])
        normed_ext[HALO:, :] = normed
        normed_ref[...] = normed

        def project(number, values):
            copies[number].wait()
            which, start, width = pieces[number]
            return jnp.dot(
                values,
                weight_refs[which][:, start : start + width],
                preferred_element_type=jnp.float32,
            )

        for number in (2, 3):
            _, start, width = pieces[number]
            part = project(number, normed_ext[...]).astype(jnp.bfloat16)
            ext_ref[:, start : start + width] = part
            ext_f32[:, start : start + width] = part.astype(jnp.float32)
        turned = rope_lanes(project(4, normed), cosine_all, sine_all).astype(jnp.bfloat16)
        turned = turned * jnp.bfloat16(HEAD_DIM ** (-0.5))
        for head in range(QHEADS):
            place = head % groups * rows
            q_ref[head // groups, place : place + rows, :] = turned[
                :, head * HEAD_DIM : (head + 1) * HEAD_DIM
            ]
        kv_raw = project(5, normed)
        kv_ref[:, :half_kv] = rope_lanes(
            kv_raw[:, :half_kv], cosine_all, sine_all
        ).astype(jnp.bfloat16)
        kv_ref[:, half_kv:] = kv_raw[:, half_kv:].astype(jnp.bfloat16)
        dt_pre = project(6, normed) + dt_bias_ref[...]
        dt_pre_ref[...] = dt_pre
        step_dt = jax.nn.softplus(dt_pre)
        order = lax.broadcasted_iota(jnp.int32, (rows, rows), 0)
        other = lax.broadcasted_iota(jnp.int32, (rows, rows), 1)
        lower = jnp.where(other <= order, 1.0, 0.0).astype(jnp.bfloat16)
        log_decay = dot_left(lower, -step_dt * jnp.exp(a_log_ref[...]), 3)
        log_ref[...] = log_decay
        for number in (0, 1):
            _, start, width = pieces[number]
            gate_ref[:, start : start + width] = project(number, normed)

        starts_now = starts_ref[...]
        places = first_ref[0] + lax.broadcasted_iota(jnp.int32, (rows, 1), 0)
        pre = jnp.zeros((rows, XBC), jnp.float32) + bias_ref[...]
        for tap in range(CONV):
            lag = CONV - 1 - tap
            kept = jnp.where(places - lag >= starts_now, 1.0, 0.0)
            pre = pre + ext_f32[HALO - lag : HALO - lag + rows, :] * kept * tap_ref[tap : tap + 1, :]
        pre_ref[...] = pre
        conv_out = pre * jax.nn.sigmoid(pre)
        last = log_decay[rows - 1 : rows, :]
        last_start = starts_ref[rows - 1 : rows, :]
        weight = jnp.exp(jnp.where(places >= last_start, last - log_decay, masked)) * step_dt
        spread = dot_parts(weight, head_spread(), 2)
        state_ref[...] = matmul_pair(
            conv_out[:, :SSM] * spread, conv_out[:, SSM : SSM + STATE], TN
        )
        passing = jnp.exp(last) * jnp.where(last_start < first_ref[0], 1.0, 0.0)
        passing_ref[...] = jnp.broadcast_to(passing, passing_ref.shape)

    f32 = jnp.float32
    shape = jax.ShapeDtypeStruct
    return pl.pallas_call(
        kernel,
        out_shape=(
            shape((rows, model), jnp.bfloat16),
            shape((rows, SSM), f32),
            shape((HALO + rows, XBC), jnp.bfloat16),
            shape((rows, XBC), f32),
            shape((KVHEADS, groups * rows, HEAD_DIM), jnp.bfloat16),
            shape((rows, KVW), jnp.bfloat16),
            shape((rows, DT_PAD), f32),
            shape((rows, DT_PAD), f32),
            shape((SSM, STATE), f32),
            shape((8, DT_PAD), f32),
        ),
        in_specs=[pl.BlockSpec(memory_space=pltpu.SMEM)]
        + [VMEM_SPEC] * 3
        + [pl.BlockSpec(memory_space=pl.ANY)] * 3
        + [VMEM_SPEC] * 9,
        out_specs=[VMEM_SPEC] * 10,
        scratch_shapes=[
            *[pltpu.VMEM(w.shape, jnp.bfloat16) for w in weights],
            pltpu.VMEM((HALO + rows, model), jnp.bfloat16),
            pltpu.VMEM((HALO + rows, XBC), f32),
            pltpu.SemaphoreType.DMA((len(pieces),)),
        ],
        compiler_params=BIG_VMEM,
        name="mixer_forward",
    )(
        first_row,
        hidden,
        halo,
        norm_gain[None],
        *weights,
        conv_weight,
        conv_bias[None],
        dt_bias,
        a_log,
        starts[:, None],
        *tables,
    )


def document_mask(first_row, starts, rows, flip):
    if flip:
        token = lax.broadcasted_iota(jnp.int32, (rows, rows), 1)
        source = lax.broadcasted_iota(jnp.int32, (rows, rows), 0)
    else:
        token = lax.broadcasted_iota(jnp.int32, (rows, rows), 0)
        source = lax.broadcasted_iota(jnp.int32, (rows, rows), 1)
    allowed = (first_row + source >= starts) & (source <= token)
    return jnp.where(allowed, 0.0, masked)


def mixer_output_body(
    pre_ref,
    dt_pre_ref,
    log_ref,
    state,
    gate_ref,
    gain_ref,
    skip_ref,
    starts_ref,
    normed_ref,
    y_ref,
    input_ref,
):
    rows = pre_ref.shape[0]
    first_row = lax.axis_index("seq") * rows
    pre_now = pre_ref[...]
    conv_out = pre_now * jax.nn.sigmoid(pre_now)
    ssm_x = conv_out[:, :SSM]
    input_b = conv_out[:, SSM : SSM + STATE]
    output_c = conv_out[:, SSM + STATE :]
    spread = head_spread()
    log_decay_now = log_ref[...]
    log_rows = jnp.transpose(log_decay_now)
    step_dt = jax.nn.softplus(dt_pre_ref[...])
    scaled_x = ssm_x * dot_parts(step_dt, spread, 2)
    for part, piece in enumerate(stacked(scaled_x, False)):
        input_ref[part * rows : (part + 1) * rows, :] = piece
    carried = jnp.exp(log_decay_now) * jnp.where(starts_ref[...] < first_row, 1.0, 0.0)
    y_ref[...] = (
        matmul_pair(output_c, state, NT) * dot_parts(carried, spread, 2)
        + skip_ref[...] * ssm_x
    )
    affinity = matmul_pair(output_c, input_b, NT)
    closed = document_mask(first_row, starts_ref[...], rows, False)
    for pair in range(MHEADS // 2):
        found = []
        for head in (2 * pair, 2 * pair + 1):
            gap = log_decay_now[:, head : head + 1] - log_rows[head : head + 1, :] + closed
            mixing = affinity * jnp.exp(gap)
            found.append(
                jnp.dot(
                    jnp.concatenate(stacked(mixing, True), axis=1),
                    input_ref[:, head * MHEAD_DIM : (head + 1) * MHEAD_DIM],
                    preferred_element_type=jnp.float32,
                )
            )
        columns = slice(2 * pair * MHEAD_DIM, (2 * pair + 2) * MHEAD_DIM)
        y_ref[:, columns] += jnp.concatenate(found, axis=1)
    gate_now = gate_ref[...]
    gated = y_ref[...] * gate_now * jax.nn.sigmoid(gate_now)
    scale = lax.rsqrt(jnp.mean(gated * gated, axis=1, keepdims=True) + epsilon)
    normed_ref[...] = (gated * scale * gain_ref[...]).astype(jnp.bfloat16)


def mixer_output(pre, dt_pre, log_decay, states_in, gate_z, ssm_gain, skip_lanes, starts):
    rows = pre.shape[0]

    def kernel(*refs):
        mixer_output_body(*refs[:3], refs[3][...], *refs[4:])

    return pl.pallas_call(
        kernel,
        out_shape=mixer_output_shapes(rows),
        in_specs=[VMEM_SPEC] * 8,
        out_specs=[VMEM_SPEC] * 2,
        scratch_shapes=[pltpu.VMEM((3 * rows, SSM), jnp.bfloat16)],
        compiler_params=BIG_VMEM,
        name="mixer_output",
    )(
        pre,
        dt_pre,
        log_decay,
        states_in,
        gate_z,
        ssm_gain,
        skip_lanes,
        starts,
    )


def mixer_output_shapes(rows):
    return [
        jax.ShapeDtypeStruct((rows, SSM), jnp.bfloat16),
        jax.ShapeDtypeStruct((rows, SSM), jnp.float32),
    ]


def mixer_backward_body(
    grad_ref,
    y_ref,
    gate_ref,
    gain_ref,
    pre_ref,
    dt_pre_ref,
    log_ref,
    state_ref,
    skip_ref,
    starts_ref,
    starts_row_ref,
    grad_gate_ref,
    gain_grad_ref,
    grad_y_ref,
    state_grad_ref,
    input_grad_ref,
    b_grad_ref,
    c_grad_ref,
    log_grad_ref,
    skip_grad_ref,
    input_ref,
    low_ref,
    sums_ref,
    tick,
):
    rows = pre_ref.shape[0]
    first_row = lax.axis_index("seq") * rows
    gate_now = gate_ref[...]
    sigmoid_gate = jax.nn.sigmoid(gate_now)
    silu_gate = gate_now * sigmoid_gate
    y_now = y_ref[...]
    gated = y_now * silu_gate
    scale = lax.rsqrt(jnp.mean(gated * gated, axis=1, keepdims=True) + epsilon)
    grad_now = grad_ref[...]
    gain_grad_ref[...] = jnp.sum(gated * scale * grad_now, axis=0, keepdims=True)
    scaled = grad_now * gain_ref[...]
    grad_gated = scale * scaled - gated * (
        scale * scale * scale * jnp.mean(gated * scaled, axis=1, keepdims=True)
    )
    grad_gate_ref[...] = (
        grad_gated * y_now * sigmoid_gate * (1.0 + gate_now * (1.0 - sigmoid_gate))
    ).astype(jnp.bfloat16)
    grad_y = grad_gated * silu_gate
    grad_y_ref[...] = grad_y
    for part, piece in enumerate(stacked(grad_y, False)):
        low_ref[part * rows : (part + 1) * rows, :] = piece

    pre_now = pre_ref[...]
    conv_out = pre_now * jax.nn.sigmoid(pre_now)
    ssm_x = conv_out[:, :SSM]
    input_b = conv_out[:, SSM : SSM + STATE]
    output_c = conv_out[:, SSM + STATE :]
    spread = head_spread()
    log_decay_now = log_ref[...]
    log_rows = jnp.transpose(log_decay_now)
    step_dt = jax.nn.softplus(dt_pre_ref[...])
    scaled_x = ssm_x * dot_parts(step_dt, spread, 2)
    high, low, _ = stacked(scaled_x, True)
    input_ref[:rows, :] = high
    input_ref[rows:, :] = low
    carried = jnp.exp(log_decay_now) * jnp.where(starts_ref[...] < first_row, 1.0, 0.0)
    carried_lanes = dot_parts(carried, spread, 2)
    from_state = matmul_pair(output_c, state_ref[...], NT)
    log_grad = carried * dot_parts(grad_y * from_state, spread, 2, NT)
    grad_from_state = grad_y * carried_lanes
    state_grad_ref[...] = matmul_pair(grad_from_state, output_c, TN).reshape(state_grad_ref.shape)
    c_grad = matmul_pair(grad_from_state, state_ref[...], NN)
    skip_grad_ref[...] = dot_parts(
        jnp.sum(grad_y * ssm_x, axis=0, keepdims=True), spread, 3, NT
    )

    affinity = matmul_pair(input_b, output_c, NT)
    closed = document_mask(first_row, starts_row_ref[...], rows, True)
    affinity_grad = jnp.zeros((rows, rows), jnp.float32)
    sums_ref[...] = jnp.zeros(sums_ref.shape, jnp.float32)
    lane = lax.broadcasted_iota(jnp.int32, (rows, DT_PAD), 1)
    for pair in range(MHEADS // 2):
        found = []
        for head in (2 * pair, 2 * pair + 1):
            columns = slice(head * MHEAD_DIM, (head + 1) * MHEAD_DIM)
            gap = log_rows[head : head + 1, :] - log_decay_now[:, head : head + 1] + closed
            decay = jnp.exp(gap)
            mixing = affinity * decay
            found.append(
                jnp.dot(
                    jnp.concatenate(stacked(mixing, True), axis=1),
                    low_ref[:, columns],
                    preferred_element_type=jnp.float32,
                )
            )
            grad_mixing = jnp.zeros((rows, rows), jnp.float32)
            for one, two in ((0, 0), (1, 0), (0, 2)):
                grad_mixing = grad_mixing + lax.dot_general(
                    input_ref[one * rows : (one + 1) * rows, columns],
                    low_ref[two * rows : (two + 1) * rows, columns],
                    (NT, ((), ())),
                    preferred_element_type=jnp.float32,
                )
            affinity_grad = affinity_grad + grad_mixing * decay
            both = grad_mixing * mixing
            sums_ref[head : head + 1, :] = jnp.sum(both, axis=0, keepdims=True)
            log_grad = log_grad - jnp.where(
                lane == head, jnp.sum(both, axis=1, keepdims=True), 0.0
            )
        columns = slice(2 * pair * MHEAD_DIM, (2 * pair + 2) * MHEAD_DIM)
        input_grad_ref[:, columns] = jnp.concatenate(found, axis=1)
        if pair % 3 == 2:
            tick()
    log_grad_ref[...] = log_grad + jnp.transpose(sums_ref[...])
    b_grad_ref[...] = matmul_pair(affinity_grad, output_c, NN)
    c_grad_ref[...] = c_grad + matmul_pair(jnp.transpose(affinity_grad), input_b, NN)


def mixer_backward_shapes(rows, state_shape):
    f32 = jnp.float32
    shape = jax.ShapeDtypeStruct
    return [
        shape((rows, SSM), jnp.bfloat16),
        shape((1, SSM), f32),
        shape((rows, SSM), f32),
        shape(state_shape, f32),
        shape((rows, SSM), f32),
        shape((rows, STATE), f32),
        shape((rows, STATE), f32),
        shape((rows, DT_PAD), f32),
        shape((1, DT_PAD), f32),
    ]


def mixer_backward_scratch(rows):
    return [
        pltpu.VMEM((2 * rows, SSM), jnp.bfloat16),
        pltpu.VMEM((3 * rows, SSM), jnp.bfloat16),
        pltpu.VMEM((DT_PAD, rows), jnp.float32),
    ]


def mixer_backward(args):
    rows = args[0].shape[0]

    def kernel(*refs):
        mixer_backward_body(*refs, lambda: None)

    return pl.pallas_call(
        kernel,
        out_shape=mixer_backward_shapes(rows, (SSM, STATE)),
        in_specs=[VMEM_SPEC] * 11,
        out_specs=[VMEM_SPEC] * 9,
        scratch_shapes=mixer_backward_scratch(rows),
        compiler_params=BIG_VMEM,
        name="mixer_backward",
    )(*args)


def mixer_input_backward(
    grad_end,
    states_in,
    passing,
    grad_y,
    input_grad,
    b_grad,
    c_grad,
    log_grad,
    pre,
    dt_pre,
    log_decay,
    ext,
    conv_weight,
    a_log,
    skip_lanes,
    starts,
):
    rows = pre.shape[0]
    first_row = (lax.axis_index("seq") * rows).astype(jnp.int32).reshape(1)

    def kernel(
        first_ref,
        end_ref,
        state_ref,
        passing_ref,
        grad_y_ref,
        input_grad_ref,
        b_grad_ref,
        c_grad_ref,
        log_grad_ref,
        pre_ref,
        dt_pre_ref,
        log_ref,
        ext_ref,
        tap_ref,
        a_log_ref,
        skip_ref,
        starts_ref,
        raw_grad_ref,
        tap_grad_ref,
        bias_grad_ref,
        dt_grad_ref,
        dt_sum_ref,
        a_log_grad_ref,
        ext_f32,
        sum_ref,
    ):
        pre_now = pre_ref[...]
        sigmoid_pre = jax.nn.sigmoid(pre_now)
        conv_out = pre_now * sigmoid_pre
        ssm_x = conv_out[:, :SSM]
        input_b = conv_out[:, SSM : SSM + STATE]
        spread = head_spread()
        log_decay_now = log_ref[...]
        dt_pre_now = dt_pre_ref[...]
        step_dt = jax.nn.softplus(dt_pre_now)
        step_lanes = dot_parts(step_dt, spread, 2)
        starts_now = starts_ref[...]
        row = lax.broadcasted_iota(jnp.int32, (rows, 1), 0)
        places = first_ref[0] + row
        last = log_decay_now[rows - 1 : rows, :]
        last_start = starts_ref[rows - 1 : rows, :]
        weight = jnp.exp(jnp.where(places >= last_start, last - log_decay_now, masked))
        weight_lanes = dot_parts(weight, spread, 2)
        weighted = ssm_x * step_lanes * weight_lanes
        grad_weighted = matmul_pair(input_b, end_ref[...], NT)
        b_total = b_grad_ref[...] + matmul_pair(weighted, end_ref[...], NN)
        input_total = input_grad_ref[...] + grad_weighted * weight_lanes
        weight_term = dot_parts(grad_weighted * weighted, spread, 3, NT)
        state_dot = end_ref[...] * state_ref[...]
        passing_grad = jnp.sum(
            jnp.transpose(dot_left(spread, state_dot, 3)), axis=0, keepdims=True
        )
        log_grad_now = log_grad_ref[...] - weight_term
        end_term = jnp.sum(weight_term, axis=0, keepdims=True) + passing_grad * passing_ref[0:1, :]
        log_grad_now = log_grad_now + jnp.where(row == rows - 1, end_term, 0.0)
        order = lax.broadcasted_iota(jnp.int32, (rows, rows), 0)
        other = lax.broadcasted_iota(jnp.int32, (rows, rows), 1)
        upper = jnp.where(other >= order, 1.0, 0.0).astype(jnp.bfloat16)
        step_grad = dot_left(upper, log_grad_now, 3)
        rate = jnp.exp(a_log_ref[...])
        a_log_grad_ref[...] = jnp.sum(-step_dt * rate * step_grad, axis=0, keepdims=True)
        dt_grad = dot_parts(input_total * ssm_x, spread, 3, NT) - rate * step_grad
        dt_raw_grad = dt_grad * jax.nn.sigmoid(dt_pre_now)
        valid = lax.broadcasted_iota(jnp.int32, (rows, DT_PAD), 1) < MHEADS
        dt_raw_grad = jnp.where(valid, dt_raw_grad, 0.0)
        dt_grad_ref[...] = dt_raw_grad.astype(jnp.bfloat16)
        dt_sum_ref[...] = jnp.sum(dt_raw_grad, axis=0, keepdims=True)
        x_grad = input_total * step_lanes + skip_ref[...] * grad_y_ref[...]
        slope = sigmoid_pre * (1.0 + pre_now * (1.0 - sigmoid_pre))
        pre_grad = jnp.concatenate([x_grad, b_total, c_grad_ref[...]], axis=1) * slope
        bias_grad_ref[...] = jnp.sum(pre_grad, axis=0, keepdims=True)
        ext_f32[...] = ext_ref[...].astype(jnp.float32)
        sum_ref[...] = jnp.zeros(sum_ref.shape, jnp.float32)
        for tap in range(CONV):
            lag = CONV - 1 - tap
            kept = pre_grad * jnp.where(places - lag >= starts_now, 1.0, 0.0)
            window = slice(HALO - lag, HALO - lag + rows)
            tap_grad_ref[tap : tap + 1, :] = jnp.sum(
                kept * ext_f32[window, :], axis=0, keepdims=True
            )
            sum_ref[window, :] += kept * tap_ref[tap : tap + 1, :]
        raw_grad_ref[...] = sum_ref[...]

    f32 = jnp.float32
    shape = jax.ShapeDtypeStruct
    return pl.pallas_call(
        kernel,
        out_shape=(
            shape((HALO + rows, XBC), f32),
            shape((CONV, XBC), f32),
            shape((1, XBC), f32),
            shape((rows, DT_PAD), jnp.bfloat16),
            shape((1, DT_PAD), f32),
            shape((1, DT_PAD), f32),
        ),
        in_specs=[pl.BlockSpec(memory_space=pltpu.SMEM)] + [VMEM_SPEC] * 16,
        out_specs=[VMEM_SPEC] * 6,
        scratch_shapes=[
            pltpu.VMEM((HALO + rows, XBC), f32),
            pltpu.VMEM((HALO + rows, XBC), f32),
        ],
        compiler_params=BIG_VMEM,
        name="mixer_input_backward",
    )(
        first_row,
        grad_end,
        states_in,
        passing,
        grad_y,
        input_grad,
        b_grad,
        c_grad,
        log_grad,
        pre,
        dt_pre,
        log_decay,
        ext,
        conv_weight,
        a_log,
        skip_lanes,
        starts[:, None],
    )


def feed_forward(hidden, normed_ssm, attention, ffn_gain, cotangent, late):
    rows, model = hidden.shape
    f32, low = jnp.float32, jnp.bfloat16
    ffn = late[0].shape[1]
    span = 1024
    steps = ffn // span

    def layout(flat, gate_up, down, ssm, out):
        pairs = [(flat[3], ssm), (flat[4], out)]
        for number in range(2):
            for start in range(0, ffn, span):
                pairs.append(
                    (
                        flat[number].at[:, pl.ds(start, span)],
                        gate_up.at[:, pl.ds(number * ffn + start, span)],
                    )
                )
        return pairs + [(flat[2], down)]

    kinds = len(late)
    early = 2
    total = early + 2 * steps + 1

    def kernel(*refs):
        hidden_ref, ssm_ref, attn_ref, gain_ref, cot_ref = refs[:5]
        flats = refs[5 : 5 + kinds]
        refs = refs[5 + kinds :]
        layer_ref, mix_ref, attn_grad_ref, ssm_grad_ref, gain_grad_ref = refs[:5]
        grad_flats = refs[5 : 5 + kinds]
        refs = refs[5 + kinds :]
        weights, grads = refs[:4], refs[4:8]
        gate_ref, up_ref, act_ref, two_ref, after_ref, grad_two_ref, in_sem, out_sem = refs[8:]
        w_gate_up, w_down, w_ssm, w_o = weights
        g_gate_up, g_down, g_ssm, g_o = grads
        loads = [
            pltpu.make_async_copy(source, target, in_sem.at[i])
            for i, (source, target) in enumerate(layout(flats, w_gate_up, w_down, w_ssm, w_o))
        ]
        for copy in loads:
            copy.start()
        stores = [
            pltpu.make_async_copy(source, target, out_sem.at[i])
            for i, (target, source) in enumerate(
                layout(grad_flats, g_gate_up, g_down, g_ssm, g_o)
            )
        ]

        def whole(ref, start=0, width=None):
            return ref[:, start : start + (ref.shape[1] if width is None else width)]

        def product(left_side, right_side, axes):
            return lax.dot_general(
                left_side, right_side, (axes, ((), ())), preferred_element_type=f32
            )

        def keep(ref, value, start=0):
            ref[:, start : start + value.shape[1]] = value.astype(low)

        for copy in loads[:early]:
            copy.wait()
        after = (
            hidden_ref[...].astype(f32)
            + product(ssm_ref[...], whole(w_ssm), NN)
            + product(attn_ref[...], whole(w_o), NN)
        )
        after_ref[...] = after
        scale = lax.rsqrt(jnp.mean(after * after, axis=1, keepdims=True) + epsilon)
        two_ref[...] = (after * scale * gain_ref[...]).astype(low)
        for step in range(steps):
            columns = slice(step * span, (step + 1) * span)
            loads[early + step].wait()
            loads[early + steps + step].wait()
            gate = product(two_ref[...], whole(w_gate_up, step * span, span), NN)
            up = product(two_ref[...], whole(w_gate_up, ffn + step * span, span), NN)
            gate_ref[:, columns] = gate
            up_ref[:, columns] = up
            act_ref[:, columns] = (gate * jax.nn.sigmoid(gate) * up).astype(low)
        for copy in loads[early + 2 * steps :]:
            copy.wait()
        layer_ref[...] = (after_ref[...] + product(act_ref[...], whole(w_down), NN)).astype(low)
        cot = cot_ref[...]
        grad_two = jnp.zeros((rows, model), f32)
        for step in range(steps):
            columns = slice(step * span, (step + 1) * span)
            w_part = w_down[columns, :]
            grad_act = product(cot, w_part, NT)
            gate, up = gate_ref[:, columns], up_ref[:, columns]
            sigmoid_gate = jax.nn.sigmoid(gate)
            grad_gate = (
                grad_act * up * sigmoid_gate * (1.0 + gate * (1.0 - sigmoid_gate))
            ).astype(low)
            grad_up = (grad_act * gate * sigmoid_gate).astype(low)
            grad_two = grad_two + product(
                grad_gate, whole(w_gate_up, step * span, span), NT
            )
            grad_two = grad_two + product(
                grad_up, whole(w_gate_up, ffn + step * span, span), NT
            )
            keep(g_gate_up, product(two_ref[...], grad_gate, TN), step * span)
            stores[early + step].start()
            keep(g_gate_up, product(two_ref[...], grad_up, TN), ffn + step * span)
            stores[early + steps + step].start()
        grad_two_ref[...] = grad_two
        keep(g_down, product(act_ref[...], cot, TN))
        for copy in stores[early + 2 * steps :]:
            copy.start()
        after = after_ref[...]
        grad_two = grad_two_ref[...]
        scale = lax.rsqrt(jnp.mean(after * after, axis=1, keepdims=True) + epsilon)
        gain_grad_ref[...] = jnp.sum(after * scale * grad_two, axis=0, keepdims=True)
        scaled = grad_two * gain_ref[...]
        mix = (
            cot.astype(f32)
            + scale * scaled
            - after * (scale * scale * scale * jnp.mean(after * scaled, axis=1, keepdims=True))
        )
        mix_ref[...] = mix
        mix_low = mix.astype(low)
        attn_grad = product(mix_low, whole(w_o), NT).astype(low)
        group_size = QHEADS // KVHEADS
        for head in range(QHEADS):
            place = head % group_size * rows
            attn_grad_ref[head // group_size, place : place + rows, :] = attn_grad[
                :, head * HEAD_DIM : (head + 1) * HEAD_DIM
            ]
        ssm_grad_ref[...] = product(mix_low, whole(w_ssm), NT)
        keep(g_ssm, product(ssm_ref[...], mix_low, TN))
        keep(g_o, product(attn_ref[...], mix_low, TN))
        for copy in stores[:early]:
            copy.start()
        for copy in stores:
            copy.wait()

    shape = jax.ShapeDtypeStruct
    hbm = pl.BlockSpec(memory_space=pl.ANY)
    buffers = [(late[0].shape[0], 2 * ffn)] + [w.shape for w in late[2:]]
    outs = pl.pallas_call(
        kernel,
        out_shape=[
            shape((rows, model), low),
            shape((rows, model), f32),
            shape((KVHEADS, QHEADS // KVHEADS * rows, HEAD_DIM), low),
            shape((rows, SSM), f32),
            shape((1, model), f32),
        ]
        + [shape(w.shape, low) for w in late],
        in_specs=[VMEM_SPEC] * 5 + [hbm] * kinds,
        out_specs=[VMEM_SPEC] * 5 + [hbm] * kinds,
        scratch_shapes=[pltpu.VMEM(size, low) for size in buffers + buffers]
        + [
            pltpu.VMEM((rows, ffn), f32),
            pltpu.VMEM((rows, ffn), f32),
            pltpu.VMEM((rows, ffn), low),
            pltpu.VMEM((rows, model), low),
            pltpu.VMEM((rows, model), f32),
            pltpu.VMEM((rows, model), f32),
            pltpu.SemaphoreType.DMA((total,)),
            pltpu.SemaphoreType.DMA((total,)),
        ],
        compiler_params=BIG_VMEM,
        name="feed_forward",
    )(hidden, normed_ssm, attention, ffn_gain[None], cotangent, *late)
    return outs[:5], outs[5:]


def projection_backward(
    normed_one,
    hidden,
    norm_gain,
    grad_mix,
    grad_gate_z,
    grad_ext,
    returned,
    grad_dt,
    grad_query,
    grad_kv,
    tables,
    weights,
):
    rows, model = hidden.shape
    f32, low = jnp.float32, jnp.bfloat16
    groups = QHEADS // KVHEADS
    half_kv = KVW // 2
    first_row = (lax.axis_index("seq") * rows).astype(jnp.int32).reshape(1)
    widths = [w.shape[1] for w in weights]

    def kernel(
        first_ref,
        normed_ref,
        hidden_ref,
        gain_ref,
        mix_ref,
        gate_ref,
        ext_ref,
        returned_ref,
        dt_ref,
        query_ref,
        kv_ref,
        base_cos_ref,
        base_sin_ref,
        far_cos_ref,
        far_sin_ref,
        *refs,
    ):
        weight_hbm, refs = refs[:3], refs[3:]
        input_ref, gain_grad_ref, refs = refs[0], refs[1], refs[2:]
        weight_grad_hbm, refs = refs[:3], refs[3:]
        weight_refs, weight_grad_refs, refs = refs[:3], refs[3:6], refs[6:]
        xbc_ref, small_ref, turned_ref, in_sem, out_sem = refs
        loads = [
            pltpu.make_async_copy(source, target, in_sem.at[i])
            for i, (source, target) in enumerate(zip(weight_hbm, weight_refs))
        ]
        for copy in loads:
            copy.start()
        stores = [
            pltpu.make_async_copy(source, target, out_sem.at[i])
            for i, (source, target) in enumerate(zip(weight_grad_refs, weight_grad_hbm))
        ]
        edge = rows - HALO
        xbc_ref[:edge, :] = ext_ref[HALO : HALO + edge, :].astype(low)
        xbc_ref[edge:, :] = (ext_ref[HALO + edge :, :] + returned_ref[...]).astype(low)
        for head in range(QHEADS):
            place = head % groups * rows
            turned_ref[:, head * HEAD_DIM : (head + 1) * HEAD_DIM] = jnp.transpose(
                query_ref[head // groups, :, place : place + rows]
            )
        cosine_all, sine_all = rope_now(
            first_ref[0] // rows, base_cos_ref, base_sin_ref, far_cos_ref, far_sin_ref
        )
        sine_all = -sine_all
        small_ref[:, :QW] = rope_lanes(
            turned_ref[...] * HEAD_DIM ** (-0.5), cosine_all, sine_all
        ).astype(low)
        kv = kv_ref[...]
        small_ref[:, QW : QW + half_kv] = rope_lanes(kv[:, :half_kv], cosine_all, sine_all).astype(
            low
        )
        small_ref[:, QW + half_kv : QW + KVW] = kv[:, half_kv:].astype(low)
        small_ref[:, QW + KVW :] = dt_ref[...]
        normed = normed_ref[...]
        grad_normed = jnp.zeros((rows, model), f32)
        for number, value_ref in enumerate((gate_ref, xbc_ref, small_ref)):
            loads[number].wait()
            for start in range(0, widths[number], 512):
                columns = slice(start, min(start + 512, widths[number]))
                part = value_ref[:, columns]
                grad_normed = grad_normed + lax.dot_general(
                    part,
                    weight_refs[number][:, columns],
                    (NT, ((), ())),
                    preferred_element_type=f32,
                )
                weight_grad_refs[number][:, columns] = lax.dot_general(
                    normed, part, (TN, ((), ())), preferred_element_type=f32
                ).astype(low)
            stores[number].start()
        values = hidden_ref[...].astype(f32)
        scale = lax.rsqrt(jnp.mean(values * values, axis=1, keepdims=True) + epsilon)
        gain_grad_ref[...] = jnp.sum(values * scale * grad_normed, axis=0, keepdims=True)
        scaled = grad_normed * gain_ref[...]
        input_ref[...] = (
            mix_ref[...]
            + scale * scaled
            - values * (scale * scale * scale * jnp.mean(values * scaled, axis=1, keepdims=True))
        ).astype(low)
        for copy in stores:
            copy.wait()

    shape = jax.ShapeDtypeStruct
    hbm = pl.BlockSpec(memory_space=pl.ANY)
    return pl.pallas_call(
        kernel,
        out_shape=[shape((rows, model), low), shape((1, model), f32)]
        + [shape(w.shape, low) for w in weights],
        in_specs=[pl.BlockSpec(memory_space=pltpu.SMEM)] + [VMEM_SPEC] * 14 + [hbm] * 3,
        out_specs=[VMEM_SPEC] * 2 + [hbm] * 3,
        scratch_shapes=[pltpu.VMEM(w.shape, low) for w in list(weights) * 2]
        + [
            pltpu.VMEM((rows, XBC), low),
            pltpu.VMEM((rows, QW + KVW + DT_PAD), low),
            pltpu.VMEM((rows, QW), f32),
            pltpu.SemaphoreType.DMA((3,)),
            pltpu.SemaphoreType.DMA((3,)),
        ],
        compiler_params=BIG_VMEM,
        name="projection_backward",
    )(
        first_row,
        normed_one,
        hidden,
        norm_gain[None],
        grad_mix,
        grad_gate_z,
        grad_ext,
        returned,
        grad_dt,
        grad_query,
        grad_kv,
        *tables,
        *weights,
    )


def per_device(
    hidden_in,
    doc_start,
    norm_gain,
    w_z,
    w_xbc,
    w_dt,
    conv_weight,
    conv_bias,
    dt_bias,
    a_log,
    d_skip,
    ssm_gain,
    w_ssm_out,
    w_q,
    w_kv,
    w_o,
    ffn_gain,
    w_gate,
    w_up,
    w_down,
    cotangent,
):
    local_rows, model = hidden_in.shape
    count = lax.axis_size("seq")
    group_size = QHEADS // KVHEADS
    small_shard = jnp.concatenate(
        [w_q, w_kv, jnp.pad(w_dt, ((0, 0), (0, DT_PAD - MHEADS)))], axis=1
    )
    *mixer_weights, halo = gather_everywhere(
        [w_xbc, small_shard, w_z], 0, 8192, hidden_in
    )
    mixer_weights = [mixer_weights[2], mixer_weights[0], mixer_weights[1]]

    tables = rope_table(local_rows, count)
    dt_bias_row = jnp.pad(dt_bias, (0, DT_PAD - MHEADS))[None]
    a_log_row = jnp.pad(a_log, (0, DT_PAD - MHEADS))[None]
    skip_lanes = jnp.repeat(d_skip, MHEAD_DIM)[None]
    (
        normed_one,
        gate_z,
        xbc_ext,
        conv_pre,
        grouped_q,
        kv_local,
        dt_pre,
        log_decay,
        local_state,
        passing,
    ) = mixer_forward(
        hidden_in,
        halo,
        norm_gain,
        mixer_weights,
        conv_weight,
        conv_bias,
        dt_bias_row,
        a_log_row,
        doc_start,
        tables,
    )
    row_starts = jnp.tile(doc_start, group_size)[None]
    kv_all, states_in, chip_decay, late, computed = front(
        kv_local,
        local_state,
        passing,
        [w_gate, w_up, w_down, w_ssm_out, w_o],
        [conv_pre, dt_pre, log_decay, gate_z, ssm_gain[None], skip_lanes, doc_start[:, None]],
        [grouped_q, row_starts],
        1,
        (16384, 16384),
    )
    normed_ssm, ssm_y, attn_grouped, log_total, attn_low = computed
    (layer_out, grad_mix, grad_attn_grouped, grad_normed_ssm, grad_ffn_gain), late_grads = (
        feed_forward(hidden_in, normed_ssm, attn_low, ffn_gain, cotangent, late)
    )
    key_terms, grad_query_grouped, late_sums = attention_backward(
        grouped_q,
        grad_attn_grouped,
        kv_all,
        row_starts,
        log_total,
        attn_grouped,
        late_grads[:2],
        4,
        16384,
    )
    shard_gate, shard_up = late_sums

    grad_kv_local, grad_end, late_sums, mixer_out = back(
        key_terms,
        [
            grad_normed_ssm,
            ssm_y,
            gate_z,
            ssm_gain[None],
            conv_pre,
            dt_pre,
            log_decay,
            states_in,
            skip_lanes,
            doc_start[:, None],
            doc_start[None],
        ],
        passing,
        chip_decay,
        late_grads[2:],
        2,
        (16384, 16384),
    )
    shard_down, shard_ssm_out, shard_o = late_sums
    (
        grad_gate_z,
        grad_ssm_gain,
        grad_ssm_y,
        _,
        grad_input_part,
        grad_b_part,
        grad_c,
        grad_log_part,
        grad_d_skip,
    ) = mixer_out
    grad_ext, grad_conv_weight, grad_conv_bias, grad_dt_raw, grad_dt_bias, grad_a_log = (
        mixer_input_backward(
            grad_end,
            states_in,
            passing,
            grad_ssm_y,
            grad_input_part,
            grad_b_part,
            grad_c,
            grad_log_part,
            conv_pre,
            dt_pre,
            log_decay,
            xbc_ext,
            conv_weight,
            a_log_row,
            skip_lanes,
            doc_start,
        )
    )
    returned = from_behind(grad_ext[:HALO], "seq", -1)
    grad_input, grad_norm_gain, *mixer_grads = projection_backward(
        normed_one,
        hidden_in,
        norm_gain,
        grad_mix,
        grad_gate_z,
        grad_ext,
        returned,
        grad_dt_raw,
        grad_query_grouped,
        grad_kv_local,
        tables,
        mixer_weights,
    )

    small = [
        grad_norm_gain[0],
        grad_ssm_gain[0],
        grad_ffn_gain[0],
        grad_conv_weight.reshape(-1),
        grad_conv_bias[0],
        grad_dt_bias[0, :MHEADS],
        grad_a_log[0, :MHEADS],
        grad_d_skip[0, :MHEADS],
    ]
    sizes = [item.shape[0] for item in small]
    small_flat = jnp.concatenate(small)
    small_flat = jnp.pad(small_flat, (0, -small_flat.shape[0] % 1024)).reshape(-1, 128)
    shard_z, shard_xbc, shard_small, small_sum = scatter_sums(mixer_grads, small_flat, 3, 8192)
    starts = [sum(sizes[:i]) for i in range(len(sizes) + 1)]
    small_sum = small_sum.reshape(-1)
    sums = [small_sum[a:b] for a, b in zip(starts[:-1], starts[1:])]
    return (
        layer_out,
        grad_input,
        sums[0],
        shard_z,
        shard_xbc,
        shard_small[:, QW + KVW : QW + KVW + MHEADS],
        sums[3].reshape(conv_weight.shape),
        sums[4],
        sums[5],
        sums[6],
        sums[7],
        sums[1],
        shard_ssm_out,
        shard_small[:, :QW],
        shard_small[:, QW : QW + KVW],
        shard_o,
        sums[2],
        shard_gate,
        shard_up,
        shard_down,
    )


def solution(mesh):
    placed = (
        P("seq", None),
        P("seq"),
        P(),
        P("seq", None),
        P("seq", None),
        P("seq", None),
        P(),
        P(),
        P(),
        P(),
        P(),
        P(),
        P("seq", None),
        P("seq", None),
        P("seq", None),
        P("seq", None),
        P(),
        P("seq", None),
        P("seq", None),
        P("seq", None),
        P("seq", None),
    )
    return jax.shard_map(
        per_device,
        mesh=mesh,
        in_specs=placed,
        out_specs=(
            P("seq", None),
            P("seq", None),
            P(),
            P("seq", None),
            P("seq", None),
            P("seq", None),
            P(),
            P(),
            P(),
            P(),
            P(),
            P(),
            P("seq", None),
            P("seq", None),
            P("seq", None),
            P("seq", None),
            P(),
            P("seq", None),
            P("seq", None),
            P("seq", None),
        ),
        check_vma=False,
    )
```

```python
from functools import partial
import math

import jax
import jax.numpy as jnp
from jax import lax
from jax.experimental import pallas as pl
from jax.experimental.pallas import tpu as pltpu
from jax.sharding import PartitionSpec as P
import numpy as np

MHEADS = 24
MHEAD_DIM = 64
STATE = 128
CONV = 4
QHEADS = 8
KVHEADS = 2
HEAD_DIM = 64
SSM = 1536
XBC = 1792
QW = 512
KVW = 256
DT_PAD = 128


epsilon = 1e-05
rope_base = 100000000000.0
masked = -1e30


def from_behind(value, axis, steps):
    count = lax.axis_size(axis)
    first, last = (max(0, -steps), min(count, count - steps))
    return lax.ppermute(value, axis, [(source, source + steps) for source in range(first, last)])


MESH = pl.DeviceIdType.MESH
HALO = 16
VMEM_SPEC = pl.BlockSpec(memory_space=pltpu.VMEM)


def lattice(count):
    sizes, left, turn = [1, 1, 1], count // 2, 0
    while left > 1:
        factor = 2 if left % 2 == 0 else left
        sizes[turn % 3] *= factor
        left //= factor
        turn += 1
    return sizes[0], sizes[1], sizes[2], 2


def coordinates(sizes):
    me = lax.axis_index("seq")
    _, size_1, size_2, cores = sizes
    return (
        me // (size_1 * size_2 * cores),
        me // (size_2 * cores) % size_1,
        me // cores % size_2,
        me % cores,
    )


def device_at(sizes, place):
    index = place[0]
    for size, at in zip(sizes[1:], place[1:]):
        index = index * size + at
    return index


def partners(sizes, place, axis):
    found = []
    for step in range(1, sizes[axis]):
        other = list(place)
        other[axis] = (place[axis] + step) % sizes[axis]
        found.append(other)
    return found


def greet(sizes, place, more=()):
    barrier = pltpu.get_barrier_semaphore()
    met = [
        device_at(sizes, other) for axis in range(4) for other in partners(sizes, place, axis)
    ] + list(more)
    for other in met:
        pl.semaphore_signal(barrier, inc=1, device_id=(other,), device_id_type=MESH)
    pl.semaphore_wait(barrier, len(met))


def block_cuts(shapes, target):
    cuts = []
    for number, (rows, columns) in enumerate(shapes):
        pieces = max(1, round(rows * columns / target))
        width = max(128, (columns // pieces + 127) // 128 * 128)
        across = -(-columns // width)
        height = rows
        if across < pieces and rows % 32 == 0:
            height = max(32, rows // -(-pieces // across) // 32 * 32)
        for top in range(0, rows, height):
            for start in range(0, columns, width):
                size = (min(height, rows - top), min(width, columns - start))
                cuts.append((number, (pl.ds(top, size[0]), pl.ds(start, size[1]))))
    return cuts


def run_together(programs):
    waiting = list(programs)
    while waiting:
        for program in list(waiting):
            try:
                next(program)
            except StopIteration:
                waiting.remove(program)


ORDERS = ((0, 1, 2), (0, 2, 1))


def axis_order(turn):
    return ORDERS[turn % len(ORDERS)]


def tick_count(cuts, stages):
    return -(-len(cuts) // len(ORDERS)) + stages - 1


def tick_turns(cuts, number):
    first = number * len(ORDERS)
    return range(first, min(first + len(ORDERS), len(cuts))) if number >= 0 else range(0)


def gather_program(sizes, cuts, ins, outs, local_sem, send_sem, recv_sem, depth=1000):
    place = coordinates(sizes)
    sibling = partners(sizes, place, 3)[0]

    def region(turn, at):
        number, window = cuts[turn]
        return outs[number].at[*at, *window]

    def before(axis, step):
        at = list(place)
        at[axis] = (place[axis] - step - 1 + sizes[axis]) % sizes[axis]
        return at

    def widened(order, stage, at):
        full = list(at)
        for axis in order[:stage]:
            full[axis] = slice(None)
        return full

    def remote(turn, slot, step, source, target, other):
        return pltpu.make_async_remote_copy(
            src_ref=source,
            dst_ref=target,
            send_sem=send_sem.at[turn, slot, step],
            recv_sem=recv_sem.at[turn, slot, step],
            device_id=(device_at(sizes, other),),
            device_id_type=MESH,
        )

    def outgoing(turn, stage, step):
        order = axis_order(turn)
        here = region(turn, widened(order, stage, place))
        number, window = cuts[turn]
        source = ins[number].at[*window] if stage == 0 else here
        other = partners(sizes, place, order[stage])[step]
        return remote(turn, stage, step, source, here, other)

    def incoming(turn, stage, step):
        order = axis_order(turn)
        here = region(turn, widened(order, stage, before(order[stage], step)))
        return remote(turn, stage, step, here, here, sibling)

    def fresh(turn, stage, step, core):
        order = axis_order(turn)
        if stage == 0:
            at = widened(order, 1, place)
        else:
            at = widened(order, stage, before(order[stage], step))
        at[3] = core
        return region(turn, at)

    def across(turn, stage, step):
        here = fresh(turn, stage, step, place[3])
        return remote(turn, 3 + stage, step, here, here, sibling)

    def from_across(turn, stage, step):
        here = fresh(turn, stage, step, sibling[3])
        return remote(turn, 3 + stage, step, here, here, sibling)

    def hops(turn, stage):
        return range(sizes[axis_order(turn)[stage]] - 1)

    def pieces(turn, stage):
        return range(1) if stage == 0 else hops(turn, stage)

    def local(turn):
        number, window = cuts[turn]
        return pltpu.make_async_copy(
            ins[number].at[*window], region(turn, list(place)), local_sem.at[turn]
        )

    def launch(number):
        for turn in tick_turns(cuts, number):
            for step in hops(turn, 0):
                outgoing(turn, 0, step).start()

    for turn in range(len(cuts)):
        local(turn).start()
    for number in range(min(depth, len(cuts))):
        launch(number)
    yield

    def advance(turn, stage):
        for step in hops(turn, stage):
            incoming(turn, stage, step).wait_recv()
        if stage == 0:
            local(turn).wait()
        if stage < 2:
            for step in hops(turn, stage + 1):
                outgoing(turn, stage + 1, step).start()
        for step in pieces(turn, stage):
            across(turn, stage, step).start()

    for tick in range(tick_count(cuts, 3)):
        launch(tick + depth)
        for stage in range(3):
            for turn in tick_turns(cuts, tick - stage):
                advance(turn, stage)
        yield
    for turn in range(len(cuts)):
        for stage in range(3):
            for step in pieces(turn, stage):
                from_across(turn, stage, step).wait_recv()
            for step in pieces(turn, stage):
                across(turn, stage, step).wait_send()
            for step in hops(turn, stage):
                outgoing(turn, stage, step).wait_send()


def gather_scratch(sizes, cuts):
    most = max(sizes[:3])
    return [
        pltpu.SemaphoreType.DMA((len(cuts),)),
        pltpu.SemaphoreType.DMA((len(cuts), 6, most)),
        pltpu.SemaphoreType.DMA((len(cuts), 6, most)),
    ]


def gather_everywhere(arrays, collective_id, target, edge):
    sizes = lattice(lax.axis_size("seq"))
    cuts = block_cuts([array.shape for array in arrays], target)
    kinds = len(arrays)

    def kernel(*refs):
        ins, edge_in, refs = refs[:kinds], refs[kinds], refs[kinds + 1 :]
        outs, edge_out, refs = refs[:kinds], refs[kinds], refs[kinds + 1 :]
        *sems, edge_sems = refs
        me, count = lax.axis_index("seq"), lax.axis_size("seq")
        following, previous = lax.rem(me + 1, count), lax.rem(me + count - 1, count)
        greet(sizes, coordinates(sizes), [following, previous])
        edge_copy = pltpu.make_async_remote_copy(
            src_ref=edge_in.at[pl.ds(edge.shape[0] - HALO, HALO), :],
            dst_ref=edge_out,
            send_sem=edge_sems.at[0],
            recv_sem=edge_sems.at[1],
            device_id=(following,),
            device_id_type=MESH,
        )
        edge_copy.start()
        run_together([gather_program(sizes, cuts, ins, outs, *sems)])
        edge_copy.wait()

    hbm = pl.BlockSpec(memory_space=pl.ANY)
    gathered = pl.pallas_call(
        kernel,
        out_shape=[jax.ShapeDtypeStruct(sizes + a.shape, a.dtype) for a in arrays]
        + [jax.ShapeDtypeStruct((HALO, edge.shape[1]), edge.dtype)],
        in_specs=[hbm] * (kinds + 1),
        out_specs=[hbm] * (kinds + 1),
        scratch_shapes=gather_scratch(sizes, cuts) + [pltpu.SemaphoreType.DMA((2,))],
        compiler_params=pltpu.CompilerParams(
            collective_id=collective_id,
            has_side_effects=True,
            vmem_limit_bytes=62 * 1024 * 1024,
        ),
        name="gather_everywhere",
    )(*arrays, edge)
    return [g.reshape(-1, a.shape[1]) for g, a in zip(gathered, arrays)] + [gathered[kinds]]


def scatter_plan(shapes, small, target):
    sizes = lattice(lax.axis_size("seq"))
    cuts = block_cuts(shapes, target)
    kinds = len(shapes)
    most = max(sizes[:3])
    used = [axis_order(turn)[::-1] for turn in range(len(cuts))]
    pairs = [[[axis for axis in range(3) if axis != axes[0]] for axes in used]][0]
    first_lead = tuple(max(sizes[pair[i]] for pair in pairs) for i in range(2))
    first_step = max(sizes[axes[0]] for axes in used) - 1
    second_lead = max(sizes[axes[2]] for axes in used)
    second_step = max(sizes[axes[1]] for axes in used) - 1
    last_step = max(sizes[axes[2]] for axes in used) - 1
    extra = 0 if small is None else 1

    def program(ins, small_in, outs, small_out, refs):
        own, core_in, first_in, second_in, last_in = [
            refs[i * kinds : (i + 1) * kinds] for i in range(5)
        ]
        refs = refs[5 * kinds :]
        local_sem, send_sem, recv_sem = refs[:3]
        place = coordinates(sizes)
        sibling = partners(sizes, place, 3)[0]
        sent = []

        def push(source, target_ref, other, sems, slot):
            copy = pltpu.make_async_remote_copy(
                src_ref=source,
                dst_ref=target_ref,
                send_sem=sems[0].at[slot],
                recv_sem=sems[1].at[slot],
                device_id=(device_at(sizes, other),),
                device_id_type=MESH,
            )
            copy.start()
            sent.append(copy)

        def arrival(here, sems, slot):
            pltpu.make_async_remote_copy(
                src_ref=here,
                dst_ref=here,
                send_sem=sems[0].at[slot],
                recv_sem=sems[1].at[slot],
                device_id=(device_at(sizes, sibling),),
                device_id_type=MESH,
            ).wait_recv()

        main_sems = (send_sem, recv_sem)

        def core_copy(turn):
            number, window = cuts[turn]
            return pltpu.make_async_remote_copy(
                src_ref=ins[number].at[:, :, :, sibling[3], *window],
                dst_ref=core_in[number].at[:, :, :, *window],
                send_sem=send_sem.at[turn, 0, 0],
                recv_sem=recv_sem.at[turn, 0, 0],
                device_id=(device_at(sizes, sibling),),
                device_id_type=MESH,
            )

        def local_copy(turn):
            number, window = cuts[turn]
            return pltpu.make_async_copy(
                ins[number].at[:, :, :, place[3], *window],
                own[number].at[:, :, :, *window],
                local_sem.at[turn],
            )

        for turn in range(len(cuts)):
            core_copy(turn).start()
            local_copy(turn).start()
        yield

        def kept(number, window, axes, stage, at):
            index = [slice(None), slice(None), slice(None)]
            for axis in axes[:stage]:
                index[axis] = at[axis]
            return own[number].at[*index, *window]

        def landed(number, window, axes, stage, step):
            if stage == 3:
                return last_in[number].at[step, *window]
            left = [sizes[axis] for axis in range(3) if axis not in axes[:stage]]
            box = (first_in, second_in)[stage - 1][number]
            return box.at[step, *[pl.ds(0, size) for size in left], *window]

        def advance(turn, stage):
            number, window = cuts[turn]
            axes = axis_order(turn)[::-1]
            lead = tuple(sizes[axis] for axis in range(3) if axis not in axes[:stage])
            if stage == 0:
                local_copy(turn).wait()
                arrival(core_in[number].at[:, :, :, *window], main_sems, (turn, 0, 0))
                pieces = [core_in[number].at[:, :, :, *window]]
            else:
                steps = range(sizes[axes[stage - 1]] - 1)
                pieces = [landed(number, window, axes, stage, step) for step in steps]
                for step in steps:
                    arrival(pieces[step], main_sems, (turn, stage, step))
            target_ref = kept(number, window, axes, stage, place)

            def total(index):
                value = target_ref[index].astype(jnp.float32)
                for piece in pieces:
                    value = value + piece[index].astype(jnp.float32)
                return value

            if stage == 3:
                outs[number][window] = total((...,))
                return
            amount = math.prod(lead)

            def add(flat, carry):
                index, rest = [], flat
                for size in lead[::-1]:
                    index.insert(0, rest % size)
                    rest = rest // size
                target_ref[tuple(index)] = total(tuple(index)).astype(jnp.bfloat16)
                return carry

            lax.fori_loop(0, amount, add, 0)
            for step in range(sizes[axes[stage]] - 1):
                onward(turn, stage, step).start()

        def onward(turn, stage, step):
            number, window = cuts[turn]
            axes = axis_order(turn)[::-1]
            other = partners(sizes, place, axes[stage])[step]
            return pltpu.make_async_remote_copy(
                src_ref=kept(number, window, axes, stage + 1, other),
                dst_ref=landed(number, window, axes, stage + 1, step),
                send_sem=send_sem.at[turn, stage + 1, step],
                recv_sem=recv_sem.at[turn, stage + 1, step],
                device_id=(device_at(sizes, other),),
                device_id_type=MESH,
            )

        if extra:
            boxes, small_sems = refs[3:7], refs[7:9]

        def small_step(tick):
            axes = (3, 2, 1, 0)
            if tick > 0:
                axis = axes[tick - 1]
                box = boxes[axis]
                for step in range(sizes[axis] - 1):
                    behind = (place[axis] - step - 1 + sizes[axis]) % sizes[axis]
                    arrival(box.at[behind], small_sems, (axis, step))
                value = box[0]
                for at in range(1, sizes[axis]):
                    value = value + box[at]
            else:
                value = small_in[0][...]
            if tick == 4:
                small_out[0][...] = value
                return
            axis = axes[tick]
            boxes[axis][place[axis]] = value
            here = boxes[axis].at[place[axis]]
            for step, other in enumerate(partners(sizes, place, axis)):
                push(here, here, other, small_sems, (axis, step))

        for tick in range(max(tick_count(cuts, 4), 5)):
            for stage in range(4):
                for turn in tick_turns(cuts, tick - stage):
                    advance(turn, stage)
            if extra and tick < 5:
                small_step(tick)
            yield
        for copy in sent:
            copy.wait_send()
        for turn in range(len(cuts)):
            core_copy(turn).wait_send()
            axes = axis_order(turn)[::-1]
            for stage in range(3):
                for step in range(sizes[axes[stage]] - 1):
                    onward(turn, stage, step).wait_send()

    scratch = []
    for lead in (
        sizes[:3],
        sizes[:3],
        (first_step,) + first_lead,
        (second_step, second_lead),
        (last_step,),
    ):
        scratch += [pltpu.VMEM(lead + s, jnp.bfloat16) for s in shapes]
    scratch += [
        pltpu.SemaphoreType.DMA((len(cuts),)),
        pltpu.SemaphoreType.DMA((len(cuts), 4, most)),
        pltpu.SemaphoreType.DMA((len(cuts), 4, most)),
    ]
    if extra:
        scratch += [pltpu.VMEM((size,) + small.shape, jnp.float32) for size in sizes]
        scratch += [pltpu.SemaphoreType.DMA((4, most)) for _ in range(2)]
    return program, scratch


def scatter_sums(parts, small, collective_id, target):
    sizes = lattice(lax.axis_size("seq"))
    count = lax.axis_size("seq")
    shapes = [(p.shape[0] // count, p.shape[1]) for p in parts]
    views = [p.reshape(sizes + s) for p, s in zip(parts, shapes)]
    program, scratch = scatter_plan(shapes, small, target)
    kinds = len(parts)

    def kernel(*refs):
        ins, small_in, refs = refs[:kinds], refs[kinds : kinds + 1], refs[kinds + 1 :]
        outs, small_out, refs = refs[:kinds], refs[kinds : kinds + 1], refs[kinds + 1 :]
        greet(sizes, coordinates(sizes))
        run_together([program(ins, small_in, outs, small_out, refs)])

    return pl.pallas_call(
        kernel,
        out_shape=[jax.ShapeDtypeStruct(s, jnp.float32) for s in shapes]
        + [jax.ShapeDtypeStruct(small.shape, jnp.float32)],
        in_specs=[pl.BlockSpec(memory_space=pl.ANY)] * kinds + [VMEM_SPEC],
        out_specs=[VMEM_SPEC] * (kinds + 1),
        scratch_shapes=scratch,
        compiler_params=pltpu.CompilerParams(
            collective_id=collective_id,
            has_side_effects=True,
            vmem_limit_bytes=62 * 1024 * 1024,
        ),
        name="scatter_sums",
    )(*views, small)


def greet_chips(chips):
    me = lax.axis_index("seq")
    chip, core = me // 2, me % 2
    barrier = pltpu.get_barrier_semaphore()

    def greet_one(step, carry):
        other = lax.rem(chip + step, chips) * 2 + core
        pl.semaphore_signal(barrier, inc=1, device_id=(other,), device_id_type=MESH)
        return carry

    lax.fori_loop(1, chips, greet_one, 0)
    pl.semaphore_signal(barrier, inc=1, device_id=(chip * 2 + 1 - core,), device_id_type=MESH)
    pl.semaphore_wait(barrier, chips)


def exchange_program(chips, part, reverse, own_ref, decay_ref, out_ref, chip_decay_ref, refs):
    (
        mine_low,
        other_low,
        other_decay,
        payload,
        landed,
        result,
        prefix,
        pair_sems,
        far_send,
        far_recv,
    ) = refs
    padded = own_ref.shape[2]
    me = lax.axis_index("seq")
    chip, core = me // 2, me % 2
    sibling = chip * 2 + 1 - core
    f32 = jnp.float32
    wire = jnp.bfloat16 if reverse else f32

    def pair_copy(source, target, slot):
        return pltpu.make_async_remote_copy(
            src_ref=source,
            dst_ref=target,
            send_sem=pair_sems.at[slot, 0],
            recv_sem=pair_sems.at[slot, 1],
            device_id=(sibling,),
            device_id_type=MESH,
        )

    def far_copy(step, turn, source, target):
        other = lax.rem(chip + step, chips)
        return pltpu.make_async_remote_copy(
            src_ref=source.at[other],
            dst_ref=target.at[chip],
            send_sem=far_send.at[turn, step],
            recv_sem=far_recv.at[turn, step],
            device_id=(other * 2 + core,),
            device_id_type=MESH,
        )

    def far_start(turn, source, target):
        def start(step, carry):
            far_copy(step, turn, source, target).start()
            return carry

        lax.fori_loop(1, chips, start, 0)

    def far_wait(turn, source, target):
        def finish(step, carry):
            far_copy(step, turn, source, target).wait()
            return carry

        lax.fori_loop(1, chips, finish, 0)

    def by_row(vector, half, shape, first=0):
        place = (
            lax.broadcasted_iota(jnp.int32, shape, 0) + first
        ) * part + lax.broadcasted_iota(jnp.int32, shape, 1)
        head = (half * (chips * part) + place) // MHEAD_DIM
        lane = lax.broadcasted_iota(jnp.int32, shape, 2)
        picked = jnp.where(lane == head, vector.reshape(1, 1, 128), 0.0)
        return jnp.sum(picked, axis=2, keepdims=True)

    mine_low[...] = own_ref[...].astype(wire)
    first_copies = [
        pair_copy(mine_low, other_low, 0),
        pair_copy(decay_ref, other_decay, 1),
    ]
    for copy in first_copies:
        copy.start()
    yield
    for copy in first_copies:
        copy.wait()
    own_decay, far_decay = decay_ref[0:1, :], other_decay[0:1, :]
    second_core = core == 1
    decays = (
        jnp.where(second_core, far_decay, own_decay),
        jnp.where(second_core, own_decay, far_decay),
    )
    weighted = 0 if reverse else 1
    whole = (chips, padded, 128)
    half_own = own_ref[core]
    half_far = other_low[core].astype(f32)
    earlier = jnp.where(second_core, half_far, half_own)
    later = jnp.where(second_core, half_own, half_far)
    factor = by_row(decays[weighted], core, whole)
    total = earlier + factor * later if reverse else factor * earlier + later
    payload[:, :padded, :] = total.astype(wire)
    if not reverse:
        both = jnp.broadcast_to(decays[0] * decays[1], (8, 128))
        for other in range(chips):
            payload[other, padded:, :] = both
    far_start(0, payload, landed)
    landed[chip] = payload[chip]
    yield
    far_wait(0, payload, landed)
    if not reverse:
        for other in range(chips):
            chip_decay_ref[other : other + 1, :] = landed[other, padded : padded + 1, :]
    state = jnp.zeros((1, padded, 128), f32)
    order = range(chips - 1, -1, -1) if reverse else range(chips)
    for other in order:
        result[other] = state[0]
        step_factor = by_row(chip_decay_ref[other : other + 1, :], core, (1, padded, 128), chip)
        state = step_factor * state + landed[other, :padded, :].astype(f32)[None]
    far_start(1, result, prefix)
    prefix[chip] = result[chip]
    yield
    far_wait(1, result, prefix)
    out_ref[core] = prefix[...]
    last_copy = pair_copy(prefix, out_ref.at[core], 2)
    last_copy.start()
    yield
    last_copy.wait()
    moved = (core == 0) if reverse else second_core
    step_decay = decays[1] if reverse else decays[0]
    for half in range(2):
        factor = jnp.where(moved, by_row(step_decay, half, whole), 1.0)
        extra = jnp.where(moved, other_low[half].astype(f32), 0.0)
        out_ref[half] = factor * out_ref[half] + extra


def exchange_scratch(chips, padded, reverse):
    f32 = jnp.float32
    low = jnp.bfloat16 if reverse else f32
    sent_rows = padded if reverse else padded + 8
    return [
        pltpu.VMEM((2, chips, padded, 128), low),
        pltpu.VMEM((2, chips, padded, 128), low),
        pltpu.VMEM((8, 128), f32),
        pltpu.VMEM((chips, sent_rows, 128), low),
        pltpu.VMEM((chips, sent_rows, 128), low),
        pltpu.VMEM((chips, padded, 128), f32),
        pltpu.VMEM((chips, padded, 128), f32),
        pltpu.SemaphoreType.DMA((3, 2)),
        pltpu.SemaphoreType.DMA((2, chips)),
        pltpu.SemaphoreType.DMA((2, chips)),
    ]


def slice_rows(values, chips):
    part = values.shape[0] // (2 * chips)
    padded = -(-part // 16) * 16
    sliced = values.reshape(2, chips, part, values.shape[1])
    return jnp.pad(sliced, ((0, 0), (0, 0), (0, padded - part), (0, 0)))


def join_rows(slices, rows):
    chips = slices.shape[1]
    return slices[:, :, : rows // (2 * chips)].reshape(rows, slices.shape[3])


def front(kv_local, local_state, passing, late, mixer_args, attention_args, collective_id, targets):
    count = lax.axis_size("seq")
    sizes, chips = lattice(count), count // 2
    cuts = block_cuts([kv_local.shape], targets[0])
    late_cuts = block_cuts([w.shape for w in late], targets[1])
    states = slice_rows(local_state, chips)
    part, padded = SSM // count, states.shape[2]
    fused = part == padded
    kinds = len(late)
    shape = jax.ShapeDtypeStruct
    rows = mixer_args[0].shape[0]
    groups, query_rows, _ = attention_args[0].shape
    tokens = kv_local.shape[0] * count
    comm_scratch = (
        gather_scratch(sizes, cuts)
        + gather_scratch(sizes, late_cuts)
        + exchange_scratch(chips, padded, False)
    )
    compute_scratch = (
        [pltpu.VMEM((3 * rows, SSM), jnp.bfloat16)]
        + attention_scratch(groups, query_rows)
        + [
            pltpu.VMEM(sizes + kv_local.shape, kv_local.dtype),
            pltpu.SemaphoreType.DMA((1,)),
        ]
    )
    extra_in = list(mixer_args) + list(attention_args) if fused else []
    extra_out = mixer_output_shapes(rows) + attention_shapes(groups, query_rows) if fused else []

    def kernel(*refs):
        kv_ref, state_ref, decay_ref, refs = refs[0], refs[1], refs[2], refs[3:]
        late_in, refs = refs[:kinds], refs[kinds:]
        ins, refs = refs[: len(extra_in)], refs[len(extra_in) :]
        kv_out, state_out, chip_decay_ref, refs = refs[0], refs[1], refs[2], refs[3:]
        late_out, refs = refs[:kinds], refs[kinds:]
        outs, refs = refs[: len(extra_out)], refs[len(extra_out) :]
        comm, refs = refs[: len(comm_scratch)], refs[len(comm_scratch) :]
        greet_chips(chips)
        exchange = exchange_program(
            chips, part, False, state_ref, decay_ref, state_out, chip_decay_ref, comm[6:]
        )
        keys = gather_program(sizes, cuts, [kv_ref], [kv_out], *comm[:3])
        weights = gather_program(sizes, late_cuts, late_in, late_out, *comm[3:6], 2)
        ahead = 0
        next(exchange)
        next(keys)
        next(weights)

        def some_weights():
            for _ in range(ahead):
                next(weights)
                yield

        run_together([exchange, keys, some_weights()])
        if not fused:
            for _ in weights:
                pass
            return
        input_ref, max_ref, acc_ref, kv_vmem, kv_sem = refs
        load = pltpu.make_async_copy(kv_out, kv_vmem, kv_sem.at[0])
        load.start()
        mixer_output_body(
            *ins[:3], state_out[...].reshape(SSM, STATE), *ins[3:7], *outs[:2], input_ref
        )
        load.wait()
        next(weights, None)
        left = tick_count(late_cuts, 3) - 1 - ahead
        steps = tokens // KEYS_STEP
        attention_forward_body(
            ins[7],
            kv_vmem.reshape(tokens, kv_local.shape[1]),
            ins[8],
            *outs[2:],
            max_ref,
            acc_ref,
            spread_ticks(weights, left, steps),
        )
        for _ in weights:
            pass

    hbm = pl.BlockSpec(memory_space=pl.ANY)
    kv_all, states_in, chip_decay, *rest = pl.pallas_call(
        kernel,
        out_shape=[
            shape(sizes + kv_local.shape, kv_local.dtype),
            shape(states.shape, jnp.float32),
            shape((chips, 128), jnp.float32),
        ]
        + [shape(sizes + w.shape, w.dtype) for w in late]
        + extra_out,
        in_specs=[hbm, VMEM_SPEC, VMEM_SPEC] + [hbm] * kinds + [VMEM_SPEC] * len(extra_in),
        out_specs=[hbm, VMEM_SPEC, VMEM_SPEC] + [hbm] * kinds + [VMEM_SPEC] * len(extra_out),
        scratch_shapes=comm_scratch + (compute_scratch if fused else []),
        compiler_params=pltpu.CompilerParams(
            collective_id=collective_id,
            has_side_effects=True,
            vmem_limit_bytes=62 * 1024 * 1024,
        ),
        name="front",
    )(kv_local, states, passing, *late, *extra_in)
    kv_all = kv_all.reshape(-1, kv_local.shape[1])
    late_full = [w.reshape(-1, w.shape[-1]) for w in rest[:kinds]]
    states_in = join_rows(states_in, SSM)
    computed = rest[kinds:]
    if not fused:
        computed = mixer_output(*mixer_args[:3], states_in, *mixer_args[3:])
        computed = list(computed) + list(
            attention_forward(attention_args[0], kv_all, attention_args[1])
        )
    return kv_all, states_in, chip_decay, late_full, computed


def back(key_terms, mixer_args, passing, chip_decay, late_grads, collective_id, targets):
    count = lax.axis_size("seq")
    sizes, chips = lattice(count), count // 2
    shape = (key_terms.shape[0] // count, key_terms.shape[1])
    late_shapes = [(g.shape[0] // count, g.shape[1]) for g in late_grads]
    keys, keys_scratch = scatter_plan([shape], None, targets[0])
    weights, weights_scratch = scatter_plan(late_shapes, None, targets[1])
    part = SSM // count
    padded = -(-part // 16) * 16
    fused = part == padded
    rows = mixer_args[0].shape[0]
    state_shape = (2, chips, padded, STATE)
    kinds = len(late_grads)
    if fused:
        first_in, mixer_shapes = list(mixer_args), mixer_backward_shapes(rows, state_shape)
        compute_scratch = mixer_backward_scratch(rows)
    else:
        mixer_out = list(mixer_backward(mixer_args))
        first_in, mixer_shapes = [slice_rows(mixer_out[3], chips)], []
        compute_scratch = []
    known = len(first_in)
    made = len(mixer_shapes)

    def kernel(kv_ref, decay_ref, chip_decay_ref, *refs):
        late_in, refs = refs[:kinds], refs[kinds:]
        ins, refs = refs[:known], refs[known:]
        kv_out, state_out, refs = refs[0], refs[1], refs[2:]
        late_out, refs = refs[:kinds], refs[kinds:]
        outs, refs = refs[:made], refs[made:]
        keys_refs, refs = refs[: len(keys_scratch)], refs[len(keys_scratch) :]
        weights_refs, refs = refs[: len(weights_scratch)], refs[len(weights_scratch) :]
        mixer_refs, refs = refs[: len(compute_scratch)], refs[len(compute_scratch) :]
        greet_chips(chips)
        runs = [
            keys([kv_ref], [], [kv_out], [], keys_refs),
            weights(late_in, [], late_out, [], weights_refs),
        ]

        def tick():
            for run in runs:
                next(run)

        tick()
        if fused:
            mixer_backward_body(*ins, *outs, *mixer_refs, tick)
            own_ref = outs[3]
        else:
            own_ref = ins[0]
        exchange = exchange_program(
            chips, part, True, own_ref, decay_ref, state_out, chip_decay_ref, refs
        )
        run_together([exchange] + runs)

    hbm = pl.BlockSpec(memory_space=pl.ANY)
    kv_sum, grad_end, *rest = pl.pallas_call(
        kernel,
        out_shape=[
            jax.ShapeDtypeStruct(shape, jnp.float32),
            jax.ShapeDtypeStruct(state_shape, jnp.float32),
        ]
        + [jax.ShapeDtypeStruct(s, jnp.float32) for s in late_shapes]
        + mixer_shapes,
        in_specs=[hbm] + [VMEM_SPEC] * 2 + [hbm] * kinds + [VMEM_SPEC] * known,
        out_specs=[VMEM_SPEC] * (2 + kinds + made),
        scratch_shapes=keys_scratch
        + weights_scratch
        + compute_scratch
        + exchange_scratch(chips, padded, True),
        compiler_params=pltpu.CompilerParams(
            collective_id=collective_id,
            has_side_effects=True,
            vmem_limit_bytes=63 * 1024 * 1024,
        ),
        name="back",
    )(
        key_terms.reshape(sizes + shape),
        passing,
        chip_decay,
        *[g.reshape(sizes + s) for g, s in zip(late_grads, late_shapes)],
        *first_in,
    )
    if fused:
        mixer_out = rest[kinds:]
    return kv_sum, join_rows(grad_end, SSM), rest[:kinds], mixer_out


KEYS_STEP = 512


def attention_forward_body(
    q_ref, kv_ref, starts_ref, out_ref, log_ref, flat_ref, max_ref, acc_ref, ticks
):
    groups, rows, _ = q_ref.shape
    group_size = QHEADS // KVHEADS
    local_rows = rows // group_size
    half_kv = KVW // 2
    steps = kv_ref.shape[0] // KEYS_STEP
    first_row = lax.axis_index("seq") * local_rows
    used = (first_row + local_rows - 1) // KEYS_STEP + 1
    starts = starts_ref[...]
    places = first_row + lax.broadcasted_iota(jnp.int32, (1, rows), 1) % local_rows
    max_ref[...] = jnp.full(max_ref.shape, masked, jnp.float32)
    acc_ref[...] = jnp.zeros(acc_ref.shape, jnp.float32)

    def block(step, general):
        first_key = pl.multiple_of(step * KEYS_STEP, KEYS_STEP)
        piece = kv_ref[pl.ds(first_key, KEYS_STEP), :]
        flipped = jnp.transpose(piece[:, half_kv:])
        ones = jnp.ones((16, KEYS_STEP), jnp.bfloat16)
        if general:
            key_pos = first_key + lax.broadcasted_iota(jnp.int32, (KEYS_STEP, 1), 0)
            allowed = (key_pos >= starts) & (key_pos <= places)
        else:
            row_open = starts <= first_key
        for group in range(groups):
            scores = lax.dot_general(
                piece[:, group * HEAD_DIM : (group + 1) * HEAD_DIM],
                q_ref[group],
                (((1,), (1,)), ((), ())),
                preferred_element_type=jnp.float32,
            )
            if general:
                scores = jnp.where(allowed, scores, masked)
            old = max_ref[group]
            new = jnp.maximum(old, jnp.max(scores, axis=0, keepdims=True))
            if general:
                shift = new
            else:
                new = jnp.where(row_open, new, old)
                shift = jnp.where(row_open, new, -masked)
            max_ref[group] = new
            weights = jnp.exp(scores - shift).astype(jnp.bfloat16)
            values = jnp.concatenate(
                [flipped[group * HEAD_DIM : (group + 1) * HEAD_DIM], ones], axis=0
            )
            acc_ref[group] = acc_ref[group] * jnp.exp(old - new) + jnp.dot(
                values, weights, preferred_element_type=jnp.float32
            )

    def body(step, carry):
        general = (step == 0) | ((step + 1) * KEYS_STEP > first_row)
        pl.when((step < used) & general)(partial(block, step, True))
        pl.when((step < used) & jnp.logical_not(general))(partial(block, step, False))
        for at, tick in ticks:
            pl.when(step == at)(tick)
        return carry

    lax.fori_loop(0, steps, body, 0)
    for group in range(groups):
        row_sum = acc_ref[group, HEAD_DIM : HEAD_DIM + 1, :]
        out = acc_ref[group, :HEAD_DIM, :] / row_sum
        out_ref[group] = out
        log_ref[group] = max_ref[group] + jnp.log(row_sum)
        for part in range(group_size):
            head = group * group_size + part
            flat_ref[:, head * HEAD_DIM : (head + 1) * HEAD_DIM] = jnp.transpose(
                out[:, part * local_rows : (part + 1) * local_rows]
            ).astype(jnp.bfloat16)


def attention_shapes(groups, rows):
    return [
        jax.ShapeDtypeStruct((groups, HEAD_DIM, rows), jnp.float32),
        jax.ShapeDtypeStruct((groups, 1, rows), jnp.float32),
        jax.ShapeDtypeStruct((rows // (QHEADS // KVHEADS), QW), jnp.bfloat16),
    ]


def attention_scratch(groups, rows):
    return [
        pltpu.VMEM((groups, 1, rows), jnp.float32),
        pltpu.VMEM((groups, HEAD_DIM + 16, rows), jnp.float32),
    ]


def attention_forward(queries, kv_all, row_starts):
    groups, rows, _ = queries.shape

    def kernel(*refs):
        attention_forward_body(*refs, [])

    return pl.pallas_call(
        kernel,
        out_shape=attention_shapes(groups, rows),
        in_specs=[VMEM_SPEC] * 3,
        out_specs=[VMEM_SPEC] * 3,
        scratch_shapes=attention_scratch(groups, rows),
        compiler_params=BIG_VMEM,
        name="attention_forward",
    )(queries, kv_all, row_starts)


def spread_ticks(program, ticks, steps):
    def make_tick():
        def tick():
            next(program, None)

        return tick

    return [(number * steps // ticks, make_tick()) for number in range(ticks)]


def attention_backward(
    queries, grads, kv_all, row_starts, log_total, outputs, late_grads, collective_id, target
):
    groups, rows, _ = queries.shape
    total = kv_all.shape[0]
    half_kv = KVW // 2
    group_size = QHEADS // KVHEADS
    local_rows = rows // group_size
    count = lax.axis_size("seq")
    sizes = lattice(count)
    shapes = [(g.shape[0] // count, g.shape[1]) for g in late_grads]
    views = [g.reshape(sizes + s) for g, s in zip(late_grads, shapes)]
    program, scratch = scatter_plan(shapes, None, target)
    kinds = len(shapes)
    ticks = max(tick_count(block_cuts(shapes, target), 4), 5)
    steps = total // KEYS_STEP

    def kernel(q_ref, g_ref, kv_ref, starts_ref, log_ref, outputs_ref, *refs):
        ins, dkv_ref, dq_ref, refs = refs[:kinds], refs[kinds], refs[kinds + 1], refs[kinds + 2 :]
        outs, delta_ref, refs = refs[:kinds], refs[kinds], refs[kinds + 1 :]
        greet(sizes, coordinates(sizes))
        sums = program(ins, [], outs, [], refs)
        next(sums)
        first_row = lax.axis_index("seq") * local_rows
        used = (first_row + local_rows - 1) // KEYS_STEP + 1
        starts = starts_ref[...]
        places = first_row + lax.broadcasted_iota(jnp.int32, (1, rows), 1) % local_rows
        dq_ref[...] = jnp.zeros(dq_ref.shape, jnp.float32)
        for group in range(groups):
            flipped_grads = jnp.transpose(g_ref[group].astype(jnp.float32))
            delta_ref[group] = jnp.sum(flipped_grads * outputs_ref[group], axis=0, keepdims=True)

        def block(step, general):
            first_key = pl.multiple_of(step * KEYS_STEP, KEYS_STEP)
            piece = kv_ref[pl.ds(first_key, KEYS_STEP), :]
            flipped = jnp.transpose(piece[:, :half_kv])
            if general:
                key_pos = first_key + lax.broadcasted_iota(jnp.int32, (KEYS_STEP, 1), 0)
                allowed = (key_pos >= starts) & (key_pos <= places)
            else:
                row_open = starts <= first_key
            found = []
            for group in range(groups):
                low, high = group * HEAD_DIM, (group + 1) * HEAD_DIM
                scores = lax.dot_general(
                    piece[:, low:high],
                    q_ref[group],
                    (((1,), (1,)), ((), ())),
                    preferred_element_type=jnp.float32,
                )
                shift = log_ref[group]
                if general:
                    scores = jnp.where(allowed, scores, masked)
                else:
                    shift = jnp.where(row_open, shift, -masked)
                weights = jnp.exp(scores - shift)
                grad_weights = lax.dot_general(
                    piece[:, half_kv + low : half_kv + high],
                    g_ref[group],
                    (((1,), (1,)), ((), ())),
                    preferred_element_type=jnp.float32,
                )
                grad_scores = (weights * (grad_weights - delta_ref[group])).astype(jnp.bfloat16)
                dq_ref[group] += jnp.dot(
                    flipped[low:high], grad_scores, preferred_element_type=jnp.float32
                )
                found.append(
                    jnp.dot(grad_scores, q_ref[group], preferred_element_type=jnp.float32)
                )
                found.append(
                    jnp.dot(
                        weights.astype(jnp.bfloat16),
                        g_ref[group],
                        preferred_element_type=jnp.float32,
                    )
                )
            dkv_ref[pl.ds(first_key, KEYS_STEP), :] = jnp.concatenate(
                found[0::2] + found[1::2], axis=1
            ).astype(dkv_ref.dtype)

        def clear(step):
            first_key = pl.multiple_of(step * KEYS_STEP, KEYS_STEP)
            dkv_ref[pl.ds(first_key, KEYS_STEP), :] = jnp.zeros((KEYS_STEP, KVW), dkv_ref.dtype)

        marks = spread_ticks(sums, ticks, steps)

        def body(step, carry):
            general = (step == 0) | ((step + 1) * KEYS_STEP > first_row)
            pl.when((step < used) & general)(partial(block, step, True))
            pl.when((step < used) & jnp.logical_not(general))(partial(block, step, False))
            pl.when(step >= used)(partial(clear, step))
            for at, tick in marks:
                pl.when(step == at)(tick)
            return carry

        lax.fori_loop(0, steps, body, 0)
        for _ in sums:
            pass

    hbm = pl.BlockSpec(memory_space=pl.ANY)
    key_terms, query_grads, *late_sums = pl.pallas_call(
        kernel,
        out_shape=[
            jax.ShapeDtypeStruct((total, KVW), jnp.bfloat16),
            jax.ShapeDtypeStruct((groups, HEAD_DIM, rows), jnp.float32),
        ]
        + [jax.ShapeDtypeStruct(s, jnp.float32) for s in shapes],
        in_specs=[VMEM_SPEC] * 6 + [hbm] * kinds,
        out_specs=[VMEM_SPEC] * (2 + kinds),
        scratch_shapes=[pltpu.VMEM((groups, 1, rows), jnp.float32)] + scratch,
        compiler_params=pltpu.CompilerParams(
            collective_id=collective_id,
            has_side_effects=True,
            vmem_limit_bytes=62 * 1024 * 1024,
        ),
        name="attention_backward",
    )(queries, grads, kv_all, row_starts, log_total, outputs, *views)
    return key_terms, query_grads, late_sums


BIG_VMEM = pltpu.CompilerParams(vmem_limit_bytes=62 * 1024 * 1024)


def dot_parts(value, exact, parts, axes=((1,), (0,))):
    total, left = None, value
    for _ in range(parts):
        piece = left.astype(jnp.bfloat16)
        left = left - piece.astype(jnp.float32)
        term = lax.dot_general(piece, exact, (axes, ((), ())), preferred_element_type=jnp.float32)
        total = term if total is None else total + term
    return total


def dot_left(exact, value, parts):
    total, left = None, value
    for _ in range(parts):
        piece = left.astype(jnp.bfloat16)
        left = left - piece.astype(jnp.float32)
        term = jnp.dot(exact, piece, preferred_element_type=jnp.float32)
        total = term if total is None else total + term
    return total


def matmul_pair(left_side, right_side, axes):
    left_high = left_side.astype(jnp.bfloat16)
    left_low = (left_side - left_high.astype(jnp.float32)).astype(jnp.bfloat16)
    right_high = right_side.astype(jnp.bfloat16)
    right_low = (right_side - right_high.astype(jnp.float32)).astype(jnp.bfloat16)
    dims = (axes, ((), ()))
    product = partial(
        lax.dot_general, dimension_numbers=dims, preferred_element_type=jnp.float32
    )
    return (
        product(left_high, right_high)
        + product(left_low, right_high)
        + product(left_high, right_low)
    )


def stacked(value, first):
    high = value.astype(jnp.bfloat16)
    low = (value - high.astype(jnp.float32)).astype(jnp.bfloat16)
    return [high, low, high] if first else [high, high, low]


def dot_fast(left_side, right_side, axes):
    return lax.dot_general(
        left_side.astype(jnp.bfloat16),
        right_side.astype(jnp.bfloat16),
        (axes, ((), ())),
        preferred_element_type=jnp.float32,
    )


NN = ((1,), (0,))
NT = ((1,), (1,))
TN = ((0,), (0,))


def head_spread():
    head = lax.broadcasted_iota(jnp.int32, (128, SSM), 0)
    column = lax.broadcasted_iota(jnp.int32, (128, SSM), 1)
    return jnp.where(column // MHEAD_DIM == head, 1.0, 0.0).astype(jnp.bfloat16)


def rope_table(rows, count):
    half = HEAD_DIM // 2
    frequency = rope_base ** (-np.arange(half) / half)
    tables = []
    for places in (np.arange(rows), rows * np.arange(count)):
        angles = np.tile(places[:, None] * frequency[None, :], (1, 4))
        tables += [np.cos(angles).astype(np.float32), np.sin(angles).astype(np.float32)]
    return tables


def rope_now(device, base_cos_ref, base_sin_ref, far_cos_ref, far_sin_ref):
    base_cos, base_sin = base_cos_ref[...], base_sin_ref[...]
    far_cos, far_sin = far_cos_ref[pl.ds(device, 1), :], far_sin_ref[pl.ds(device, 1), :]
    cosine_part = far_cos * base_cos - far_sin * base_sin
    sine_part = far_sin * base_cos + far_cos * base_sin
    lane = lax.broadcasted_iota(jnp.int32, base_cos.shape, 1)
    return cosine_part, jnp.where(lane % HEAD_DIM < HEAD_DIM // 2, -sine_part, sine_part)


def rope_lanes(values, cosine_all, sine_all):
    width = values.shape[1]
    repeat = width // cosine_all.shape[1]
    half = HEAD_DIM // 2
    column = lax.broadcasted_iota(jnp.int32, values.shape, 1)
    partner = jnp.where(
        column % HEAD_DIM < half,
        pltpu.roll(values, width - half, 1),
        pltpu.roll(values, half, 1),
    )
    if repeat > 1:
        cosine_all = jnp.concatenate([cosine_all] * repeat, axis=1)
        sine_all = jnp.concatenate([sine_all] * repeat, axis=1)
    return values * cosine_all + partner * sine_all


def mixer_forward(
    hidden, halo, norm_gain, weights, conv_weight, conv_bias, dt_bias, a_log, starts, tables
):
    rows, model = hidden.shape
    groups = QHEADS // KVHEADS
    half_kv = KVW // 2
    first_row = (lax.axis_index("seq") * rows).astype(jnp.int32).reshape(1)
    pieces = [
        (0, 0, SSM // 2),
        (0, SSM // 2, SSM // 2),
        (1, 0, XBC // 2),
        (1, XBC // 2, XBC // 2),
        (2, 0, QW),
        (2, QW, KVW),
        (2, QW + KVW, DT_PAD),
    ]
    load_order = (2, 3, 4, 5, 6, 0, 1)

    def kernel(
        first_ref,
        hidden_ref,
        halo_ref,
        gain_ref,
        z_hbm,
        xbc_hbm,
        small_hbm,
        tap_ref,
        bias_ref,
        dt_bias_ref,
        a_log_ref,
        starts_ref,
        base_cos_ref,
        base_sin_ref,
        far_cos_ref,
        far_sin_ref,
        normed_ref,
        gate_ref,
        ext_ref,
        pre_ref,
        q_ref,
        kv_ref,
        dt_pre_ref,
        log_ref,
        state_ref,
        passing_ref,
        z_ref,
        xbc_ref,
        small_ref,
        normed_ext,
        ext_f32,
        sems,
    ):
        weight_hbm, weight_refs = (z_hbm, xbc_hbm, small_hbm), (z_ref, xbc_ref, small_ref)
        copies = [
            pltpu.make_async_copy(
                weight_hbm[which].at[:, pl.ds(start, width)],
                weight_refs[which].at[:, pl.ds(start, width)],
                sems.at[number],
            )
            for number, (which, start, width) in enumerate(pieces)
        ]
        for number in load_order:
            copies[number].start()
        cosine_all, sine_all = rope_now(
            first_ref[0] // rows, base_cos_ref, base_sin_ref, far_cos_ref, far_sin_ref
        )

        def norm(block):
            values = block.astype(jnp.float32)
            scale = lax.rsqrt(jnp.mean(values * values, axis=1, keepdims=True) + epsilon)
            return (values * scale * gain_ref[...]).astype(jnp.bfloat16)

        normed_ext[:HALO, :] = norm(halo_ref[...])
        normed = norm(hidden_ref[...])
        normed_ext[HALO:, :] = normed
        normed_ref[...] = normed

        def project(number, values):
            copies[number].wait()
            which, start, width = pieces[number]
            return jnp.dot(
                values,
                weight_refs[which][:, start : start + width],
                preferred_element_type=jnp.float32,
            )

        for number in (2, 3):
            _, start, width = pieces[number]
            part = project(number, normed_ext[...]).astype(jnp.bfloat16)
            ext_ref[:, start : start + width] = part
            ext_f32[:, start : start + width] = part.astype(jnp.float32)
        turned = rope_lanes(project(4, normed), cosine_all, sine_all).astype(jnp.bfloat16)
        turned = turned * jnp.bfloat16(HEAD_DIM ** (-0.5))
        for head in range(QHEADS):
            place = head % groups * rows
            q_ref[head // groups, place : place + rows, :] = turned[
                :, head * HEAD_DIM : (head + 1) * HEAD_DIM
            ]
        kv_raw = project(5, normed)
        kv_ref[:, :half_kv] = rope_lanes(
            kv_raw[:, :half_kv], cosine_all, sine_all
        ).astype(jnp.bfloat16)
        kv_ref[:, half_kv:] = kv_raw[:, half_kv:].astype(jnp.bfloat16)
        dt_pre = project(6, normed) + dt_bias_ref[...]
        dt_pre_ref[...] = dt_pre
        step_dt = jax.nn.softplus(dt_pre)
        order = lax.broadcasted_iota(jnp.int32, (rows, rows), 0)
        other = lax.broadcasted_iota(jnp.int32, (rows, rows), 1)
        lower = jnp.where(other <= order, 1.0, 0.0).astype(jnp.bfloat16)
        log_decay = dot_left(lower, -step_dt * jnp.exp(a_log_ref[...]), 3)
        log_ref[...] = log_decay
        for number in (0, 1):
            _, start, width = pieces[number]
            gate_ref[:, start : start + width] = project(number, normed)

        starts_now = starts_ref[...]
        places = first_ref[0] + lax.broadcasted_iota(jnp.int32, (rows, 1), 0)
        pre = jnp.zeros((rows, XBC), jnp.float32) + bias_ref[...]
        for tap in range(CONV):
            lag = CONV - 1 - tap
            kept = jnp.where(places - lag >= starts_now, 1.0, 0.0)
            pre = pre + ext_f32[HALO - lag : HALO - lag + rows, :] * kept * tap_ref[tap : tap + 1, :]
        pre_ref[...] = pre
        conv_out = pre * jax.nn.sigmoid(pre)
        last = log_decay[rows - 1 : rows, :]
        last_start = starts_ref[rows - 1 : rows, :]
        weight = jnp.exp(jnp.where(places >= last_start, last - log_decay, masked)) * step_dt
        spread = dot_parts(weight, head_spread(), 2)
        state_ref[...] = matmul_pair(
            conv_out[:, :SSM] * spread, conv_out[:, SSM : SSM + STATE], TN
        )
        passing = jnp.exp(last) * jnp.where(last_start < first_ref[0], 1.0, 0.0)
        passing_ref[...] = jnp.broadcast_to(passing, passing_ref.shape)

    f32 = jnp.float32
    shape = jax.ShapeDtypeStruct
    return pl.pallas_call(
        kernel,
        out_shape=(
            shape((rows, model), jnp.bfloat16),
            shape((rows, SSM), f32),
            shape((HALO + rows, XBC), jnp.bfloat16),
            shape((rows, XBC), f32),
            shape((KVHEADS, groups * rows, HEAD_DIM), jnp.bfloat16),
            shape((rows, KVW), jnp.bfloat16),
            shape((rows, DT_PAD), f32),
            shape((rows, DT_PAD), f32),
            shape((SSM, STATE), f32),
            shape((8, DT_PAD), f32),
        ),
        in_specs=[pl.BlockSpec(memory_space=pltpu.SMEM)]
        + [VMEM_SPEC] * 3
        + [pl.BlockSpec(memory_space=pl.ANY)] * 3
        + [VMEM_SPEC] * 9,
        out_specs=[VMEM_SPEC] * 10,
        scratch_shapes=[
            *[pltpu.VMEM(w.shape, jnp.bfloat16) for w in weights],
            pltpu.VMEM((HALO + rows, model), jnp.bfloat16),
            pltpu.VMEM((HALO + rows, XBC), f32),
            pltpu.SemaphoreType.DMA((len(pieces),)),
        ],
        compiler_params=BIG_VMEM,
        name="mixer_forward",
    )(
        first_row,
        hidden,
        halo,
        norm_gain[None],
        *weights,
        conv_weight,
        conv_bias[None],
        dt_bias,
        a_log,
        starts[:, None],
        *tables,
    )


def document_mask(first_row, starts, rows, flip):
    if flip:
        token = lax.broadcasted_iota(jnp.int32, (rows, rows), 1)
        source = lax.broadcasted_iota(jnp.int32, (rows, rows), 0)
    else:
        token = lax.broadcasted_iota(jnp.int32, (rows, rows), 0)
        source = lax.broadcasted_iota(jnp.int32, (rows, rows), 1)
    allowed = (first_row + source >= starts) & (source <= token)
    return jnp.where(allowed, 0.0, masked)


def mixer_output_body(
    pre_ref,
    dt_pre_ref,
    log_ref,
    state,
    gate_ref,
    gain_ref,
    skip_ref,
    starts_ref,
    normed_ref,
    y_ref,
    input_ref,
):
    rows = pre_ref.shape[0]
    first_row = lax.axis_index("seq") * rows
    pre_now = pre_ref[...]
    conv_out = pre_now * jax.nn.sigmoid(pre_now)
    ssm_x = conv_out[:, :SSM]
    input_b = conv_out[:, SSM : SSM + STATE]
    output_c = conv_out[:, SSM + STATE :]
    spread = head_spread()
    log_decay_now = log_ref[...]
    log_rows = jnp.transpose(log_decay_now)
    step_dt = jax.nn.softplus(dt_pre_ref[...])
    scaled_x = ssm_x * dot_parts(step_dt, spread, 2)
    for part, piece in enumerate(stacked(scaled_x, False)):
        input_ref[part * rows : (part + 1) * rows, :] = piece
    carried = jnp.exp(log_decay_now) * jnp.where(starts_ref[...] < first_row, 1.0, 0.0)
    y_ref[...] = (
        matmul_pair(output_c, state, NT) * dot_parts(carried, spread, 2)
        + skip_ref[...] * ssm_x
    )
    affinity = matmul_pair(output_c, input_b, NT)
    closed = document_mask(first_row, starts_ref[...], rows, False)
    for pair in range(MHEADS // 2):
        found = []
        for head in (2 * pair, 2 * pair + 1):
            gap = log_decay_now[:, head : head + 1] - log_rows[head : head + 1, :] + closed
            mixing = affinity * jnp.exp(gap)
            found.append(
                jnp.dot(
                    jnp.concatenate(stacked(mixing, True), axis=1),
                    input_ref[:, head * MHEAD_DIM : (head + 1) * MHEAD_DIM],
                    preferred_element_type=jnp.float32,
                )
            )
        columns = slice(2 * pair * MHEAD_DIM, (2 * pair + 2) * MHEAD_DIM)
        y_ref[:, columns] += jnp.concatenate(found, axis=1)
    gate_now = gate_ref[...]
    gated = y_ref[...] * gate_now * jax.nn.sigmoid(gate_now)
    scale = lax.rsqrt(jnp.mean(gated * gated, axis=1, keepdims=True) + epsilon)
    normed_ref[...] = (gated * scale * gain_ref[...]).astype(jnp.bfloat16)


def mixer_output(pre, dt_pre, log_decay, states_in, gate_z, ssm_gain, skip_lanes, starts):
    rows = pre.shape[0]

    def kernel(*refs):
        mixer_output_body(*refs[:3], refs[3][...], *refs[4:])

    return pl.pallas_call(
        kernel,
        out_shape=mixer_output_shapes(rows),
        in_specs=[VMEM_SPEC] * 8,
        out_specs=[VMEM_SPEC] * 2,
        scratch_shapes=[pltpu.VMEM((3 * rows, SSM), jnp.bfloat16)],
        compiler_params=BIG_VMEM,
        name="mixer_output",
    )(
        pre,
        dt_pre,
        log_decay,
        states_in,
        gate_z,
        ssm_gain,
        skip_lanes,
        starts,
    )


def mixer_output_shapes(rows):
    return [
        jax.ShapeDtypeStruct((rows, SSM), jnp.bfloat16),
        jax.ShapeDtypeStruct((rows, SSM), jnp.float32),
    ]


def mixer_backward_body(
    grad_ref,
    y_ref,
    gate_ref,
    gain_ref,
    pre_ref,
    dt_pre_ref,
    log_ref,
    state_ref,
    skip_ref,
    starts_ref,
    starts_row_ref,
    grad_gate_ref,
    gain_grad_ref,
    grad_y_ref,
    state_grad_ref,
    input_grad_ref,
    b_grad_ref,
    c_grad_ref,
    log_grad_ref,
    skip_grad_ref,
    input_ref,
    low_ref,
    sums_ref,
    tick,
):
    rows = pre_ref.shape[0]
    first_row = lax.axis_index("seq") * rows
    gate_now = gate_ref[...]
    sigmoid_gate = jax.nn.sigmoid(gate_now)
    silu_gate = gate_now * sigmoid_gate
    y_now = y_ref[...]
    gated = y_now * silu_gate
    scale = lax.rsqrt(jnp.mean(gated * gated, axis=1, keepdims=True) + epsilon)
    grad_now = grad_ref[...]
    gain_grad_ref[...] = jnp.sum(gated * scale * grad_now, axis=0, keepdims=True)
    scaled = grad_now * gain_ref[...]
    grad_gated = scale * scaled - gated * (
        scale * scale * scale * jnp.mean(gated * scaled, axis=1, keepdims=True)
    )
    grad_gate_ref[...] = (
        grad_gated * y_now * sigmoid_gate * (1.0 + gate_now * (1.0 - sigmoid_gate))
    ).astype(jnp.bfloat16)
    grad_y = grad_gated * silu_gate
    grad_y_ref[...] = grad_y
    for part, piece in enumerate(stacked(grad_y, False)):
        low_ref[part * rows : (part + 1) * rows, :] = piece

    pre_now = pre_ref[...]
    conv_out = pre_now * jax.nn.sigmoid(pre_now)
    ssm_x = conv_out[:, :SSM]
    input_b = conv_out[:, SSM : SSM + STATE]
    output_c = conv_out[:, SSM + STATE :]
    spread = head_spread()
    log_decay_now = log_ref[...]
    log_rows = jnp.transpose(log_decay_now)
    step_dt = jax.nn.softplus(dt_pre_ref[...])
    scaled_x = ssm_x * dot_parts(step_dt, spread, 2)
    high, low, _ = stacked(scaled_x, True)
    input_ref[:rows, :] = high
    input_ref[rows:, :] = low
    carried = jnp.exp(log_decay_now) * jnp.where(starts_ref[...] < first_row, 1.0, 0.0)
    carried_lanes = dot_parts(carried, spread, 2)
    from_state = matmul_pair(output_c, state_ref[...], NT)
    log_grad = carried * dot_parts(grad_y * from_state, spread, 2, NT)
    grad_from_state = grad_y * carried_lanes
    state_grad_ref[...] = matmul_pair(grad_from_state, output_c, TN).reshape(state_grad_ref.shape)
    c_grad = matmul_pair(grad_from_state, state_ref[...], NN)
    skip_grad_ref[...] = dot_parts(
        jnp.sum(grad_y * ssm_x, axis=0, keepdims=True), spread, 3, NT
    )

    affinity = matmul_pair(input_b, output_c, NT)
    closed = document_mask(first_row, starts_row_ref[...], rows, True)
    affinity_grad = jnp.zeros((rows, rows), jnp.float32)
    sums_ref[...] = jnp.zeros(sums_ref.shape, jnp.float32)
    lane = lax.broadcasted_iota(jnp.int32, (rows, DT_PAD), 1)
    for pair in range(MHEADS // 2):
        found = []
        for head in (2 * pair, 2 * pair + 1):
            columns = slice(head * MHEAD_DIM, (head + 1) * MHEAD_DIM)
            gap = log_rows[head : head + 1, :] - log_decay_now[:, head : head + 1] + closed
            decay = jnp.exp(gap)
            mixing = affinity * decay
            found.append(
                jnp.dot(
                    jnp.concatenate(stacked(mixing, True), axis=1),
                    low_ref[:, columns],
                    preferred_element_type=jnp.float32,
                )
            )
            grad_mixing = jnp.zeros((rows, rows), jnp.float32)
            for one, two in ((0, 0), (1, 0), (0, 2)):
                grad_mixing = grad_mixing + lax.dot_general(
                    input_ref[one * rows : (one + 1) * rows, columns],
                    low_ref[two * rows : (two + 1) * rows, columns],
                    (NT, ((), ())),
                    preferred_element_type=jnp.float32,
                )
            affinity_grad = affinity_grad + grad_mixing * decay
            both = grad_mixing * mixing
            sums_ref[head : head + 1, :] = jnp.sum(both, axis=0, keepdims=True)
            log_grad = log_grad - jnp.where(
                lane == head, jnp.sum(both, axis=1, keepdims=True), 0.0
            )
        columns = slice(2 * pair * MHEAD_DIM, (2 * pair + 2) * MHEAD_DIM)
        input_grad_ref[:, columns] = jnp.concatenate(found, axis=1)
        if pair % 3 == 2:
            tick()
    log_grad_ref[...] = log_grad + jnp.transpose(sums_ref[...])
    b_grad_ref[...] = matmul_pair(affinity_grad, output_c, NN)
    c_grad_ref[...] = c_grad + matmul_pair(jnp.transpose(affinity_grad), input_b, NN)


def mixer_backward_shapes(rows, state_shape):
    f32 = jnp.float32
    shape = jax.ShapeDtypeStruct
    return [
        shape((rows, SSM), jnp.bfloat16),
        shape((1, SSM), f32),
        shape((rows, SSM), f32),
        shape(state_shape, f32),
        shape((rows, SSM), f32),
        shape((rows, STATE), f32),
        shape((rows, STATE), f32),
        shape((rows, DT_PAD), f32),
        shape((1, DT_PAD), f32),
    ]


def mixer_backward_scratch(rows):
    return [
        pltpu.VMEM((2 * rows, SSM), jnp.bfloat16),
        pltpu.VMEM((3 * rows, SSM), jnp.bfloat16),
        pltpu.VMEM((DT_PAD, rows), jnp.float32),
    ]


def mixer_backward(args):
    rows = args[0].shape[0]

    def kernel(*refs):
        mixer_backward_body(*refs, lambda: None)

    return pl.pallas_call(
        kernel,
        out_shape=mixer_backward_shapes(rows, (SSM, STATE)),
        in_specs=[VMEM_SPEC] * 11,
        out_specs=[VMEM_SPEC] * 9,
        scratch_shapes=mixer_backward_scratch(rows),
        compiler_params=BIG_VMEM,
        name="mixer_backward",
    )(*args)


def mixer_input_backward(
    grad_end,
    states_in,
    passing,
    grad_y,
    input_grad,
    b_grad,
    c_grad,
    log_grad,
    pre,
    dt_pre,
    log_decay,
    ext,
    conv_weight,
    a_log,
    skip_lanes,
    starts,
):
    rows = pre.shape[0]
    first_row = (lax.axis_index("seq") * rows).astype(jnp.int32).reshape(1)

    def kernel(
        first_ref,
        end_ref,
        state_ref,
        passing_ref,
        grad_y_ref,
        input_grad_ref,
        b_grad_ref,
        c_grad_ref,
        log_grad_ref,
        pre_ref,
        dt_pre_ref,
        log_ref,
        ext_ref,
        tap_ref,
        a_log_ref,
        skip_ref,
        starts_ref,
        raw_grad_ref,
        tap_grad_ref,
        bias_grad_ref,
        dt_grad_ref,
        dt_sum_ref,
        a_log_grad_ref,
        ext_f32,
        sum_ref,
    ):
        pre_now = pre_ref[...]
        sigmoid_pre = jax.nn.sigmoid(pre_now)
        conv_out = pre_now * sigmoid_pre
        ssm_x = conv_out[:, :SSM]
        input_b = conv_out[:, SSM : SSM + STATE]
        spread = head_spread()
        log_decay_now = log_ref[...]
        dt_pre_now = dt_pre_ref[...]
        step_dt = jax.nn.softplus(dt_pre_now)
        step_lanes = dot_parts(step_dt, spread, 2)
        starts_now = starts_ref[...]
        row = lax.broadcasted_iota(jnp.int32, (rows, 1), 0)
        places = first_ref[0] + row
        last = log_decay_now[rows - 1 : rows, :]
        last_start = starts_ref[rows - 1 : rows, :]
        weight = jnp.exp(jnp.where(places >= last_start, last - log_decay_now, masked))
        weight_lanes = dot_parts(weight, spread, 2)
        weighted = ssm_x * step_lanes * weight_lanes
        grad_weighted = matmul_pair(input_b, end_ref[...], NT)
        b_total = b_grad_ref[...] + matmul_pair(weighted, end_ref[...], NN)
        input_total = input_grad_ref[...] + grad_weighted * weight_lanes
        weight_term = dot_parts(grad_weighted * weighted, spread, 3, NT)
        state_dot = end_ref[...] * state_ref[...]
        passing_grad = jnp.sum(
            jnp.transpose(dot_left(spread, state_dot, 3)), axis=0, keepdims=True
        )
        log_grad_now = log_grad_ref[...] - weight_term
        end_term = jnp.sum(weight_term, axis=0, keepdims=True) + passing_grad * passing_ref[0:1, :]
        log_grad_now = log_grad_now + jnp.where(row == rows - 1, end_term, 0.0)
        order = lax.broadcasted_iota(jnp.int32, (rows, rows), 0)
        other = lax.broadcasted_iota(jnp.int32, (rows, rows), 1)
        upper = jnp.where(other >= order, 1.0, 0.0).astype(jnp.bfloat16)
        step_grad = dot_left(upper, log_grad_now, 3)
        rate = jnp.exp(a_log_ref[...])
        a_log_grad_ref[...] = jnp.sum(-step_dt * rate * step_grad, axis=0, keepdims=True)
        dt_grad = dot_parts(input_total * ssm_x, spread, 3, NT) - rate * step_grad
        dt_raw_grad = dt_grad * jax.nn.sigmoid(dt_pre_now)
        valid = lax.broadcasted_iota(jnp.int32, (rows, DT_PAD), 1) < MHEADS
        dt_raw_grad = jnp.where(valid, dt_raw_grad, 0.0)
        dt_grad_ref[...] = dt_raw_grad.astype(jnp.bfloat16)
        dt_sum_ref[...] = jnp.sum(dt_raw_grad, axis=0, keepdims=True)
        x_grad = input_total * step_lanes + skip_ref[...] * grad_y_ref[...]
        slope = sigmoid_pre * (1.0 + pre_now * (1.0 - sigmoid_pre))
        pre_grad = jnp.concatenate([x_grad, b_total, c_grad_ref[...]], axis=1) * slope
        bias_grad_ref[...] = jnp.sum(pre_grad, axis=0, keepdims=True)
        ext_f32[...] = ext_ref[...].astype(jnp.float32)
        sum_ref[...] = jnp.zeros(sum_ref.shape, jnp.float32)
        for tap in range(CONV):
            lag = CONV - 1 - tap
            kept = pre_grad * jnp.where(places - lag >= starts_now, 1.0, 0.0)
            window = slice(HALO - lag, HALO - lag + rows)
            tap_grad_ref[tap : tap + 1, :] = jnp.sum(
                kept * ext_f32[window, :], axis=0, keepdims=True
            )
            sum_ref[window, :] += kept * tap_ref[tap : tap + 1, :]
        raw_grad_ref[...] = sum_ref[...]

    f32 = jnp.float32
    shape = jax.ShapeDtypeStruct
    return pl.pallas_call(
        kernel,
        out_shape=(
            shape((HALO + rows, XBC), f32),
            shape((CONV, XBC), f32),
            shape((1, XBC), f32),
            shape((rows, DT_PAD), jnp.bfloat16),
            shape((1, DT_PAD), f32),
            shape((1, DT_PAD), f32),
        ),
        in_specs=[pl.BlockSpec(memory_space=pltpu.SMEM)] + [VMEM_SPEC] * 16,
        out_specs=[VMEM_SPEC] * 6,
        scratch_shapes=[
            pltpu.VMEM((HALO + rows, XBC), f32),
            pltpu.VMEM((HALO + rows, XBC), f32),
        ],
        compiler_params=BIG_VMEM,
        name="mixer_input_backward",
    )(
        first_row,
        grad_end,
        states_in,
        passing,
        grad_y,
        input_grad,
        b_grad,
        c_grad,
        log_grad,
        pre,
        dt_pre,
        log_decay,
        ext,
        conv_weight,
        a_log,
        skip_lanes,
        starts[:, None],
    )


def feed_forward(hidden, normed_ssm, attention, ffn_gain, cotangent, late):
    rows, model = hidden.shape
    f32, low = jnp.float32, jnp.bfloat16
    ffn = late[0].shape[1]
    span = 1024
    steps = ffn // span

    def layout(flat, gate_up, down, ssm, out):
        pairs = [(flat[3], ssm), (flat[4], out)]
        for number in range(2):
            for start in range(0, ffn, span):
                pairs.append(
                    (
                        flat[number].at[:, pl.ds(start, span)],
                        gate_up.at[:, pl.ds(number * ffn + start, span)],
                    )
                )
        return pairs + [(flat[2], down)]

    kinds = len(late)
    early = 2
    total = early + 2 * steps + 1

    def kernel(*refs):
        hidden_ref, ssm_ref, attn_ref, gain_ref, cot_ref = refs[:5]
        flats = refs[5 : 5 + kinds]
        refs = refs[5 + kinds :]
        layer_ref, mix_ref, attn_grad_ref, ssm_grad_ref, gain_grad_ref = refs[:5]
        grad_flats = refs[5 : 5 + kinds]
        refs = refs[5 + kinds :]
        weights, grads = refs[:4], refs[4:8]
        gate_ref, up_ref, act_ref, two_ref, after_ref, grad_two_ref, in_sem, out_sem = refs[8:]
        w_gate_up, w_down, w_ssm, w_o = weights
        g_gate_up, g_down, g_ssm, g_o = grads
        loads = [
            pltpu.make_async_copy(source, target, in_sem.at[i])
            for i, (source, target) in enumerate(layout(flats, w_gate_up, w_down, w_ssm, w_o))
        ]
        for copy in loads:
            copy.start()
        stores = [
            pltpu.make_async_copy(source, target, out_sem.at[i])
            for i, (target, source) in enumerate(
                layout(grad_flats, g_gate_up, g_down, g_ssm, g_o)
            )
        ]

        def whole(ref, start=0, width=None):
            return ref[:, start : start + (ref.shape[1] if width is None else width)]

        def product(left_side, right_side, axes):
            return lax.dot_general(
                left_side, right_side, (axes, ((), ())), preferred_element_type=f32
            )

        def keep(ref, value, start=0):
            ref[:, start : start + value.shape[1]] = value.astype(low)

        for copy in loads[:early]:
            copy.wait()
        after = (
            hidden_ref[...].astype(f32)
            + product(ssm_ref[...], whole(w_ssm), NN)
            + product(attn_ref[...], whole(w_o), NN)
        )
        after_ref[...] = after
        scale = lax.rsqrt(jnp.mean(after * after, axis=1, keepdims=True) + epsilon)
        two_ref[...] = (after * scale * gain_ref[...]).astype(low)
        for step in range(steps):
            columns = slice(step * span, (step + 1) * span)
            loads[early + step].wait()
            loads[early + steps + step].wait()
            gate = product(two_ref[...], whole(w_gate_up, step * span, span), NN)
            up = product(two_ref[...], whole(w_gate_up, ffn + step * span, span), NN)
            gate_ref[:, columns] = gate
            up_ref[:, columns] = up
            act_ref[:, columns] = (gate * jax.nn.sigmoid(gate) * up).astype(low)
        for copy in loads[early + 2 * steps :]:
            copy.wait()
        layer_ref[...] = (after_ref[...] + product(act_ref[...], whole(w_down), NN)).astype(low)
        cot = cot_ref[...]
        grad_two = jnp.zeros((rows, model), f32)
        for step in range(steps):
            columns = slice(step * span, (step + 1) * span)
            w_part = w_down[columns, :]
            grad_act = product(cot, w_part, NT)
            gate, up = gate_ref[:, columns], up_ref[:, columns]
            sigmoid_gate = jax.nn.sigmoid(gate)
            grad_gate = (
                grad_act * up * sigmoid_gate * (1.0 + gate * (1.0 - sigmoid_gate))
            ).astype(low)
            grad_up = (grad_act * gate * sigmoid_gate).astype(low)
            grad_two = grad_two + product(
                grad_gate, whole(w_gate_up, step * span, span), NT
            )
            grad_two = grad_two + product(
                grad_up, whole(w_gate_up, ffn + step * span, span), NT
            )
            keep(g_gate_up, product(two_ref[...], grad_gate, TN), step * span)
            stores[early + step].start()
            keep(g_gate_up, product(two_ref[...], grad_up, TN), ffn + step * span)
            stores[early + steps + step].start()
        grad_two_ref[...] = grad_two
        keep(g_down, product(act_ref[...], cot, TN))
        for copy in stores[early + 2 * steps :]:
            copy.start()
        after = after_ref[...]
        grad_two = grad_two_ref[...]
        scale = lax.rsqrt(jnp.mean(after * after, axis=1, keepdims=True) + epsilon)
        gain_grad_ref[...] = jnp.sum(after * scale * grad_two, axis=0, keepdims=True)
        scaled = grad_two * gain_ref[...]
        mix = (
            cot.astype(f32)
            + scale * scaled
            - after * (scale * scale * scale * jnp.mean(after * scaled, axis=1, keepdims=True))
        )
        mix_ref[...] = mix
        mix_low = mix.astype(low)
        attn_grad = product(mix_low, whole(w_o), NT).astype(low)
        group_size = QHEADS // KVHEADS
        for head in range(QHEADS):
            place = head % group_size * rows
            attn_grad_ref[head // group_size, place : place + rows, :] = attn_grad[
                :, head * HEAD_DIM : (head + 1) * HEAD_DIM
            ]
        ssm_grad_ref[...] = product(mix_low, whole(w_ssm), NT)
        keep(g_ssm, product(ssm_ref[...], mix_low, TN))
        keep(g_o, product(attn_ref[...], mix_low, TN))
        for copy in stores[:early]:
            copy.start()
        for copy in stores:
            copy.wait()

    shape = jax.ShapeDtypeStruct
    hbm = pl.BlockSpec(memory_space=pl.ANY)
    buffers = [(late[0].shape[0], 2 * ffn)] + [w.shape for w in late[2:]]
    outs = pl.pallas_call(
        kernel,
        out_shape=[
            shape((rows, model), low),
            shape((rows, model), f32),
            shape((KVHEADS, QHEADS // KVHEADS * rows, HEAD_DIM), low),
            shape((rows, SSM), f32),
            shape((1, model), f32),
        ]
        + [shape(w.shape, low) for w in late],
        in_specs=[VMEM_SPEC] * 5 + [hbm] * kinds,
        out_specs=[VMEM_SPEC] * 5 + [hbm] * kinds,
        scratch_shapes=[pltpu.VMEM(size, low) for size in buffers + buffers]
        + [
            pltpu.VMEM((rows, ffn), f32),
            pltpu.VMEM((rows, ffn), f32),
            pltpu.VMEM((rows, ffn), low),
            pltpu.VMEM((rows, model), low),
            pltpu.VMEM((rows, model), f32),
            pltpu.VMEM((rows, model), f32),
            pltpu.SemaphoreType.DMA((total,)),
            pltpu.SemaphoreType.DMA((total,)),
        ],
        compiler_params=BIG_VMEM,
        name="feed_forward",
    )(hidden, normed_ssm, attention, ffn_gain[None], cotangent, *late)
    return outs[:5], outs[5:]


def projection_backward(
    normed_one,
    hidden,
    norm_gain,
    grad_mix,
    grad_gate_z,
    grad_ext,
    returned,
    grad_dt,
    grad_query,
    grad_kv,
    tables,
    weights,
):
    rows, model = hidden.shape
    f32, low = jnp.float32, jnp.bfloat16
    groups = QHEADS // KVHEADS
    half_kv = KVW // 2
    first_row = (lax.axis_index("seq") * rows).astype(jnp.int32).reshape(1)
    widths = [w.shape[1] for w in weights]

    def kernel(
        first_ref,
        normed_ref,
        hidden_ref,
        gain_ref,
        mix_ref,
        gate_ref,
        ext_ref,
        returned_ref,
        dt_ref,
        query_ref,
        kv_ref,
        base_cos_ref,
        base_sin_ref,
        far_cos_ref,
        far_sin_ref,
        *refs,
    ):
        weight_hbm, refs = refs[:3], refs[3:]
        input_ref, gain_grad_ref, refs = refs[0], refs[1], refs[2:]
        weight_grad_hbm, refs = refs[:3], refs[3:]
        weight_refs, weight_grad_refs, refs = refs[:3], refs[3:6], refs[6:]
        xbc_ref, small_ref, turned_ref, in_sem, out_sem = refs
        loads = [
            pltpu.make_async_copy(source, target, in_sem.at[i])
            for i, (source, target) in enumerate(zip(weight_hbm, weight_refs))
        ]
        for copy in loads:
            copy.start()
        stores = [
            pltpu.make_async_copy(source, target, out_sem.at[i])
            for i, (source, target) in enumerate(zip(weight_grad_refs, weight_grad_hbm))
        ]
        edge = rows - HALO
        xbc_ref[:edge, :] = ext_ref[HALO : HALO + edge, :].astype(low)
        xbc_ref[edge:, :] = (ext_ref[HALO + edge :, :] + returned_ref[...]).astype(low)
        for head in range(QHEADS):
            place = head % groups * rows
            turned_ref[:, head * HEAD_DIM : (head + 1) * HEAD_DIM] = jnp.transpose(
                query_ref[head // groups, :, place : place + rows]
            )
        cosine_all, sine_all = rope_now(
            first_ref[0] // rows, base_cos_ref, base_sin_ref, far_cos_ref, far_sin_ref
        )
        sine_all = -sine_all
        small_ref[:, :QW] = rope_lanes(
            turned_ref[...] * HEAD_DIM ** (-0.5), cosine_all, sine_all
        ).astype(low)
        kv = kv_ref[...]
        small_ref[:, QW : QW + half_kv] = rope_lanes(kv[:, :half_kv], cosine_all, sine_all).astype(
            low
        )
        small_ref[:, QW + half_kv : QW + KVW] = kv[:, half_kv:].astype(low)
        small_ref[:, QW + KVW :] = dt_ref[...]
        normed = normed_ref[...]
        grad_normed = jnp.zeros((rows, model), f32)
        for number, value_ref in enumerate((gate_ref, xbc_ref, small_ref)):
            loads[number].wait()
            for start in range(0, widths[number], 512):
                columns = slice(start, min(start + 512, widths[number]))
                part = value_ref[:, columns]
                grad_normed = grad_normed + lax.dot_general(
                    part,
                    weight_refs[number][:, columns],
                    (NT, ((), ())),
                    preferred_element_type=f32,
                )
                weight_grad_refs[number][:, columns] = lax.dot_general(
                    normed, part, (TN, ((), ())), preferred_element_type=f32
                ).astype(low)
            stores[number].start()
        values = hidden_ref[...].astype(f32)
        scale = lax.rsqrt(jnp.mean(values * values, axis=1, keepdims=True) + epsilon)
        gain_grad_ref[...] = jnp.sum(values * scale * grad_normed, axis=0, keepdims=True)
        scaled = grad_normed * gain_ref[...]
        input_ref[...] = (
            mix_ref[...]
            + scale * scaled
            - values * (scale * scale * scale * jnp.mean(values * scaled, axis=1, keepdims=True))
        ).astype(low)
        for copy in stores:
            copy.wait()

    shape = jax.ShapeDtypeStruct
    hbm = pl.BlockSpec(memory_space=pl.ANY)
    return pl.pallas_call(
        kernel,
        out_shape=[shape((rows, model), low), shape((1, model), f32)]
        + [shape(w.shape, low) for w in weights],
        in_specs=[pl.BlockSpec(memory_space=pltpu.SMEM)] + [VMEM_SPEC] * 14 + [hbm] * 3,
        out_specs=[VMEM_SPEC] * 2 + [hbm] * 3,
        scratch_shapes=[pltpu.VMEM(w.shape, low) for w in list(weights) * 2]
        + [
            pltpu.VMEM((rows, XBC), low),
            pltpu.VMEM((rows, QW + KVW + DT_PAD), low),
            pltpu.VMEM((rows, QW), f32),
            pltpu.SemaphoreType.DMA((3,)),
            pltpu.SemaphoreType.DMA((3,)),
        ],
        compiler_params=BIG_VMEM,
        name="projection_backward",
    )(
        first_row,
        normed_one,
        hidden,
        norm_gain[None],
        grad_mix,
        grad_gate_z,
        grad_ext,
        returned,
        grad_dt,
        grad_query,
        grad_kv,
        *tables,
        *weights,
    )


def projection_scatter(
    normed_one,
    hidden,
    norm_gain,
    grad_mix,
    grad_gate_z,
    grad_ext,
    grad_dt,
    grad_query,
    grad_kv,
    tables,
    weights,
    small,
    collective_id,
    target,
):
    rows, model = hidden.shape
    f32, low = jnp.float32, jnp.bfloat16
    groups = QHEADS // KVHEADS
    half_kv = KVW // 2
    first_row = (lax.axis_index("seq") * rows).astype(jnp.int32).reshape(1)
    widths = [w.shape[1] for w in weights]
    count = lax.axis_size("seq")
    sizes = lattice(count)
    shapes = [(w.shape[0] // count, w.shape[1]) for w in weights]
    plans = [
        scatter_plan([s], small if number == 1 else None, target)
        for number, s in enumerate(shapes)
    ]

    def kernel(
        first_ref,
        normed_ref,
        hidden_ref,
        gain_ref,
        mix_ref,
        gate_ref,
        ext_ref,
        dt_ref,
        query_ref,
        kv_ref,
        base_cos_ref,
        base_sin_ref,
        far_cos_ref,
        far_sin_ref,
        *refs,
    ):
        small_in, refs = refs[0], refs[1:]
        weight_hbm, refs = refs[:3], refs[3:]
        input_ref, shard_refs, small_out, refs = refs[0], refs[1:4], refs[4], refs[5:]
        weight_refs, weight_grad_refs, refs = refs[:3], refs[3:6], refs[6:]
        xbc_ref, small_ref, turned_ref, returned_ref, small_vmem, in_sem, edge_sems = refs[:7]
        refs = refs[7:]
        runs = []
        for number, (program, scratch) in enumerate(plans):
            mine, refs = refs[: len(scratch)], refs[len(scratch) :]
            has_small = number == 1
            runs.append(
                program(
                    [weight_grad_refs[number]],
                    [small_vmem] if has_small else [],
                    [shard_refs[number]],
                    [small_out] if has_small else [],
                    mine,
                )
            )
        me = lax.axis_index("seq")
        following, previous = lax.rem(me + 1, count), lax.rem(me + count - 1, count)
        loads = [
            pltpu.make_async_copy(source, target, in_sem.at[i])
            for i, (source, target) in enumerate(zip(weight_hbm, weight_refs))
        ]
        for copy in loads:
            copy.start()
        greet(sizes, coordinates(sizes), [following, previous])
        edge_copy = pltpu.make_async_remote_copy(
            src_ref=ext_ref.at[pl.ds(0, HALO), :],
            dst_ref=returned_ref,
            send_sem=edge_sems.at[0],
            recv_sem=edge_sems.at[1],
            device_id=(previous,),
            device_id_type=MESH,
        )
        edge_copy.start()
        small_vmem[...] = small_in[...]
        edge = rows - HALO
        xbc_ref[:edge, :] = ext_ref[HALO : HALO + edge, :].astype(low)
        for head in range(QHEADS):
            place = head % groups * rows
            turned_ref[:, head * HEAD_DIM : (head + 1) * HEAD_DIM] = jnp.transpose(
                query_ref[head // groups, :, place : place + rows]
            )
        cosine_all, sine_all = rope_now(
            first_ref[0] // rows, base_cos_ref, base_sin_ref, far_cos_ref, far_sin_ref
        )
        sine_all = -sine_all
        small_ref[:, :QW] = rope_lanes(
            turned_ref[...] * HEAD_DIM ** (-0.5), cosine_all, sine_all
        ).astype(low)
        kv = kv_ref[...]
        small_ref[:, QW : QW + half_kv] = rope_lanes(kv[:, :half_kv], cosine_all, sine_all).astype(
            low
        )
        small_ref[:, QW + half_kv : QW + KVW] = kv[:, half_kv:].astype(low)
        small_ref[:, QW + KVW :] = dt_ref[...]
        normed = normed_ref[...]
        grad_normed = jnp.zeros((rows, model), f32)
        for number, value_ref in ((0, gate_ref), (2, small_ref), (1, xbc_ref)):
            loads[number].wait()
            if number == 1:
                edge_copy.wait()
                xbc_ref[edge:, :] = (ext_ref[HALO + edge :, :] + returned_ref[...]).astype(low)
            for start in range(0, widths[number], 512):
                columns = slice(start, min(start + 512, widths[number]))
                part = value_ref[:, columns]
                weight_grad_refs[number][..., columns] = (
                    lax.dot_general(normed, part, (TN, ((), ())), preferred_element_type=f32)
                    .astype(low)
                    .reshape(*sizes, shapes[number][0], part.shape[1])
                )
            next(runs[number])
            for start in range(0, widths[number], 512):
                columns = slice(start, min(start + 512, widths[number]))
                grad_normed = grad_normed + lax.dot_general(
                    value_ref[:, columns],
                    weight_refs[number][:, columns],
                    (NT, ((), ())),
                    preferred_element_type=f32,
                )
            if number != 1:
                next(runs[number])
        values = hidden_ref[...].astype(f32)
        scale = lax.rsqrt(jnp.mean(values * values, axis=1, keepdims=True) + epsilon)
        gain_grad = jnp.sum(values * scale * grad_normed, axis=0, keepdims=True)
        for step in range(model // 128):
            small_vmem[step : step + 1, :] = gain_grad[:, step * 128 : (step + 1) * 128]
        scaled = grad_normed * gain_ref[...]
        input_ref[...] = (
            mix_ref[...]
            + scale * scaled
            - values * (scale * scale * scale * jnp.mean(values * scaled, axis=1, keepdims=True))
        ).astype(low)
        run_together([runs[1], runs[0], runs[2]])

    shape = jax.ShapeDtypeStruct
    hbm = pl.BlockSpec(memory_space=pl.ANY)
    return pl.pallas_call(
        kernel,
        out_shape=[shape((rows, model), low)]
        + [shape(s, f32) for s in shapes]
        + [shape(small.shape, f32)],
        in_specs=[pl.BlockSpec(memory_space=pltpu.SMEM)] + [VMEM_SPEC] * 14 + [hbm] * 3,
        out_specs=[VMEM_SPEC] * 5,
        scratch_shapes=[pltpu.VMEM(w.shape, low) for w in weights]
        + [pltpu.VMEM(sizes + s, low) for s in shapes]
        + [
            pltpu.VMEM((rows, XBC), low),
            pltpu.VMEM((rows, QW + KVW + DT_PAD), low),
            pltpu.VMEM((rows, QW), f32),
            pltpu.VMEM((HALO, XBC), f32),
            pltpu.VMEM(small.shape, f32),
            pltpu.SemaphoreType.DMA((3,)),
            pltpu.SemaphoreType.DMA((2,)),
        ]
        + [item for _, scratch in plans for item in scratch],
        compiler_params=pltpu.CompilerParams(
            collective_id=collective_id,
            has_side_effects=True,
            vmem_limit_bytes=62 * 1024 * 1024,
        ),
        name="projection_scatter",
    )(
        first_row,
        normed_one,
        hidden,
        norm_gain[None],
        grad_mix,
        grad_gate_z,
        grad_ext,
        grad_dt,
        grad_query,
        grad_kv,
        *tables,
        small,
        *weights,
    )


def finish(shard_z, shard_xbc, shard_small, small_sum, late_sums, lengths):
    f32 = jnp.float32
    shape = jax.ShapeDtypeStruct
    rows = shard_z.shape[0]
    starts = [sum(lengths[:i]) // 128 for i in range(len(lengths))]
    tail = sum(lengths) // 128
    tap_rows = XBC // 128
    model_rows, ssm_rows = lengths[0] // 128, lengths[1] // 128

    def kernel(z_ref, xbc_ref, small_ref, sum_ref, *refs):
        late, refs = refs[: len(late_sums)], refs[len(late_sums) :]
        outs, refs = refs[: len(late_sums)], refs[len(late_sums) :]
        for source, target in zip(late, outs):
            target[...] = source[...]
        z_out, xbc_out, q_out, kv_out, dt_out, *vectors, tap_out, three_out = refs
        z_out[...] = z_ref[...]
        xbc_out[...] = xbc_ref[...]
        q_out[...] = small_ref[:, :QW]
        kv_out[...] = small_ref[:, QW : QW + KVW]
        dt_out[...] = small_ref[:, QW + KVW :]
        for target, start in zip(vectors, (starts[0], starts[1], starts[2], starts[4])):
            target[...] = sum_ref[start : start + target.shape[0], :]
        for tap in range(CONV):
            for step in range(tap_rows):
                row = starts[3] + tap * tap_rows + step
                tap_out[tap : tap + 1, step * 128 : (step + 1) * 128] = sum_ref[row : row + 1, :]
        three_out[...] = sum_ref[tail : tail + 8, :]

    results = pl.pallas_call(
        kernel,
        out_shape=[shape(s.shape, f32) for s in late_sums]
        + [shape(shard_z.shape, f32), shape(shard_xbc.shape, f32)]
        + [shape((rows, width), f32) for width in (QW, KVW, DT_PAD)]
        + [shape((n, 128), f32) for n in (model_rows, ssm_rows, model_rows, tap_rows)]
        + [shape((CONV, XBC), f32), shape((8, 128), f32)],
        in_specs=[VMEM_SPEC] * (4 + len(late_sums)),
        out_specs=[VMEM_SPEC] * (11 + len(late_sums)),
        name="finish",
    )(shard_z, shard_xbc, shard_small, small_sum, *late_sums)
    return results[: len(late_sums)], results[len(late_sums) :]


def per_device(
    hidden_in,
    doc_start,
    norm_gain,
    w_z,
    w_xbc,
    w_dt,
    conv_weight,
    conv_bias,
    dt_bias,
    a_log,
    d_skip,
    ssm_gain,
    w_ssm_out,
    w_q,
    w_kv,
    w_o,
    ffn_gain,
    w_gate,
    w_up,
    w_down,
    cotangent,
):
    local_rows, model = hidden_in.shape
    count = lax.axis_size("seq")
    group_size = QHEADS // KVHEADS
    small_shard = jnp.concatenate(
        [w_q, w_kv, jnp.pad(w_dt, ((0, 0), (0, DT_PAD - MHEADS)))], axis=1
    )
    *mixer_weights, halo = gather_everywhere(
        [w_xbc, small_shard, w_z], 0, 8192, hidden_in
    )
    mixer_weights = [mixer_weights[2], mixer_weights[0], mixer_weights[1]]

    tables = rope_table(local_rows, count)
    dt_bias_row = jnp.pad(dt_bias, (0, DT_PAD - MHEADS))[None]
    a_log_row = jnp.pad(a_log, (0, DT_PAD - MHEADS))[None]
    skip_lanes = jnp.repeat(d_skip, MHEAD_DIM)[None]
    (
        normed_one,
        gate_z,
        xbc_ext,
        conv_pre,
        grouped_q,
        kv_local,
        dt_pre,
        log_decay,
        local_state,
        passing,
    ) = mixer_forward(
        hidden_in,
        halo,
        norm_gain,
        mixer_weights,
        conv_weight,
        conv_bias,
        dt_bias_row,
        a_log_row,
        doc_start,
        tables,
    )
    row_starts = jnp.tile(doc_start, group_size)[None]
    kv_all, states_in, chip_decay, late, computed = front(
        kv_local,
        local_state,
        passing,
        [w_gate, w_up, w_down, w_ssm_out, w_o],
        [conv_pre, dt_pre, log_decay, gate_z, ssm_gain[None], skip_lanes, doc_start[:, None]],
        [grouped_q, row_starts],
        1,
        (16384, 16384),
    )
    normed_ssm, ssm_y, attn_grouped, log_total, attn_low = computed
    (layer_out, grad_mix, grad_attn_grouped, grad_normed_ssm, grad_ffn_gain), late_grads = (
        feed_forward(hidden_in, normed_ssm, attn_low, ffn_gain, cotangent, late)
    )
    key_terms, grad_query_grouped, late_sums = attention_backward(
        grouped_q,
        grad_attn_grouped,
        kv_all,
        row_starts,
        log_total,
        attn_grouped,
        late_grads[:2],
        4,
        16384,
    )
    shard_gate, shard_up = late_sums

    grad_kv_local, grad_end, late_sums, mixer_out = back(
        key_terms,
        [
            grad_normed_ssm,
            ssm_y,
            gate_z,
            ssm_gain[None],
            conv_pre,
            dt_pre,
            log_decay,
            states_in,
            skip_lanes,
            doc_start[:, None],
            doc_start[None],
        ],
        passing,
        chip_decay,
        late_grads[2:],
        2,
        (8192, 8192),
    )
    shard_down, shard_ssm_out, shard_o = late_sums
    (
        grad_gate_z,
        grad_ssm_gain,
        grad_ssm_y,
        _,
        grad_input_part,
        grad_b_part,
        grad_c,
        grad_log_part,
        grad_d_skip,
    ) = mixer_out
    grad_ext, grad_conv_weight, grad_conv_bias, grad_dt_raw, grad_dt_bias, grad_a_log = (
        mixer_input_backward(
            grad_end,
            states_in,
            passing,
            grad_ssm_y,
            grad_input_part,
            grad_b_part,
            grad_c,
            grad_log_part,
            conv_pre,
            dt_pre,
            log_decay,
            xbc_ext,
            conv_weight,
            a_log_row,
            skip_lanes,
            doc_start,
        )
    )
    rows_small = -(-(model // 128 * 2 + SSM // 128 + (CONV + 1) * XBC // 128 + 8) // 8) * 8
    lengths = [model, SSM, model, CONV * XBC, XBC]
    three = jnp.concatenate(
        [grad_dt_bias[:, :128], grad_a_log[:, :128], grad_d_skip[:, :128]], axis=0
    )
    small = jnp.concatenate(
        [
            jnp.zeros((model // 128, 128), jnp.float32),
            grad_ssm_gain.reshape(-1, 128),
            grad_ffn_gain.reshape(-1, 128),
            grad_conv_weight.reshape(-1, 128),
            grad_conv_bias.reshape(-1, 128),
            three,
        ],
        axis=0,
    )
    small = jnp.pad(small, ((0, rows_small - small.shape[0]), (0, 0)))
    grad_args = (
        normed_one,
        hidden_in,
        norm_gain,
        grad_mix,
        grad_gate_z,
        grad_ext,
    )
    last_args = (grad_dt_raw, grad_query_grouped, grad_kv_local, tables, mixer_weights)
    if w_gate.shape[0] % 16 == 0:
        grad_input, shard_z, shard_xbc, shard_small, small_sum = projection_scatter(
            *grad_args, *last_args, small, 3, 8192
        )
    else:
        returned = from_behind(grad_ext[:HALO], "seq", -1)
        grad_input, grad_norm_gain, *mixer_grads = projection_backward(
            *grad_args, returned, *last_args
        )
        small = small.at[: model // 128].set(grad_norm_gain.reshape(-1, 128))
        shard_z, shard_xbc, shard_small, small_sum = scatter_sums(mixer_grads, small, 3, 8192)
    late_shards, others = finish(
        shard_z,
        shard_xbc,
        shard_small,
        small_sum,
        [shard_gate, shard_up, shard_down, shard_ssm_out, shard_o],
        lengths,
    )
    shard_gate, shard_up, shard_down, shard_ssm_out, shard_o = late_shards
    shard_z, shard_xbc, shard_q, shard_kv, shard_dt, *vectors, sum_taps, sum_three = others
    sum_norm, sum_ssm_gain, sum_ffn_gain, sum_conv_bias = [v.reshape(-1) for v in vectors]
    return (
        layer_out,
        grad_input,
        sum_norm,
        shard_z,
        shard_xbc,
        shard_dt[:, :MHEADS],
        sum_taps,
        sum_conv_bias,
        sum_three[0, :MHEADS],
        sum_three[1, :MHEADS],
        sum_three[2, :MHEADS],
        sum_ssm_gain,
        shard_ssm_out,
        shard_q,
        shard_kv,
        shard_o,
        sum_ffn_gain,
        shard_gate,
        shard_up,
        shard_down,
    )


def solution(mesh):
    placed = (
        P("seq", None),
        P("seq"),
        P(),
        P("seq", None),
        P("seq", None),
        P("seq", None),
        P(),
        P(),
        P(),
        P(),
        P(),
        P(),
        P("seq", None),
        P("seq", None),
        P("seq", None),
        P("seq", None),
        P(),
        P("seq", None),
        P("seq", None),
        P("seq", None),
        P("seq", None),
    )
    return jax.shard_map(
        per_device,
        mesh=mesh,
        in_specs=placed,
        out_specs=(
            P("seq", None),
            P("seq", None),
            P(),
            P("seq", None),
            P("seq", None),
            P("seq", None),
            P(),
            P(),
            P(),
            P(),
            P(),
            P(),
            P("seq", None),
            P("seq", None),
            P("seq", None),
            P("seq", None),
            P(),
            P("seq", None),
            P("seq", None),
            P("seq", None),
        ),
        check_vma=False,
    )
```

```python
from functools import partial
import math

import jax
import jax.numpy as jnp
from jax import lax
from jax.experimental import pallas as pl
from jax.experimental.pallas import tpu as pltpu
from jax.sharding import PartitionSpec as P
import numpy as np

MHEADS = 24
MHEAD_DIM = 64
STATE = 128
CONV = 4
QHEADS = 8
KVHEADS = 2
HEAD_DIM = 64
SSM = 1536
XBC = 1792
QW = 512
KVW = 256
DT_PAD = 128


epsilon = 1e-05
rope_base = 100000000000.0
masked = -1e30


def from_behind(value, axis, steps):
    count = lax.axis_size(axis)
    first, last = (max(0, -steps), min(count, count - steps))
    return lax.ppermute(value, axis, [(source, source + steps) for source in range(first, last)])


MESH = pl.DeviceIdType.MESH
HALO = 16
VMEM_SPEC = pl.BlockSpec(memory_space=pltpu.VMEM)


def lattice(count):
    sizes, left, turn = [1, 1, 1], count // 2, 0
    while left > 1:
        factor = 2 if left % 2 == 0 else left
        sizes[turn % 3] *= factor
        left //= factor
        turn += 1
    return sizes[0], sizes[1], sizes[2], 2


def coordinates(sizes):
    me = lax.axis_index("seq")
    _, size_1, size_2, cores = sizes
    return (
        me // (size_1 * size_2 * cores),
        me // (size_2 * cores) % size_1,
        me // cores % size_2,
        me % cores,
    )


def device_at(sizes, place):
    index = place[0]
    for size, at in zip(sizes[1:], place[1:]):
        index = index * size + at
    return index


def partners(sizes, place, axis):
    found = []
    for step in range(1, sizes[axis]):
        other = list(place)
        other[axis] = (place[axis] + step) % sizes[axis]
        found.append(other)
    return found


def greet(sizes, place, more=()):
    barrier = pltpu.get_barrier_semaphore()
    met = [
        device_at(sizes, other) for axis in range(4) for other in partners(sizes, place, axis)
    ] + list(more)
    for other in met:
        pl.semaphore_signal(barrier, inc=1, device_id=(other,), device_id_type=MESH)
    pl.semaphore_wait(barrier, len(met))


def block_cuts(shapes, target):
    cuts = []
    for number, (rows, columns) in enumerate(shapes):
        pieces = max(1, round(rows * columns / target))
        width = max(128, (columns // pieces + 127) // 128 * 128)
        across = -(-columns // width)
        height = rows
        if across < pieces and rows % 32 == 0:
            height = max(32, rows // -(-pieces // across) // 32 * 32)
        for top in range(0, rows, height):
            for start in range(0, columns, width):
                size = (min(height, rows - top), min(width, columns - start))
                cuts.append((number, (pl.ds(top, size[0]), pl.ds(start, size[1]))))
    return cuts


def run_together(programs):
    waiting = list(programs)
    while waiting:
        for program in list(waiting):
            try:
                next(program)
            except StopIteration:
                waiting.remove(program)


ORDERS = ((0, 1, 2), (0, 2, 1))


def axis_order(turn):
    return ORDERS[turn % len(ORDERS)]


def tick_count(cuts, stages):
    return -(-len(cuts) // len(ORDERS)) + stages - 1


def tick_turns(cuts, number):
    first = number * len(ORDERS)
    return range(first, min(first + len(ORDERS), len(cuts))) if number >= 0 else range(0)


def gather_program(sizes, cuts, ins, outs, local_sem, send_sem, recv_sem, depth=1000):
    place = coordinates(sizes)
    sibling = partners(sizes, place, 3)[0]

    def region(turn, at):
        number, window = cuts[turn]
        return outs[number].at[*at, *window]

    def before(axis, step):
        at = list(place)
        at[axis] = (place[axis] - step - 1 + sizes[axis]) % sizes[axis]
        return at

    def widened(order, stage, at):
        full = list(at)
        for axis in order[:stage]:
            full[axis] = slice(None)
        return full

    def remote(turn, slot, step, source, target, other):
        return pltpu.make_async_remote_copy(
            src_ref=source,
            dst_ref=target,
            send_sem=send_sem.at[turn, slot, step],
            recv_sem=recv_sem.at[turn, slot, step],
            device_id=(device_at(sizes, other),),
            device_id_type=MESH,
        )

    def outgoing(turn, stage, step):
        order = axis_order(turn)
        here = region(turn, widened(order, stage, place))
        number, window = cuts[turn]
        source = ins[number].at[*window] if stage == 0 else here
        other = partners(sizes, place, order[stage])[step]
        return remote(turn, stage, step, source, here, other)

    def incoming(turn, stage, step):
        order = axis_order(turn)
        here = region(turn, widened(order, stage, before(order[stage], step)))
        return remote(turn, stage, step, here, here, sibling)

    def fresh(turn, stage, step, core):
        order = axis_order(turn)
        if stage == 0:
            at = widened(order, 1, place)
        else:
            at = widened(order, stage, before(order[stage], step))
        at[3] = core
        return region(turn, at)

    def across(turn, stage, step):
        here = fresh(turn, stage, step, place[3])
        return remote(turn, 3 + stage, step, here, here, sibling)

    def from_across(turn, stage, step):
        here = fresh(turn, stage, step, sibling[3])
        return remote(turn, 3 + stage, step, here, here, sibling)

    def hops(turn, stage):
        return range(sizes[axis_order(turn)[stage]] - 1)

    def pieces(turn, stage):
        return range(1) if stage == 0 else hops(turn, stage)

    def local(turn):
        number, window = cuts[turn]
        return pltpu.make_async_copy(
            ins[number].at[*window], region(turn, list(place)), local_sem.at[turn]
        )

    def launch(number):
        for turn in tick_turns(cuts, number):
            for step in hops(turn, 0):
                outgoing(turn, 0, step).start()

    for turn in range(len(cuts)):
        local(turn).start()
    for number in range(min(depth, len(cuts))):
        launch(number)
    yield

    def advance(turn, stage):
        for step in hops(turn, stage):
            incoming(turn, stage, step).wait_recv()
        if stage == 0:
            local(turn).wait()
        if stage < 2:
            for step in hops(turn, stage + 1):
                outgoing(turn, stage + 1, step).start()
        for step in pieces(turn, stage):
            across(turn, stage, step).start()

    for tick in range(tick_count(cuts, 3)):
        launch(tick + depth)
        for stage in range(3):
            for turn in tick_turns(cuts, tick - stage):
                advance(turn, stage)
        yield
    for turn in range(len(cuts)):
        for stage in range(3):
            for step in pieces(turn, stage):
                from_across(turn, stage, step).wait_recv()
            for step in pieces(turn, stage):
                across(turn, stage, step).wait_send()
            for step in hops(turn, stage):
                outgoing(turn, stage, step).wait_send()


def gather_scratch(sizes, cuts):
    most = max(sizes[:3])
    return [
        pltpu.SemaphoreType.DMA((len(cuts),)),
        pltpu.SemaphoreType.DMA((len(cuts), 6, most)),
        pltpu.SemaphoreType.DMA((len(cuts), 6, most)),
    ]


def gather_everywhere(arrays, collective_id, target, edge):
    sizes = lattice(lax.axis_size("seq"))
    cuts = block_cuts([array.shape for array in arrays], target)
    kinds = len(arrays)

    def kernel(*refs):
        ins, edge_in, refs = refs[:kinds], refs[kinds], refs[kinds + 1 :]
        outs, edge_out, refs = refs[:kinds], refs[kinds], refs[kinds + 1 :]
        *sems, edge_sems = refs
        me, count = lax.axis_index("seq"), lax.axis_size("seq")
        following, previous = lax.rem(me + 1, count), lax.rem(me + count - 1, count)
        greet(sizes, coordinates(sizes), [following, previous])
        edge_copy = pltpu.make_async_remote_copy(
            src_ref=edge_in.at[pl.ds(edge.shape[0] - HALO, HALO), :],
            dst_ref=edge_out,
            send_sem=edge_sems.at[0],
            recv_sem=edge_sems.at[1],
            device_id=(following,),
            device_id_type=MESH,
        )
        edge_copy.start()
        run_together([gather_program(sizes, cuts, ins, outs, *sems)])
        edge_copy.wait()

    hbm = pl.BlockSpec(memory_space=pl.ANY)
    gathered = pl.pallas_call(
        kernel,
        out_shape=[jax.ShapeDtypeStruct(sizes + a.shape, a.dtype) for a in arrays]
        + [jax.ShapeDtypeStruct((HALO, edge.shape[1]), edge.dtype)],
        in_specs=[hbm] * (kinds + 1),
        out_specs=[hbm] * (kinds + 1),
        scratch_shapes=gather_scratch(sizes, cuts) + [pltpu.SemaphoreType.DMA((2,))],
        compiler_params=pltpu.CompilerParams(
            collective_id=collective_id,
            has_side_effects=True,
            vmem_limit_bytes=62 * 1024 * 1024,
        ),
        name="gather_everywhere",
    )(*arrays, edge)
    return [g.reshape(-1, a.shape[1]) for g, a in zip(gathered, arrays)] + [gathered[kinds]]


def scatter_plan(shapes, small, target):
    sizes = lattice(lax.axis_size("seq"))
    cuts = block_cuts(shapes, target)
    kinds = len(shapes)
    most = max(sizes[:3])
    used = [axis_order(turn)[::-1] for turn in range(len(cuts))]
    pairs = [[[axis for axis in range(3) if axis != axes[0]] for axes in used]][0]
    first_lead = tuple(max(sizes[pair[i]] for pair in pairs) for i in range(2))
    first_step = max(sizes[axes[0]] for axes in used) - 1
    second_lead = max(sizes[axes[2]] for axes in used)
    second_step = max(sizes[axes[1]] for axes in used) - 1
    last_step = max(sizes[axes[2]] for axes in used) - 1
    extra = 0 if small is None else 1

    def program(ins, small_in, outs, small_out, refs):
        own, core_in, first_in, second_in, last_in = [
            refs[i * kinds : (i + 1) * kinds] for i in range(5)
        ]
        refs = refs[5 * kinds :]
        local_sem, send_sem, recv_sem = refs[:3]
        place = coordinates(sizes)
        sibling = partners(sizes, place, 3)[0]
        sent = []

        def push(source, target_ref, other, sems, slot):
            copy = pltpu.make_async_remote_copy(
                src_ref=source,
                dst_ref=target_ref,
                send_sem=sems[0].at[slot],
                recv_sem=sems[1].at[slot],
                device_id=(device_at(sizes, other),),
                device_id_type=MESH,
            )
            copy.start()
            sent.append(copy)

        def arrival(here, sems, slot):
            pltpu.make_async_remote_copy(
                src_ref=here,
                dst_ref=here,
                send_sem=sems[0].at[slot],
                recv_sem=sems[1].at[slot],
                device_id=(device_at(sizes, sibling),),
                device_id_type=MESH,
            ).wait_recv()

        main_sems = (send_sem, recv_sem)

        def core_copy(turn):
            number, window = cuts[turn]
            return pltpu.make_async_remote_copy(
                src_ref=ins[number].at[:, :, :, sibling[3], *window],
                dst_ref=core_in[number].at[:, :, :, *window],
                send_sem=send_sem.at[turn, 0, 0],
                recv_sem=recv_sem.at[turn, 0, 0],
                device_id=(device_at(sizes, sibling),),
                device_id_type=MESH,
            )

        def local_copy(turn):
            number, window = cuts[turn]
            return pltpu.make_async_copy(
                ins[number].at[:, :, :, place[3], *window],
                own[number].at[:, :, :, *window],
                local_sem.at[turn],
            )

        for turn in range(len(cuts)):
            core_copy(turn).start()
            local_copy(turn).start()
        yield

        def kept(number, window, axes, stage, at):
            index = [slice(None), slice(None), slice(None)]
            for axis in axes[:stage]:
                index[axis] = at[axis]
            return own[number].at[*index, *window]

        def landed(number, window, axes, stage, step):
            if stage == 3:
                return last_in[number].at[step, *window]
            left = [sizes[axis] for axis in range(3) if axis not in axes[:stage]]
            box = (first_in, second_in)[stage - 1][number]
            return box.at[step, *[pl.ds(0, size) for size in left], *window]

        def advance(turn, stage):
            number, window = cuts[turn]
            axes = axis_order(turn)[::-1]
            lead = tuple(sizes[axis] for axis in range(3) if axis not in axes[:stage])
            if stage == 0:
                local_copy(turn).wait()
                arrival(core_in[number].at[:, :, :, *window], main_sems, (turn, 0, 0))
                pieces = [core_in[number].at[:, :, :, *window]]
            else:
                steps = range(sizes[axes[stage - 1]] - 1)
                pieces = [landed(number, window, axes, stage, step) for step in steps]
                for step in steps:
                    arrival(pieces[step], main_sems, (turn, stage, step))
            target_ref = kept(number, window, axes, stage, place)

            def total(index):
                value = target_ref[index].astype(jnp.float32)
                for piece in pieces:
                    value = value + piece[index].astype(jnp.float32)
                return value

            if stage == 3:
                outs[number][window] = total((...,))
                return
            amount = math.prod(lead)

            def add(flat, carry):
                index, rest = [], flat
                for size in lead[::-1]:
                    index.insert(0, rest % size)
                    rest = rest // size
                target_ref[tuple(index)] = total(tuple(index)).astype(jnp.bfloat16)
                return carry

            lax.fori_loop(0, amount, add, 0)
            for step in range(sizes[axes[stage]] - 1):
                onward(turn, stage, step).start()

        def onward(turn, stage, step):
            number, window = cuts[turn]
            axes = axis_order(turn)[::-1]
            other = partners(sizes, place, axes[stage])[step]
            return pltpu.make_async_remote_copy(
                src_ref=kept(number, window, axes, stage + 1, other),
                dst_ref=landed(number, window, axes, stage + 1, step),
                send_sem=send_sem.at[turn, stage + 1, step],
                recv_sem=recv_sem.at[turn, stage + 1, step],
                device_id=(device_at(sizes, other),),
                device_id_type=MESH,
            )

        if extra:
            boxes, small_sems = refs[3:7], refs[7:9]

        def small_step(tick):
            axes = (3, 2, 1, 0)
            if tick > 0:
                axis = axes[tick - 1]
                box = boxes[axis]
                for step in range(sizes[axis] - 1):
                    behind = (place[axis] - step - 1 + sizes[axis]) % sizes[axis]
                    arrival(box.at[behind], small_sems, (axis, step))
                value = box[0]
                for at in range(1, sizes[axis]):
                    value = value + box[at]
            else:
                value = small_in[0][...]
            if tick == 4:
                small_out[0][...] = value
                return
            axis = axes[tick]
            boxes[axis][place[axis]] = value
            here = boxes[axis].at[place[axis]]
            for step, other in enumerate(partners(sizes, place, axis)):
                push(here, here, other, small_sems, (axis, step))

        for tick in range(max(tick_count(cuts, 4), 5)):
            for stage in range(4):
                for turn in tick_turns(cuts, tick - stage):
                    advance(turn, stage)
            if extra and tick < 5:
                small_step(tick)
            yield
        for copy in sent:
            copy.wait_send()
        for turn in range(len(cuts)):
            core_copy(turn).wait_send()
            axes = axis_order(turn)[::-1]
            for stage in range(3):
                for step in range(sizes[axes[stage]] - 1):
                    onward(turn, stage, step).wait_send()

    scratch = []
    for lead in (
        sizes[:3],
        sizes[:3],
        (first_step,) + first_lead,
        (second_step, second_lead),
        (last_step,),
    ):
        scratch += [pltpu.VMEM(lead + s, jnp.bfloat16) for s in shapes]
    scratch += [
        pltpu.SemaphoreType.DMA((len(cuts),)),
        pltpu.SemaphoreType.DMA((len(cuts), 4, most)),
        pltpu.SemaphoreType.DMA((len(cuts), 4, most)),
    ]
    if extra:
        scratch += [pltpu.VMEM((size,) + small.shape, jnp.float32) for size in sizes]
        scratch += [pltpu.SemaphoreType.DMA((4, most)) for _ in range(2)]
    return program, scratch


def scatter_sums(parts, small, collective_id, target):
    sizes = lattice(lax.axis_size("seq"))
    count = lax.axis_size("seq")
    shapes = [(p.shape[0] // count, p.shape[1]) for p in parts]
    views = [p.reshape(sizes + s) for p, s in zip(parts, shapes)]
    program, scratch = scatter_plan(shapes, small, target)
    kinds = len(parts)

    def kernel(*refs):
        ins, small_in, refs = refs[:kinds], refs[kinds : kinds + 1], refs[kinds + 1 :]
        outs, small_out, refs = refs[:kinds], refs[kinds : kinds + 1], refs[kinds + 1 :]
        greet(sizes, coordinates(sizes))
        run_together([program(ins, small_in, outs, small_out, refs)])

    return pl.pallas_call(
        kernel,
        out_shape=[jax.ShapeDtypeStruct(s, jnp.float32) for s in shapes]
        + [jax.ShapeDtypeStruct(small.shape, jnp.float32)],
        in_specs=[pl.BlockSpec(memory_space=pl.ANY)] * kinds + [VMEM_SPEC],
        out_specs=[VMEM_SPEC] * (kinds + 1),
        scratch_shapes=scratch,
        compiler_params=pltpu.CompilerParams(
            collective_id=collective_id,
            has_side_effects=True,
            vmem_limit_bytes=62 * 1024 * 1024,
        ),
        name="scatter_sums",
    )(*views, small)


def greet_chips(chips):
    me = lax.axis_index("seq")
    chip, core = me // 2, me % 2
    barrier = pltpu.get_barrier_semaphore()

    def greet_one(step, carry):
        other = lax.rem(chip + step, chips) * 2 + core
        pl.semaphore_signal(barrier, inc=1, device_id=(other,), device_id_type=MESH)
        return carry

    lax.fori_loop(1, chips, greet_one, 0)
    pl.semaphore_signal(barrier, inc=1, device_id=(chip * 2 + 1 - core,), device_id_type=MESH)
    pl.semaphore_wait(barrier, chips)


def exchange_program(chips, part, reverse, own_ref, decay_ref, out_ref, chip_decay_ref, refs):
    (
        mine_low,
        other_low,
        other_decay,
        payload,
        landed,
        result,
        prefix,
        pair_sems,
        far_send,
        far_recv,
    ) = refs
    padded = own_ref.shape[2]
    me = lax.axis_index("seq")
    chip, core = me // 2, me % 2
    sibling = chip * 2 + 1 - core
    f32 = jnp.float32
    wire = jnp.bfloat16 if reverse else f32

    def pair_copy(source, target, slot):
        return pltpu.make_async_remote_copy(
            src_ref=source,
            dst_ref=target,
            send_sem=pair_sems.at[slot, 0],
            recv_sem=pair_sems.at[slot, 1],
            device_id=(sibling,),
            device_id_type=MESH,
        )

    def far_copy(step, turn, source, target):
        other = lax.rem(chip + step, chips)
        return pltpu.make_async_remote_copy(
            src_ref=source.at[other],
            dst_ref=target.at[chip],
            send_sem=far_send.at[turn, step],
            recv_sem=far_recv.at[turn, step],
            device_id=(other * 2 + core,),
            device_id_type=MESH,
        )

    def far_start(turn, source, target):
        def start(step, carry):
            far_copy(step, turn, source, target).start()
            return carry

        lax.fori_loop(1, chips, start, 0)

    def far_wait(turn, source, target):
        def finish(step, carry):
            far_copy(step, turn, source, target).wait()
            return carry

        lax.fori_loop(1, chips, finish, 0)

    def by_row(vector, half, shape, first=0):
        place = (
            lax.broadcasted_iota(jnp.int32, shape, 0) + first
        ) * part + lax.broadcasted_iota(jnp.int32, shape, 1)
        head = (half * (chips * part) + place) // MHEAD_DIM
        lane = lax.broadcasted_iota(jnp.int32, shape, 2)
        picked = jnp.where(lane == head, vector.reshape(1, 1, 128), 0.0)
        return jnp.sum(picked, axis=2, keepdims=True)

    mine_low[...] = own_ref[...].astype(wire)
    first_copies = [
        pair_copy(mine_low, other_low, 0),
        pair_copy(decay_ref, other_decay, 1),
    ]
    for copy in first_copies:
        copy.start()
    yield
    for copy in first_copies:
        copy.wait()
    own_decay, far_decay = decay_ref[0:1, :], other_decay[0:1, :]
    second_core = core == 1
    decays = (
        jnp.where(second_core, far_decay, own_decay),
        jnp.where(second_core, own_decay, far_decay),
    )
    weighted = 0 if reverse else 1
    whole = (chips, padded, 128)
    half_own = own_ref[core]
    half_far = other_low[core].astype(f32)
    earlier = jnp.where(second_core, half_far, half_own)
    later = jnp.where(second_core, half_own, half_far)
    factor = by_row(decays[weighted], core, whole)
    total = earlier + factor * later if reverse else factor * earlier + later
    payload[:, :padded, :] = total.astype(wire)
    if not reverse:
        both = jnp.broadcast_to(decays[0] * decays[1], (8, 128))
        for other in range(chips):
            payload[other, padded:, :] = both
    far_start(0, payload, landed)
    landed[chip] = payload[chip]
    yield
    far_wait(0, payload, landed)
    if not reverse:
        for other in range(chips):
            chip_decay_ref[other : other + 1, :] = landed[other, padded : padded + 1, :]
    state = jnp.zeros((1, padded, 128), f32)
    order = range(chips - 1, -1, -1) if reverse else range(chips)
    for other in order:
        result[other] = state[0]
        step_factor = by_row(chip_decay_ref[other : other + 1, :], core, (1, padded, 128), chip)
        state = step_factor * state + landed[other, :padded, :].astype(f32)[None]
    far_start(1, result, prefix)
    prefix[chip] = result[chip]
    yield
    far_wait(1, result, prefix)
    out_ref[core] = prefix[...]
    last_copy = pair_copy(prefix, out_ref.at[core], 2)
    last_copy.start()
    yield
    last_copy.wait()
    moved = (core == 0) if reverse else second_core
    step_decay = decays[1] if reverse else decays[0]
    for half in range(2):
        factor = jnp.where(moved, by_row(step_decay, half, whole), 1.0)
        extra = jnp.where(moved, other_low[half].astype(f32), 0.0)
        out_ref[half] = factor * out_ref[half] + extra


def exchange_scratch(chips, padded, reverse):
    f32 = jnp.float32
    low = jnp.bfloat16 if reverse else f32
    sent_rows = padded if reverse else padded + 8
    return [
        pltpu.VMEM((2, chips, padded, 128), low),
        pltpu.VMEM((2, chips, padded, 128), low),
        pltpu.VMEM((8, 128), f32),
        pltpu.VMEM((chips, sent_rows, 128), low),
        pltpu.VMEM((chips, sent_rows, 128), low),
        pltpu.VMEM((chips, padded, 128), f32),
        pltpu.VMEM((chips, padded, 128), f32),
        pltpu.SemaphoreType.DMA((3, 2)),
        pltpu.SemaphoreType.DMA((2, chips)),
        pltpu.SemaphoreType.DMA((2, chips)),
    ]


def slice_rows(values, chips):
    part = values.shape[0] // (2 * chips)
    padded = -(-part // 16) * 16
    sliced = values.reshape(2, chips, part, values.shape[1])
    return jnp.pad(sliced, ((0, 0), (0, 0), (0, padded - part), (0, 0)))


def join_rows(slices, rows):
    chips = slices.shape[1]
    return slices[:, :, : rows // (2 * chips)].reshape(rows, slices.shape[3])


def front(forward_args, late, output_args, row_starts, collective_id, targets):
    count = lax.axis_size("seq")
    sizes, chips = lattice(count), count // 2
    rows, model = forward_args[0].shape
    shape = jax.ShapeDtypeStruct
    forward_shapes = mixer_forward_shapes(rows, model)
    kv_shape, query_shape = forward_shapes[5], forward_shapes[4]
    cuts = block_cuts([kv_shape.shape], targets[0])
    late_cuts = block_cuts([w.shape for w in late], targets[1])
    part = SSM // count
    padded = -(-part // 16) * 16
    fused = part == padded
    kinds = len(late)
    state_shape = (2, chips, padded, STATE)
    groups, query_rows, _ = query_shape.shape
    tokens = rows * count
    comm_scratch = (
        gather_scratch(sizes, cuts)
        + gather_scratch(sizes, late_cuts)
        + exchange_scratch(chips, padded, False)
    )
    compute_scratch = (
        [pltpu.VMEM((3 * rows, SSM), jnp.bfloat16)]
        + attention_scratch(groups, query_rows)
        + [
            pltpu.VMEM(sizes + kv_shape.shape, kv_shape.dtype),
            pltpu.SemaphoreType.DMA((1,)),
            pltpu.VMEM(kv_shape.shape, kv_shape.dtype),
            pltpu.VMEM(state_shape, jnp.float32),
        ]
        + mixer_forward_scratch(rows, model, forward_args[3:6])
    )
    hbm = pl.BlockSpec(memory_space=pl.ANY)
    kept = (0, 1, 2, 3, 4, 6, 7, 9)
    if fused:
        first_in = list(forward_args) + list(output_args) + [row_starts]
        first_specs = mixer_forward_specs() + [VMEM_SPEC] * (len(output_args) + 1)
        first_out = (
            [forward_shapes[i] for i in kept]
            + mixer_output_shapes(rows)
            + attention_shapes(groups, query_rows)
        )
    else:
        forward = list(mixer_forward(forward_args))
        first_in = [forward[5], slice_rows(forward[8], chips), forward[9]]
        first_specs = [hbm, VMEM_SPEC, VMEM_SPEC]
        first_out = []

    def kernel(*refs):
        late_in, refs = refs[:kinds], refs[kinds:]
        ins, refs = refs[: len(first_in)], refs[len(first_in) :]
        kv_out, state_out, chip_decay_ref, refs = refs[0], refs[1], refs[2], refs[3:]
        late_out, refs = refs[:kinds], refs[kinds:]
        outs, refs = refs[: len(first_out)], refs[len(first_out) :]
        comm, refs = refs[: len(comm_scratch)], refs[len(comm_scratch) :]
        greet_chips(chips)
        weights = gather_program(sizes, late_cuts, late_in, late_out, *comm[3:6], 2)
        done = [0]

        def tick():
            done[0] += 1
            next(weights)

        next(weights)
        if fused:
            input_ref, max_ref, acc_ref, kv_vmem, kv_sem, kv_ref, state_ref, *scratch = refs
            normed_ref, gate_ref, ext_ref, pre_ref, q_ref, dt_pre_ref, log_ref, decay_ref = outs[:8]
            given = len(forward_args)
            mixer_forward_body(
                *ins[:given],
                normed_ref,
                gate_ref,
                ext_ref,
                pre_ref,
                q_ref,
                kv_ref,
                dt_pre_ref,
                log_ref,
                state_ref,
                decay_ref,
                *scratch,
                tick,
            )
        else:
            kv_ref, state_ref, decay_ref = ins
        exchange = exchange_program(
            chips, part, False, state_ref, decay_ref, state_out, chip_decay_ref, comm[6:]
        )
        keys = gather_program(sizes, cuts, [kv_ref], [kv_out], *comm[:3])
        run_together([exchange, keys])
        if not fused:
            for _ in weights:
                pass
            return
        load = pltpu.make_async_copy(kv_out, kv_vmem, kv_sem.at[0])
        load.start()
        tick()
        mixer_output_body(
            pre_ref,
            dt_pre_ref,
            log_ref,
            state_out[...].reshape(SSM, STATE),
            gate_ref,
            *ins[given:-1],
            *outs[8:10],
            input_ref,
        )
        load.wait()
        tick()
        attention_forward_body(
            q_ref,
            kv_vmem.reshape(tokens, kv_shape.shape[1]),
            ins[-1],
            *outs[10:],
            max_ref,
            acc_ref,
            spread_ticks(weights, tick_count(late_cuts, 3) - done[0], tokens // KEYS_STEP),
        )
        for _ in weights:
            pass

    kv_all, states_in, chip_decay, *rest = pl.pallas_call(
        kernel,
        out_shape=[
            shape(sizes + kv_shape.shape, kv_shape.dtype),
            shape(state_shape, jnp.float32),
            shape((chips, 128), jnp.float32),
        ]
        + [shape(sizes + w.shape, w.dtype) for w in late]
        + first_out,
        in_specs=[hbm] * kinds + first_specs,
        out_specs=[hbm, VMEM_SPEC, VMEM_SPEC] + [hbm] * kinds + [VMEM_SPEC] * len(first_out),
        scratch_shapes=comm_scratch + (compute_scratch if fused else []),
        compiler_params=pltpu.CompilerParams(
            collective_id=collective_id,
            has_side_effects=True,
            vmem_limit_bytes=63 * 1024 * 1024,
        ),
        name="front",
    )(*late, *first_in)
    kv_all = kv_all.reshape(-1, kv_shape.shape[1])
    late_full = [w.reshape(-1, w.shape[-1]) for w in rest[:kinds]]
    states_in = join_rows(states_in, SSM)
    computed = list(rest[kinds:])
    if not fused:
        computed = [forward[i] for i in kept]
        computed += mixer_output(
            forward[3], forward[6], forward[7], states_in, forward[1], *output_args
        )
        computed += attention_forward(forward[4], kv_all, row_starts)
    return kv_all, states_in, chip_decay, late_full, computed


def some_ticks(program, amount):
    for _ in range(amount):
        next(program, None)
        yield


def back(
    key_terms, mixer_args, input_args, passing, chip_decay, late_grads, collective_id, targets
):
    count = lax.axis_size("seq")
    sizes, chips = lattice(count), count // 2
    shape = (key_terms.shape[0] // count, key_terms.shape[1])
    late_shapes = [(g.shape[0] // count, g.shape[1]) for g in late_grads]
    keys, keys_scratch = scatter_plan([shape], None, targets[0])
    weights, weights_scratch = scatter_plan(late_shapes, None, targets[1])
    part = SSM // count
    padded = -(-part // 16) * 16
    fused = part == padded
    rows = mixer_args[0].shape[0]
    state_shape = (2, chips, padded, STATE)
    kinds = len(late_grads)
    if fused:
        first_in = list(mixer_args) + list(input_args)
        made_shapes = mixer_backward_shapes(rows, state_shape)
        outer = (0, 1, 8)
        inner = (2, 3, 4, 5, 6, 7)
        mixer_shapes = [made_shapes[i] for i in outer] + mixer_input_shapes(rows)
        compute_scratch = (
            mixer_backward_scratch(rows)
            + [pltpu.VMEM(made_shapes[i].shape, made_shapes[i].dtype) for i in inner]
            + mixer_input_scratch(rows)
        )
    else:
        mixer_out = list(mixer_backward(mixer_args))
        first_in, mixer_shapes = [slice_rows(mixer_out[3], chips)], []
        compute_scratch = []
    known = len(first_in)
    made = len(mixer_shapes)

    def kernel(kv_ref, decay_ref, chip_decay_ref, *refs):
        late_in, refs = refs[:kinds], refs[kinds:]
        ins, refs = refs[:known], refs[known:]
        kv_out, state_out, refs = refs[0], refs[1], refs[2:]
        late_out, refs = refs[:kinds], refs[kinds:]
        outs, refs = refs[:made], refs[made:]
        keys_refs, refs = refs[: len(keys_scratch)], refs[len(keys_scratch) :]
        weights_refs, refs = refs[: len(weights_scratch)], refs[len(weights_scratch) :]
        mixer_refs, refs = refs[: len(compute_scratch)], refs[len(compute_scratch) :]
        greet_chips(chips)
        runs = [
            keys([kv_ref], [], [kv_out], [], keys_refs),
            weights(late_in, [], late_out, [], weights_refs),
        ]

        def tick():
            for run in runs:
                next(run)

        tick()
        if fused:
            given = len(mixer_args)
            held = dict(zip(outer, outs[:3])) | dict(zip(inner, mixer_refs[3:9]))
            made_refs = [held[i] for i in range(9)]
            mixer_backward_body(*ins[:given], *made_refs, *mixer_refs[:3], tick)
            own_ref = made_refs[3]
        else:
            own_ref = ins[0]
        exchange = exchange_program(
            chips, part, True, own_ref, decay_ref, state_out, chip_decay_ref, refs
        )
        if not fused:
            run_together([exchange] + runs)
            return
        run_together([exchange, runs[0], some_ticks(runs[1], 3)])
        pre_ref, dt_pre_ref, log_ref, state_ref = ins[4:8]
        skip_ref, starts_ref = ins[8:10]
        ext_ref, tap_ref, a_log_ref = ins[given:]

        def late_tick():
            next(runs[1], None)

        mixer_input_backward_body(
            state_out[...].reshape(SSM, STATE),
            state_ref,
            decay_ref,
            made_refs[2],
            *made_refs[4:8],
            pre_ref,
            dt_pre_ref,
            log_ref,
            ext_ref,
            tap_ref,
            a_log_ref,
            skip_ref,
            starts_ref,
            *outs[3:],
            *mixer_refs[9:],
            late_tick,
        )
        for _ in runs[1]:
            pass

    hbm = pl.BlockSpec(memory_space=pl.ANY)
    kv_sum, grad_end, *rest = pl.pallas_call(
        kernel,
        out_shape=[
            jax.ShapeDtypeStruct(shape, jnp.float32),
            jax.ShapeDtypeStruct(state_shape, jnp.float32),
        ]
        + [jax.ShapeDtypeStruct(s, jnp.float32) for s in late_shapes]
        + mixer_shapes,
        in_specs=[hbm] + [VMEM_SPEC] * 2 + [hbm] * kinds + [VMEM_SPEC] * known,
        out_specs=[VMEM_SPEC] * (2 + kinds + made),
        scratch_shapes=keys_scratch
        + weights_scratch
        + compute_scratch
        + exchange_scratch(chips, padded, True),
        compiler_params=pltpu.CompilerParams(
            collective_id=collective_id,
            has_side_effects=True,
            vmem_limit_bytes=63 * 1024 * 1024,
        ),
        name="back",
    )(
        key_terms.reshape(sizes + shape),
        passing,
        chip_decay,
        *[g.reshape(sizes + s) for g, s in zip(late_grads, late_shapes)],
        *first_in,
    )
    late_sums = rest[:kinds]
    if fused:
        return kv_sum, late_sums, rest[kinds:]
    grad_end = join_rows(grad_end, SSM)
    input_out = mixer_input_backward(
        [grad_end, mixer_args[7], passing, mixer_out[2], *mixer_out[4:8]]
        + [*mixer_args[4:7], *input_args, *mixer_args[8:10]]
    )
    return kv_sum, late_sums, [mixer_out[0], mixer_out[1], mixer_out[8], *input_out]


KEYS_STEP = 512


def attention_forward_body(
    q_ref, kv_ref, starts_ref, out_ref, log_ref, flat_ref, max_ref, acc_ref, ticks
):
    groups, rows, _ = q_ref.shape
    group_size = QHEADS // KVHEADS
    local_rows = rows // group_size
    half_kv = KVW // 2
    steps = kv_ref.shape[0] // KEYS_STEP
    first_row = lax.axis_index("seq") * local_rows
    used = (first_row + local_rows - 1) // KEYS_STEP + 1
    starts = starts_ref[...]
    places = first_row + lax.broadcasted_iota(jnp.int32, (1, rows), 1) % local_rows
    max_ref[...] = jnp.full(max_ref.shape, masked, jnp.float32)
    acc_ref[...] = jnp.zeros(acc_ref.shape, jnp.float32)

    def block(step, general):
        first_key = pl.multiple_of(step * KEYS_STEP, KEYS_STEP)
        piece = kv_ref[pl.ds(first_key, KEYS_STEP), :]
        flipped = jnp.transpose(piece[:, half_kv:])
        ones = jnp.ones((16, KEYS_STEP), jnp.bfloat16)
        if general:
            key_pos = first_key + lax.broadcasted_iota(jnp.int32, (KEYS_STEP, 1), 0)
            allowed = (key_pos >= starts) & (key_pos <= places)
        else:
            row_open = starts <= first_key
        for group in range(groups):
            scores = lax.dot_general(
                piece[:, group * HEAD_DIM : (group + 1) * HEAD_DIM],
                q_ref[group],
                (((1,), (1,)), ((), ())),
                preferred_element_type=jnp.float32,
            )
            if general:
                scores = jnp.where(allowed, scores, masked)
            old = max_ref[group]
            new = jnp.maximum(old, jnp.max(scores, axis=0, keepdims=True))
            if general:
                shift = new
            else:
                new = jnp.where(row_open, new, old)
                shift = jnp.where(row_open, new, -masked)
            max_ref[group] = new
            weights = jnp.exp(scores - shift).astype(jnp.bfloat16)
            values = jnp.concatenate(
                [flipped[group * HEAD_DIM : (group + 1) * HEAD_DIM], ones], axis=0
            )
            acc_ref[group] = acc_ref[group] * jnp.exp(old - new) + jnp.dot(
                values, weights, preferred_element_type=jnp.float32
            )

    def body(step, carry):
        general = (step == 0) | ((step + 1) * KEYS_STEP > first_row)
        pl.when((step < used) & general)(partial(block, step, True))
        pl.when((step < used) & jnp.logical_not(general))(partial(block, step, False))
        for at, tick in ticks:
            pl.when(step == at)(tick)
        return carry

    lax.fori_loop(0, steps, body, 0)
    for group in range(groups):
        row_sum = acc_ref[group, HEAD_DIM : HEAD_DIM + 1, :]
        out = acc_ref[group, :HEAD_DIM, :] / row_sum
        out_ref[group] = out
        log_ref[group] = max_ref[group] + jnp.log(row_sum)
        for part in range(group_size):
            head = group * group_size + part
            flat_ref[:, head * HEAD_DIM : (head + 1) * HEAD_DIM] = jnp.transpose(
                out[:, part * local_rows : (part + 1) * local_rows]
            ).astype(jnp.bfloat16)


def attention_shapes(groups, rows):
    return [
        jax.ShapeDtypeStruct((groups, HEAD_DIM, rows), jnp.float32),
        jax.ShapeDtypeStruct((groups, 1, rows), jnp.float32),
        jax.ShapeDtypeStruct((rows // (QHEADS // KVHEADS), QW), jnp.bfloat16),
    ]


def attention_scratch(groups, rows):
    return [
        pltpu.VMEM((groups, 1, rows), jnp.float32),
        pltpu.VMEM((groups, HEAD_DIM + 16, rows), jnp.float32),
    ]


def attention_forward(queries, kv_all, row_starts):
    groups, rows, _ = queries.shape

    def kernel(*refs):
        attention_forward_body(*refs, [])

    return pl.pallas_call(
        kernel,
        out_shape=attention_shapes(groups, rows),
        in_specs=[VMEM_SPEC] * 3,
        out_specs=[VMEM_SPEC] * 3,
        scratch_shapes=attention_scratch(groups, rows),
        compiler_params=BIG_VMEM,
        name="attention_forward",
    )(queries, kv_all, row_starts)


def spread_ticks(program, ticks, steps):
    def make_tick():
        def tick():
            next(program, None)

        return tick

    return [(number * steps // ticks, make_tick()) for number in range(ticks)]


def attention_backward(
    queries, grads, kv_all, row_starts, log_total, outputs, late_grads, collective_id, target
):
    groups, rows, _ = queries.shape
    total = kv_all.shape[0]
    half_kv = KVW // 2
    group_size = QHEADS // KVHEADS
    local_rows = rows // group_size
    count = lax.axis_size("seq")
    sizes = lattice(count)
    shapes = [(g.shape[0] // count, g.shape[1]) for g in late_grads]
    views = [g.reshape(sizes + s) for g, s in zip(late_grads, shapes)]
    program, scratch = scatter_plan(shapes, None, target)
    kinds = len(shapes)
    ticks = max(tick_count(block_cuts(shapes, target), 4), 5)
    steps = total // KEYS_STEP

    def kernel(q_ref, g_ref, kv_ref, starts_ref, log_ref, outputs_ref, *refs):
        ins, dkv_ref, dq_ref, refs = refs[:kinds], refs[kinds], refs[kinds + 1], refs[kinds + 2 :]
        outs, delta_ref, refs = refs[:kinds], refs[kinds], refs[kinds + 1 :]
        greet(sizes, coordinates(sizes))
        sums = program(ins, [], outs, [], refs)
        next(sums)
        first_row = lax.axis_index("seq") * local_rows
        used = (first_row + local_rows - 1) // KEYS_STEP + 1
        starts = starts_ref[...]
        places = first_row + lax.broadcasted_iota(jnp.int32, (1, rows), 1) % local_rows
        dq_ref[...] = jnp.zeros(dq_ref.shape, jnp.float32)
        for group in range(groups):
            flipped_grads = jnp.transpose(g_ref[group].astype(jnp.float32))
            delta_ref[group] = jnp.sum(flipped_grads * outputs_ref[group], axis=0, keepdims=True)

        def block(step, general):
            first_key = pl.multiple_of(step * KEYS_STEP, KEYS_STEP)
            piece = kv_ref[pl.ds(first_key, KEYS_STEP), :]
            flipped = jnp.transpose(piece[:, :half_kv])
            if general:
                key_pos = first_key + lax.broadcasted_iota(jnp.int32, (KEYS_STEP, 1), 0)
                allowed = (key_pos >= starts) & (key_pos <= places)
            else:
                row_open = starts <= first_key
            found = []
            for group in range(groups):
                low, high = group * HEAD_DIM, (group + 1) * HEAD_DIM
                scores = lax.dot_general(
                    piece[:, low:high],
                    q_ref[group],
                    (((1,), (1,)), ((), ())),
                    preferred_element_type=jnp.float32,
                )
                shift = log_ref[group]
                if general:
                    scores = jnp.where(allowed, scores, masked)
                else:
                    shift = jnp.where(row_open, shift, -masked)
                weights = jnp.exp(scores - shift)
                grad_weights = lax.dot_general(
                    piece[:, half_kv + low : half_kv + high],
                    g_ref[group],
                    (((1,), (1,)), ((), ())),
                    preferred_element_type=jnp.float32,
                )
                grad_scores = (weights * (grad_weights - delta_ref[group])).astype(jnp.bfloat16)
                dq_ref[group] += jnp.dot(
                    flipped[low:high], grad_scores, preferred_element_type=jnp.float32
                )
                found.append(
                    jnp.dot(grad_scores, q_ref[group], preferred_element_type=jnp.float32)
                )
                found.append(
                    jnp.dot(
                        weights.astype(jnp.bfloat16),
                        g_ref[group],
                        preferred_element_type=jnp.float32,
                    )
                )
            dkv_ref[pl.ds(first_key, KEYS_STEP), :] = jnp.concatenate(
                found[0::2] + found[1::2], axis=1
            ).astype(dkv_ref.dtype)

        def clear(step):
            first_key = pl.multiple_of(step * KEYS_STEP, KEYS_STEP)
            dkv_ref[pl.ds(first_key, KEYS_STEP), :] = jnp.zeros((KEYS_STEP, KVW), dkv_ref.dtype)

        marks = spread_ticks(sums, ticks, steps)

        def body(step, carry):
            general = (step == 0) | ((step + 1) * KEYS_STEP > first_row)
            pl.when((step < used) & general)(partial(block, step, True))
            pl.when((step < used) & jnp.logical_not(general))(partial(block, step, False))
            pl.when(step >= used)(partial(clear, step))
            for at, tick in marks:
                pl.when(step == at)(tick)
            return carry

        lax.fori_loop(0, steps, body, 0)
        for _ in sums:
            pass

    hbm = pl.BlockSpec(memory_space=pl.ANY)
    key_terms, query_grads, *late_sums = pl.pallas_call(
        kernel,
        out_shape=[
            jax.ShapeDtypeStruct((total, KVW), jnp.bfloat16),
            jax.ShapeDtypeStruct((groups, HEAD_DIM, rows), jnp.float32),
        ]
        + [jax.ShapeDtypeStruct(s, jnp.float32) for s in shapes],
        in_specs=[VMEM_SPEC] * 6 + [hbm] * kinds,
        out_specs=[VMEM_SPEC] * (2 + kinds),
        scratch_shapes=[pltpu.VMEM((groups, 1, rows), jnp.float32)] + scratch,
        compiler_params=pltpu.CompilerParams(
            collective_id=collective_id,
            has_side_effects=True,
            vmem_limit_bytes=62 * 1024 * 1024,
        ),
        name="attention_backward",
    )(queries, grads, kv_all, row_starts, log_total, outputs, *views)
    return key_terms, query_grads, late_sums


BIG_VMEM = pltpu.CompilerParams(vmem_limit_bytes=62 * 1024 * 1024)


def dot_parts(value, exact, parts, axes=((1,), (0,))):
    total, left = None, value
    for _ in range(parts):
        piece = left.astype(jnp.bfloat16)
        left = left - piece.astype(jnp.float32)
        term = lax.dot_general(piece, exact, (axes, ((), ())), preferred_element_type=jnp.float32)
        total = term if total is None else total + term
    return total


def dot_left(exact, value, parts):
    total, left = None, value
    for _ in range(parts):
        piece = left.astype(jnp.bfloat16)
        left = left - piece.astype(jnp.float32)
        term = jnp.dot(exact, piece, preferred_element_type=jnp.float32)
        total = term if total is None else total + term
    return total


def matmul_pair(left_side, right_side, axes):
    left_high = left_side.astype(jnp.bfloat16)
    left_low = (left_side - left_high.astype(jnp.float32)).astype(jnp.bfloat16)
    right_high = right_side.astype(jnp.bfloat16)
    right_low = (right_side - right_high.astype(jnp.float32)).astype(jnp.bfloat16)
    dims = (axes, ((), ()))
    product = partial(
        lax.dot_general, dimension_numbers=dims, preferred_element_type=jnp.float32
    )
    return (
        product(left_high, right_high)
        + product(left_low, right_high)
        + product(left_high, right_low)
    )


def stacked(value, first):
    high = value.astype(jnp.bfloat16)
    low = (value - high.astype(jnp.float32)).astype(jnp.bfloat16)
    return [high, low, high] if first else [high, high, low]


def dot_fast(left_side, right_side, axes):
    return lax.dot_general(
        left_side.astype(jnp.bfloat16),
        right_side.astype(jnp.bfloat16),
        (axes, ((), ())),
        preferred_element_type=jnp.float32,
    )


NN = ((1,), (0,))
NT = ((1,), (1,))
TN = ((0,), (0,))


def head_spread():
    head = lax.broadcasted_iota(jnp.int32, (128, SSM), 0)
    column = lax.broadcasted_iota(jnp.int32, (128, SSM), 1)
    return jnp.where(column // MHEAD_DIM == head, 1.0, 0.0).astype(jnp.bfloat16)


def rope_table(rows, count):
    half = HEAD_DIM // 2
    frequency = rope_base ** (-np.arange(half) / half)
    tables = []
    for places in (np.arange(rows), rows * np.arange(count)):
        angles = np.tile(places[:, None] * frequency[None, :], (1, 4))
        tables += [np.cos(angles).astype(np.float32), np.sin(angles).astype(np.float32)]
    return tables


def rope_now(device, base_cos_ref, base_sin_ref, far_cos_ref, far_sin_ref):
    base_cos, base_sin = base_cos_ref[...], base_sin_ref[...]
    far_cos, far_sin = far_cos_ref[pl.ds(device, 1), :], far_sin_ref[pl.ds(device, 1), :]
    cosine_part = far_cos * base_cos - far_sin * base_sin
    sine_part = far_sin * base_cos + far_cos * base_sin
    lane = lax.broadcasted_iota(jnp.int32, base_cos.shape, 1)
    return cosine_part, jnp.where(lane % HEAD_DIM < HEAD_DIM // 2, -sine_part, sine_part)


def rope_lanes(values, cosine_all, sine_all):
    width = values.shape[1]
    repeat = width // cosine_all.shape[1]
    half = HEAD_DIM // 2
    column = lax.broadcasted_iota(jnp.int32, values.shape, 1)
    partner = jnp.where(
        column % HEAD_DIM < half,
        pltpu.roll(values, width - half, 1),
        pltpu.roll(values, half, 1),
    )
    if repeat > 1:
        cosine_all = jnp.concatenate([cosine_all] * repeat, axis=1)
        sine_all = jnp.concatenate([sine_all] * repeat, axis=1)
    return values * cosine_all + partner * sine_all


def mixer_forward_body(
    hidden_ref,
    halo_ref,
    gain_ref,
    z_hbm,
    xbc_hbm,
    small_hbm,
    tap_ref,
    bias_ref,
    dt_bias_ref,
    a_log_ref,
    starts_ref,
    base_cos_ref,
    base_sin_ref,
    far_cos_ref,
    far_sin_ref,
    normed_ref,
    gate_ref,
    ext_ref,
    pre_ref,
    q_ref,
    kv_ref,
    dt_pre_ref,
    log_ref,
    state_ref,
    passing_ref,
    z_ref,
    xbc_ref,
    small_ref,
    normed_ext,
    ext_f32,
    sems,
    tick,
):
    rows, model = hidden_ref.shape
    groups = QHEADS // KVHEADS
    half_kv = KVW // 2
    first_row = lax.axis_index("seq") * rows
    pieces = [
        (0, 0, SSM // 2),
        (0, SSM // 2, SSM // 2),
        (1, 0, XBC // 2),
        (1, XBC // 2, XBC // 2),
        (2, 0, QW),
        (2, QW, KVW),
        (2, QW + KVW, DT_PAD),
    ]
    load_order = (2, 3, 4, 5, 6, 0, 1)
    weight_hbm, weight_refs = (z_hbm, xbc_hbm, small_hbm), (z_ref, xbc_ref, small_ref)
    copies = [
        pltpu.make_async_copy(
            weight_hbm[which].at[:, pl.ds(start, width)],
            weight_refs[which].at[:, pl.ds(start, width)],
            sems.at[number],
        )
        for number, (which, start, width) in enumerate(pieces)
    ]
    for number in load_order:
        copies[number].start()
    cosine_all, sine_all = rope_now(
        lax.axis_index("seq"), base_cos_ref, base_sin_ref, far_cos_ref, far_sin_ref
    )

    def norm(block):
        values = block.astype(jnp.float32)
        scale = lax.rsqrt(jnp.mean(values * values, axis=1, keepdims=True) + epsilon)
        return (values * scale * gain_ref[...]).astype(jnp.bfloat16)

    normed_ext[:HALO, :] = norm(halo_ref[...])
    normed = norm(hidden_ref[...])
    normed_ext[HALO:, :] = normed
    normed_ref[...] = normed

    def project(number, values):
        copies[number].wait()
        which, start, width = pieces[number]
        return jnp.dot(
            values,
            weight_refs[which][:, start : start + width],
            preferred_element_type=jnp.float32,
        )

    for number in (2, 3):
        _, start, width = pieces[number]
        part = project(number, normed_ext[...]).astype(jnp.bfloat16)
        ext_ref[:, start : start + width] = part
        ext_f32[:, start : start + width] = part.astype(jnp.float32)
    turned = rope_lanes(project(4, normed), cosine_all, sine_all).astype(jnp.bfloat16)
    turned = turned * jnp.bfloat16(HEAD_DIM ** (-0.5))
    for head in range(QHEADS):
        place = head % groups * rows
        q_ref[head // groups, place : place + rows, :] = turned[
            :, head * HEAD_DIM : (head + 1) * HEAD_DIM
        ]
    kv_raw = project(5, normed)
    kv_ref[:, :half_kv] = rope_lanes(
        kv_raw[:, :half_kv], cosine_all, sine_all
    ).astype(jnp.bfloat16)
    kv_ref[:, half_kv:] = kv_raw[:, half_kv:].astype(jnp.bfloat16)
    dt_pre = project(6, normed) + dt_bias_ref[...]
    dt_pre_ref[...] = dt_pre
    step_dt = jax.nn.softplus(dt_pre)
    order = lax.broadcasted_iota(jnp.int32, (rows, rows), 0)
    other = lax.broadcasted_iota(jnp.int32, (rows, rows), 1)
    lower = jnp.where(other <= order, 1.0, 0.0).astype(jnp.bfloat16)
    log_decay = dot_left(lower, -step_dt * jnp.exp(a_log_ref[...]), 3)
    log_ref[...] = log_decay
    for number in (0, 1):
        _, start, width = pieces[number]
        gate_ref[:, start : start + width] = project(number, normed)

    tick()
    starts_now = starts_ref[...]
    places = first_row + lax.broadcasted_iota(jnp.int32, (rows, 1), 0)
    pre = jnp.zeros((rows, XBC), jnp.float32) + bias_ref[...]
    for tap in range(CONV):
        lag = CONV - 1 - tap
        kept = jnp.where(places - lag >= starts_now, 1.0, 0.0)
        pre = pre + ext_f32[HALO - lag : HALO - lag + rows, :] * kept * tap_ref[tap : tap + 1, :]
    pre_ref[...] = pre
    conv_out = pre * jax.nn.sigmoid(pre)
    last = log_decay[rows - 1 : rows, :]
    last_start = starts_ref[rows - 1 : rows, :]
    weight = jnp.exp(jnp.where(places >= last_start, last - log_decay, masked)) * step_dt
    spread = dot_parts(weight, head_spread(), 2)
    state_ref[...] = matmul_pair(
        conv_out[:, :SSM] * spread, conv_out[:, SSM : SSM + STATE], TN
    ).reshape(state_ref.shape)
    passing = jnp.exp(last) * jnp.where(last_start < first_row, 1.0, 0.0)
    passing_ref[...] = jnp.broadcast_to(passing, passing_ref.shape)


def mixer_forward_shapes(rows, model):
    f32, low = jnp.float32, jnp.bfloat16
    shape = jax.ShapeDtypeStruct
    return [
        shape((rows, model), low),
        shape((rows, SSM), f32),
        shape((HALO + rows, XBC), low),
        shape((rows, XBC), f32),
        shape((KVHEADS, QHEADS // KVHEADS * rows, HEAD_DIM), low),
        shape((rows, KVW), low),
        shape((rows, DT_PAD), f32),
        shape((rows, DT_PAD), f32),
        shape((SSM, STATE), f32),
        shape((8, DT_PAD), f32),
    ]


def mixer_forward_scratch(rows, model, weights):
    return [pltpu.VMEM(w.shape, jnp.bfloat16) for w in weights] + [
        pltpu.VMEM((HALO + rows, model), jnp.bfloat16),
        pltpu.VMEM((HALO + rows, XBC), jnp.float32),
        pltpu.SemaphoreType.DMA((7,)),
    ]


def mixer_forward_specs():
    return [VMEM_SPEC] * 3 + [pl.BlockSpec(memory_space=pl.ANY)] * 3 + [VMEM_SPEC] * 9


def mixer_forward(args):
    rows, model = args[0].shape

    def kernel(*refs):
        mixer_forward_body(*refs, lambda: None)

    return pl.pallas_call(
        kernel,
        out_shape=mixer_forward_shapes(rows, model),
        in_specs=mixer_forward_specs(),
        out_specs=[VMEM_SPEC] * 10,
        scratch_shapes=mixer_forward_scratch(rows, model, args[3:6]),
        compiler_params=BIG_VMEM,
        name="mixer_forward",
    )(*args)


def document_mask(first_row, starts, rows, flip):
    if flip:
        token = lax.broadcasted_iota(jnp.int32, (rows, rows), 1)
        source = lax.broadcasted_iota(jnp.int32, (rows, rows), 0)
    else:
        token = lax.broadcasted_iota(jnp.int32, (rows, rows), 0)
        source = lax.broadcasted_iota(jnp.int32, (rows, rows), 1)
    allowed = (first_row + source >= starts) & (source <= token)
    return jnp.where(allowed, 0.0, masked)


def mixer_output_body(
    pre_ref,
    dt_pre_ref,
    log_ref,
    state,
    gate_ref,
    gain_ref,
    skip_ref,
    starts_ref,
    normed_ref,
    y_ref,
    input_ref,
):
    rows = pre_ref.shape[0]
    first_row = lax.axis_index("seq") * rows
    pre_now = pre_ref[...]
    conv_out = pre_now * jax.nn.sigmoid(pre_now)
    ssm_x = conv_out[:, :SSM]
    input_b = conv_out[:, SSM : SSM + STATE]
    output_c = conv_out[:, SSM + STATE :]
    spread = head_spread()
    log_decay_now = log_ref[...]
    log_rows = jnp.transpose(log_decay_now)
    step_dt = jax.nn.softplus(dt_pre_ref[...])
    scaled_x = ssm_x * dot_parts(step_dt, spread, 2)
    for part, piece in enumerate(stacked(scaled_x, False)):
        input_ref[part * rows : (part + 1) * rows, :] = piece
    carried = jnp.exp(log_decay_now) * jnp.where(starts_ref[...] < first_row, 1.0, 0.0)
    y_ref[...] = (
        matmul_pair(output_c, state, NT) * dot_parts(carried, spread, 2)
        + skip_ref[...] * ssm_x
    )
    affinity = matmul_pair(output_c, input_b, NT)
    closed = document_mask(first_row, starts_ref[...], rows, False)
    for pair in range(MHEADS // 2):
        found = []
        for head in (2 * pair, 2 * pair + 1):
            gap = log_decay_now[:, head : head + 1] - log_rows[head : head + 1, :] + closed
            mixing = affinity * jnp.exp(gap)
            found.append(
                jnp.dot(
                    jnp.concatenate(stacked(mixing, True), axis=1),
                    input_ref[:, head * MHEAD_DIM : (head + 1) * MHEAD_DIM],
                    preferred_element_type=jnp.float32,
                )
            )
        columns = slice(2 * pair * MHEAD_DIM, (2 * pair + 2) * MHEAD_DIM)
        y_ref[:, columns] += jnp.concatenate(found, axis=1)
    gate_now = gate_ref[...]
    gated = y_ref[...] * gate_now * jax.nn.sigmoid(gate_now)
    scale = lax.rsqrt(jnp.mean(gated * gated, axis=1, keepdims=True) + epsilon)
    normed_ref[...] = (gated * scale * gain_ref[...]).astype(jnp.bfloat16)


def mixer_output(pre, dt_pre, log_decay, states_in, gate_z, ssm_gain, skip_lanes, starts):
    rows = pre.shape[0]

    def kernel(*refs):
        mixer_output_body(*refs[:3], refs[3][...], *refs[4:])

    return pl.pallas_call(
        kernel,
        out_shape=mixer_output_shapes(rows),
        in_specs=[VMEM_SPEC] * 8,
        out_specs=[VMEM_SPEC] * 2,
        scratch_shapes=[pltpu.VMEM((3 * rows, SSM), jnp.bfloat16)],
        compiler_params=BIG_VMEM,
        name="mixer_output",
    )(
        pre,
        dt_pre,
        log_decay,
        states_in,
        gate_z,
        ssm_gain,
        skip_lanes,
        starts,
    )


def mixer_output_shapes(rows):
    return [
        jax.ShapeDtypeStruct((rows, SSM), jnp.bfloat16),
        jax.ShapeDtypeStruct((rows, SSM), jnp.float32),
    ]


def mixer_backward_body(
    grad_ref,
    y_ref,
    gate_ref,
    gain_ref,
    pre_ref,
    dt_pre_ref,
    log_ref,
    state_ref,
    skip_ref,
    starts_ref,
    starts_row_ref,
    grad_gate_ref,
    gain_grad_ref,
    grad_y_ref,
    state_grad_ref,
    input_grad_ref,
    b_grad_ref,
    c_grad_ref,
    log_grad_ref,
    skip_grad_ref,
    input_ref,
    low_ref,
    sums_ref,
    tick,
):
    rows = pre_ref.shape[0]
    first_row = lax.axis_index("seq") * rows
    gate_now = gate_ref[...]
    sigmoid_gate = jax.nn.sigmoid(gate_now)
    silu_gate = gate_now * sigmoid_gate
    y_now = y_ref[...]
    gated = y_now * silu_gate
    scale = lax.rsqrt(jnp.mean(gated * gated, axis=1, keepdims=True) + epsilon)
    grad_now = grad_ref[...]
    gain_grad_ref[...] = jnp.sum(gated * scale * grad_now, axis=0, keepdims=True)
    scaled = grad_now * gain_ref[...]
    grad_gated = scale * scaled - gated * (
        scale * scale * scale * jnp.mean(gated * scaled, axis=1, keepdims=True)
    )
    grad_gate_ref[...] = (
        grad_gated * y_now * sigmoid_gate * (1.0 + gate_now * (1.0 - sigmoid_gate))
    ).astype(jnp.bfloat16)
    grad_y = grad_gated * silu_gate
    grad_y_ref[...] = grad_y
    for part, piece in enumerate(stacked(grad_y, False)):
        low_ref[part * rows : (part + 1) * rows, :] = piece

    pre_now = pre_ref[...]
    conv_out = pre_now * jax.nn.sigmoid(pre_now)
    ssm_x = conv_out[:, :SSM]
    input_b = conv_out[:, SSM : SSM + STATE]
    output_c = conv_out[:, SSM + STATE :]
    spread = head_spread()
    log_decay_now = log_ref[...]
    log_rows = jnp.transpose(log_decay_now)
    step_dt = jax.nn.softplus(dt_pre_ref[...])
    scaled_x = ssm_x * dot_parts(step_dt, spread, 2)
    high, low, _ = stacked(scaled_x, True)
    input_ref[:rows, :] = high
    input_ref[rows:, :] = low
    carried = jnp.exp(log_decay_now) * jnp.where(starts_ref[...] < first_row, 1.0, 0.0)
    carried_lanes = dot_parts(carried, spread, 2)
    from_state = matmul_pair(output_c, state_ref[...], NT)
    log_grad = carried * dot_parts(grad_y * from_state, spread, 2, NT)
    grad_from_state = grad_y * carried_lanes
    state_grad_ref[...] = matmul_pair(grad_from_state, output_c, TN).reshape(state_grad_ref.shape)
    c_grad = matmul_pair(grad_from_state, state_ref[...], NN)
    skip_grad_ref[...] = dot_parts(
        jnp.sum(grad_y * ssm_x, axis=0, keepdims=True), spread, 3, NT
    )

    affinity = matmul_pair(input_b, output_c, NT)
    closed = document_mask(first_row, starts_row_ref[...], rows, True)
    affinity_grad = jnp.zeros((rows, rows), jnp.float32)
    sums_ref[...] = jnp.zeros(sums_ref.shape, jnp.float32)
    lane = lax.broadcasted_iota(jnp.int32, (rows, DT_PAD), 1)
    for pair in range(MHEADS // 2):
        found = []
        for head in (2 * pair, 2 * pair + 1):
            columns = slice(head * MHEAD_DIM, (head + 1) * MHEAD_DIM)
            gap = log_rows[head : head + 1, :] - log_decay_now[:, head : head + 1] + closed
            decay = jnp.exp(gap)
            mixing = affinity * decay
            found.append(
                jnp.dot(
                    jnp.concatenate(stacked(mixing, True), axis=1),
                    low_ref[:, columns],
                    preferred_element_type=jnp.float32,
                )
            )
            grad_mixing = jnp.zeros((rows, rows), jnp.float32)
            for one, two in ((0, 0), (1, 0), (0, 2)):
                grad_mixing = grad_mixing + lax.dot_general(
                    input_ref[one * rows : (one + 1) * rows, columns],
                    low_ref[two * rows : (two + 1) * rows, columns],
                    (NT, ((), ())),
                    preferred_element_type=jnp.float32,
                )
            affinity_grad = affinity_grad + grad_mixing * decay
            both = grad_mixing * mixing
            sums_ref[head : head + 1, :] = jnp.sum(both, axis=0, keepdims=True)
            log_grad = log_grad - jnp.where(
                lane == head, jnp.sum(both, axis=1, keepdims=True), 0.0
            )
        columns = slice(2 * pair * MHEAD_DIM, (2 * pair + 2) * MHEAD_DIM)
        input_grad_ref[:, columns] = jnp.concatenate(found, axis=1)
        if pair % 3 == 2:
            tick()
    log_grad_ref[...] = log_grad + jnp.transpose(sums_ref[...])
    b_grad_ref[...] = matmul_pair(affinity_grad, output_c, NN)
    c_grad_ref[...] = c_grad + matmul_pair(jnp.transpose(affinity_grad), input_b, NN)


def mixer_backward_shapes(rows, state_shape):
    f32 = jnp.float32
    shape = jax.ShapeDtypeStruct
    return [
        shape((rows, SSM), jnp.bfloat16),
        shape((1, SSM), f32),
        shape((rows, SSM), f32),
        shape(state_shape, f32),
        shape((rows, SSM), f32),
        shape((rows, STATE), f32),
        shape((rows, STATE), f32),
        shape((rows, DT_PAD), f32),
        shape((1, DT_PAD), f32),
    ]


def mixer_backward_scratch(rows):
    return [
        pltpu.VMEM((2 * rows, SSM), jnp.bfloat16),
        pltpu.VMEM((3 * rows, SSM), jnp.bfloat16),
        pltpu.VMEM((DT_PAD, rows), jnp.float32),
    ]


def mixer_backward(args):
    rows = args[0].shape[0]

    def kernel(*refs):
        mixer_backward_body(*refs, lambda: None)

    return pl.pallas_call(
        kernel,
        out_shape=mixer_backward_shapes(rows, (SSM, STATE)),
        in_specs=[VMEM_SPEC] * 11,
        out_specs=[VMEM_SPEC] * 9,
        scratch_shapes=mixer_backward_scratch(rows),
        compiler_params=BIG_VMEM,
        name="mixer_backward",
    )(*args)


def mixer_input_backward_body(
    end,
    state_ref,
    passing_ref,
    grad_y_ref,
    input_grad_ref,
    b_grad_ref,
    c_grad_ref,
    log_grad_ref,
    pre_ref,
    dt_pre_ref,
    log_ref,
    ext_ref,
    tap_ref,
    a_log_ref,
    skip_ref,
    starts_ref,
    raw_grad_ref,
    tap_grad_ref,
    bias_grad_ref,
    dt_grad_ref,
    dt_sum_ref,
    a_log_grad_ref,
    ext_f32,
    sum_ref,
    tick,
):
    rows = pre_ref.shape[0]
    first_row = lax.axis_index("seq") * rows
    tick()
    pre_now = pre_ref[...]
    sigmoid_pre = jax.nn.sigmoid(pre_now)
    conv_out = pre_now * sigmoid_pre
    ssm_x = conv_out[:, :SSM]
    input_b = conv_out[:, SSM : SSM + STATE]
    spread = head_spread()
    log_decay_now = log_ref[...]
    dt_pre_now = dt_pre_ref[...]
    step_dt = jax.nn.softplus(dt_pre_now)
    step_lanes = dot_parts(step_dt, spread, 2)
    starts_now = starts_ref[...]
    row = lax.broadcasted_iota(jnp.int32, (rows, 1), 0)
    places = first_row + row
    last = log_decay_now[rows - 1 : rows, :]
    last_start = starts_ref[rows - 1 : rows, :]
    weight = jnp.exp(jnp.where(places >= last_start, last - log_decay_now, masked))
    weight_lanes = dot_parts(weight, spread, 2)
    weighted = ssm_x * step_lanes * weight_lanes
    grad_weighted = matmul_pair(input_b, end, NT)
    b_total = b_grad_ref[...] + matmul_pair(weighted, end, NN)
    input_total = input_grad_ref[...] + grad_weighted * weight_lanes
    weight_term = dot_parts(grad_weighted * weighted, spread, 3, NT)
    state_dot = end * state_ref[...]
    passing_grad = jnp.sum(
        jnp.transpose(dot_left(spread, state_dot, 3)), axis=0, keepdims=True
    )
    log_grad_now = log_grad_ref[...] - weight_term
    end_term = jnp.sum(weight_term, axis=0, keepdims=True) + passing_grad * passing_ref[0:1, :]
    log_grad_now = log_grad_now + jnp.where(row == rows - 1, end_term, 0.0)
    order = lax.broadcasted_iota(jnp.int32, (rows, rows), 0)
    other = lax.broadcasted_iota(jnp.int32, (rows, rows), 1)
    upper = jnp.where(other >= order, 1.0, 0.0).astype(jnp.bfloat16)
    step_grad = dot_left(upper, log_grad_now, 3)
    rate = jnp.exp(a_log_ref[...])
    a_log_grad_ref[...] = jnp.sum(-step_dt * rate * step_grad, axis=0, keepdims=True)
    dt_grad = dot_parts(input_total * ssm_x, spread, 3, NT) - rate * step_grad
    dt_raw_grad = dt_grad * jax.nn.sigmoid(dt_pre_now)
    valid = lax.broadcasted_iota(jnp.int32, (rows, DT_PAD), 1) < MHEADS
    dt_raw_grad = jnp.where(valid, dt_raw_grad, 0.0)
    dt_grad_ref[...] = dt_raw_grad.astype(jnp.bfloat16)
    dt_sum_ref[...] = jnp.sum(dt_raw_grad, axis=0, keepdims=True)
    x_grad = input_total * step_lanes + skip_ref[...] * grad_y_ref[...]
    tick()
    slope = sigmoid_pre * (1.0 + pre_now * (1.0 - sigmoid_pre))
    pre_grad = jnp.concatenate([x_grad, b_total, c_grad_ref[...]], axis=1) * slope
    bias_grad_ref[...] = jnp.sum(pre_grad, axis=0, keepdims=True)
    ext_f32[...] = ext_ref[...].astype(jnp.float32)
    sum_ref[...] = jnp.zeros(sum_ref.shape, jnp.float32)
    for tap in range(CONV):
        lag = CONV - 1 - tap
        kept = pre_grad * jnp.where(places - lag >= starts_now, 1.0, 0.0)
        window = slice(HALO - lag, HALO - lag + rows)
        tap_grad_ref[tap : tap + 1, :] = jnp.sum(
            kept * ext_f32[window, :], axis=0, keepdims=True
        )
        sum_ref[window, :] += kept * tap_ref[tap : tap + 1, :]
    raw_grad_ref[...] = sum_ref[...]


def mixer_input_shapes(rows):
    f32 = jnp.float32
    shape = jax.ShapeDtypeStruct
    return [
        shape((HALO + rows, XBC), f32),
        shape((CONV, XBC), f32),
        shape((1, XBC), f32),
        shape((rows, DT_PAD), jnp.bfloat16),
        shape((1, DT_PAD), f32),
        shape((1, DT_PAD), f32),
    ]


def mixer_input_scratch(rows):
    return [pltpu.VMEM((HALO + rows, XBC), jnp.float32) for _ in range(2)]


def mixer_input_backward(args):
    rows = args[8].shape[0]

    def kernel(*refs):
        mixer_input_backward_body(refs[0][...], *refs[1:], lambda: None)

    return pl.pallas_call(
        kernel,
        out_shape=mixer_input_shapes(rows),
        in_specs=[VMEM_SPEC] * 16,
        out_specs=[VMEM_SPEC] * 6,
        scratch_shapes=mixer_input_scratch(rows),
        compiler_params=BIG_VMEM,
        name="mixer_input_backward",
    )(*args)


def feed_forward(hidden, normed_ssm, attention, ffn_gain, cotangent, late):
    rows, model = hidden.shape
    f32, low = jnp.float32, jnp.bfloat16
    ffn = late[0].shape[1]
    span = 1024
    steps = ffn // span

    def layout(flat, gate_up, down, ssm, out):
        pairs = [(flat[3], ssm), (flat[4], out)]
        for number in range(2):
            for start in range(0, ffn, span):
                pairs.append(
                    (
                        flat[number].at[:, pl.ds(start, span)],
                        gate_up.at[:, pl.ds(number * ffn + start, span)],
                    )
                )
        return pairs + [(flat[2], down)]

    kinds = len(late)
    early = 2
    total = early + 2 * steps + 1

    def kernel(*refs):
        hidden_ref, ssm_ref, attn_ref, gain_ref, cot_ref = refs[:5]
        flats = refs[5 : 5 + kinds]
        refs = refs[5 + kinds :]
        layer_ref, mix_ref, attn_grad_ref, ssm_grad_ref, gain_grad_ref = refs[:5]
        grad_flats = refs[5 : 5 + kinds]
        refs = refs[5 + kinds :]
        weights, grads = refs[:4], refs[4:8]
        gate_ref, up_ref, act_ref, two_ref, after_ref, grad_two_ref, in_sem, out_sem = refs[8:]
        w_gate_up, w_down, w_ssm, w_o = weights
        g_gate_up, g_down, g_ssm, g_o = grads
        loads = [
            pltpu.make_async_copy(source, target, in_sem.at[i])
            for i, (source, target) in enumerate(layout(flats, w_gate_up, w_down, w_ssm, w_o))
        ]
        for copy in loads:
            copy.start()
        stores = [
            pltpu.make_async_copy(source, target, out_sem.at[i])
            for i, (target, source) in enumerate(
                layout(grad_flats, g_gate_up, g_down, g_ssm, g_o)
            )
        ]

        def whole(ref, start=0, width=None):
            return ref[:, start : start + (ref.shape[1] if width is None else width)]

        def product(left_side, right_side, axes):
            return lax.dot_general(
                left_side, right_side, (axes, ((), ())), preferred_element_type=f32
            )

        def keep(ref, value, start=0):
            ref[:, start : start + value.shape[1]] = value.astype(low)

        for copy in loads[:early]:
            copy.wait()
        after = (
            hidden_ref[...].astype(f32)
            + product(ssm_ref[...], whole(w_ssm), NN)
            + product(attn_ref[...], whole(w_o), NN)
        )
        after_ref[...] = after
        scale = lax.rsqrt(jnp.mean(after * after, axis=1, keepdims=True) + epsilon)
        two_ref[...] = (after * scale * gain_ref[...]).astype(low)
        for step in range(steps):
            columns = slice(step * span, (step + 1) * span)
            loads[early + step].wait()
            loads[early + steps + step].wait()
            gate = product(two_ref[...], whole(w_gate_up, step * span, span), NN)
            up = product(two_ref[...], whole(w_gate_up, ffn + step * span, span), NN)
            gate_ref[:, columns] = gate
            up_ref[:, columns] = up
            act_ref[:, columns] = (gate * jax.nn.sigmoid(gate) * up).astype(low)
        for copy in loads[early + 2 * steps :]:
            copy.wait()
        layer_ref[...] = (after_ref[...] + product(act_ref[...], whole(w_down), NN)).astype(low)
        cot = cot_ref[...]
        grad_two = jnp.zeros((rows, model), f32)
        for step in range(steps):
            columns = slice(step * span, (step + 1) * span)
            w_part = w_down[columns, :]
            grad_act = product(cot, w_part, NT)
            gate, up = gate_ref[:, columns], up_ref[:, columns]
            sigmoid_gate = jax.nn.sigmoid(gate)
            grad_gate = (
                grad_act * up * sigmoid_gate * (1.0 + gate * (1.0 - sigmoid_gate))
            ).astype(low)
            grad_up = (grad_act * gate * sigmoid_gate).astype(low)
            grad_two = grad_two + product(
                grad_gate, whole(w_gate_up, step * span, span), NT
            )
            grad_two = grad_two + product(
                grad_up, whole(w_gate_up, ffn + step * span, span), NT
            )
            keep(g_gate_up, product(two_ref[...], grad_gate, TN), step * span)
            stores[early + step].start()
            keep(g_gate_up, product(two_ref[...], grad_up, TN), ffn + step * span)
            stores[early + steps + step].start()
        grad_two_ref[...] = grad_two
        keep(g_down, product(act_ref[...], cot, TN))
        for copy in stores[early + 2 * steps :]:
            copy.start()
        after = after_ref[...]
        grad_two = grad_two_ref[...]
        scale = lax.rsqrt(jnp.mean(after * after, axis=1, keepdims=True) + epsilon)
        gain_grad_ref[...] = jnp.sum(after * scale * grad_two, axis=0, keepdims=True)
        scaled = grad_two * gain_ref[...]
        mix = (
            cot.astype(f32)
            + scale * scaled
            - after * (scale * scale * scale * jnp.mean(after * scaled, axis=1, keepdims=True))
        )
        mix_ref[...] = mix
        mix_low = mix.astype(low)
        attn_grad = product(mix_low, whole(w_o), NT).astype(low)
        group_size = QHEADS // KVHEADS
        for head in range(QHEADS):
            place = head % group_size * rows
            attn_grad_ref[head // group_size, place : place + rows, :] = attn_grad[
                :, head * HEAD_DIM : (head + 1) * HEAD_DIM
            ]
        ssm_grad_ref[...] = product(mix_low, whole(w_ssm), NT)
        keep(g_ssm, product(ssm_ref[...], mix_low, TN))
        keep(g_o, product(attn_ref[...], mix_low, TN))
        for copy in stores[:early]:
            copy.start()
        for copy in stores:
            copy.wait()

    shape = jax.ShapeDtypeStruct
    hbm = pl.BlockSpec(memory_space=pl.ANY)
    buffers = [(late[0].shape[0], 2 * ffn)] + [w.shape for w in late[2:]]
    outs = pl.pallas_call(
        kernel,
        out_shape=[
            shape((rows, model), low),
            shape((rows, model), f32),
            shape((KVHEADS, QHEADS // KVHEADS * rows, HEAD_DIM), low),
            shape((rows, SSM), f32),
            shape((1, model), f32),
        ]
        + [shape(w.shape, low) for w in late],
        in_specs=[VMEM_SPEC] * 5 + [hbm] * kinds,
        out_specs=[VMEM_SPEC] * 5 + [hbm] * kinds,
        scratch_shapes=[pltpu.VMEM(size, low) for size in buffers + buffers]
        + [
            pltpu.VMEM((rows, ffn), f32),
            pltpu.VMEM((rows, ffn), f32),
            pltpu.VMEM((rows, ffn), low),
            pltpu.VMEM((rows, model), low),
            pltpu.VMEM((rows, model), f32),
            pltpu.VMEM((rows, model), f32),
            pltpu.SemaphoreType.DMA((total,)),
            pltpu.SemaphoreType.DMA((total,)),
        ],
        compiler_params=BIG_VMEM,
        name="feed_forward",
    )(hidden, normed_ssm, attention, ffn_gain[None], cotangent, *late)
    return outs[:5], outs[5:]


def projection_backward(
    normed_one,
    hidden,
    norm_gain,
    grad_mix,
    grad_gate_z,
    grad_ext,
    returned,
    grad_dt,
    grad_query,
    grad_kv,
    tables,
    weights,
):
    rows, model = hidden.shape
    f32, low = jnp.float32, jnp.bfloat16
    groups = QHEADS // KVHEADS
    half_kv = KVW // 2
    first_row = (lax.axis_index("seq") * rows).astype(jnp.int32).reshape(1)
    widths = [w.shape[1] for w in weights]

    def kernel(
        first_ref,
        normed_ref,
        hidden_ref,
        gain_ref,
        mix_ref,
        gate_ref,
        ext_ref,
        returned_ref,
        dt_ref,
        query_ref,
        kv_ref,
        base_cos_ref,
        base_sin_ref,
        far_cos_ref,
        far_sin_ref,
        *refs,
    ):
        weight_hbm, refs = refs[:3], refs[3:]
        input_ref, gain_grad_ref, refs = refs[0], refs[1], refs[2:]
        weight_grad_hbm, refs = refs[:3], refs[3:]
        weight_refs, weight_grad_refs, refs = refs[:3], refs[3:6], refs[6:]
        xbc_ref, small_ref, turned_ref, in_sem, out_sem = refs
        loads = [
            pltpu.make_async_copy(source, target, in_sem.at[i])
            for i, (source, target) in enumerate(zip(weight_hbm, weight_refs))
        ]
        for copy in loads:
            copy.start()
        stores = [
            pltpu.make_async_copy(source, target, out_sem.at[i])
            for i, (source, target) in enumerate(zip(weight_grad_refs, weight_grad_hbm))
        ]
        edge = rows - HALO
        xbc_ref[:edge, :] = ext_ref[HALO : HALO + edge, :].astype(low)
        xbc_ref[edge:, :] = (ext_ref[HALO + edge :, :] + returned_ref[...]).astype(low)
        for head in range(QHEADS):
            place = head % groups * rows
            turned_ref[:, head * HEAD_DIM : (head + 1) * HEAD_DIM] = jnp.transpose(
                query_ref[head // groups, :, place : place + rows]
            )
        cosine_all, sine_all = rope_now(
            first_ref[0] // rows, base_cos_ref, base_sin_ref, far_cos_ref, far_sin_ref
        )
        sine_all = -sine_all
        small_ref[:, :QW] = rope_lanes(
            turned_ref[...] * HEAD_DIM ** (-0.5), cosine_all, sine_all
        ).astype(low)
        kv = kv_ref[...]
        small_ref[:, QW : QW + half_kv] = rope_lanes(kv[:, :half_kv], cosine_all, sine_all).astype(
            low
        )
        small_ref[:, QW + half_kv : QW + KVW] = kv[:, half_kv:].astype(low)
        small_ref[:, QW + KVW :] = dt_ref[...]
        normed = normed_ref[...]
        grad_normed = jnp.zeros((rows, model), f32)
        for number, value_ref in enumerate((gate_ref, xbc_ref, small_ref)):
            loads[number].wait()
            for start in range(0, widths[number], 512):
                columns = slice(start, min(start + 512, widths[number]))
                part = value_ref[:, columns]
                grad_normed = grad_normed + lax.dot_general(
                    part,
                    weight_refs[number][:, columns],
                    (NT, ((), ())),
                    preferred_element_type=f32,
                )
                weight_grad_refs[number][:, columns] = lax.dot_general(
                    normed, part, (TN, ((), ())), preferred_element_type=f32
                ).astype(low)
            stores[number].start()
        values = hidden_ref[...].astype(f32)
        scale = lax.rsqrt(jnp.mean(values * values, axis=1, keepdims=True) + epsilon)
        gain_grad_ref[...] = jnp.sum(values * scale * grad_normed, axis=0, keepdims=True)
        scaled = grad_normed * gain_ref[...]
        input_ref[...] = (
            mix_ref[...]
            + scale * scaled
            - values * (scale * scale * scale * jnp.mean(values * scaled, axis=1, keepdims=True))
        ).astype(low)
        for copy in stores:
            copy.wait()

    shape = jax.ShapeDtypeStruct
    hbm = pl.BlockSpec(memory_space=pl.ANY)
    return pl.pallas_call(
        kernel,
        out_shape=[shape((rows, model), low), shape((1, model), f32)]
        + [shape(w.shape, low) for w in weights],
        in_specs=[pl.BlockSpec(memory_space=pltpu.SMEM)] + [VMEM_SPEC] * 14 + [hbm] * 3,
        out_specs=[VMEM_SPEC] * 2 + [hbm] * 3,
        scratch_shapes=[pltpu.VMEM(w.shape, low) for w in list(weights) * 2]
        + [
            pltpu.VMEM((rows, XBC), low),
            pltpu.VMEM((rows, QW + KVW + DT_PAD), low),
            pltpu.VMEM((rows, QW), f32),
            pltpu.SemaphoreType.DMA((3,)),
            pltpu.SemaphoreType.DMA((3,)),
        ],
        compiler_params=BIG_VMEM,
        name="projection_backward",
    )(
        first_row,
        normed_one,
        hidden,
        norm_gain[None],
        grad_mix,
        grad_gate_z,
        grad_ext,
        returned,
        grad_dt,
        grad_query,
        grad_kv,
        *tables,
        *weights,
    )


def projection_scatter(
    normed_one,
    hidden,
    norm_gain,
    grad_mix,
    grad_gate_z,
    grad_ext,
    grad_dt,
    grad_query,
    grad_kv,
    tables,
    weights,
    small_parts,
    small_rows,
    collective_id,
    target,
):
    rows, model = hidden.shape
    f32, low = jnp.float32, jnp.bfloat16
    groups = QHEADS // KVHEADS
    half_kv = KVW // 2
    first_row = (lax.axis_index("seq") * rows).astype(jnp.int32).reshape(1)
    widths = [w.shape[1] for w in weights]
    count = lax.axis_size("seq")
    sizes = lattice(count)
    shapes = [(w.shape[0] // count, w.shape[1]) for w in weights]
    small = jax.ShapeDtypeStruct((small_rows, 128), jnp.float32)
    plans = [
        scatter_plan([s], small if number == 1 else None, target)
        for number, s in enumerate(shapes)
    ]

    def kernel(
        first_ref,
        normed_ref,
        hidden_ref,
        gain_ref,
        mix_ref,
        gate_ref,
        ext_ref,
        dt_ref,
        query_ref,
        kv_ref,
        base_cos_ref,
        base_sin_ref,
        far_cos_ref,
        far_sin_ref,
        *refs,
    ):
        small_in, refs = refs[: len(small_parts)], refs[len(small_parts) :]
        weight_hbm, refs = refs[:3], refs[3:]
        input_ref, shard_refs, small_out, refs = refs[0], refs[1:4], refs[4], refs[5:]
        weight_refs, weight_grad_refs, refs = refs[:3], refs[3:6], refs[6:]
        xbc_ref, small_ref, turned_ref, returned_ref, small_vmem, in_sem, edge_sems = refs[:7]
        refs = refs[7:]
        runs = []
        for number, (program, scratch) in enumerate(plans):
            mine, refs = refs[: len(scratch)], refs[len(scratch) :]
            has_small = number == 1
            runs.append(
                program(
                    [weight_grad_refs[number]],
                    [small_vmem] if has_small else [],
                    [shard_refs[number]],
                    [small_out] if has_small else [],
                    mine,
                )
            )
        me = lax.axis_index("seq")
        following, previous = lax.rem(me + 1, count), lax.rem(me + count - 1, count)
        loads = [
            pltpu.make_async_copy(source, target, in_sem.at[i])
            for i, (source, target) in enumerate(zip(weight_hbm, weight_refs))
        ]
        for copy in loads:
            copy.start()
        greet(sizes, coordinates(sizes), [following, previous])
        edge_copy = pltpu.make_async_remote_copy(
            src_ref=ext_ref.at[pl.ds(0, HALO), :],
            dst_ref=returned_ref,
            send_sem=edge_sems.at[0],
            recv_sem=edge_sems.at[1],
            device_id=(previous,),
            device_id_type=MESH,
        )
        edge_copy.start()
        small_vmem[...] = jnp.zeros(small.shape, f32)
        row = model // 128
        for part_ref in small_in:
            for line in range(part_ref.shape[0]):
                for step in range(part_ref.shape[1] // 128):
                    small_vmem[row : row + 1, :] = part_ref[
                        line : line + 1, step * 128 : (step + 1) * 128
                    ]
                    row += 1
        edge = rows - HALO
        xbc_ref[:edge, :] = ext_ref[HALO : HALO + edge, :].astype(low)
        for head in range(QHEADS):
            place = head % groups * rows
            turned_ref[:, head * HEAD_DIM : (head + 1) * HEAD_DIM] = jnp.transpose(
                query_ref[head // groups, :, place : place + rows]
            )
        cosine_all, sine_all = rope_now(
            first_ref[0] // rows, base_cos_ref, base_sin_ref, far_cos_ref, far_sin_ref
        )
        sine_all = -sine_all
        small_ref[:, :QW] = rope_lanes(
            turned_ref[...] * HEAD_DIM ** (-0.5), cosine_all, sine_all
        ).astype(low)
        kv = kv_ref[...]
        small_ref[:, QW : QW + half_kv] = rope_lanes(kv[:, :half_kv], cosine_all, sine_all).astype(
            low
        )
        small_ref[:, QW + half_kv : QW + KVW] = kv[:, half_kv:].astype(low)
        small_ref[:, QW + KVW :] = dt_ref[...]
        normed = normed_ref[...]
        grad_normed = jnp.zeros((rows, model), f32)
        for number, value_ref in ((0, gate_ref), (2, small_ref), (1, xbc_ref)):
            loads[number].wait()
            if number == 1:
                edge_copy.wait()
                xbc_ref[edge:, :] = (ext_ref[HALO + edge :, :] + returned_ref[...]).astype(low)
            for start in range(0, widths[number], 512):
                columns = slice(start, min(start + 512, widths[number]))
                part = value_ref[:, columns]
                weight_grad_refs[number][..., columns] = (
                    lax.dot_general(normed, part, (TN, ((), ())), preferred_element_type=f32)
                    .astype(low)
                    .reshape(*sizes, shapes[number][0], part.shape[1])
                )
            next(runs[number])
            for start in range(0, widths[number], 512):
                columns = slice(start, min(start + 512, widths[number]))
                grad_normed = grad_normed + lax.dot_general(
                    value_ref[:, columns],
                    weight_refs[number][:, columns],
                    (NT, ((), ())),
                    preferred_element_type=f32,
                )
            if number != 1:
                next(runs[number])
        values = hidden_ref[...].astype(f32)
        scale = lax.rsqrt(jnp.mean(values * values, axis=1, keepdims=True) + epsilon)
        gain_grad = jnp.sum(values * scale * grad_normed, axis=0, keepdims=True)
        for step in range(model // 128):
            small_vmem[step : step + 1, :] = gain_grad[:, step * 128 : (step + 1) * 128]
        scaled = grad_normed * gain_ref[...]
        input_ref[...] = (
            mix_ref[...]
            + scale * scaled
            - values * (scale * scale * scale * jnp.mean(values * scaled, axis=1, keepdims=True))
        ).astype(low)
        run_together([runs[1], runs[0], runs[2]])

    shape = jax.ShapeDtypeStruct
    hbm = pl.BlockSpec(memory_space=pl.ANY)
    return pl.pallas_call(
        kernel,
        out_shape=[shape((rows, model), low)]
        + [shape(s, f32) for s in shapes]
        + [shape(small.shape, f32)],
        in_specs=[pl.BlockSpec(memory_space=pltpu.SMEM)]
        + [VMEM_SPEC] * (13 + len(small_parts))
        + [hbm] * 3,
        out_specs=[VMEM_SPEC] * 5,
        scratch_shapes=[pltpu.VMEM(w.shape, low) for w in weights]
        + [pltpu.VMEM(sizes + s, low) for s in shapes]
        + [
            pltpu.VMEM((rows, XBC), low),
            pltpu.VMEM((rows, QW + KVW + DT_PAD), low),
            pltpu.VMEM((rows, QW), f32),
            pltpu.VMEM((HALO, XBC), f32),
            pltpu.VMEM(small.shape, f32),
            pltpu.SemaphoreType.DMA((3,)),
            pltpu.SemaphoreType.DMA((2,)),
        ]
        + [item for _, scratch in plans for item in scratch],
        compiler_params=pltpu.CompilerParams(
            collective_id=collective_id,
            has_side_effects=True,
            vmem_limit_bytes=62 * 1024 * 1024,
        ),
        name="projection_scatter",
    )(
        first_row,
        normed_one,
        hidden,
        norm_gain[None],
        grad_mix,
        grad_gate_z,
        grad_ext,
        grad_dt,
        grad_query,
        grad_kv,
        *tables,
        *small_parts,
        *weights,
    )


def finish(shard_z, shard_xbc, shard_small, small_sum, late_sums, lengths):
    f32 = jnp.float32
    shape = jax.ShapeDtypeStruct
    rows = shard_z.shape[0]
    starts = [sum(lengths[:i]) // 128 for i in range(len(lengths))]
    tail = sum(lengths) // 128
    tap_rows = XBC // 128
    model_rows, ssm_rows = lengths[0] // 128, lengths[1] // 128

    def kernel(z_ref, xbc_ref, small_ref, sum_ref, *refs):
        late, refs = refs[: len(late_sums)], refs[len(late_sums) :]
        outs, refs = refs[: len(late_sums)], refs[len(late_sums) :]
        for source, target in zip(late, outs):
            target[...] = source[...]
        z_out, xbc_out, q_out, kv_out, dt_out, *vectors, tap_out, three_out = refs
        z_out[...] = z_ref[...]
        xbc_out[...] = xbc_ref[...]
        q_out[...] = small_ref[:, :QW]
        kv_out[...] = small_ref[:, QW : QW + KVW]
        dt_out[...] = small_ref[:, QW + KVW :]
        for target, start in zip(vectors, (starts[0], starts[1], starts[2], starts[4])):
            target[...] = sum_ref[start : start + target.shape[0], :]
        for tap in range(CONV):
            for step in range(tap_rows):
                row = starts[3] + tap * tap_rows + step
                tap_out[tap : tap + 1, step * 128 : (step + 1) * 128] = sum_ref[row : row + 1, :]
        three_out[...] = sum_ref[tail : tail + 8, :]

    results = pl.pallas_call(
        kernel,
        out_shape=[shape(s.shape, f32) for s in late_sums]
        + [shape(shard_z.shape, f32), shape(shard_xbc.shape, f32)]
        + [shape((rows, width), f32) for width in (QW, KVW, DT_PAD)]
        + [shape((n, 128), f32) for n in (model_rows, ssm_rows, model_rows, tap_rows)]
        + [shape((CONV, XBC), f32), shape((8, 128), f32)],
        in_specs=[VMEM_SPEC] * (4 + len(late_sums)),
        out_specs=[VMEM_SPEC] * (11 + len(late_sums)),
        name="finish",
    )(shard_z, shard_xbc, shard_small, small_sum, *late_sums)
    return results[: len(late_sums)], results[len(late_sums) :]


def per_device(
    hidden_in,
    doc_start,
    norm_gain,
    w_z,
    w_xbc,
    w_dt,
    conv_weight,
    conv_bias,
    dt_bias,
    a_log,
    d_skip,
    ssm_gain,
    w_ssm_out,
    w_q,
    w_kv,
    w_o,
    ffn_gain,
    w_gate,
    w_up,
    w_down,
    cotangent,
):
    local_rows, model = hidden_in.shape
    count = lax.axis_size("seq")
    group_size = QHEADS // KVHEADS
    small_shard = jnp.concatenate(
        [w_q, w_kv, jnp.pad(w_dt, ((0, 0), (0, DT_PAD - MHEADS)))], axis=1
    )
    *mixer_weights, halo = gather_everywhere(
        [w_xbc, small_shard, w_z], 0, 12288, hidden_in
    )
    mixer_weights = [mixer_weights[2], mixer_weights[0], mixer_weights[1]]

    tables = rope_table(local_rows, count)
    dt_bias_row = jnp.pad(dt_bias, (0, DT_PAD - MHEADS))[None]
    a_log_row = jnp.pad(a_log, (0, DT_PAD - MHEADS))[None]
    skip_lanes = jnp.repeat(d_skip, MHEAD_DIM)[None]
    row_starts = jnp.tile(doc_start, group_size)[None]
    kv_all, states_in, chip_decay, late, computed = front(
        [
            hidden_in,
            halo,
            norm_gain[None],
            *mixer_weights,
            conv_weight,
            conv_bias[None],
            dt_bias_row,
            a_log_row,
            doc_start[:, None],
            *tables,
        ],
        [w_gate, w_up, w_down, w_ssm_out, w_o],
        [ssm_gain[None], skip_lanes, doc_start[:, None]],
        row_starts,
        1,
        (16384, 16384),
    )
    normed_one, gate_z, xbc_ext, conv_pre, grouped_q, dt_pre, log_decay, passing = computed[:8]
    normed_ssm, ssm_y, attn_grouped, log_total, attn_low = computed[8:]
    (layer_out, grad_mix, grad_attn_grouped, grad_normed_ssm, grad_ffn_gain), late_grads = (
        feed_forward(hidden_in, normed_ssm, attn_low, ffn_gain, cotangent, late)
    )
    key_terms, grad_query_grouped, late_sums = attention_backward(
        grouped_q,
        grad_attn_grouped,
        kv_all,
        row_starts,
        log_total,
        attn_grouped,
        late_grads[:2],
        4,
        16384,
    )
    shard_gate, shard_up = late_sums

    grad_kv_local, late_sums, mixer_out = back(
        key_terms,
        [
            grad_normed_ssm,
            ssm_y,
            gate_z,
            ssm_gain[None],
            conv_pre,
            dt_pre,
            log_decay,
            states_in,
            skip_lanes,
            doc_start[:, None],
            doc_start[None],
        ],
        [xbc_ext, conv_weight, a_log_row],
        passing,
        chip_decay,
        late_grads[2:],
        2,
        (16384, 8192),
    )
    shard_down, shard_ssm_out, shard_o = late_sums
    (
        grad_gate_z,
        grad_ssm_gain,
        grad_d_skip,
        grad_ext,
        grad_conv_weight,
        grad_conv_bias,
        grad_dt_raw,
        grad_dt_bias,
        grad_a_log,
    ) = mixer_out
    rows_small = -(-(model // 128 * 2 + SSM // 128 + (CONV + 1) * XBC // 128 + 8) // 8) * 8
    lengths = [model, SSM, model, CONV * XBC, XBC]
    small_parts = [
        grad_ssm_gain,
        grad_ffn_gain,
        grad_conv_weight,
        grad_conv_bias,
        grad_dt_bias,
        grad_a_log,
        grad_d_skip,
    ]
    grad_args = (
        normed_one,
        hidden_in,
        norm_gain,
        grad_mix,
        grad_gate_z,
        grad_ext,
    )
    last_args = (grad_dt_raw, grad_query_grouped, grad_kv_local, tables, mixer_weights)
    if w_gate.shape[0] % 16 == 0:
        grad_input, shard_z, shard_xbc, shard_small, small_sum = projection_scatter(
            *grad_args, *last_args, small_parts, rows_small, 3, 12288
        )
    else:
        returned = from_behind(grad_ext[:HALO], "seq", -1)
        grad_input, grad_norm_gain, *mixer_grads = projection_backward(
            *grad_args, returned, *last_args
        )
        small = jnp.concatenate(
            [part.reshape(-1, 128) for part in [grad_norm_gain] + small_parts], axis=0
        )
        small = jnp.pad(small, ((0, rows_small - small.shape[0]), (0, 0)))
        shard_z, shard_xbc, shard_small, small_sum = scatter_sums(mixer_grads, small, 3, 8192)
    late_shards, others = finish(
        shard_z,
        shard_xbc,
        shard_small,
        small_sum,
        [shard_gate, shard_up, shard_down, shard_ssm_out, shard_o],
        lengths,
    )
    shard_gate, shard_up, shard_down, shard_ssm_out, shard_o = late_shards
    shard_z, shard_xbc, shard_q, shard_kv, shard_dt, *vectors, sum_taps, sum_three = others
    sum_norm, sum_ssm_gain, sum_ffn_gain, sum_conv_bias = [v.reshape(-1) for v in vectors]
    return (
        layer_out,
        grad_input,
        sum_norm,
        shard_z,
        shard_xbc,
        shard_dt[:, :MHEADS],
        sum_taps,
        sum_conv_bias,
        sum_three[0, :MHEADS],
        sum_three[1, :MHEADS],
        sum_three[2, :MHEADS],
        sum_ssm_gain,
        shard_ssm_out,
        shard_q,
        shard_kv,
        shard_o,
        sum_ffn_gain,
        shard_gate,
        shard_up,
        shard_down,
    )


def solution(mesh):
    placed = (
        P("seq", None),
        P("seq"),
        P(),
        P("seq", None),
        P("seq", None),
        P("seq", None),
        P(),
        P(),
        P(),
        P(),
        P(),
        P(),
        P("seq", None),
        P("seq", None),
        P("seq", None),
        P("seq", None),
        P(),
        P("seq", None),
        P("seq", None),
        P("seq", None),
        P("seq", None),
    )
    return jax.shard_map(
        per_device,
        mesh=mesh,
        in_specs=placed,
        out_specs=(
            P("seq", None),
            P("seq", None),
            P(),
            P("seq", None),
            P("seq", None),
            P("seq", None),
            P(),
            P(),
            P(),
            P(),
            P(),
            P(),
            P("seq", None),
            P("seq", None),
            P("seq", None),
            P("seq", None),
            P(),
            P("seq", None),
            P("seq", None),
            P("seq", None),
        ),
        check_vma=False,
    )
```

```python
from functools import partial
import math

import jax
import jax.numpy as jnp
from jax import lax
from jax.experimental import pallas as pl
from jax.experimental.pallas import tpu as pltpu
from jax.sharding import PartitionSpec as P
import numpy as np

MHEADS = 24
MHEAD_DIM = 64
STATE = 128
CONV = 4
QHEADS = 8
KVHEADS = 2
HEAD_DIM = 64
SSM = 1536
XBC = 1792
QW = 512
KVW = 256
DT_PAD = 128


epsilon = 1e-05
rope_base = 100000000000.0
masked = -1e30


def from_behind(value, axis, steps):
    count = lax.axis_size(axis)
    first, last = (max(0, -steps), min(count, count - steps))
    return lax.ppermute(value, axis, [(source, source + steps) for source in range(first, last)])


MESH = pl.DeviceIdType.MESH
HALO = 16
VMEM_SPEC = pl.BlockSpec(memory_space=pltpu.VMEM)


def lattice(count):
    sizes, left, turn = [1, 1, 1], count // 2, 0
    while left > 1:
        factor = 2 if left % 2 == 0 else left
        sizes[turn % 3] *= factor
        left //= factor
        turn += 1
    return sizes[0], sizes[1], sizes[2], 2


def coordinates(sizes):
    me = lax.axis_index("seq")
    _, size_1, size_2, cores = sizes
    return (
        me // (size_1 * size_2 * cores),
        me // (size_2 * cores) % size_1,
        me // cores % size_2,
        me % cores,
    )


def device_at(sizes, place):
    index = place[0]
    for size, at in zip(sizes[1:], place[1:]):
        index = index * size + at
    return index


def partners(sizes, place, axis):
    found = []
    for step in range(1, sizes[axis]):
        other = list(place)
        other[axis] = (place[axis] + step) % sizes[axis]
        found.append(other)
    return found


def greet(sizes, place, more=()):
    barrier = pltpu.get_barrier_semaphore()
    met = [
        device_at(sizes, other) for axis in range(4) for other in partners(sizes, place, axis)
    ] + list(more)
    for other in met:
        pl.semaphore_signal(barrier, inc=1, device_id=(other,), device_id_type=MESH)
    pl.semaphore_wait(barrier, len(met))


def block_cuts(shapes, target):
    cuts = []
    for number, (rows, columns) in enumerate(shapes):
        pieces = max(1, round(rows * columns / target))
        width = max(128, (columns // pieces + 127) // 128 * 128)
        across = -(-columns // width)
        height = rows
        if across < pieces and rows % 32 == 0:
            height = max(32, rows // -(-pieces // across) // 32 * 32)
        for top in range(0, rows, height):
            for start in range(0, columns, width):
                size = (min(height, rows - top), min(width, columns - start))
                cuts.append((number, (pl.ds(top, size[0]), pl.ds(start, size[1]))))
    return cuts


def run_together(programs):
    waiting = list(programs)
    while waiting:
        for program in list(waiting):
            try:
                next(program)
            except StopIteration:
                waiting.remove(program)


ORDERS = ((0, 1, 2), (0, 2, 1))


def axis_order(turn):
    return ORDERS[turn % len(ORDERS)]


def tick_count(cuts, stages):
    return -(-len(cuts) // len(ORDERS)) + stages - 1


def tick_turns(cuts, number):
    first = number * len(ORDERS)
    return range(first, min(first + len(ORDERS), len(cuts))) if number >= 0 else range(0)


def gather_program(sizes, cuts, ins, outs, local_sem, send_sem, recv_sem, depth=1000):
    place = coordinates(sizes)
    sibling = partners(sizes, place, 3)[0]

    def region(turn, at):
        number, window = cuts[turn]
        return outs[number].at[*at, *window]

    def before(axis, step):
        at = list(place)
        at[axis] = (place[axis] - step - 1 + sizes[axis]) % sizes[axis]
        return at

    def widened(order, stage, at):
        full = list(at)
        for axis in order[:stage]:
            full[axis] = slice(None)
        return full

    def remote(turn, slot, step, source, target, other):
        return pltpu.make_async_remote_copy(
            src_ref=source,
            dst_ref=target,
            send_sem=send_sem.at[turn, slot, step],
            recv_sem=recv_sem.at[turn, slot, step],
            device_id=(device_at(sizes, other),),
            device_id_type=MESH,
        )

    def outgoing(turn, stage, step):
        order = axis_order(turn)
        here = region(turn, widened(order, stage, place))
        number, window = cuts[turn]
        source = ins[number].at[*window] if stage == 0 else here
        other = partners(sizes, place, order[stage])[step]
        return remote(turn, stage, step, source, here, other)

    def incoming(turn, stage, step):
        order = axis_order(turn)
        here = region(turn, widened(order, stage, before(order[stage], step)))
        return remote(turn, stage, step, here, here, sibling)

    def fresh(turn, stage, step, core):
        order = axis_order(turn)
        if stage == 0:
            at = widened(order, 1, place)
        else:
            at = widened(order, stage, before(order[stage], step))
        at[3] = core
        return region(turn, at)

    def across(turn, stage, step):
        here = fresh(turn, stage, step, place[3])
        return remote(turn, 3 + stage, step, here, here, sibling)

    def from_across(turn, stage, step):
        here = fresh(turn, stage, step, sibling[3])
        return remote(turn, 3 + stage, step, here, here, sibling)

    def hops(turn, stage):
        return range(sizes[axis_order(turn)[stage]] - 1)

    def pieces(turn, stage):
        return range(1) if stage == 0 else hops(turn, stage)

    def local(turn):
        number, window = cuts[turn]
        return pltpu.make_async_copy(
            ins[number].at[*window], region(turn, list(place)), local_sem.at[turn]
        )

    def launch(number):
        for turn in tick_turns(cuts, number):
            for step in hops(turn, 0):
                outgoing(turn, 0, step).start()

    for turn in range(len(cuts)):
        local(turn).start()
    for number in range(min(depth, len(cuts))):
        launch(number)
    yield

    def advance(turn, stage):
        for step in hops(turn, stage):
            incoming(turn, stage, step).wait_recv()
        if stage == 0:
            local(turn).wait()
        if stage < 2:
            for step in hops(turn, stage + 1):
                outgoing(turn, stage + 1, step).start()
        for step in pieces(turn, stage):
            across(turn, stage, step).start()

    for tick in range(tick_count(cuts, 3)):
        launch(tick + depth)
        for stage in range(3):
            for turn in tick_turns(cuts, tick - stage):
                advance(turn, stage)
        yield
    for turn in range(len(cuts)):
        for stage in range(3):
            for step in pieces(turn, stage):
                from_across(turn, stage, step).wait_recv()
            for step in pieces(turn, stage):
                across(turn, stage, step).wait_send()
            for step in hops(turn, stage):
                outgoing(turn, stage, step).wait_send()


def gather_scratch(sizes, cuts):
    most = max(sizes[:3])
    return [
        pltpu.SemaphoreType.DMA((len(cuts),)),
        pltpu.SemaphoreType.DMA((len(cuts), 6, most)),
        pltpu.SemaphoreType.DMA((len(cuts), 6, most)),
    ]


def gather_everywhere(arrays, collective_id, target, edge):
    sizes = lattice(lax.axis_size("seq"))
    cuts = block_cuts([array.shape for array in arrays], target)
    kinds = len(arrays)

    def kernel(*refs):
        ins, edge_in, refs = refs[:kinds], refs[kinds], refs[kinds + 1 :]
        outs, edge_out, refs = refs[:kinds], refs[kinds], refs[kinds + 1 :]
        *sems, edge_sems = refs
        me, count = lax.axis_index("seq"), lax.axis_size("seq")
        following, previous = lax.rem(me + 1, count), lax.rem(me + count - 1, count)
        greet(sizes, coordinates(sizes), [following, previous])
        edge_copy = pltpu.make_async_remote_copy(
            src_ref=edge_in.at[pl.ds(edge.shape[0] - HALO, HALO), :],
            dst_ref=edge_out,
            send_sem=edge_sems.at[0],
            recv_sem=edge_sems.at[1],
            device_id=(following,),
            device_id_type=MESH,
        )
        edge_copy.start()
        run_together([gather_program(sizes, cuts, ins, outs, *sems)])
        edge_copy.wait()

    hbm = pl.BlockSpec(memory_space=pl.ANY)
    gathered = pl.pallas_call(
        kernel,
        out_shape=[jax.ShapeDtypeStruct(sizes + a.shape, a.dtype) for a in arrays]
        + [jax.ShapeDtypeStruct((HALO, edge.shape[1]), edge.dtype)],
        in_specs=[hbm] * (kinds + 1),
        out_specs=[hbm] * (kinds + 1),
        scratch_shapes=gather_scratch(sizes, cuts) + [pltpu.SemaphoreType.DMA((2,))],
        compiler_params=pltpu.CompilerParams(
            collective_id=collective_id,
            has_side_effects=True,
            vmem_limit_bytes=62 * 1024 * 1024,
        ),
        name="gather_everywhere",
    )(*arrays, edge)
    return [g.reshape(-1, a.shape[1]) for g, a in zip(gathered, arrays)] + [gathered[kinds]]


def scatter_plan(shapes, small, target):
    sizes = lattice(lax.axis_size("seq"))
    cuts = block_cuts(shapes, target)
    kinds = len(shapes)
    most = max(sizes[:3])
    used = [axis_order(turn)[::-1] for turn in range(len(cuts))]
    pairs = [[[axis for axis in range(3) if axis != axes[0]] for axes in used]][0]
    first_lead = tuple(max(sizes[pair[i]] for pair in pairs) for i in range(2))
    first_step = max(sizes[axes[0]] for axes in used) - 1
    second_lead = max(sizes[axes[2]] for axes in used)
    second_step = max(sizes[axes[1]] for axes in used) - 1
    last_step = max(sizes[axes[2]] for axes in used) - 1
    extra = 0 if small is None else 1

    def program(ins, small_in, outs, small_out, refs):
        own, core_in, first_in, second_in, last_in = [
            refs[i * kinds : (i + 1) * kinds] for i in range(5)
        ]
        refs = refs[5 * kinds :]
        local_sem, send_sem, recv_sem = refs[:3]
        place = coordinates(sizes)
        sibling = partners(sizes, place, 3)[0]
        sent = []

        def push(source, target_ref, other, sems, slot):
            copy = pltpu.make_async_remote_copy(
                src_ref=source,
                dst_ref=target_ref,
                send_sem=sems[0].at[slot],
                recv_sem=sems[1].at[slot],
                device_id=(device_at(sizes, other),),
                device_id_type=MESH,
            )
            copy.start()
            sent.append(copy)

        def arrival(here, sems, slot):
            pltpu.make_async_remote_copy(
                src_ref=here,
                dst_ref=here,
                send_sem=sems[0].at[slot],
                recv_sem=sems[1].at[slot],
                device_id=(device_at(sizes, sibling),),
                device_id_type=MESH,
            ).wait_recv()

        main_sems = (send_sem, recv_sem)

        def core_copy(turn):
            number, window = cuts[turn]
            return pltpu.make_async_remote_copy(
                src_ref=ins[number].at[:, :, :, sibling[3], *window],
                dst_ref=core_in[number].at[:, :, :, *window],
                send_sem=send_sem.at[turn, 0, 0],
                recv_sem=recv_sem.at[turn, 0, 0],
                device_id=(device_at(sizes, sibling),),
                device_id_type=MESH,
            )

        def local_copy(turn):
            number, window = cuts[turn]
            return pltpu.make_async_copy(
                ins[number].at[:, :, :, place[3], *window],
                own[number].at[:, :, :, *window],
                local_sem.at[turn],
            )

        for turn in range(len(cuts)):
            core_copy(turn).start()
            local_copy(turn).start()
        yield

        def kept(number, window, axes, stage, at):
            index = [slice(None), slice(None), slice(None)]
            for axis in axes[:stage]:
                index[axis] = at[axis]
            return own[number].at[*index, *window]

        def landed(number, window, axes, stage, step):
            if stage == 3:
                return last_in[number].at[step, *window]
            left = [sizes[axis] for axis in range(3) if axis not in axes[:stage]]
            box = (first_in, second_in)[stage - 1][number]
            return box.at[step, *[pl.ds(0, size) for size in left], *window]

        def advance(turn, stage):
            number, window = cuts[turn]
            axes = axis_order(turn)[::-1]
            lead = tuple(sizes[axis] for axis in range(3) if axis not in axes[:stage])
            if stage == 0:
                local_copy(turn).wait()
                arrival(core_in[number].at[:, :, :, *window], main_sems, (turn, 0, 0))
                pieces = [core_in[number].at[:, :, :, *window]]
            else:
                steps = range(sizes[axes[stage - 1]] - 1)
                pieces = [landed(number, window, axes, stage, step) for step in steps]
                for step in steps:
                    arrival(pieces[step], main_sems, (turn, stage, step))
            target_ref = kept(number, window, axes, stage, place)

            def total(index):
                value = target_ref[index].astype(jnp.float32)
                for piece in pieces:
                    value = value + piece[index].astype(jnp.float32)
                return value

            if stage == 3:
                outs[number][window] = total((...,))
                return
            amount = math.prod(lead)

            def add(flat, carry):
                index, rest = [], flat
                for size in lead[::-1]:
                    index.insert(0, rest % size)
                    rest = rest // size
                target_ref[tuple(index)] = total(tuple(index)).astype(jnp.bfloat16)
                return carry

            lax.fori_loop(0, amount, add, 0)
            for step in range(sizes[axes[stage]] - 1):
                onward(turn, stage, step).start()

        def onward(turn, stage, step):
            number, window = cuts[turn]
            axes = axis_order(turn)[::-1]
            other = partners(sizes, place, axes[stage])[step]
            return pltpu.make_async_remote_copy(
                src_ref=kept(number, window, axes, stage + 1, other),
                dst_ref=landed(number, window, axes, stage + 1, step),
                send_sem=send_sem.at[turn, stage + 1, step],
                recv_sem=recv_sem.at[turn, stage + 1, step],
                device_id=(device_at(sizes, other),),
                device_id_type=MESH,
            )

        if extra:
            boxes, small_sems = refs[3:7], refs[7:9]

        def small_step(tick):
            axes = (3, 2, 1, 0)
            if tick > 0:
                axis = axes[tick - 1]
                box = boxes[axis]
                for step in range(sizes[axis] - 1):
                    behind = (place[axis] - step - 1 + sizes[axis]) % sizes[axis]
                    arrival(box.at[behind], small_sems, (axis, step))
                value = box[0]
                for at in range(1, sizes[axis]):
                    value = value + box[at]
            else:
                value = small_in[0][...]
            if tick == 4:
                small_out[0][...] = value
                return
            axis = axes[tick]
            boxes[axis][place[axis]] = value
            here = boxes[axis].at[place[axis]]
            for step, other in enumerate(partners(sizes, place, axis)):
                push(here, here, other, small_sems, (axis, step))

        for tick in range(max(tick_count(cuts, 4), 5)):
            for stage in range(4):
                for turn in tick_turns(cuts, tick - stage):
                    advance(turn, stage)
            if extra and tick < 5:
                small_step(tick)
            yield
        for copy in sent:
            copy.wait_send()
        for turn in range(len(cuts)):
            core_copy(turn).wait_send()
            axes = axis_order(turn)[::-1]
            for stage in range(3):
                for step in range(sizes[axes[stage]] - 1):
                    onward(turn, stage, step).wait_send()

    scratch = []
    for lead in (
        sizes[:3],
        sizes[:3],
        (first_step,) + first_lead,
        (second_step, second_lead),
        (last_step,),
    ):
        scratch += [pltpu.VMEM(lead + s, jnp.bfloat16) for s in shapes]
    scratch += [
        pltpu.SemaphoreType.DMA((len(cuts),)),
        pltpu.SemaphoreType.DMA((len(cuts), 4, most)),
        pltpu.SemaphoreType.DMA((len(cuts), 4, most)),
    ]
    if extra:
        scratch += [pltpu.VMEM((size,) + small.shape, jnp.float32) for size in sizes]
        scratch += [pltpu.SemaphoreType.DMA((4, most)) for _ in range(2)]
    return program, scratch


def scatter_sums(parts, small, collective_id, target):
    sizes = lattice(lax.axis_size("seq"))
    count = lax.axis_size("seq")
    shapes = [(p.shape[0] // count, p.shape[1]) for p in parts]
    views = [p.reshape(sizes + s) for p, s in zip(parts, shapes)]
    program, scratch = scatter_plan(shapes, small, target)
    kinds = len(parts)

    def kernel(*refs):
        ins, small_in, refs = refs[:kinds], refs[kinds : kinds + 1], refs[kinds + 1 :]
        outs, small_out, refs = refs[:kinds], refs[kinds : kinds + 1], refs[kinds + 1 :]
        greet(sizes, coordinates(sizes))
        run_together([program(ins, small_in, outs, small_out, refs)])

    return pl.pallas_call(
        kernel,
        out_shape=[jax.ShapeDtypeStruct(s, jnp.float32) for s in shapes]
        + [jax.ShapeDtypeStruct(small.shape, jnp.float32)],
        in_specs=[pl.BlockSpec(memory_space=pl.ANY)] * kinds + [VMEM_SPEC],
        out_specs=[VMEM_SPEC] * (kinds + 1),
        scratch_shapes=scratch,
        compiler_params=pltpu.CompilerParams(
            collective_id=collective_id,
            has_side_effects=True,
            vmem_limit_bytes=62 * 1024 * 1024,
        ),
        name="scatter_sums",
    )(*views, small)


def greet_chips(chips):
    me = lax.axis_index("seq")
    chip, core = me // 2, me % 2
    barrier = pltpu.get_barrier_semaphore()

    def greet_one(step, carry):
        other = lax.rem(chip + step, chips) * 2 + core
        pl.semaphore_signal(barrier, inc=1, device_id=(other,), device_id_type=MESH)
        return carry

    lax.fori_loop(1, chips, greet_one, 0)
    pl.semaphore_signal(barrier, inc=1, device_id=(chip * 2 + 1 - core,), device_id_type=MESH)
    pl.semaphore_wait(barrier, chips)


def exchange_program(chips, part, reverse, own_ref, decay_ref, out_ref, chip_decay_ref, refs):
    (
        mine_low,
        other_low,
        other_decay,
        payload,
        landed,
        result,
        prefix,
        pair_sems,
        far_send,
        far_recv,
    ) = refs
    padded = own_ref.shape[2]
    me = lax.axis_index("seq")
    chip, core = me // 2, me % 2
    sibling = chip * 2 + 1 - core
    f32 = jnp.float32
    wire = jnp.bfloat16 if reverse else f32

    def pair_copy(source, target, slot):
        return pltpu.make_async_remote_copy(
            src_ref=source,
            dst_ref=target,
            send_sem=pair_sems.at[slot, 0],
            recv_sem=pair_sems.at[slot, 1],
            device_id=(sibling,),
            device_id_type=MESH,
        )

    def far_copy(step, turn, source, target):
        other = lax.rem(chip + step, chips)
        return pltpu.make_async_remote_copy(
            src_ref=source.at[other],
            dst_ref=target.at[chip],
            send_sem=far_send.at[turn, step],
            recv_sem=far_recv.at[turn, step],
            device_id=(other * 2 + core,),
            device_id_type=MESH,
        )

    def far_start(turn, source, target):
        def start(step, carry):
            far_copy(step, turn, source, target).start()
            return carry

        lax.fori_loop(1, chips, start, 0)

    def far_wait(turn, source, target):
        def finish(step, carry):
            far_copy(step, turn, source, target).wait()
            return carry

        lax.fori_loop(1, chips, finish, 0)

    def by_row(vector, half, shape, first=0):
        place = (
            lax.broadcasted_iota(jnp.int32, shape, 0) + first
        ) * part + lax.broadcasted_iota(jnp.int32, shape, 1)
        head = (half * (chips * part) + place) // MHEAD_DIM
        lane = lax.broadcasted_iota(jnp.int32, shape, 2)
        picked = jnp.where(lane == head, vector.reshape(1, 1, 128), 0.0)
        return jnp.sum(picked, axis=2, keepdims=True)

    mine_low[...] = own_ref[...].astype(wire)
    first_copies = [
        pair_copy(mine_low, other_low, 0),
        pair_copy(decay_ref, other_decay, 1),
    ]
    for copy in first_copies:
        copy.start()
    yield
    for copy in first_copies:
        copy.wait()
    own_decay, far_decay = decay_ref[0:1, :], other_decay[0:1, :]
    second_core = core == 1
    decays = (
        jnp.where(second_core, far_decay, own_decay),
        jnp.where(second_core, own_decay, far_decay),
    )
    weighted = 0 if reverse else 1
    whole = (chips, padded, 128)
    half_own = own_ref[core]
    half_far = other_low[core].astype(f32)
    earlier = jnp.where(second_core, half_far, half_own)
    later = jnp.where(second_core, half_own, half_far)
    factor = by_row(decays[weighted], core, whole)
    total = earlier + factor * later if reverse else factor * earlier + later
    payload[:, :padded, :] = total.astype(wire)
    if not reverse:
        both = jnp.broadcast_to(decays[0] * decays[1], (8, 128))
        for other in range(chips):
            payload[other, padded:, :] = both
    far_start(0, payload, landed)
    landed[chip] = payload[chip]
    yield
    far_wait(0, payload, landed)
    if not reverse:
        for other in range(chips):
            chip_decay_ref[other : other + 1, :] = landed[other, padded : padded + 1, :]
    state = jnp.zeros((1, padded, 128), f32)
    order = range(chips - 1, -1, -1) if reverse else range(chips)
    for other in order:
        result[other] = state[0]
        step_factor = by_row(chip_decay_ref[other : other + 1, :], core, (1, padded, 128), chip)
        state = step_factor * state + landed[other, :padded, :].astype(f32)[None]
    far_start(1, result, prefix)
    prefix[chip] = result[chip]
    yield
    far_wait(1, result, prefix)
    out_ref[core] = prefix[...]
    last_copy = pair_copy(prefix, out_ref.at[core], 2)
    last_copy.start()
    yield
    last_copy.wait()
    moved = (core == 0) if reverse else second_core
    step_decay = decays[1] if reverse else decays[0]
    for half in range(2):
        factor = jnp.where(moved, by_row(step_decay, half, whole), 1.0)
        extra = jnp.where(moved, other_low[half].astype(f32), 0.0)
        out_ref[half] = factor * out_ref[half] + extra


def exchange_scratch(chips, padded, reverse):
    f32 = jnp.float32
    low = jnp.bfloat16 if reverse else f32
    sent_rows = padded if reverse else padded + 8
    return [
        pltpu.VMEM((2, chips, padded, 128), low),
        pltpu.VMEM((2, chips, padded, 128), low),
        pltpu.VMEM((8, 128), f32),
        pltpu.VMEM((chips, sent_rows, 128), low),
        pltpu.VMEM((chips, sent_rows, 128), low),
        pltpu.VMEM((chips, padded, 128), f32),
        pltpu.VMEM((chips, padded, 128), f32),
        pltpu.SemaphoreType.DMA((3, 2)),
        pltpu.SemaphoreType.DMA((2, chips)),
        pltpu.SemaphoreType.DMA((2, chips)),
    ]


def slice_rows(values, chips):
    part = values.shape[0] // (2 * chips)
    padded = -(-part // 16) * 16
    sliced = values.reshape(2, chips, part, values.shape[1])
    return jnp.pad(sliced, ((0, 0), (0, 0), (0, padded - part), (0, 0)))


def join_rows(slices, rows):
    chips = slices.shape[1]
    return slices[:, :, : rows // (2 * chips)].reshape(rows, slices.shape[3])


def front(forward_args, late, output_args, row_starts, collective_id, targets):
    count = lax.axis_size("seq")
    sizes, chips = lattice(count), count // 2
    rows, model = forward_args[0].shape
    shape = jax.ShapeDtypeStruct
    forward_shapes = mixer_forward_shapes(rows, model)
    kv_shape, query_shape = forward_shapes[5], forward_shapes[4]
    cuts = block_cuts([kv_shape.shape], targets[0])
    late_cuts = block_cuts([w.shape for w in late], targets[1])
    part = SSM // count
    padded = -(-part // 16) * 16
    fused = part == padded
    kinds = len(late)
    state_shape = (2, chips, padded, STATE)
    groups, query_rows, _ = query_shape.shape
    tokens = rows * count
    comm_scratch = (
        gather_scratch(sizes, cuts)
        + gather_scratch(sizes, late_cuts)
        + exchange_scratch(chips, padded, False)
    )
    compute_scratch = (
        [pltpu.VMEM((3 * rows, SSM), jnp.bfloat16)]
        + attention_scratch(groups, query_rows)
        + [
            pltpu.VMEM(sizes + kv_shape.shape, kv_shape.dtype),
            pltpu.SemaphoreType.DMA((1,)),
            pltpu.VMEM(kv_shape.shape, kv_shape.dtype),
            pltpu.VMEM(state_shape, jnp.float32),
        ]
        + mixer_forward_scratch(rows, model, forward_args[3:6])
    )
    hbm = pl.BlockSpec(memory_space=pl.ANY)
    kept = (0, 1, 2, 3, 4, 6, 7, 9)
    if fused:
        first_in = list(forward_args) + list(output_args) + [row_starts]
        first_specs = mixer_forward_specs() + [VMEM_SPEC] * (len(output_args) + 1)
        first_out = (
            [forward_shapes[i] for i in kept]
            + mixer_output_shapes(rows)
            + attention_shapes(groups, query_rows)
        )
    else:
        forward = list(mixer_forward(forward_args))
        first_in = [forward[5], slice_rows(forward[8], chips), forward[9]]
        first_specs = [hbm, VMEM_SPEC, VMEM_SPEC]
        first_out = []

    def kernel(*refs):
        late_in, refs = refs[:kinds], refs[kinds:]
        ins, refs = refs[: len(first_in)], refs[len(first_in) :]
        kv_out, state_out, chip_decay_ref, refs = refs[0], refs[1], refs[2], refs[3:]
        late_out, refs = refs[:kinds], refs[kinds:]
        outs, refs = refs[: len(first_out)], refs[len(first_out) :]
        comm, refs = refs[: len(comm_scratch)], refs[len(comm_scratch) :]
        greet_chips(chips)
        weights = gather_program(sizes, late_cuts, late_in, late_out, *comm[3:6], 2)
        done = [0]

        def tick():
            done[0] += 1
            next(weights)

        next(weights)
        if fused:
            input_ref, max_ref, acc_ref, kv_vmem, kv_sem, kv_ref, state_ref, *scratch = refs
            normed_ref, gate_ref, ext_ref, pre_ref, q_ref, dt_pre_ref, log_ref, decay_ref = outs[:8]
            given = len(forward_args)
            mixer_forward_body(
                *ins[:given],
                normed_ref,
                gate_ref,
                ext_ref,
                pre_ref,
                q_ref,
                kv_ref,
                dt_pre_ref,
                log_ref,
                state_ref,
                decay_ref,
                *scratch,
                tick,
            )
        else:
            kv_ref, state_ref, decay_ref = ins
        exchange = exchange_program(
            chips, part, False, state_ref, decay_ref, state_out, chip_decay_ref, comm[6:]
        )
        keys = gather_program(sizes, cuts, [kv_ref], [kv_out], *comm[:3])
        run_together([exchange, keys])
        if not fused:
            for _ in weights:
                pass
            return
        load = pltpu.make_async_copy(kv_out, kv_vmem, kv_sem.at[0])
        load.start()
        tick()
        mixer_output_body(
            pre_ref,
            dt_pre_ref,
            log_ref,
            state_out[...].reshape(SSM, STATE),
            gate_ref,
            *ins[given:-1],
            *outs[8:10],
            input_ref,
        )
        load.wait()
        tick()
        attention_forward_body(
            q_ref,
            kv_vmem.reshape(tokens, kv_shape.shape[1]),
            ins[-1],
            *outs[10:],
            max_ref,
            acc_ref,
            spread_ticks(weights, tick_count(late_cuts, 3) - done[0], tokens // KEYS_STEP),
        )
        for _ in weights:
            pass

    kv_all, states_in, chip_decay, *rest = pl.pallas_call(
        kernel,
        out_shape=[
            shape(sizes + kv_shape.shape, kv_shape.dtype),
            shape(state_shape, jnp.float32),
            shape((chips, 128), jnp.float32),
        ]
        + [shape(sizes + w.shape, w.dtype) for w in late]
        + first_out,
        in_specs=[hbm] * kinds + first_specs,
        out_specs=[hbm, VMEM_SPEC, VMEM_SPEC] + [hbm] * kinds + [VMEM_SPEC] * len(first_out),
        scratch_shapes=comm_scratch + (compute_scratch if fused else []),
        compiler_params=pltpu.CompilerParams(
            collective_id=collective_id,
            has_side_effects=True,
            vmem_limit_bytes=63 * 1024 * 1024,
        ),
        name="front",
    )(*late, *first_in)
    kv_all = kv_all.reshape(-1, kv_shape.shape[1])
    late_full = [w.reshape(-1, w.shape[-1]) for w in rest[:kinds]]
    states_in = join_rows(states_in, SSM)
    computed = list(rest[kinds:])
    if not fused:
        computed = [forward[i] for i in kept]
        computed += mixer_output(
            forward[3], forward[6], forward[7], states_in, forward[1], *output_args
        )
        computed += attention_forward(forward[4], kv_all, row_starts)
    return kv_all, states_in, chip_decay, late_full, computed


def some_ticks(program, amount):
    for _ in range(amount):
        next(program, None)
        yield


def back(
    key_terms, mixer_args, input_args, passing, chip_decay, late_grads, collective_id, targets
):
    count = lax.axis_size("seq")
    sizes, chips = lattice(count), count // 2
    shape = (key_terms.shape[0] // count, key_terms.shape[1])
    late_shapes = [(g.shape[0] // count, g.shape[1]) for g in late_grads]
    keys, keys_scratch = scatter_plan([shape], None, targets[0])
    weights, weights_scratch = scatter_plan(late_shapes, None, targets[1])
    part = SSM // count
    padded = -(-part // 16) * 16
    fused = part == padded
    rows = mixer_args[0].shape[0]
    state_shape = (2, chips, padded, STATE)
    kinds = len(late_grads)
    if fused:
        first_in = list(mixer_args) + list(input_args)
        made_shapes = mixer_backward_shapes(rows, state_shape)
        outer = (0, 1, 8)
        inner = (2, 3, 4, 5, 6, 7)
        mixer_shapes = [made_shapes[i] for i in outer] + mixer_input_shapes(rows)
        compute_scratch = (
            mixer_backward_scratch(rows)
            + [pltpu.VMEM(made_shapes[i].shape, made_shapes[i].dtype) for i in inner]
            + mixer_input_scratch(rows)
        )
    else:
        mixer_out = list(mixer_backward(mixer_args))
        first_in, mixer_shapes = [slice_rows(mixer_out[3], chips)], []
        compute_scratch = []
    known = len(first_in)
    made = len(mixer_shapes)

    def kernel(kv_ref, decay_ref, chip_decay_ref, *refs):
        late_in, refs = refs[:kinds], refs[kinds:]
        ins, refs = refs[:known], refs[known:]
        kv_out, state_out, refs = refs[0], refs[1], refs[2:]
        late_out, refs = refs[:kinds], refs[kinds:]
        outs, refs = refs[:made], refs[made:]
        keys_refs, refs = refs[: len(keys_scratch)], refs[len(keys_scratch) :]
        weights_refs, refs = refs[: len(weights_scratch)], refs[len(weights_scratch) :]
        mixer_refs, refs = refs[: len(compute_scratch)], refs[len(compute_scratch) :]
        greet_chips(chips)
        runs = [
            keys([kv_ref], [], [kv_out], [], keys_refs),
            weights(late_in, [], late_out, [], weights_refs),
        ]

        def tick():
            for run in runs:
                next(run)

        tick()
        if fused:
            given = len(mixer_args)
            held = dict(zip(outer, outs[:3])) | dict(zip(inner, mixer_refs[3:9]))
            made_refs = [held[i] for i in range(9)]
            mixer_backward_body(*ins[:given], *made_refs, *mixer_refs[:3], tick)
            own_ref = made_refs[3]
        else:
            own_ref = ins[0]
        exchange = exchange_program(
            chips, part, True, own_ref, decay_ref, state_out, chip_decay_ref, refs
        )
        if not fused:
            run_together([exchange] + runs)
            return
        run_together([exchange, runs[0], some_ticks(runs[1], 3)])
        pre_ref, dt_pre_ref, log_ref, state_ref = ins[4:8]
        skip_ref, starts_ref = ins[8:10]
        ext_ref, tap_ref, a_log_ref = ins[given:]

        def late_tick():
            next(runs[1], None)

        mixer_input_backward_body(
            state_out[...].reshape(SSM, STATE),
            state_ref,
            decay_ref,
            made_refs[2],
            *made_refs[4:8],
            pre_ref,
            dt_pre_ref,
            log_ref,
            ext_ref,
            tap_ref,
            a_log_ref,
            skip_ref,
            starts_ref,
            *outs[3:],
            *mixer_refs[9:],
            late_tick,
        )
        for _ in runs[1]:
            pass

    hbm = pl.BlockSpec(memory_space=pl.ANY)
    kv_sum, grad_end, *rest = pl.pallas_call(
        kernel,
        out_shape=[
            jax.ShapeDtypeStruct(shape, jnp.float32),
            jax.ShapeDtypeStruct(state_shape, jnp.float32),
        ]
        + [jax.ShapeDtypeStruct(s, jnp.float32) for s in late_shapes]
        + mixer_shapes,
        in_specs=[hbm] + [VMEM_SPEC] * 2 + [hbm] * kinds + [VMEM_SPEC] * known,
        out_specs=[VMEM_SPEC] * (2 + kinds + made),
        scratch_shapes=keys_scratch
        + weights_scratch
        + compute_scratch
        + exchange_scratch(chips, padded, True),
        compiler_params=pltpu.CompilerParams(
            collective_id=collective_id,
            has_side_effects=True,
            vmem_limit_bytes=63 * 1024 * 1024,
        ),
        name="back",
    )(
        key_terms.reshape(sizes + shape),
        passing,
        chip_decay,
        *[g.reshape(sizes + s) for g, s in zip(late_grads, late_shapes)],
        *first_in,
    )
    late_sums = rest[:kinds]
    if fused:
        return kv_sum, late_sums, rest[kinds:]
    grad_end = join_rows(grad_end, SSM)
    input_out = mixer_input_backward(
        [grad_end, mixer_args[7], passing, mixer_out[2], *mixer_out[4:8]]
        + [*mixer_args[4:7], *input_args, *mixer_args[8:10]]
    )
    return kv_sum, late_sums, [mixer_out[0], mixer_out[1], mixer_out[8], *input_out]


KEYS_STEP = 512


def attention_forward_body(
    q_ref, kv_ref, starts_ref, out_ref, log_ref, flat_ref, max_ref, acc_ref, ticks
):
    groups, rows, _ = q_ref.shape
    group_size = QHEADS // KVHEADS
    local_rows = rows // group_size
    half_kv = KVW // 2
    steps = kv_ref.shape[0] // KEYS_STEP
    first_row = lax.axis_index("seq") * local_rows
    used = (first_row + local_rows - 1) // KEYS_STEP + 1
    starts = jnp.concatenate([starts_ref[...]] * group_size, axis=1)
    places = first_row + lax.broadcasted_iota(jnp.int32, (1, rows), 1) % local_rows
    max_ref[...] = jnp.full(max_ref.shape, masked, jnp.float32)
    acc_ref[...] = jnp.zeros(acc_ref.shape, jnp.float32)

    def block(step, general):
        first_key = pl.multiple_of(step * KEYS_STEP, KEYS_STEP)
        piece = kv_ref[pl.ds(first_key, KEYS_STEP), :]
        flipped = jnp.transpose(piece[:, half_kv:])
        ones = jnp.ones((16, KEYS_STEP), jnp.bfloat16)
        if general:
            key_pos = first_key + lax.broadcasted_iota(jnp.int32, (KEYS_STEP, 1), 0)
            allowed = (key_pos >= starts) & (key_pos <= places)
        else:
            row_open = starts <= first_key
        for group in range(groups):
            scores = lax.dot_general(
                piece[:, group * HEAD_DIM : (group + 1) * HEAD_DIM],
                q_ref[group],
                (((1,), (1,)), ((), ())),
                preferred_element_type=jnp.float32,
            )
            if general:
                scores = jnp.where(allowed, scores, masked)
            old = max_ref[group]
            new = jnp.maximum(old, jnp.max(scores, axis=0, keepdims=True))
            if general:
                shift = new
            else:
                new = jnp.where(row_open, new, old)
                shift = jnp.where(row_open, new, -masked)
            max_ref[group] = new
            weights = jnp.exp(scores - shift).astype(jnp.bfloat16)
            values = jnp.concatenate(
                [flipped[group * HEAD_DIM : (group + 1) * HEAD_DIM], ones], axis=0
            )
            acc_ref[group] = acc_ref[group] * jnp.exp(old - new) + jnp.dot(
                values, weights, preferred_element_type=jnp.float32
            )

    def body(step, carry):
        general = (step == 0) | ((step + 1) * KEYS_STEP > first_row)
        pl.when((step < used) & general)(partial(block, step, True))
        pl.when((step < used) & jnp.logical_not(general))(partial(block, step, False))
        for at, tick in ticks:
            pl.when(step == at)(tick)
        return carry

    lax.fori_loop(0, steps, body, 0)
    for group in range(groups):
        row_sum = acc_ref[group, HEAD_DIM : HEAD_DIM + 1, :]
        out = acc_ref[group, :HEAD_DIM, :] / row_sum
        out_ref[group] = out
        log_ref[group] = max_ref[group] + jnp.log(row_sum)
        for part in range(group_size):
            head = group * group_size + part
            flat_ref[:, head * HEAD_DIM : (head + 1) * HEAD_DIM] = jnp.transpose(
                out[:, part * local_rows : (part + 1) * local_rows]
            ).astype(jnp.bfloat16)


def attention_shapes(groups, rows):
    return [
        jax.ShapeDtypeStruct((groups, HEAD_DIM, rows), jnp.float32),
        jax.ShapeDtypeStruct((groups, 1, rows), jnp.float32),
        jax.ShapeDtypeStruct((rows // (QHEADS // KVHEADS), QW), jnp.bfloat16),
    ]


def attention_scratch(groups, rows):
    return [
        pltpu.VMEM((groups, 1, rows), jnp.float32),
        pltpu.VMEM((groups, HEAD_DIM + 16, rows), jnp.float32),
    ]


def attention_forward(queries, kv_all, row_starts):
    groups, rows, _ = queries.shape

    def kernel(*refs):
        attention_forward_body(*refs, [])

    return pl.pallas_call(
        kernel,
        out_shape=attention_shapes(groups, rows),
        in_specs=[VMEM_SPEC] * 3,
        out_specs=[VMEM_SPEC] * 3,
        scratch_shapes=attention_scratch(groups, rows),
        compiler_params=BIG_VMEM,
        name="attention_forward",
    )(queries, kv_all, row_starts)


def spread_ticks(program, ticks, steps):
    def make_tick():
        def tick():
            next(program, None)

        return tick

    return [(number * steps // ticks, make_tick()) for number in range(ticks)]


def attention_backward(
    queries, grads, kv_all, row_starts, log_total, outputs, late_grads, collective_id, target
):
    groups, rows, _ = queries.shape
    total = kv_all.shape[0]
    half_kv = KVW // 2
    group_size = QHEADS // KVHEADS
    local_rows = rows // group_size
    count = lax.axis_size("seq")
    sizes = lattice(count)
    shapes = [(g.shape[0] // count, g.shape[1]) for g in late_grads]
    views = [g.reshape(sizes + s) for g, s in zip(late_grads, shapes)]
    program, scratch = scatter_plan(shapes, None, target)
    kinds = len(shapes)
    ticks = max(tick_count(block_cuts(shapes, target), 4), 5)
    steps = total // KEYS_STEP

    def kernel(q_ref, g_ref, kv_ref, starts_ref, log_ref, outputs_ref, *refs):
        ins, dkv_ref, dq_ref, refs = refs[:kinds], refs[kinds], refs[kinds + 1], refs[kinds + 2 :]
        outs, delta_ref, refs = refs[:kinds], refs[kinds], refs[kinds + 1 :]
        greet(sizes, coordinates(sizes))
        sums = program(ins, [], outs, [], refs)
        next(sums)
        first_row = lax.axis_index("seq") * local_rows
        used = (first_row + local_rows - 1) // KEYS_STEP + 1
        starts = jnp.concatenate([starts_ref[...]] * group_size, axis=1)
        places = first_row + lax.broadcasted_iota(jnp.int32, (1, rows), 1) % local_rows
        dq_ref[...] = jnp.zeros(dq_ref.shape, jnp.float32)
        for group in range(groups):
            flipped_grads = jnp.transpose(g_ref[group].astype(jnp.float32))
            delta_ref[group] = jnp.sum(flipped_grads * outputs_ref[group], axis=0, keepdims=True)

        def block(step, general):
            first_key = pl.multiple_of(step * KEYS_STEP, KEYS_STEP)
            piece = kv_ref[pl.ds(first_key, KEYS_STEP), :]
            flipped = jnp.transpose(piece[:, :half_kv])
            if general:
                key_pos = first_key + lax.broadcasted_iota(jnp.int32, (KEYS_STEP, 1), 0)
                allowed = (key_pos >= starts) & (key_pos <= places)
            else:
                row_open = starts <= first_key
            found = []
            for group in range(groups):
                low, high = group * HEAD_DIM, (group + 1) * HEAD_DIM
                scores = lax.dot_general(
                    piece[:, low:high],
                    q_ref[group],
                    (((1,), (1,)), ((), ())),
                    preferred_element_type=jnp.float32,
                )
                shift = log_ref[group]
                if general:
                    scores = jnp.where(allowed, scores, masked)
                else:
                    shift = jnp.where(row_open, shift, -masked)
                weights = jnp.exp(scores - shift)
                grad_weights = lax.dot_general(
                    piece[:, half_kv + low : half_kv + high],
                    g_ref[group],
                    (((1,), (1,)), ((), ())),
                    preferred_element_type=jnp.float32,
                )
                grad_scores = (weights * (grad_weights - delta_ref[group])).astype(jnp.bfloat16)
                dq_ref[group] += jnp.dot(
                    flipped[low:high], grad_scores, preferred_element_type=jnp.float32
                )
                found.append(
                    jnp.dot(grad_scores, q_ref[group], preferred_element_type=jnp.float32)
                )
                found.append(
                    jnp.dot(
                        weights.astype(jnp.bfloat16),
                        g_ref[group],
                        preferred_element_type=jnp.float32,
                    )
                )
            dkv_ref[pl.ds(first_key, KEYS_STEP), :] = jnp.concatenate(
                found[0::2] + found[1::2], axis=1
            ).astype(dkv_ref.dtype)

        def clear(step):
            first_key = pl.multiple_of(step * KEYS_STEP, KEYS_STEP)
            dkv_ref[pl.ds(first_key, KEYS_STEP), :] = jnp.zeros((KEYS_STEP, KVW), dkv_ref.dtype)

        marks = spread_ticks(sums, ticks, steps)

        def body(step, carry):
            general = (step == 0) | ((step + 1) * KEYS_STEP > first_row)
            pl.when((step < used) & general)(partial(block, step, True))
            pl.when((step < used) & jnp.logical_not(general))(partial(block, step, False))
            pl.when(step >= used)(partial(clear, step))
            for at, tick in marks:
                pl.when(step == at)(tick)
            return carry

        lax.fori_loop(0, steps, body, 0)
        for _ in sums:
            pass

    hbm = pl.BlockSpec(memory_space=pl.ANY)
    key_terms, query_grads, *late_sums = pl.pallas_call(
        kernel,
        out_shape=[
            jax.ShapeDtypeStruct((total, KVW), jnp.bfloat16),
            jax.ShapeDtypeStruct((groups, HEAD_DIM, rows), jnp.float32),
        ]
        + [jax.ShapeDtypeStruct(s, jnp.float32) for s in shapes],
        in_specs=[VMEM_SPEC] * 6 + [hbm] * kinds,
        out_specs=[VMEM_SPEC] * (2 + kinds),
        scratch_shapes=[pltpu.VMEM((groups, 1, rows), jnp.float32)] + scratch,
        compiler_params=pltpu.CompilerParams(
            collective_id=collective_id,
            has_side_effects=True,
            vmem_limit_bytes=62 * 1024 * 1024,
        ),
        name="attention_backward",
    )(queries, grads, kv_all, row_starts, log_total, outputs, *views)
    return key_terms, query_grads, late_sums


BIG_VMEM = pltpu.CompilerParams(vmem_limit_bytes=62 * 1024 * 1024)


def dot_parts(value, exact, parts, axes=((1,), (0,))):
    total, left = None, value
    for _ in range(parts):
        piece = left.astype(jnp.bfloat16)
        left = left - piece.astype(jnp.float32)
        term = lax.dot_general(piece, exact, (axes, ((), ())), preferred_element_type=jnp.float32)
        total = term if total is None else total + term
    return total


def dot_left(exact, value, parts):
    total, left = None, value
    for _ in range(parts):
        piece = left.astype(jnp.bfloat16)
        left = left - piece.astype(jnp.float32)
        term = jnp.dot(exact, piece, preferred_element_type=jnp.float32)
        total = term if total is None else total + term
    return total


def matmul_pair(left_side, right_side, axes):
    left_high = left_side.astype(jnp.bfloat16)
    left_low = (left_side - left_high.astype(jnp.float32)).astype(jnp.bfloat16)
    right_high = right_side.astype(jnp.bfloat16)
    right_low = (right_side - right_high.astype(jnp.float32)).astype(jnp.bfloat16)
    dims = (axes, ((), ()))
    product = partial(
        lax.dot_general, dimension_numbers=dims, preferred_element_type=jnp.float32
    )
    return (
        product(left_high, right_high)
        + product(left_low, right_high)
        + product(left_high, right_low)
    )


def stacked(value, first):
    high = value.astype(jnp.bfloat16)
    low = (value - high.astype(jnp.float32)).astype(jnp.bfloat16)
    return [high, low, high] if first else [high, high, low]


def dot_fast(left_side, right_side, axes):
    return lax.dot_general(
        left_side.astype(jnp.bfloat16),
        right_side.astype(jnp.bfloat16),
        (axes, ((), ())),
        preferred_element_type=jnp.float32,
    )


NN = ((1,), (0,))
NT = ((1,), (1,))
TN = ((0,), (0,))


def head_spread():
    head = lax.broadcasted_iota(jnp.int32, (128, SSM), 0)
    column = lax.broadcasted_iota(jnp.int32, (128, SSM), 1)
    return jnp.where(column // MHEAD_DIM == head, 1.0, 0.0).astype(jnp.bfloat16)


def rope_table(rows, count):
    half = HEAD_DIM // 2
    frequency = rope_base ** (-np.arange(half) / half)
    tables = []
    for places in (np.arange(rows), rows * np.arange(count)):
        angles = np.tile(places[:, None] * frequency[None, :], (1, 4))
        tables += [np.cos(angles).astype(np.float32), np.sin(angles).astype(np.float32)]
    return tables


def rope_now(device, base_cos_ref, base_sin_ref, far_cos_ref, far_sin_ref):
    base_cos, base_sin = base_cos_ref[...], base_sin_ref[...]
    far_cos, far_sin = far_cos_ref[pl.ds(device, 1), :], far_sin_ref[pl.ds(device, 1), :]
    cosine_part = far_cos * base_cos - far_sin * base_sin
    sine_part = far_sin * base_cos + far_cos * base_sin
    lane = lax.broadcasted_iota(jnp.int32, base_cos.shape, 1)
    return cosine_part, jnp.where(lane % HEAD_DIM < HEAD_DIM // 2, -sine_part, sine_part)


def rope_lanes(values, cosine_all, sine_all):
    width = values.shape[1]
    repeat = width // cosine_all.shape[1]
    half = HEAD_DIM // 2
    column = lax.broadcasted_iota(jnp.int32, values.shape, 1)
    partner = jnp.where(
        column % HEAD_DIM < half,
        pltpu.roll(values, width - half, 1),
        pltpu.roll(values, half, 1),
    )
    if repeat > 1:
        cosine_all = jnp.concatenate([cosine_all] * repeat, axis=1)
        sine_all = jnp.concatenate([sine_all] * repeat, axis=1)
    return values * cosine_all + partner * sine_all


def mixer_forward_body(
    hidden_ref,
    halo_ref,
    gain_ref,
    z_hbm,
    xbc_hbm,
    small_hbm,
    tap_ref,
    bias_ref,
    dt_bias_ref,
    a_log_ref,
    starts_ref,
    base_cos_ref,
    base_sin_ref,
    far_cos_ref,
    far_sin_ref,
    normed_ref,
    gate_ref,
    ext_ref,
    pre_ref,
    q_ref,
    kv_ref,
    dt_pre_ref,
    log_ref,
    state_ref,
    passing_ref,
    z_ref,
    xbc_ref,
    small_ref,
    normed_ext,
    ext_f32,
    sems,
    tick,
):
    rows, model = hidden_ref.shape
    groups = QHEADS // KVHEADS
    half_kv = KVW // 2
    first_row = lax.axis_index("seq") * rows
    pieces = [
        (0, 0, SSM // 2),
        (0, SSM // 2, SSM // 2),
        (1, 0, XBC // 2),
        (1, XBC // 2, XBC // 2),
        (2, 0, QW),
        (2, QW, KVW),
        (2, QW + KVW, DT_PAD),
    ]
    load_order = (2, 3, 4, 5, 6, 0, 1)
    weight_hbm, weight_refs = (z_hbm, xbc_hbm, small_hbm), (z_ref, xbc_ref, small_ref)
    copies = [
        pltpu.make_async_copy(
            weight_hbm[which].at[:, pl.ds(start, width)],
            weight_refs[which].at[:, pl.ds(start, width)],
            sems.at[number],
        )
        for number, (which, start, width) in enumerate(pieces)
    ]
    for number in load_order:
        copies[number].start()
    cosine_all, sine_all = rope_now(
        lax.axis_index("seq"), base_cos_ref, base_sin_ref, far_cos_ref, far_sin_ref
    )

    def norm(block):
        values = block.astype(jnp.float32)
        scale = lax.rsqrt(jnp.mean(values * values, axis=1, keepdims=True) + epsilon)
        return (values * scale * gain_ref[...]).astype(jnp.bfloat16)

    normed_ext[:HALO, :] = norm(halo_ref[...])
    normed = norm(hidden_ref[...])
    normed_ext[HALO:, :] = normed
    normed_ref[...] = normed

    def project(number, values):
        copies[number].wait()
        which, start, width = pieces[number]
        return jnp.dot(
            values,
            weight_refs[which][:, start : start + width],
            preferred_element_type=jnp.float32,
        )

    for number in (2, 3):
        _, start, width = pieces[number]
        part = project(number, normed_ext[...]).astype(jnp.bfloat16)
        ext_ref[:, start : start + width] = part
        ext_f32[:, start : start + width] = part.astype(jnp.float32)
    turned = rope_lanes(project(4, normed), cosine_all, sine_all).astype(jnp.bfloat16)
    turned = turned * jnp.bfloat16(HEAD_DIM ** (-0.5))
    for head in range(QHEADS):
        place = head % groups * rows
        q_ref[head // groups, place : place + rows, :] = turned[
            :, head * HEAD_DIM : (head + 1) * HEAD_DIM
        ]
    kv_raw = project(5, normed)
    kv_ref[:, :half_kv] = rope_lanes(
        kv_raw[:, :half_kv], cosine_all, sine_all
    ).astype(jnp.bfloat16)
    kv_ref[:, half_kv:] = kv_raw[:, half_kv:].astype(jnp.bfloat16)
    dt_pre = project(6, normed) + dt_bias_ref[...]
    dt_pre_ref[...] = dt_pre
    step_dt = jax.nn.softplus(dt_pre)
    order = lax.broadcasted_iota(jnp.int32, (rows, rows), 0)
    other = lax.broadcasted_iota(jnp.int32, (rows, rows), 1)
    lower = jnp.where(other <= order, 1.0, 0.0).astype(jnp.bfloat16)
    log_decay = dot_left(lower, -step_dt * jnp.exp(a_log_ref[...]), 3)
    log_ref[...] = log_decay
    for number in (0, 1):
        _, start, width = pieces[number]
        gate_ref[:, start : start + width] = project(number, normed)

    tick()
    starts_now = starts_ref[...]
    places = first_row + lax.broadcasted_iota(jnp.int32, (rows, 1), 0)
    pre = jnp.zeros((rows, XBC), jnp.float32) + bias_ref[...]
    for tap in range(CONV):
        lag = CONV - 1 - tap
        kept = jnp.where(places - lag >= starts_now, 1.0, 0.0)
        pre = pre + ext_f32[HALO - lag : HALO - lag + rows, :] * kept * tap_ref[tap : tap + 1, :]
    pre_ref[...] = pre
    conv_out = pre * jax.nn.sigmoid(pre)
    last = log_decay[rows - 1 : rows, :]
    last_start = starts_ref[rows - 1 : rows, :]
    weight = jnp.exp(jnp.where(places >= last_start, last - log_decay, masked)) * step_dt
    spread = dot_parts(weight, head_spread(), 2)
    state_ref[...] = matmul_pair(
        conv_out[:, :SSM] * spread, conv_out[:, SSM : SSM + STATE], TN
    ).reshape(state_ref.shape)
    passing = jnp.exp(last) * jnp.where(last_start < first_row, 1.0, 0.0)
    passing_ref[...] = jnp.broadcast_to(passing, passing_ref.shape)


def mixer_forward_shapes(rows, model):
    f32, low = jnp.float32, jnp.bfloat16
    shape = jax.ShapeDtypeStruct
    return [
        shape((rows, model), low),
        shape((rows, SSM), f32),
        shape((HALO + rows, XBC), low),
        shape((rows, XBC), f32),
        shape((KVHEADS, QHEADS // KVHEADS * rows, HEAD_DIM), low),
        shape((rows, KVW), low),
        shape((rows, DT_PAD), f32),
        shape((rows, DT_PAD), f32),
        shape((SSM, STATE), f32),
        shape((8, DT_PAD), f32),
    ]


def mixer_forward_scratch(rows, model, weights):
    return [pltpu.VMEM(w.shape, jnp.bfloat16) for w in weights] + [
        pltpu.VMEM((HALO + rows, model), jnp.bfloat16),
        pltpu.VMEM((HALO + rows, XBC), jnp.float32),
        pltpu.SemaphoreType.DMA((7,)),
    ]


def mixer_forward_specs():
    return [VMEM_SPEC] * 3 + [pl.BlockSpec(memory_space=pl.ANY)] * 3 + [VMEM_SPEC] * 9


def mixer_forward(args):
    rows, model = args[0].shape

    def kernel(*refs):
        mixer_forward_body(*refs, lambda: None)

    return pl.pallas_call(
        kernel,
        out_shape=mixer_forward_shapes(rows, model),
        in_specs=mixer_forward_specs(),
        out_specs=[VMEM_SPEC] * 10,
        scratch_shapes=mixer_forward_scratch(rows, model, args[3:6]),
        compiler_params=BIG_VMEM,
        name="mixer_forward",
    )(*args)


def document_mask(first_row, starts, rows, flip):
    if flip:
        token = lax.broadcasted_iota(jnp.int32, (rows, rows), 1)
        source = lax.broadcasted_iota(jnp.int32, (rows, rows), 0)
    else:
        token = lax.broadcasted_iota(jnp.int32, (rows, rows), 0)
        source = lax.broadcasted_iota(jnp.int32, (rows, rows), 1)
    allowed = (first_row + source >= starts) & (source <= token)
    return jnp.where(allowed, 0.0, masked)


def mixer_output_body(
    pre_ref,
    dt_pre_ref,
    log_ref,
    state,
    gate_ref,
    gain_ref,
    skip_ref,
    starts_ref,
    normed_ref,
    y_ref,
    input_ref,
):
    rows = pre_ref.shape[0]
    first_row = lax.axis_index("seq") * rows
    pre_now = pre_ref[...]
    conv_out = pre_now * jax.nn.sigmoid(pre_now)
    ssm_x = conv_out[:, :SSM]
    input_b = conv_out[:, SSM : SSM + STATE]
    output_c = conv_out[:, SSM + STATE :]
    spread = head_spread()
    log_decay_now = log_ref[...]
    log_rows = jnp.transpose(log_decay_now)
    step_dt = jax.nn.softplus(dt_pre_ref[...])
    scaled_x = ssm_x * dot_parts(step_dt, spread, 2)
    for part, piece in enumerate(stacked(scaled_x, False)):
        input_ref[part * rows : (part + 1) * rows, :] = piece
    carried = jnp.exp(log_decay_now) * jnp.where(starts_ref[...] < first_row, 1.0, 0.0)
    y_ref[...] = (
        matmul_pair(output_c, state, NT) * dot_parts(carried, spread, 2)
        + dot_parts(skip_ref[...], spread, 3) * ssm_x
    )
    affinity = matmul_pair(output_c, input_b, NT)
    closed = document_mask(first_row, starts_ref[...], rows, False)
    for pair in range(MHEADS // 2):
        found = []
        for head in (2 * pair, 2 * pair + 1):
            gap = log_decay_now[:, head : head + 1] - log_rows[head : head + 1, :] + closed
            mixing = affinity * jnp.exp(gap)
            found.append(
                jnp.dot(
                    jnp.concatenate(stacked(mixing, True), axis=1),
                    input_ref[:, head * MHEAD_DIM : (head + 1) * MHEAD_DIM],
                    preferred_element_type=jnp.float32,
                )
            )
        columns = slice(2 * pair * MHEAD_DIM, (2 * pair + 2) * MHEAD_DIM)
        y_ref[:, columns] += jnp.concatenate(found, axis=1)
    gate_now = gate_ref[...]
    gated = y_ref[...] * gate_now * jax.nn.sigmoid(gate_now)
    scale = lax.rsqrt(jnp.mean(gated * gated, axis=1, keepdims=True) + epsilon)
    normed_ref[...] = (gated * scale * gain_ref[...]).astype(jnp.bfloat16)


def mixer_output(pre, dt_pre, log_decay, states_in, gate_z, ssm_gain, skip_row, starts):
    rows = pre.shape[0]

    def kernel(*refs):
        mixer_output_body(*refs[:3], refs[3][...], *refs[4:])

    return pl.pallas_call(
        kernel,
        out_shape=mixer_output_shapes(rows),
        in_specs=[VMEM_SPEC] * 8,
        out_specs=[VMEM_SPEC] * 2,
        scratch_shapes=[pltpu.VMEM((3 * rows, SSM), jnp.bfloat16)],
        compiler_params=BIG_VMEM,
        name="mixer_output",
    )(
        pre,
        dt_pre,
        log_decay,
        states_in,
        gate_z,
        ssm_gain,
        skip_row,
        starts,
    )


def mixer_output_shapes(rows):
    return [
        jax.ShapeDtypeStruct((rows, SSM), jnp.bfloat16),
        jax.ShapeDtypeStruct((rows, SSM), jnp.float32),
    ]


def mixer_backward_body(
    grad_ref,
    y_ref,
    gate_ref,
    gain_ref,
    pre_ref,
    dt_pre_ref,
    log_ref,
    state_ref,
    skip_ref,
    starts_ref,
    starts_row_ref,
    grad_gate_ref,
    gain_grad_ref,
    grad_y_ref,
    state_grad_ref,
    input_grad_ref,
    b_grad_ref,
    c_grad_ref,
    log_grad_ref,
    skip_grad_ref,
    input_ref,
    low_ref,
    sums_ref,
    tick,
):
    rows = pre_ref.shape[0]
    first_row = lax.axis_index("seq") * rows
    gate_now = gate_ref[...]
    sigmoid_gate = jax.nn.sigmoid(gate_now)
    silu_gate = gate_now * sigmoid_gate
    y_now = y_ref[...]
    gated = y_now * silu_gate
    scale = lax.rsqrt(jnp.mean(gated * gated, axis=1, keepdims=True) + epsilon)
    grad_now = grad_ref[...]
    gain_grad_ref[...] = jnp.sum(gated * scale * grad_now, axis=0, keepdims=True)
    scaled = grad_now * gain_ref[...]
    grad_gated = scale * scaled - gated * (
        scale * scale * scale * jnp.mean(gated * scaled, axis=1, keepdims=True)
    )
    grad_gate_ref[...] = (
        grad_gated * y_now * sigmoid_gate * (1.0 + gate_now * (1.0 - sigmoid_gate))
    ).astype(jnp.bfloat16)
    grad_y = grad_gated * silu_gate
    grad_y_ref[...] = grad_y
    for part, piece in enumerate(stacked(grad_y, False)):
        low_ref[part * rows : (part + 1) * rows, :] = piece

    pre_now = pre_ref[...]
    conv_out = pre_now * jax.nn.sigmoid(pre_now)
    ssm_x = conv_out[:, :SSM]
    input_b = conv_out[:, SSM : SSM + STATE]
    output_c = conv_out[:, SSM + STATE :]
    spread = head_spread()
    log_decay_now = log_ref[...]
    log_rows = jnp.transpose(log_decay_now)
    step_dt = jax.nn.softplus(dt_pre_ref[...])
    scaled_x = ssm_x * dot_parts(step_dt, spread, 2)
    high, low, _ = stacked(scaled_x, True)
    input_ref[:rows, :] = high
    input_ref[rows:, :] = low
    carried = jnp.exp(log_decay_now) * jnp.where(starts_ref[...] < first_row, 1.0, 0.0)
    carried_lanes = dot_parts(carried, spread, 2)
    from_state = matmul_pair(output_c, state_ref[...], NT)
    log_grad = carried * dot_parts(grad_y * from_state, spread, 2, NT)
    grad_from_state = grad_y * carried_lanes
    state_grad_ref[...] = matmul_pair(grad_from_state, output_c, TN).reshape(state_grad_ref.shape)
    c_grad = matmul_pair(grad_from_state, state_ref[...], NN)
    skip_grad_ref[...] = dot_parts(
        jnp.sum(grad_y * ssm_x, axis=0, keepdims=True), spread, 3, NT
    )

    affinity = matmul_pair(input_b, output_c, NT)
    closed = document_mask(first_row, starts_row_ref[...], rows, True)
    affinity_grad = jnp.zeros((rows, rows), jnp.float32)
    sums_ref[...] = jnp.zeros(sums_ref.shape, jnp.float32)
    lane = lax.broadcasted_iota(jnp.int32, (rows, DT_PAD), 1)
    for pair in range(MHEADS // 2):
        found = []
        for head in (2 * pair, 2 * pair + 1):
            columns = slice(head * MHEAD_DIM, (head + 1) * MHEAD_DIM)
            gap = log_rows[head : head + 1, :] - log_decay_now[:, head : head + 1] + closed
            decay = jnp.exp(gap)
            mixing = affinity * decay
            found.append(
                jnp.dot(
                    jnp.concatenate(stacked(mixing, True), axis=1),
                    low_ref[:, columns],
                    preferred_element_type=jnp.float32,
                )
            )
            grad_mixing = jnp.zeros((rows, rows), jnp.float32)
            for one, two in ((0, 0), (1, 0), (0, 2)):
                grad_mixing = grad_mixing + lax.dot_general(
                    input_ref[one * rows : (one + 1) * rows, columns],
                    low_ref[two * rows : (two + 1) * rows, columns],
                    (NT, ((), ())),
                    preferred_element_type=jnp.float32,
                )
            affinity_grad = affinity_grad + grad_mixing * decay
            both = grad_mixing * mixing
            sums_ref[head : head + 1, :] = jnp.sum(both, axis=0, keepdims=True)
            log_grad = log_grad - jnp.where(
                lane == head, jnp.sum(both, axis=1, keepdims=True), 0.0
            )
        columns = slice(2 * pair * MHEAD_DIM, (2 * pair + 2) * MHEAD_DIM)
        input_grad_ref[:, columns] = jnp.concatenate(found, axis=1)
        if pair % 3 == 2:
            tick()
    log_grad_ref[...] = log_grad + jnp.transpose(sums_ref[...])
    b_grad_ref[...] = matmul_pair(affinity_grad, output_c, NN)
    c_grad_ref[...] = c_grad + matmul_pair(jnp.transpose(affinity_grad), input_b, NN)


def mixer_backward_shapes(rows, state_shape):
    f32 = jnp.float32
    shape = jax.ShapeDtypeStruct
    return [
        shape((rows, SSM), jnp.bfloat16),
        shape((1, SSM), f32),
        shape((rows, SSM), f32),
        shape(state_shape, f32),
        shape((rows, SSM), f32),
        shape((rows, STATE), f32),
        shape((rows, STATE), f32),
        shape((rows, DT_PAD), f32),
        shape((1, DT_PAD), f32),
    ]


def mixer_backward_scratch(rows):
    return [
        pltpu.VMEM((2 * rows, SSM), jnp.bfloat16),
        pltpu.VMEM((3 * rows, SSM), jnp.bfloat16),
        pltpu.VMEM((DT_PAD, rows), jnp.float32),
    ]


def mixer_backward(args):
    rows = args[0].shape[0]

    def kernel(*refs):
        mixer_backward_body(*refs, lambda: None)

    return pl.pallas_call(
        kernel,
        out_shape=mixer_backward_shapes(rows, (SSM, STATE)),
        in_specs=[VMEM_SPEC] * 11,
        out_specs=[VMEM_SPEC] * 9,
        scratch_shapes=mixer_backward_scratch(rows),
        compiler_params=BIG_VMEM,
        name="mixer_backward",
    )(*args)


def mixer_input_backward_body(
    end,
    state_ref,
    passing_ref,
    grad_y_ref,
    input_grad_ref,
    b_grad_ref,
    c_grad_ref,
    log_grad_ref,
    pre_ref,
    dt_pre_ref,
    log_ref,
    ext_ref,
    tap_ref,
    a_log_ref,
    skip_ref,
    starts_ref,
    raw_grad_ref,
    tap_grad_ref,
    bias_grad_ref,
    dt_grad_ref,
    dt_sum_ref,
    a_log_grad_ref,
    ext_f32,
    sum_ref,
    tick,
):
    rows = pre_ref.shape[0]
    first_row = lax.axis_index("seq") * rows
    tick()
    pre_now = pre_ref[...]
    sigmoid_pre = jax.nn.sigmoid(pre_now)
    conv_out = pre_now * sigmoid_pre
    ssm_x = conv_out[:, :SSM]
    input_b = conv_out[:, SSM : SSM + STATE]
    spread = head_spread()
    log_decay_now = log_ref[...]
    dt_pre_now = dt_pre_ref[...]
    step_dt = jax.nn.softplus(dt_pre_now)
    step_lanes = dot_parts(step_dt, spread, 2)
    starts_now = starts_ref[...]
    row = lax.broadcasted_iota(jnp.int32, (rows, 1), 0)
    places = first_row + row
    last = log_decay_now[rows - 1 : rows, :]
    last_start = starts_ref[rows - 1 : rows, :]
    weight = jnp.exp(jnp.where(places >= last_start, last - log_decay_now, masked))
    weight_lanes = dot_parts(weight, spread, 2)
    weighted = ssm_x * step_lanes * weight_lanes
    grad_weighted = matmul_pair(input_b, end, NT)
    b_total = b_grad_ref[...] + matmul_pair(weighted, end, NN)
    input_total = input_grad_ref[...] + grad_weighted * weight_lanes
    weight_term = dot_parts(grad_weighted * weighted, spread, 3, NT)
    state_dot = end * state_ref[...]
    passing_grad = jnp.sum(
        jnp.transpose(dot_left(spread, state_dot, 3)), axis=0, keepdims=True
    )
    log_grad_now = log_grad_ref[...] - weight_term
    end_term = jnp.sum(weight_term, axis=0, keepdims=True) + passing_grad * passing_ref[0:1, :]
    log_grad_now = log_grad_now + jnp.where(row == rows - 1, end_term, 0.0)
    order = lax.broadcasted_iota(jnp.int32, (rows, rows), 0)
    other = lax.broadcasted_iota(jnp.int32, (rows, rows), 1)
    upper = jnp.where(other >= order, 1.0, 0.0).astype(jnp.bfloat16)
    step_grad = dot_left(upper, log_grad_now, 3)
    rate = jnp.exp(a_log_ref[...])
    a_log_grad_ref[...] = jnp.sum(-step_dt * rate * step_grad, axis=0, keepdims=True)
    dt_grad = dot_parts(input_total * ssm_x, spread, 3, NT) - rate * step_grad
    dt_raw_grad = dt_grad * jax.nn.sigmoid(dt_pre_now)
    valid = lax.broadcasted_iota(jnp.int32, (rows, DT_PAD), 1) < MHEADS
    dt_raw_grad = jnp.where(valid, dt_raw_grad, 0.0)
    dt_grad_ref[...] = dt_raw_grad.astype(jnp.bfloat16)
    dt_sum_ref[...] = jnp.sum(dt_raw_grad, axis=0, keepdims=True)
    x_grad = input_total * step_lanes + dot_parts(skip_ref[...], spread, 3) * grad_y_ref[...]
    tick()
    slope = sigmoid_pre * (1.0 + pre_now * (1.0 - sigmoid_pre))
    pre_grad = jnp.concatenate([x_grad, b_total, c_grad_ref[...]], axis=1) * slope
    bias_grad_ref[...] = jnp.sum(pre_grad, axis=0, keepdims=True)
    ext_f32[...] = ext_ref[...].astype(jnp.float32)
    sum_ref[...] = jnp.zeros(sum_ref.shape, jnp.float32)
    for tap in range(CONV):
        lag = CONV - 1 - tap
        kept = pre_grad * jnp.where(places - lag >= starts_now, 1.0, 0.0)
        window = slice(HALO - lag, HALO - lag + rows)
        tap_grad_ref[tap : tap + 1, :] = jnp.sum(
            kept * ext_f32[window, :], axis=0, keepdims=True
        )
        sum_ref[window, :] += kept * tap_ref[tap : tap + 1, :]
    raw_grad_ref[...] = sum_ref[...]


def mixer_input_shapes(rows):
    f32 = jnp.float32
    shape = jax.ShapeDtypeStruct
    return [
        shape((HALO + rows, XBC), f32),
        shape((CONV, XBC), f32),
        shape((1, XBC), f32),
        shape((rows, DT_PAD), jnp.bfloat16),
        shape((1, DT_PAD), f32),
        shape((1, DT_PAD), f32),
    ]


def mixer_input_scratch(rows):
    return [pltpu.VMEM((HALO + rows, XBC), jnp.float32) for _ in range(2)]


def mixer_input_backward(args):
    rows = args[8].shape[0]

    def kernel(*refs):
        mixer_input_backward_body(refs[0][...], *refs[1:], lambda: None)

    return pl.pallas_call(
        kernel,
        out_shape=mixer_input_shapes(rows),
        in_specs=[VMEM_SPEC] * 16,
        out_specs=[VMEM_SPEC] * 6,
        scratch_shapes=mixer_input_scratch(rows),
        compiler_params=BIG_VMEM,
        name="mixer_input_backward",
    )(*args)


def feed_forward(hidden, normed_ssm, attention, ffn_gain, cotangent, late):
    rows, model = hidden.shape
    f32, low = jnp.float32, jnp.bfloat16
    ffn = late[0].shape[1]
    span = 1024
    steps = ffn // span

    def layout(flat, gate_up, down, ssm, out):
        pairs = [(flat[3], ssm), (flat[4], out)]
        for number in range(2):
            for start in range(0, ffn, span):
                pairs.append(
                    (
                        flat[number].at[:, pl.ds(start, span)],
                        gate_up.at[:, pl.ds(number * ffn + start, span)],
                    )
                )
        return pairs + [(flat[2], down)]

    kinds = len(late)
    early = 2
    total = early + 2 * steps + 1

    def kernel(*refs):
        hidden_ref, ssm_ref, attn_ref, gain_ref, cot_ref = refs[:5]
        flats = refs[5 : 5 + kinds]
        refs = refs[5 + kinds :]
        layer_ref, mix_ref, attn_grad_ref, ssm_grad_ref, gain_grad_ref = refs[:5]
        grad_flats = refs[5 : 5 + kinds]
        refs = refs[5 + kinds :]
        weights, grads = refs[:4], refs[4:8]
        gate_ref, up_ref, act_ref, two_ref, after_ref, grad_two_ref, in_sem, out_sem = refs[8:]
        w_gate_up, w_down, w_ssm, w_o = weights
        g_gate_up, g_down, g_ssm, g_o = grads
        loads = [
            pltpu.make_async_copy(source, target, in_sem.at[i])
            for i, (source, target) in enumerate(layout(flats, w_gate_up, w_down, w_ssm, w_o))
        ]
        for copy in loads:
            copy.start()
        stores = [
            pltpu.make_async_copy(source, target, out_sem.at[i])
            for i, (target, source) in enumerate(
                layout(grad_flats, g_gate_up, g_down, g_ssm, g_o)
            )
        ]

        def whole(ref, start=0, width=None):
            return ref[:, start : start + (ref.shape[1] if width is None else width)]

        def product(left_side, right_side, axes):
            return lax.dot_general(
                left_side, right_side, (axes, ((), ())), preferred_element_type=f32
            )

        def keep(ref, value, start=0):
            ref[:, start : start + value.shape[1]] = value.astype(low)

        for copy in loads[:early]:
            copy.wait()
        after = (
            hidden_ref[...].astype(f32)
            + product(ssm_ref[...], whole(w_ssm), NN)
            + product(attn_ref[...], whole(w_o), NN)
        )
        after_ref[...] = after
        scale = lax.rsqrt(jnp.mean(after * after, axis=1, keepdims=True) + epsilon)
        two_ref[...] = (after * scale * gain_ref[...]).astype(low)
        for step in range(steps):
            columns = slice(step * span, (step + 1) * span)
            loads[early + step].wait()
            loads[early + steps + step].wait()
            gate = product(two_ref[...], whole(w_gate_up, step * span, span), NN)
            up = product(two_ref[...], whole(w_gate_up, ffn + step * span, span), NN)
            gate_ref[:, columns] = gate
            up_ref[:, columns] = up
            act_ref[:, columns] = (gate * jax.nn.sigmoid(gate) * up).astype(low)
        for copy in loads[early + 2 * steps :]:
            copy.wait()
        layer_ref[...] = (after_ref[...] + product(act_ref[...], whole(w_down), NN)).astype(low)
        cot = cot_ref[...]
        grad_two = jnp.zeros((rows, model), f32)
        for step in range(steps):
            columns = slice(step * span, (step + 1) * span)
            w_part = w_down[columns, :]
            grad_act = product(cot, w_part, NT)
            gate, up = gate_ref[:, columns], up_ref[:, columns]
            sigmoid_gate = jax.nn.sigmoid(gate)
            grad_gate = (
                grad_act * up * sigmoid_gate * (1.0 + gate * (1.0 - sigmoid_gate))
            ).astype(low)
            grad_up = (grad_act * gate * sigmoid_gate).astype(low)
            grad_two = grad_two + product(
                grad_gate, whole(w_gate_up, step * span, span), NT
            )
            grad_two = grad_two + product(
                grad_up, whole(w_gate_up, ffn + step * span, span), NT
            )
            keep(g_gate_up, product(two_ref[...], grad_gate, TN), step * span)
            stores[early + step].start()
            keep(g_gate_up, product(two_ref[...], grad_up, TN), ffn + step * span)
            stores[early + steps + step].start()
        grad_two_ref[...] = grad_two
        keep(g_down, product(act_ref[...], cot, TN))
        for copy in stores[early + 2 * steps :]:
            copy.start()
        after = after_ref[...]
        grad_two = grad_two_ref[...]
        scale = lax.rsqrt(jnp.mean(after * after, axis=1, keepdims=True) + epsilon)
        gain_grad_ref[...] = jnp.sum(after * scale * grad_two, axis=0, keepdims=True)
        scaled = grad_two * gain_ref[...]
        mix = (
            cot.astype(f32)
            + scale * scaled
            - after * (scale * scale * scale * jnp.mean(after * scaled, axis=1, keepdims=True))
        )
        mix_ref[...] = mix
        mix_low = mix.astype(low)
        attn_grad = product(mix_low, whole(w_o), NT).astype(low)
        group_size = QHEADS // KVHEADS
        for head in range(QHEADS):
            place = head % group_size * rows
            attn_grad_ref[head // group_size, place : place + rows, :] = attn_grad[
                :, head * HEAD_DIM : (head + 1) * HEAD_DIM
            ]
        ssm_grad_ref[...] = product(mix_low, whole(w_ssm), NT)
        keep(g_ssm, product(ssm_ref[...], mix_low, TN))
        keep(g_o, product(attn_ref[...], mix_low, TN))
        for copy in stores[:early]:
            copy.start()
        for copy in stores:
            copy.wait()

    shape = jax.ShapeDtypeStruct
    hbm = pl.BlockSpec(memory_space=pl.ANY)
    buffers = [(late[0].shape[0], 2 * ffn)] + [w.shape for w in late[2:]]
    outs = pl.pallas_call(
        kernel,
        out_shape=[
            shape((rows, model), low),
            shape((rows, model), f32),
            shape((KVHEADS, QHEADS // KVHEADS * rows, HEAD_DIM), low),
            shape((rows, SSM), f32),
            shape((1, model), f32),
        ]
        + [shape(w.shape, low) for w in late],
        in_specs=[VMEM_SPEC] * 5 + [hbm] * kinds,
        out_specs=[VMEM_SPEC] * 5 + [hbm] * kinds,
        scratch_shapes=[pltpu.VMEM(size, low) for size in buffers + buffers]
        + [
            pltpu.VMEM((rows, ffn), f32),
            pltpu.VMEM((rows, ffn), f32),
            pltpu.VMEM((rows, ffn), low),
            pltpu.VMEM((rows, model), low),
            pltpu.VMEM((rows, model), f32),
            pltpu.VMEM((rows, model), f32),
            pltpu.SemaphoreType.DMA((total,)),
            pltpu.SemaphoreType.DMA((total,)),
        ],
        compiler_params=BIG_VMEM,
        name="feed_forward",
    )(hidden, normed_ssm, attention, ffn_gain[None], cotangent, *late)
    return outs[:5], outs[5:]


def projection_backward(
    normed_one,
    hidden,
    norm_gain,
    grad_mix,
    grad_gate_z,
    grad_ext,
    returned,
    grad_dt,
    grad_query,
    grad_kv,
    tables,
    weights,
):
    rows, model = hidden.shape
    f32, low = jnp.float32, jnp.bfloat16
    groups = QHEADS // KVHEADS
    half_kv = KVW // 2
    first_row = (lax.axis_index("seq") * rows).astype(jnp.int32).reshape(1)
    widths = [w.shape[1] for w in weights]

    def kernel(
        first_ref,
        normed_ref,
        hidden_ref,
        gain_ref,
        mix_ref,
        gate_ref,
        ext_ref,
        returned_ref,
        dt_ref,
        query_ref,
        kv_ref,
        base_cos_ref,
        base_sin_ref,
        far_cos_ref,
        far_sin_ref,
        *refs,
    ):
        weight_hbm, refs = refs[:3], refs[3:]
        input_ref, gain_grad_ref, refs = refs[0], refs[1], refs[2:]
        weight_grad_hbm, refs = refs[:3], refs[3:]
        weight_refs, weight_grad_refs, refs = refs[:3], refs[3:6], refs[6:]
        xbc_ref, small_ref, turned_ref, in_sem, out_sem = refs
        loads = [
            pltpu.make_async_copy(source, target, in_sem.at[i])
            for i, (source, target) in enumerate(zip(weight_hbm, weight_refs))
        ]
        for copy in loads:
            copy.start()
        stores = [
            pltpu.make_async_copy(source, target, out_sem.at[i])
            for i, (source, target) in enumerate(zip(weight_grad_refs, weight_grad_hbm))
        ]
        edge = rows - HALO
        xbc_ref[:edge, :] = ext_ref[HALO : HALO + edge, :].astype(low)
        xbc_ref[edge:, :] = (ext_ref[HALO + edge :, :] + returned_ref[...]).astype(low)
        for head in range(QHEADS):
            place = head % groups * rows
            turned_ref[:, head * HEAD_DIM : (head + 1) * HEAD_DIM] = jnp.transpose(
                query_ref[head // groups, :, place : place + rows]
            )
        cosine_all, sine_all = rope_now(
            first_ref[0] // rows, base_cos_ref, base_sin_ref, far_cos_ref, far_sin_ref
        )
        sine_all = -sine_all
        small_ref[:, :QW] = rope_lanes(
            turned_ref[...] * HEAD_DIM ** (-0.5), cosine_all, sine_all
        ).astype(low)
        kv = kv_ref[...]
        small_ref[:, QW : QW + half_kv] = rope_lanes(kv[:, :half_kv], cosine_all, sine_all).astype(
            low
        )
        small_ref[:, QW + half_kv : QW + KVW] = kv[:, half_kv:].astype(low)
        small_ref[:, QW + KVW :] = dt_ref[...]
        normed = normed_ref[...]
        grad_normed = jnp.zeros((rows, model), f32)
        for number, value_ref in enumerate((gate_ref, xbc_ref, small_ref)):
            loads[number].wait()
            for start in range(0, widths[number], 512):
                columns = slice(start, min(start + 512, widths[number]))
                part = value_ref[:, columns]
                grad_normed = grad_normed + lax.dot_general(
                    part,
                    weight_refs[number][:, columns],
                    (NT, ((), ())),
                    preferred_element_type=f32,
                )
                weight_grad_refs[number][:, columns] = lax.dot_general(
                    normed, part, (TN, ((), ())), preferred_element_type=f32
                ).astype(low)
            stores[number].start()
        values = hidden_ref[...].astype(f32)
        scale = lax.rsqrt(jnp.mean(values * values, axis=1, keepdims=True) + epsilon)
        gain_grad_ref[...] = jnp.sum(values * scale * grad_normed, axis=0, keepdims=True)
        scaled = grad_normed * gain_ref[...]
        input_ref[...] = (
            mix_ref[...]
            + scale * scaled
            - values * (scale * scale * scale * jnp.mean(values * scaled, axis=1, keepdims=True))
        ).astype(low)
        for copy in stores:
            copy.wait()

    shape = jax.ShapeDtypeStruct
    hbm = pl.BlockSpec(memory_space=pl.ANY)
    return pl.pallas_call(
        kernel,
        out_shape=[shape((rows, model), low), shape((1, model), f32)]
        + [shape(w.shape, low) for w in weights],
        in_specs=[pl.BlockSpec(memory_space=pltpu.SMEM)] + [VMEM_SPEC] * 14 + [hbm] * 3,
        out_specs=[VMEM_SPEC] * 2 + [hbm] * 3,
        scratch_shapes=[pltpu.VMEM(w.shape, low) for w in list(weights) * 2]
        + [
            pltpu.VMEM((rows, XBC), low),
            pltpu.VMEM((rows, QW + KVW + DT_PAD), low),
            pltpu.VMEM((rows, QW), f32),
            pltpu.SemaphoreType.DMA((3,)),
            pltpu.SemaphoreType.DMA((3,)),
        ],
        compiler_params=BIG_VMEM,
        name="projection_backward",
    )(
        first_row,
        normed_one,
        hidden,
        norm_gain[None],
        grad_mix,
        grad_gate_z,
        grad_ext,
        returned,
        grad_dt,
        grad_query,
        grad_kv,
        *tables,
        *weights,
    )


def projection_scatter(
    normed_one,
    hidden,
    norm_gain,
    grad_mix,
    grad_gate_z,
    grad_ext,
    grad_dt,
    grad_query,
    grad_kv,
    tables,
    weights,
    small_parts,
    small_rows,
    collective_id,
    target,
):
    rows, model = hidden.shape
    f32, low = jnp.float32, jnp.bfloat16
    groups = QHEADS // KVHEADS
    half_kv = KVW // 2
    first_row = (lax.axis_index("seq") * rows).astype(jnp.int32).reshape(1)
    widths = [w.shape[1] for w in weights]
    count = lax.axis_size("seq")
    sizes = lattice(count)
    shapes = [(w.shape[0] // count, w.shape[1]) for w in weights]
    small = jax.ShapeDtypeStruct((small_rows, 128), jnp.float32)
    plans = [
        scatter_plan([s], small if number == 1 else None, target)
        for number, s in enumerate(shapes)
    ]

    def kernel(
        first_ref,
        normed_ref,
        hidden_ref,
        gain_ref,
        mix_ref,
        gate_ref,
        ext_ref,
        dt_ref,
        query_ref,
        kv_ref,
        base_cos_ref,
        base_sin_ref,
        far_cos_ref,
        far_sin_ref,
        *refs,
    ):
        small_in, refs = refs[: len(small_parts)], refs[len(small_parts) :]
        weight_hbm, refs = refs[:3], refs[3:]
        input_ref, shard_refs, small_out, refs = refs[0], refs[1:4], refs[4], refs[5:]
        weight_refs, weight_grad_refs, refs = refs[:3], refs[3:6], refs[6:]
        xbc_ref, small_ref, turned_ref, returned_ref, small_vmem, in_sem, edge_sems = refs[:7]
        refs = refs[7:]
        runs = []
        for number, (program, scratch) in enumerate(plans):
            mine, refs = refs[: len(scratch)], refs[len(scratch) :]
            has_small = number == 1
            runs.append(
                program(
                    [weight_grad_refs[number]],
                    [small_vmem] if has_small else [],
                    [shard_refs[number]],
                    [small_out] if has_small else [],
                    mine,
                )
            )
        me = lax.axis_index("seq")
        following, previous = lax.rem(me + 1, count), lax.rem(me + count - 1, count)
        loads = [
            pltpu.make_async_copy(source, target, in_sem.at[i])
            for i, (source, target) in enumerate(zip(weight_hbm, weight_refs))
        ]
        for copy in loads:
            copy.start()
        greet(sizes, coordinates(sizes), [following, previous])
        edge_copy = pltpu.make_async_remote_copy(
            src_ref=ext_ref.at[pl.ds(0, HALO), :],
            dst_ref=returned_ref,
            send_sem=edge_sems.at[0],
            recv_sem=edge_sems.at[1],
            device_id=(previous,),
            device_id_type=MESH,
        )
        edge_copy.start()
        small_vmem[...] = jnp.zeros(small.shape, f32)
        row = model // 128
        for part_ref in small_in:
            for line in range(part_ref.shape[0]):
                for step in range(part_ref.shape[1] // 128):
                    small_vmem[row : row + 1, :] = part_ref[
                        line : line + 1, step * 128 : (step + 1) * 128
                    ]
                    row += 1
        edge = rows - HALO
        xbc_ref[:edge, :] = ext_ref[HALO : HALO + edge, :].astype(low)
        for head in range(QHEADS):
            place = head % groups * rows
            turned_ref[:, head * HEAD_DIM : (head + 1) * HEAD_DIM] = jnp.transpose(
                query_ref[head // groups, :, place : place + rows]
            )
        cosine_all, sine_all = rope_now(
            first_ref[0] // rows, base_cos_ref, base_sin_ref, far_cos_ref, far_sin_ref
        )
        sine_all = -sine_all
        small_ref[:, :QW] = rope_lanes(
            turned_ref[...] * HEAD_DIM ** (-0.5), cosine_all, sine_all
        ).astype(low)
        kv = kv_ref[...]
        small_ref[:, QW : QW + half_kv] = rope_lanes(kv[:, :half_kv], cosine_all, sine_all).astype(
            low
        )
        small_ref[:, QW + half_kv : QW + KVW] = kv[:, half_kv:].astype(low)
        small_ref[:, QW + KVW :] = dt_ref[...]
        normed = normed_ref[...]
        grad_normed = jnp.zeros((rows, model), f32)
        for number, value_ref in ((0, gate_ref), (2, small_ref), (1, xbc_ref)):
            loads[number].wait()
            if number == 1:
                edge_copy.wait()
                xbc_ref[edge:, :] = (ext_ref[HALO + edge :, :] + returned_ref[...]).astype(low)
            for start in range(0, widths[number], 512):
                columns = slice(start, min(start + 512, widths[number]))
                part = value_ref[:, columns]
                weight_grad_refs[number][..., columns] = (
                    lax.dot_general(normed, part, (TN, ((), ())), preferred_element_type=f32)
                    .astype(low)
                    .reshape(*sizes, shapes[number][0], part.shape[1])
                )
            next(runs[number])
            for start in range(0, widths[number], 512):
                columns = slice(start, min(start + 512, widths[number]))
                grad_normed = grad_normed + lax.dot_general(
                    value_ref[:, columns],
                    weight_refs[number][:, columns],
                    (NT, ((), ())),
                    preferred_element_type=f32,
                )
            if number != 1:
                next(runs[number])
        values = hidden_ref[...].astype(f32)
        scale = lax.rsqrt(jnp.mean(values * values, axis=1, keepdims=True) + epsilon)
        gain_grad = jnp.sum(values * scale * grad_normed, axis=0, keepdims=True)
        for step in range(model // 128):
            small_vmem[step : step + 1, :] = gain_grad[:, step * 128 : (step + 1) * 128]
        scaled = grad_normed * gain_ref[...]
        input_ref[...] = (
            mix_ref[...]
            + scale * scaled
            - values * (scale * scale * scale * jnp.mean(values * scaled, axis=1, keepdims=True))
        ).astype(low)
        run_together([runs[1], runs[0], runs[2]])

    shape = jax.ShapeDtypeStruct
    hbm = pl.BlockSpec(memory_space=pl.ANY)
    return pl.pallas_call(
        kernel,
        out_shape=[shape((rows, model), low)]
        + [shape(s, f32) for s in shapes]
        + [shape(small.shape, f32)],
        in_specs=[pl.BlockSpec(memory_space=pltpu.SMEM)]
        + [VMEM_SPEC] * (13 + len(small_parts))
        + [hbm] * 3,
        out_specs=[VMEM_SPEC] * 5,
        scratch_shapes=[pltpu.VMEM(w.shape, low) for w in weights]
        + [pltpu.VMEM(sizes + s, low) for s in shapes]
        + [
            pltpu.VMEM((rows, XBC), low),
            pltpu.VMEM((rows, QW + KVW + DT_PAD), low),
            pltpu.VMEM((rows, QW), f32),
            pltpu.VMEM((HALO, XBC), f32),
            pltpu.VMEM(small.shape, f32),
            pltpu.SemaphoreType.DMA((3,)),
            pltpu.SemaphoreType.DMA((2,)),
        ]
        + [item for _, scratch in plans for item in scratch],
        compiler_params=pltpu.CompilerParams(
            collective_id=collective_id,
            has_side_effects=True,
            vmem_limit_bytes=62 * 1024 * 1024,
        ),
        name="projection_scatter",
    )(
        first_row,
        normed_one,
        hidden,
        norm_gain[None],
        grad_mix,
        grad_gate_z,
        grad_ext,
        grad_dt,
        grad_query,
        grad_kv,
        *tables,
        *small_parts,
        *weights,
    )


def finish(shard_z, shard_xbc, shard_small, small_sum, late_sums, lengths):
    f32 = jnp.float32
    shape = jax.ShapeDtypeStruct
    rows = shard_z.shape[0]
    starts = [sum(lengths[:i]) // 128 for i in range(len(lengths))]
    tail = sum(lengths) // 128
    tap_rows = XBC // 128
    model_rows, ssm_rows = lengths[0] // 128, lengths[1] // 128

    def kernel(z_ref, xbc_ref, small_ref, sum_ref, *refs):
        late, refs = refs[: len(late_sums)], refs[len(late_sums) :]
        outs, refs = refs[: len(late_sums)], refs[len(late_sums) :]
        for source, target in zip(late, outs):
            target[...] = source[...]
        z_out, xbc_out, q_out, kv_out, dt_out, *vectors, tap_out, three_out = refs
        z_out[...] = z_ref[...]
        xbc_out[...] = xbc_ref[...]
        q_out[...] = small_ref[:, :QW]
        kv_out[...] = small_ref[:, QW : QW + KVW]
        dt_out[...] = small_ref[:, QW + KVW :]
        for target, start in zip(vectors, (starts[0], starts[1], starts[2], starts[4])):
            target[...] = sum_ref[start : start + target.shape[0], :]
        for tap in range(CONV):
            for step in range(tap_rows):
                row = starts[3] + tap * tap_rows + step
                tap_out[tap : tap + 1, step * 128 : (step + 1) * 128] = sum_ref[row : row + 1, :]
        three_out[...] = sum_ref[tail : tail + 8, :]

    results = pl.pallas_call(
        kernel,
        out_shape=[shape(s.shape, f32) for s in late_sums]
        + [shape(shard_z.shape, f32), shape(shard_xbc.shape, f32)]
        + [shape((rows, width), f32) for width in (QW, KVW, DT_PAD)]
        + [shape((n, 128), f32) for n in (model_rows, ssm_rows, model_rows, tap_rows)]
        + [shape((CONV, XBC), f32), shape((8, 128), f32)],
        in_specs=[VMEM_SPEC] * (4 + len(late_sums)),
        out_specs=[VMEM_SPEC] * (11 + len(late_sums)),
        name="finish",
    )(shard_z, shard_xbc, shard_small, small_sum, *late_sums)
    return results[: len(late_sums)], results[len(late_sums) :]


def per_device(
    hidden_in,
    doc_start,
    norm_gain,
    w_z,
    w_xbc,
    w_dt,
    conv_weight,
    conv_bias,
    dt_bias,
    a_log,
    d_skip,
    ssm_gain,
    w_ssm_out,
    w_q,
    w_kv,
    w_o,
    ffn_gain,
    w_gate,
    w_up,
    w_down,
    cotangent,
):
    local_rows, model = hidden_in.shape
    count = lax.axis_size("seq")
    small_shard = jnp.concatenate(
        [w_q, w_kv, jnp.pad(w_dt, ((0, 0), (0, DT_PAD - MHEADS)))], axis=1
    )
    *mixer_weights, halo = gather_everywhere(
        [w_xbc, small_shard, w_z], 0, 12288, hidden_in
    )
    mixer_weights = [mixer_weights[2], mixer_weights[0], mixer_weights[1]]

    tables = rope_table(local_rows, count)
    dt_bias_row = jnp.pad(dt_bias, (0, DT_PAD - MHEADS))[None]
    a_log_row = jnp.pad(a_log, (0, DT_PAD - MHEADS))[None]
    skip_row = jnp.pad(d_skip, (0, DT_PAD - MHEADS))[None]
    row_starts = doc_start[None]
    kv_all, states_in, chip_decay, late, computed = front(
        [
            hidden_in,
            halo,
            norm_gain[None],
            *mixer_weights,
            conv_weight,
            conv_bias[None],
            dt_bias_row,
            a_log_row,
            doc_start[:, None],
            *tables,
        ],
        [w_gate, w_up, w_down, w_ssm_out, w_o],
        [ssm_gain[None], skip_row, doc_start[:, None]],
        row_starts,
        1,
        (16384, 16384),
    )
    normed_one, gate_z, xbc_ext, conv_pre, grouped_q, dt_pre, log_decay, passing = computed[:8]
    normed_ssm, ssm_y, attn_grouped, log_total, attn_low = computed[8:]
    (layer_out, grad_mix, grad_attn_grouped, grad_normed_ssm, grad_ffn_gain), late_grads = (
        feed_forward(hidden_in, normed_ssm, attn_low, ffn_gain, cotangent, late)
    )
    key_terms, grad_query_grouped, late_sums = attention_backward(
        grouped_q,
        grad_attn_grouped,
        kv_all,
        row_starts,
        log_total,
        attn_grouped,
        late_grads[:2],
        4,
        16384,
    )
    shard_gate, shard_up = late_sums

    grad_kv_local, late_sums, mixer_out = back(
        key_terms,
        [
            grad_normed_ssm,
            ssm_y,
            gate_z,
            ssm_gain[None],
            conv_pre,
            dt_pre,
            log_decay,
            states_in,
            skip_row,
            doc_start[:, None],
            doc_start[None],
        ],
        [xbc_ext, conv_weight, a_log_row],
        passing,
        chip_decay,
        late_grads[2:],
        2,
        (16384, 8192),
    )
    shard_down, shard_ssm_out, shard_o = late_sums
    (
        grad_gate_z,
        grad_ssm_gain,
        grad_d_skip,
        grad_ext,
        grad_conv_weight,
        grad_conv_bias,
        grad_dt_raw,
        grad_dt_bias,
        grad_a_log,
    ) = mixer_out
    rows_small = -(-(model // 128 * 2 + SSM // 128 + (CONV + 1) * XBC // 128 + 8) // 8) * 8
    lengths = [model, SSM, model, CONV * XBC, XBC]
    small_parts = [
        grad_ssm_gain,
        grad_ffn_gain,
        grad_conv_weight,
        grad_conv_bias,
        grad_dt_bias,
        grad_a_log,
        grad_d_skip,
    ]
    grad_args = (
        normed_one,
        hidden_in,
        norm_gain,
        grad_mix,
        grad_gate_z,
        grad_ext,
    )
    last_args = (grad_dt_raw, grad_query_grouped, grad_kv_local, tables, mixer_weights)
    if w_gate.shape[0] % 16 == 0:
        grad_input, shard_z, shard_xbc, shard_small, small_sum = projection_scatter(
            *grad_args, *last_args, small_parts, rows_small, 3, 12288
        )
    else:
        returned = from_behind(grad_ext[:HALO], "seq", -1)
        grad_input, grad_norm_gain, *mixer_grads = projection_backward(
            *grad_args, returned, *last_args
        )
        small = jnp.concatenate(
            [part.reshape(-1, 128) for part in [grad_norm_gain] + small_parts], axis=0
        )
        small = jnp.pad(small, ((0, rows_small - small.shape[0]), (0, 0)))
        shard_z, shard_xbc, shard_small, small_sum = scatter_sums(mixer_grads, small, 3, 8192)
    late_shards, others = finish(
        shard_z,
        shard_xbc,
        shard_small,
        small_sum,
        [shard_gate, shard_up, shard_down, shard_ssm_out, shard_o],
        lengths,
    )
    shard_gate, shard_up, shard_down, shard_ssm_out, shard_o = late_shards
    shard_z, shard_xbc, shard_q, shard_kv, shard_dt, *vectors, sum_taps, sum_three = others
    sum_norm, sum_ssm_gain, sum_ffn_gain, sum_conv_bias = [v.reshape(-1) for v in vectors]
    return (
        layer_out,
        grad_input,
        sum_norm,
        shard_z,
        shard_xbc,
        shard_dt[:, :MHEADS],
        sum_taps,
        sum_conv_bias,
        sum_three[0, :MHEADS],
        sum_three[1, :MHEADS],
        sum_three[2, :MHEADS],
        sum_ssm_gain,
        shard_ssm_out,
        shard_q,
        shard_kv,
        shard_o,
        sum_ffn_gain,
        shard_gate,
        shard_up,
        shard_down,
    )


def solution(mesh):
    placed = (
        P("seq", None),
        P("seq"),
        P(),
        P("seq", None),
        P("seq", None),
        P("seq", None),
        P(),
        P(),
        P(),
        P(),
        P(),
        P(),
        P("seq", None),
        P("seq", None),
        P("seq", None),
        P("seq", None),
        P(),
        P("seq", None),
        P("seq", None),
        P("seq", None),
        P("seq", None),
    )
    return jax.shard_map(
        per_device,
        mesh=mesh,
        in_specs=placed,
        out_specs=(
            P("seq", None),
            P("seq", None),
            P(),
            P("seq", None),
            P("seq", None),
            P("seq", None),
            P(),
            P(),
            P(),
            P(),
            P(),
            P(),
            P("seq", None),
            P("seq", None),
            P("seq", None),
            P("seq", None),
            P(),
            P("seq", None),
            P("seq", None),
            P("seq", None),
        ),
        check_vma=False,
    )
```
